32 devices in a mesh: seq: 8 (over z, x), tp: 4 (over y, core).
Axes of the slice: x: 2, y: 2, z: 4, core: 2. Of those that a mesh axis runs over, the one named last changes fastest.
Arguments:
- layer_input: bfloat16 [2, 4096, 768], P(None, 'seq'), may hold values from -8 to 8
- out_grad: bfloat16 [2, 4096, 768], P(None, 'seq'), may hold values from -6 to 6
- norm1_gain: float32 [768], replicated, may hold values from 0.5 to 1.5
- norm1_shift: float32 [768], replicated, may hold values from -1 to 1
- w_qkv: bfloat16 [768, 3, 768], P(None, None, 'tp'), may hold values from -0.21875 to 0.21875
- w_out: bfloat16 [768, 768], P(None, 'tp'), may hold values from -0.875 to 0.875
- norm2_gain: float32 [768], replicated, may hold values from 0.5 to 1.5
- norm2_shift: float32 [768], replicated, may hold values from -1 to 1
- w_up: bfloat16 [768, 3072], P(None, 'tp'), may hold values from -0.21875 to 0.21875
- w_down: bfloat16 [768, 3072], P(None, 'tp'), may hold values from -0.21875 to 0.21875
- key_keep: int32 [2, 4096], replicated, may hold values from 0 to 1, as said below
- rand_blocks: int32 [2, 64, 3], replicated, may hold values from 0 to 63, as said below
Outputs:
- layer_output: float32 [2, 4096, 768], P(None, ('seq', 'tp'))
- input_grad: float32 [2, 4096, 768], P(None, ('seq', 'tp'))
- grad_w_qkv: float32 [768, 3, 768], P('seq', None, 'tp')
- grad_w_out: float32 [768, 768], P('seq', 'tp')
- grad_w_up: float32 [768, 3072], P('seq', 'tp')
- grad_w_down: float32 [768, 3072], P('seq', 'tp')
- grad_norm1_gain: float32 [768], P('seq')
- grad_norm1_shift: float32 [768], P('seq')
- grad_norm2_gain: float32 [768], P('seq')
- grad_norm2_shift: float32 [768], P('seq')
The draws below stay inside these ranges and needn't reach their ends.
Inputs may be any that keep to these rules, and one draw needn't show every extreme that they name: `key_keep`: in every block of 64 positions the kept positions come first, 16 or more of them. `rand_blocks`: entry [m, b, j] names a key block of sequence m. Over all 2 sequences, the random blocks of the query blocks held by one index of seq lie on any one index at most 6 times, and exactly 6 times on some index.
All inputs are finite; a program needn't handle non-finite values.
Results may differ from the reference program's by a relative error of at most 0.012.
Values may be sent and summed in bfloat16 or wider, within the bound.
No kernel may reach another device: no remote copies, remote signals or barrier semaphores. Data moves between devices by JAX's collectives and lax.ppermute only.
A program may use at most 384 MiB of HBM per device.

```python
import math
import jax
import jax.numpy as jnp
from jax import lax

D = 768
HEADS = 12
HEAD_DIM = 64
FF = 3072
BLOCK = 64
RANDS = 3
NBLOCKS = 64
BLK_DEV = 8
TOKENS = 4096
SEQS = 2
CAP = 6
N_SEQ = 8


def draw_layer_input(key, part):
    key = jax.random.fold_in(key, 31)
    noise_key, dir_key = jax.random.split(key)
    ramp = jnp.linspace(-1.0, 1.0, TOKENS, dtype=jnp.float32)[None, :, None]
    direction = jax.random.normal(dir_key, (1, 1, D), jnp.float32)
    noise = jax.random.normal(noise_key, (SEQS, TOKENS, D), jnp.float32)
    return jnp.clip(noise + ramp * direction, -8.0, 8.0).astype(jnp.bfloat16)


def draw_key_keep(key, part):
    key = jax.random.fold_in(key, 11)
    counts = jax.random.randint(key, (SEQS, NBLOCKS, 1), BLOCK // 4, BLOCK + 1)
    position = jnp.arange(BLOCK, dtype=jnp.int32)[None, None, :]
    return (position < counts).astype(jnp.int32).reshape(SEQS, NBLOCKS * BLOCK)


def draw_rand_blocks(key, part):
    key = jax.random.fold_in(key, 23)
    ref_count = SEQS * BLK_DEV * RANDS

    def one_device(device_key):
        owner_key, local_key = jax.random.split(device_key)
        slots = jnp.tile(jnp.arange(N_SEQ, dtype=jnp.int32), CAP)
        owners = jax.random.permutation(owner_key, slots)[:ref_count]
        lead_owner = owners[0]
        lead_count = jnp.sum((owners == lead_owner).astype(jnp.int32))
        second = jnp.where(lead_count < CAP, lead_owner, owners[1])
        owners = owners.at[1].set(second)
        local = jax.random.randint(local_key, (ref_count,), 0, BLK_DEV)
        return (owners * BLK_DEV + local).reshape(SEQS, BLK_DEV, RANDS)
    device_keys = jax.random.split(key, N_SEQ)
    ref_table = jax.vmap(one_device)(device_keys)
    return jnp.transpose(ref_table, (1, 0, 2, 3)).reshape(SEQS, N_SEQ * BLK_DEV, RANDS).astype(jnp.int32)


def level_of(rng, dims, shards, smallest, largest):
    level, own = 1.0, jax.random.fold_in(rng, 6)
    for axis_at, parts in shards:
        steps = jnp.exp(jax.random.uniform(jax.random.fold_in(own, axis_at), (parts,), jnp.float32, smallest / len(shards), largest / len(shards)))
        level = level * jnp.repeat(steps, dims[axis_at] // parts).reshape([-1 if axis == axis_at else 1 for axis in range(len(dims))])
    return level


def centred(stream_key, dims, deviation, limit, cuts=(), kind=jnp.bfloat16):
    values = deviation * jax.random.normal(stream_key, dims, jnp.float32)
    if cuts:
        values = values * level_of(stream_key, dims, cuts, -0.22, 0.18)
    return jnp.clip(values, -limit, limit).astype(kind)


def setup_inputs(seed: int = 0) -> dict:
    seeds = jax.random.split(jax.random.key(seed), 13)
    layer_input = draw_layer_input(jax.random.fold_in(seeds[12], 71), 0)
    out_grad = centred(seeds[1], (SEQS, TOKENS, D), 1.0, 6.0, ((1, 8),))
    norm1_gain = jnp.clip(1.0 + 0.1 * jax.random.normal(seeds[2], (D,), jnp.float32), 0.5, 1.5)
    norm1_shift = centred(seeds[3], (D,), 0.2, 1.0, (), jnp.float32)
    w_qkv = centred(seeds[4], (D, 3, D), D ** -0.5, 0.21875, ((2, 4),))
    w_out = centred(seeds[5], (D, D), (D // 16) ** -0.5, 0.875, ((1, 4),))
    norm2_gain = jnp.clip(1.0 + 0.1 * jax.random.normal(seeds[6], (D,), jnp.float32), 0.5, 1.5)
    norm2_shift = centred(seeds[7], (D,), 0.2, 1.0, (), jnp.float32)
    w_up = centred(seeds[8], (D, FF), D ** -0.5, 0.21875, ((1, 4),))
    w_down = centred(seeds[9], (D, FF), (FF // 4) ** -0.5, 0.21875, ((1, 4),))
    key_keep = draw_key_keep(jax.random.fold_in(seeds[12], 71), 0)
    rand_blocks = draw_rand_blocks(jax.random.fold_in(seeds[12], 71), 0)
    return dict(layer_input=layer_input, out_grad=out_grad, norm1_gain=norm1_gain, norm1_shift=norm1_shift, w_qkv=w_qkv, w_out=w_out, norm2_gain=norm2_gain, norm2_shift=norm2_shift, w_up=w_up, w_down=w_down, key_keep=key_keep, rand_blocks=rand_blocks)


EPS = 1e-06
HIGH = lax.Precision.HIGHEST

@jax.custom_vjp
def low(v):
    return lax.optimization_barrier(v.astype(jnp.bfloat16)).astype(jnp.float32)

@jax.custom_vjp
def low_back(v):
    return v

def low_keep(v):
    return (low(v), None)

def low_pass(kept, grad):
    return (grad,)

def back_keep(v):
    return (v, None)

def back_low(kept, grad):
    return (low(grad),)
low.defvjp(low_keep, low_pass)
low_back.defvjp(back_keep, back_low)

def rounded_both(value):
    return low_back(low(value))

def normalize(hidden, gain, shift):
    center = hidden - lax.optimization_barrier(jnp.mean(hidden, -1, keepdims=True))
    return center * lax.rsqrt(lax.optimization_barrier(jnp.mean(center * center, -1, keepdims=True)) + EPS) * gain + shift

def attend(packed):
    proj_qkv, keep_mask, rand_rows = packed
    inv_root = 1.0 / math.sqrt(HEAD_DIM)
    blocks = proj_qkv.reshape(NBLOCKS, BLOCK, 3, HEADS, HEAD_DIM)
    block_ids = jnp.arange(NBLOCKS, dtype=jnp.int32)[:, None]
    listed = jnp.concatenate([block_ids - 1, block_ids, block_ids + 1, block_ids * 0, block_ids * 0 + (NBLOCKS - 1), rand_rows.astype(jnp.int32)], axis=1)
    inside = ((listed >= 0) & (listed < NBLOCKS)).astype(jnp.float32)
    clipped = jnp.clip(listed, 0, NBLOCKS - 1)
    keep_blocks = keep_mask.reshape(NBLOCKS, BLOCK)
    weight = (inside[:, :, None] * keep_blocks[clipped]).reshape(NBLOCKS, -1)
    chosen = blocks[clipped]
    key_rows = chosen[:, :, :, 1].reshape(NBLOCKS, -1, HEADS, HEAD_DIM)
    value_rows = chosen[:, :, :, 2].reshape(NBLOCKS, -1, HEADS, HEAD_DIM)
    queries = blocks[:, :, 0]
    scores = low_back(jnp.einsum('nqhd,nkhd->nhqk', queries, key_rows, precision=HIGH) * inv_root)
    row_top = lax.optimization_barrier(jnp.max(scores, -1, keepdims=True))
    expo_rows = jnp.exp(scores - row_top) * weight[:, None, None, :]
    prob_rows = low(expo_rows / lax.optimization_barrier(jnp.sum(expo_rows, -1, keepdims=True)))
    sparse = jnp.einsum('nhqk,nkhd->nqhd', prob_rows, value_rows, precision=HIGH).reshape(TOKENS, HEADS * HEAD_DIM)
    lead_q = jnp.concatenate([blocks[0, :, 0], blocks[NBLOCKS - 1, :, 0]], axis=0)
    all_keys = proj_qkv[:, 1].reshape(TOKENS, HEADS, HEAD_DIM)
    all_values = proj_qkv[:, 2].reshape(TOKENS, HEADS, HEAD_DIM)
    lead_scores = low_back(jnp.einsum('qhd,khd->hqk', lead_q, all_keys, precision=HIGH) * inv_root)
    lead_top = lax.optimization_barrier(jnp.max(lead_scores, -1, keepdims=True))
    lead_expo = jnp.exp(lead_scores - lead_top) * keep_mask[None, None, :]
    lead_probs = lead_expo / lax.optimization_barrier(jnp.sum(lead_expo, -1, keepdims=True))
    lead_out = jnp.einsum('hqk,khd->qhd', lead_probs, all_values, precision=HIGH).reshape(2 * BLOCK, HEADS * HEAD_DIM)
    return jnp.concatenate([lead_out[:BLOCK], sparse[BLOCK:TOKENS - BLOCK], lead_out[BLOCK:]], axis=0)

def layer_fwd(hidden0, gain1, shift1, weight_qkv, weight_out, gain2, shift2, weight_up, weight_down, keep_mask, rand_rows):
    first_act = low(normalize(hidden0, gain1, shift1))
    proj_qkv = rounded_both(jnp.einsum('mtd,dcf->mtcf', first_act, weight_qkv, precision=HIGH))
    attended = lax.map(jax.checkpoint(attend), (proj_qkv, keep_mask, rand_rows))
    attn_mixed = rounded_both(attended)
    attn_branch = low_back(jnp.einsum('mtf,df->mtd', attn_mixed, weight_out, precision=HIGH))
    hidden1 = hidden0 + attn_branch
    second_act = low(normalize(hidden1, gain2, shift2))
    pre_act = low_back(jnp.einsum('mtd,df->mtf', second_act, weight_up, precision=HIGH))
    up_act = low(jax.nn.gelu(pre_act, approximate=False))
    ffn_branch = low_back(jnp.einsum('mtf,df->mtd', up_act, weight_down, precision=HIGH))
    return hidden1 + ffn_branch

def reference(layer_input, out_grad, norm1_gain, norm1_shift, w_qkv, w_out, norm2_gain, norm2_shift, w_up, w_down, key_keep, rand_blocks):
    keep_mask = key_keep.astype(jnp.float32)

    def forward(hidden0, gain1, shift1, weight_qkv, weight_out, gain2, shift2, weight_up, weight_down):
        return layer_fwd(hidden0, gain1, shift1, weight_qkv, weight_out, gain2, shift2, weight_up, weight_down, keep_mask, rand_blocks)
    primals = (layer_input.astype(jnp.float32), norm1_gain.astype(jnp.float32), norm1_shift.astype(jnp.float32), w_qkv.astype(jnp.float32), w_out.astype(jnp.float32), norm2_gain.astype(jnp.float32), norm2_shift.astype(jnp.float32), w_up.astype(jnp.float32), w_down.astype(jnp.float32))
    result, pullback = jax.vjp(forward, *primals)
    cotangents = pullback(out_grad.astype(jnp.float32))
    return (result, cotangents[0], cotangents[3], cotangents[4], cotangents[7], cotangents[8], cotangents[1], cotangents[2], cotangents[5], cotangents[6])
```

```python
from functools import partial
import math

import jax
import jax.numpy as jnp
from jax import lax
from jax.experimental import pallas as pl
from jax.experimental.pallas import tpu as pltpu
from jax.sharding import PartitionSpec as P

HD = 64
BLOCK = 64
RANDS = 3
EPS = 1e-06
SWAP = (0, 2, 1, 3)
NEG = -1e30
F32 = jnp.float32
BF16 = jnp.bfloat16
VMEM = pl.BlockSpec(memory_space=pltpu.VMEM)
SMEM = pl.BlockSpec(memory_space=pltpu.SMEM)
PARAMS = pltpu.CompilerParams(vmem_limit_bytes=56 * 1024 * 1024)


def sds(shape, kind):
    return jax.ShapeDtypeStruct(shape, kind)


def call(body, outs, scratch=(), name=None):
    def run(*args, smem=()):
        specs = [SMEM] * len(smem) + [VMEM] * len(args)
        return pl.pallas_call(
            body,
            out_shape=outs,
            in_specs=specs,
            out_specs=jax.tree.map(lambda _: VMEM, outs),
            scratch_shapes=list(scratch),
            compiler_params=PARAMS,
            name=name,
        )(*smem, *args)

    return run


def dot_nt(a, b):
    return lax.dot_general(a, b, (((1,), (1,)), ((), ())), preferred_element_type=F32)


def dot_tn(a, b):
    return lax.dot_general(a, b, (((0,), (0,)), ((), ())), preferred_element_type=F32)


def dot_nn(a, b):
    return lax.dot_general(a, b, (((1,), (0,)), ((), ())), preferred_element_type=F32)


def two_heads(tile):
    lane = lax.broadcasted_iota(jnp.int32, tile.shape, 1)
    zero = jnp.zeros_like(tile)
    return jnp.concatenate([jnp.where(lane < HD, tile, zero), jnp.where(lane >= HD, tile, zero)], 0)


def pick_heads(pair, rows):
    lane = lax.broadcasted_iota(jnp.int32, (rows, 2 * HD), 1)
    return jnp.where(lane < HD, pair[:rows], pair[rows:])


def half(tile, upper):
    lane = lax.broadcasted_iota(jnp.int32, tile.shape, 1)
    return jnp.where((lane >= HD) if upper else (lane < HD), tile, jnp.zeros_like(tile))


def lanes_of(columns, rows):
    lane = lax.broadcasted_iota(jnp.int32, (rows, 2 * HD), 1)
    out = jnp.zeros((rows, 2 * HD), F32)
    for at, column in enumerate(columns):
        out = jnp.where(lane == at, column, out)
    return out


def hi_lo(value):
    hi = value.astype(BF16).astype(F32)
    return hi, value - hi


def norm_rows(hidden):
    center = hidden - jnp.mean(hidden, -1, keepdims=True)
    inverse = lax.rsqrt(jnp.mean(center * center, -1, keepdims=True) + EPS)
    return center * inverse, inverse


def norm_rows_back(grad, normed, inverse, gain):
    scaled = grad * gain
    return inverse * (
        scaled
        - jnp.mean(scaled, -1, keepdims=True)
        - normed * jnp.mean(scaled * normed, -1, keepdims=True)
    )


def project_kernel(x_ref, gain_ref, shift_ref, w_ref, first_ref, q_ref, kv_ref):
    normed, _ = norm_rows(x_ref[...].astype(F32))
    first = (normed * gain_ref[...] + shift_ref[...]).astype(BF16)
    first_ref[...] = first
    out = dot_nn(first, w_ref[...]).astype(BF16)
    q_ref[...] = out[:, : 4 * HD]
    kv_ref[...] = out[:, 4 * HD :]


def project(x, gain, shift, w640):
    rows, width = x.shape
    tile = min(rows, 256)
    row = lambda w: pl.BlockSpec((tile, w), lambda i: (i, 0))
    whole = lambda s: pl.BlockSpec(s, lambda i: (0, 0))
    return pl.pallas_call(
        project_kernel,
        grid=(rows // tile,),
        out_shape=(sds((rows, width), BF16), sds((rows, 4 * HD), BF16), sds((rows, 6 * HD), BF16)),
        in_specs=[row(width), whole((1, width)), whole((1, width)), whole(w640.shape)],
        out_specs=(row(width), row(4 * HD), row(6 * HD)),
        compiler_params=PARAMS,
        name="project",
    )(x, gain, shift, w640)


def gather_kernel(index_ref, blocks_ref, out_ref):
    def step(slot, _):
        out_ref[slot] = blocks_ref[index_ref[slot]]
        return 0

    lax.fori_loop(0, out_ref.shape[0], step, 0)


def gather(blocks, index):
    return call(gather_kernel, sds((index.shape[0],) + blocks.shape[1:], BF16), name="gather")(
        blocks, smem=(index,)
    )


def lead_fwd_kernel(q0_ref, q1_ref, kv_ref, bias_ref, part0_ref, part1_ref):
    batches, per, _ = kv_ref.shape
    rows = 2 * BLOCK
    for m in range(batches):
        tile0 = jnp.concatenate([q0_ref[m, :, : 2 * HD], q1_ref[m, :, : 2 * HD]], 0)
        tile1 = jnp.concatenate([q0_ref[m, :, 2 * HD : 4 * HD], q1_ref[m, :, 2 * HD : 4 * HD]], 0)
        bias = bias_ref[m]
        pair = dot_nt(two_heads(tile0), kv_ref[m, :, : 2 * HD]) + bias
        last = dot_nt(tile1, kv_ref[m, :, 4 * HD :]) + bias
        top_a = jnp.max(pair, -1, keepdims=True)
        top_b = jnp.max(last, -1, keepdims=True)
        exp_a = jnp.exp(pair - top_a)
        exp_b = jnp.exp(last - top_b)
        sum_a = jnp.sum(exp_a, -1, keepdims=True)
        sum_b = jnp.sum(exp_b, -1, keepdims=True)
        out0 = pick_heads(dot_nn(exp_a.astype(BF16), kv_ref[m, :, 2 * HD : 4 * HD]), rows)
        out1 = half(dot_nn(exp_b.astype(BF16), kv_ref[m, :, 4 * HD :]), True)
        stats = lanes_of(
            [top_a[:rows], top_a[rows:], top_b, sum_a[:rows], sum_a[rows:], sum_b], rows
        )
        out1 = out1 + stats
        for end, part_ref in enumerate((part0_ref, part1_ref)):
            at = slice(end * BLOCK, (end + 1) * BLOCK)
            part_ref[m, :, : 2 * HD] = out0[at]
            part_ref[m, :, 2 * HD :] = out1[at]


def merge_kernel(a_ref, b_ref, out_ref):
    for m in range(a_ref.shape[0]):
        st_a = a_ref[m, :, 2 * HD :]
        st_b = b_ref[m, :, 2 * HD :]
        scales_a, scales_b, tops, sums = [], [], [], []
        for h in range(3):
            top_a, top_b = st_a[:, h : h + 1], st_b[:, h : h + 1]
            top = jnp.maximum(top_a, top_b)
            sa, sb = jnp.exp(top_a - top), jnp.exp(top_b - top)
            scales_a.append(sa)
            scales_b.append(sb)
            tops.append(top)
            sums.append(st_a[:, 3 + h : 4 + h] * sa + st_b[:, 3 + h : 4 + h] * sb)
        lane = lax.broadcasted_iota(jnp.int32, (BLOCK, 2 * HD), 1)
        pick = lambda s: jnp.where(lane < HD, s[0], s[1])
        out_ref[m, :, : 2 * HD] = a_ref[m, :, : 2 * HD] * pick(scales_a) + b_ref[
            m, :, : 2 * HD
        ] * pick(scales_b)
        joint = st_a * scales_a[2] + st_b * scales_b[2]
        out_ref[m, :, 2 * HD :] = jnp.where(lane >= HD, joint, lanes_of(tops + sums, BLOCK))


def merge(a, b):
    return call(merge_kernel, sds(a.shape, F32), name="merge")(a, b)


def lead_finish_kernel(part_ref, out_ref, lse_ref):
    for m in range(part_ref.shape[0]):
        st = part_ref[m, :, 2 * HD :]
        lane = lax.broadcasted_iota(jnp.int32, (BLOCK, 2 * HD), 1)
        sums = [st[:, 3 + h : 4 + h] for h in range(3)]
        out_ref[m, :, : 2 * HD] = (
            part_ref[m, :, : 2 * HD] / jnp.where(lane < HD, sums[0], sums[1])
        ).astype(BF16)
        out_ref[m, :, 2 * HD :] = jnp.where(lane >= HD, st / sums[2], 0.0).astype(BF16)
        lse_ref[m] = lanes_of([st[:, h : h + 1] + jnp.log(sums[h]) for h in range(3)], BLOCK)


def fill_ext(ext_ref, kv_ref, low_ref, high_ref, seqs, per):
    for m in range(seqs):
        ext_ref[m, :BLOCK] = low_ref[m]
        ext_ref[m, BLOCK : BLOCK + per] = kv_ref[m]
        ext_ref[m, BLOCK + per :] = high_ref[m]


def fill_listed(listed_ref, ext_ref, lead0_ref, lead1_ref, rand_ref, slot_ref, m, b, block):
    listed_ref[: 3 * BLOCK] = ext_ref[m, pl.ds(pl.multiple_of(b * BLOCK, BLOCK), 3 * BLOCK)]
    listed_ref[3 * BLOCK : 4 * BLOCK] = lead0_ref[m, :, 4 * HD :]
    listed_ref[4 * BLOCK : 5 * BLOCK] = lead1_ref[m, :, 4 * HD :]
    for j in range(RANDS):
        listed_ref[(5 + j) * BLOCK : (6 + j) * BLOCK] = rand_ref[slot_ref[block * RANDS + j]]


def pos_row(meta_ref, m, b, c, chunk, share, seqs):
    token = b * BLOCK + c * chunk
    at = token // share
    j = at ^ meta_ref[0]
    k = ((j & 1) << 1) | (j >> 1)
    return pl.multiple_of(k * (seqs * share) + m * share + (token - at * share), chunk)


def sparse_fwd_kernel(
    first, seqs, per, share, slot_ref, meta_ref, q_ref, kv_ref, low_ref, high_ref, lead0_ref,
    lead1_ref, rand_ref, bias_ref, lead_out_ref, out_ref, lse_ref, ext_ref, listed_ref,
):
    blocks = per // BLOCK
    chunk = min(share, BLOCK)
    fill_ext(ext_ref, kv_ref, low_ref, high_ref, seqs, per)

    def step(i, _):
        m, b = i // blocks, i % blocks
        fill_listed(
            listed_ref, ext_ref, lead0_ref, lead1_ref, rand_ref, slot_ref, m, b, first + i
        )
        bias = bias_ref[i]
        pair = dot_nt(two_heads(q_ref[i, :, : 2 * HD]), listed_ref[:, : 2 * HD]) + bias
        last = dot_nt(q_ref[i, :, 2 * HD :], listed_ref[:, 4 * HD :]) + bias
        top_a = jnp.max(pair, -1, keepdims=True)
        top_b = jnp.max(last, -1, keepdims=True)
        exp_a = jnp.exp(pair - top_a)
        exp_b = jnp.exp(last - top_b)
        sum_a = jnp.sum(exp_a, -1, keepdims=True)
        sum_b = jnp.sum(exp_b, -1, keepdims=True)
        prob_a = (exp_a * (1.0 / sum_a)).astype(BF16)
        prob_b = (exp_b * (1.0 / sum_b)).astype(BF16)
        out0 = pick_heads(dot_nn(prob_a, listed_ref[:, 2 * HD : 4 * HD]), BLOCK).astype(BF16)
        out1 = half(dot_nn(prob_b, listed_ref[:, 4 * HD :]), True).astype(BF16)
        lse_a = top_a + jnp.log(sum_a)
        lse_b = top_b + jnp.log(sum_b)
        lse_ref[i] = lanes_of([lse_a[:BLOCK], lse_a[BLOCK:], lse_b], BLOCK)
        is_lead = ((b == 0) & (meta_ref[1] == 1)) | ((b == blocks - 1) & (meta_ref[2] == 1))
        out0 = jnp.where(is_lead, lead_out_ref[m, :, : 2 * HD], out0)
        out1 = jnp.where(is_lead, lead_out_ref[m, :, 2 * HD :], out1)
        for c in range(BLOCK // chunk):
            row = pos_row(meta_ref, m, b, c, chunk, share, seqs)
            at = slice(c * chunk, (c + 1) * chunk)
            out_ref[pl.ds(row, chunk), : 2 * HD] = out0[at]
            out_ref[pl.ds(row, chunk), 2 * HD :] = out1[at]
        return 0

    lax.fori_loop(0, seqs * blocks, step, 0, unroll=2)


def mid_fwd_kernel(keep_ref, got_ref, x_ref, gain_ref, shift_ref, hidden_ref, act_ref):
    hidden = keep_ref[...] + got_ref[...].astype(F32) + x_ref[...].astype(F32)
    normed, _ = norm_rows(hidden)
    hidden_ref[...] = hidden
    act_ref[...] = (normed * gain_ref[...] + shift_ref[...]).astype(BF16)


def ffn_kernel(act_ref, gu_ref, up_w_ref, up_ref, pre_ref, back_ref):
    pre = dot_nn(act_ref[...], up_w_ref[...])
    phi = 0.5 + 0.5 * lax.erf(pre * (1.0 / math.sqrt(2.0)))
    density = jnp.exp(-0.5 * pre * pre) * (1.0 / math.sqrt(2.0 * math.pi))
    up_ref[...] = (pre * phi).astype(BF16)
    grad_pre = (gu_ref[...] * (phi + pre * density)).astype(BF16)
    pre_ref[...] = grad_pre
    back_ref[...] = dot_nt(grad_pre, up_w_ref[...]).astype(BF16)


def ffn(act, gu, w_up):
    rows, width = act.shape
    hidden = w_up.shape[1]
    tile = 128
    row = lambda w: pl.BlockSpec((tile, w), lambda i: (i, 0))
    return pl.pallas_call(
        ffn_kernel,
        grid=(rows // tile,),
        out_shape=(sds((rows, hidden), BF16), sds((rows, hidden), BF16), sds((rows, width), BF16)),
        in_specs=[row(width), row(hidden), pl.BlockSpec((width, hidden), lambda i: (0, 0))],
        out_specs=(row(hidden), row(hidden), row(width)),
        compiler_params=PARAMS,
        name="ffn",
    )(act, gu, w_up)


def mid_bwd_kernel(keep_ref, got_ref, hidden_ref, out_grad_ref, gain_ref, total_ref, low_ref, sums_ref):
    grad = keep_ref[...] + got_ref[...].astype(F32)
    normed, inverse = norm_rows(hidden_ref[...])
    total = out_grad_ref[...].astype(F32) + norm_rows_back(grad, normed, inverse, gain_ref[...])
    total_ref[...] = total
    low_ref[...] = total.astype(BF16)
    sums_ref[0:1] = jnp.sum(grad * normed, 0, keepdims=True)
    sums_ref[1:2] = jnp.sum(grad, 0, keepdims=True)


def end_kernel(keep_ref, got_ref, x_ref, total_ref, gain_ref, out_ref):
    grad = keep_ref[...] + got_ref[...].astype(F32)
    normed, inverse = norm_rows(x_ref[...].astype(F32))
    out_ref[...] = total_ref[...] + norm_rows_back(grad, normed, inverse, gain_ref[...])


def heads_grad_kernel(
    groups, seqs, per, share, index_ref, meta_ref, *refs,
):
    mixed_refs, outs_refs = refs[:groups], refs[groups : 2 * groups]
    lse_ref, lead_lse_ref, grads_ref, sent_ref, lead_ref, lead_grad = refs[2 * groups :]
    blocks = per // BLOCK
    chunk = min(share, BLOCK)
    for g in range(groups):

        def step(i, _, g=g):
            m, b = i // blocks, i % blocks
            at = g * seqs * blocks + i
            gsum, dsum = [], []
            for c in range(BLOCK // chunk):
                row = pos_row(meta_ref, m, b, c, chunk, share, seqs)
                gsum.append(mixed_refs[g][pl.ds(row, chunk)])
                dsum.append(outs_refs[g][pl.ds(row, chunk)])
            grad = gsum[0] if len(gsum) == 1 else jnp.concatenate(gsum, 0)
            outs = dsum[0] if len(dsum) == 1 else jnp.concatenate(dsum, 0)
            prod = grad.astype(F32) * outs.astype(F32)
            first, second = prod[:, : 2 * HD], prod[:, 2 * HD :]
            deltas = [
                jnp.sum(half(first, False), -1, keepdims=True),
                jnp.sum(half(first, True), -1, keepdims=True),
                jnp.sum(half(second, True), -1, keepdims=True),
            ]
            d_hi, d_lo = zip(*(hi_lo(d) for d in deltas))
            is_lead = ((b == 0) & (meta_ref[1] == 1)) | ((b == blocks - 1) & (meta_ref[2] == 1))

            def stats(lse):
                l_hi, l_lo = zip(*(hi_lo(lse[:, h : h + 1]) for h in range(3)))
                return l_hi + l_lo

            low = half(grad[:, 2 * HD :], True).astype(F32)
            zero = jnp.zeros_like(deltas[0])

            @pl.when(is_lead)
            def _():
                lead_ref[g * seqs + m, :, : 2 * HD] = grad[:, : 2 * HD]
                lead_ref[g * seqs + m, :, 2 * HD :] = (
                    low + lanes_of(stats(lead_lse_ref[g * seqs + m]) + d_hi + d_lo, BLOCK)
                ).astype(BF16)

            scale = jnp.where(is_lead, 0.0, 1.0)
            grads_ref[at, :, : 2 * HD] = (grad[:, : 2 * HD].astype(F32) * scale).astype(BF16)
            grads_ref[at, :, 2 * HD :] = (
                low * scale
                + lanes_of(
                    stats(lse_ref[at]) + tuple(d * scale for d in d_hi) + tuple(d * scale for d in d_lo),
                    BLOCK,
                )
            ).astype(BF16)
            return 0

        lax.fori_loop(0, seqs * blocks, step, 0)

    def send(slot, _):
        sent_ref[slot] = grads_ref[index_ref[slot]]
        return 0

    lax.fori_loop(0, sent_ref.shape[0], send, 0)


def row_stats(tile):
    st = tile.astype(F32)
    lse = [st[:, h : h + 1] + st[:, 3 + h : 4 + h] for h in range(3)]
    delta = [st[:, 6 + h : 7 + h] + st[:, 9 + h : 10 + h] for h in range(3)]
    return lse, delta


def sparse_bwd_kernel(
    batches, per, slot_ref, q_ref, kv_ref, low_ref, high_ref, lead0_ref, lead1_ref, rand_ref,
    bias_ref, grads_ref, dq_ref, dkv_ref, ret_low_ref, ret_high_ref, dlead0_ref, dlead1_ref,
    ext_ref, listed_ref, dext_ref, dlead_ref,
):
    blocks = per // BLOCK
    fill_ext(ext_ref, kv_ref, low_ref, high_ref, batches, per)
    dext_ref[...] = jnp.zeros_like(dext_ref)
    dlead_ref[...] = jnp.zeros_like(dlead_ref)

    def step(i, _):
        m, b = i // blocks, i % blocks
        fill_listed(listed_ref, ext_ref, lead0_ref, lead1_ref, rand_ref, slot_ref, m, b, i)
        bias = bias_ref[i]
        tile1 = grads_ref[i, :, 2 * HD :]
        lse, delta = row_stats(tile1)
        q_a, q_b = two_heads(q_ref[i, :, : 2 * HD]), q_ref[i, :, 2 * HD :]
        do_a, do_b = two_heads(grads_ref[i, :, : 2 * HD]), half(tile1, True)
        prob_a = jnp.exp(
            dot_nt(q_a, listed_ref[:, : 2 * HD]) + bias - jnp.concatenate(lse[:2], 0)
        )
        prob_b = jnp.exp(dot_nt(q_b, listed_ref[:, 4 * HD :]) + bias - lse[2])
        ds_a = prob_a * (
            dot_nt(do_a, listed_ref[:, 2 * HD : 4 * HD]) - jnp.concatenate(delta[:2], 0)
        )
        ds_b = prob_b * (dot_nt(do_b, listed_ref[:, 4 * HD :]) - delta[2])
        ds_a, ds_b = ds_a.astype(BF16), ds_b.astype(BF16)
        dq_ref[i, :, : 2 * HD] = pick_heads(dot_nn(ds_a, listed_ref[:, : 2 * HD]), BLOCK)
        dq_ref[i, :, 2 * HD :] = half(dot_nn(ds_b, listed_ref[:, 4 * HD :]), False)
        near = 6 * BLOCK
        prob_a, prob_b = prob_a[:, :near].astype(BF16), prob_b[:, :near].astype(BF16)
        dkv = jnp.concatenate(
            [
                dot_tn(ds_a[:, :near], q_a),
                dot_tn(prob_a, do_a),
                dot_tn(ds_b[:, :near], q_b) + dot_tn(prob_b, do_b),
            ],
            1,
        )
        dext_ref[m, pl.ds(pl.multiple_of(b * BLOCK, BLOCK), 3 * BLOCK)] += dkv[: 3 * BLOCK]
        dlead_ref[m] += dkv[3 * BLOCK : 5 * BLOCK]
        return 0

    lax.fori_loop(0, batches * blocks, step, 0, unroll=2)
    for m in range(batches):
        ret_low_ref[m] = dext_ref[m, :BLOCK].astype(BF16)
        dkv_ref[m] = dext_ref[m, BLOCK : BLOCK + per]
        ret_high_ref[m] = dext_ref[m, BLOCK + per :].astype(BF16)
        dlead0_ref[m] = dlead_ref[m, :BLOCK]
        dlead1_ref[m] = dlead_ref[m, BLOCK:]


def lead_bwd_kernel(q0_ref, q1_ref, do0_ref, do1_ref, kv_ref, bias_ref, dkv_ref, dq0_ref, dq1_ref):
    rows = 2 * BLOCK
    for m in range(kv_ref.shape[0]):
        both = lambda a, b, lo, hi: jnp.concatenate([a[m, :, lo:hi], b[m, :, lo:hi]], 0)
        tile1 = both(do0_ref, do1_ref, 2 * HD, 4 * HD)
        lse, delta = row_stats(tile1)
        q_a = two_heads(both(q0_ref, q1_ref, 0, 2 * HD))
        q_b = both(q0_ref, q1_ref, 2 * HD, 4 * HD)
        do_a, do_b = two_heads(both(do0_ref, do1_ref, 0, 2 * HD)), half(tile1, True)
        k_a, v_a, kv_b = kv_ref[m, :, : 2 * HD], kv_ref[m, :, 2 * HD : 4 * HD], kv_ref[m, :, 4 * HD :]
        bias = bias_ref[m]
        prob_a = jnp.exp(dot_nt(q_a, k_a) + bias - jnp.concatenate(lse[:2], 0))
        prob_b = jnp.exp(dot_nt(q_b, kv_b) + bias - lse[2])
        ds_a = (prob_a * (dot_nt(do_a, v_a) - jnp.concatenate(delta[:2], 0))).astype(BF16)
        ds_b = (prob_b * (dot_nt(do_b, kv_b) - delta[2])).astype(BF16)
        dq_a = pick_heads(dot_nn(ds_a, k_a), rows)
        dq_b = half(dot_nn(ds_b, kv_b), False)
        for end, dq_ref in enumerate((dq0_ref, dq1_ref)):
            at = slice(end * BLOCK, (end + 1) * BLOCK)
            dq_ref[m, :, : 2 * HD] = dq_a[at]
            dq_ref[m, :, 2 * HD :] = dq_b[at]
        dkv_ref[m, :, : 2 * HD] = dot_tn(ds_a, q_a)
        dkv_ref[m, :, 2 * HD : 4 * HD] = dot_tn(prob_a.astype(BF16), do_a)
        dkv_ref[m, :, 4 * HD :] = dot_tn(ds_b, q_b) + dot_tn(prob_b.astype(BF16), do_b)


def tail_kernel(
    groups, seqs, per, share, index_ref, valid_ref, meta_ref, q_got_ref, do_got_ref, kv_ref,
    column_ref, dq_ref, dkv_ref, dkv_lead_ref, ret_low_ref, ret_high_ref, ends_ref, first_ref, x_ref, w_ref,
    gw_ref, back_ref, sums_ref, acc_ref, gqkv_ref,
):
    blocks = per // BLOCK
    chunk = min(share, BLOCK)
    total = groups * seqs * blocks
    head, tail = meta_ref[1], meta_ref[2]

    def start(i, _):
        m, b = i // blocks, i % blocks
        acc_ref[i] = dkv_ref[i] + dkv_lead_ref[i]

        @pl.when(b == 0)
        def _():
            acc_ref[i] += ret_low_ref[m].astype(F32)

        @pl.when(b == blocks - 1)
        def _():
            acc_ref[i] += ret_high_ref[m].astype(F32)

        @pl.when(((b == 0) & (head == 1)) | ((b == blocks - 1) & (tail == 1)))
        def _():
            acc_ref[i] += ends_ref[m, :, 4 * HD :].astype(F32)

        return 0

    lax.fori_loop(0, total, start, 0)

    def slot(c, _):
        @pl.when(valid_ref[c] == 1)
        def _():
            at = index_ref[c]
            kv = kv_ref[at]
            tile1 = do_got_ref[c, :, 2 * HD :]
            stats = jnp.transpose(tile1.astype(F32))
            lse = [stats[h : h + 1] + stats[3 + h : 4 + h] for h in range(3)]
            delta = [stats[6 + h : 7 + h] + stats[9 + h : 10 + h] for h in range(3)]
            q_a, q_b = two_heads(q_got_ref[c, :, : 2 * HD]), q_got_ref[c, :, 2 * HD :]
            do_a, do_b = two_heads(do_got_ref[c, :, : 2 * HD]), half(tile1, True)
            bias = column_ref[at]
            prob_a = jnp.exp(
                dot_nt(kv[:, : 2 * HD], q_a) + bias - jnp.concatenate(lse[:2], 1)
            )
            prob_b = jnp.exp(dot_nt(kv[:, 4 * HD :], q_b) + bias[:, :BLOCK] - lse[2])
            ds_a = prob_a * (
                dot_nt(kv[:, 2 * HD : 4 * HD], do_a) - jnp.concatenate(delta[:2], 1)
            )
            ds_b = prob_b * (dot_nt(kv[:, 4 * HD :], do_b) - delta[2])
            acc_ref[at] += jnp.concatenate(
                [
                    dot_nn(ds_a.astype(BF16), q_a),
                    dot_nn(prob_a.astype(BF16), do_a),
                    dot_nn(ds_b.astype(BF16), q_b) + dot_nn(prob_b.astype(BF16), do_b),
                ],
                1,
            )

        return 0

    lax.fori_loop(0, q_got_ref.shape[0], slot, 0, unroll=2)

    def finish(i, _):
        m, b = i // blocks, i % blocks
        dq = dq_ref[i]
        is_end = ((b == 0) & (head == 1)) | ((b == blocks - 1) & (tail == 1))
        dq = dq + jnp.where(is_end, ends_ref[m, :, : 4 * HD].astype(F32), 0.0)
        rows = pl.ds(pl.multiple_of(i * BLOCK, BLOCK), BLOCK)
        gqkv_ref[rows, : 4 * HD] = dq.astype(BF16)
        gqkv_ref[rows, 4 * HD :] = acc_ref[i].astype(BF16)
        return 0

    lax.fori_loop(0, total, finish, 0)
    sums_ref[...] = jnp.zeros_like(sums_ref)
    tile = 128 if per % 128 == 0 else BLOCK

    def project_back(i, _):
        rows = pl.ds(pl.multiple_of(i * tile, tile), tile)
        back = dot_nt(gqkv_ref[rows], w_ref[...])
        normed, _ = norm_rows(x_ref[rows].astype(F32))
        sums_ref[0:1] += jnp.sum(back * normed, 0, keepdims=True)
        sums_ref[1:2] += jnp.sum(back, 0, keepdims=True)
        low = back.astype(BF16)
        m, inside = i // (per // tile), (i % (per // tile)) * tile
        g, m = m // seqs, m % seqs
        for c in range(tile // chunk):
            token = inside + c * chunk
            at = token // share
            j = at ^ meta_ref[0]
            k = ((j & 1) << 1) | (j >> 1)
            row = pl.multiple_of(k * (seqs * share) + m * share + (token - at * share), chunk)
            back_ref[g, pl.ds(row, chunk)] = low[c * chunk : (c + 1) * chunk]
        return 0

    lax.fori_loop(0, total * BLOCK // tile, project_back, 0)
    gw_ref[...] = dot_tn(first_ref[...], gqkv_ref[...]).astype(BF16)


def swap_tp(value, bit):
    return lax.ppermute(value, "tp", [(i, i ^ bit) for i in range(lax.axis_size("tp"))])


def scatter_tp(part):
    rows = part.shape[0] // 2
    got = swap_tp(part[rows:], 1)
    both = part[:rows].astype(F32) + got.astype(F32)
    piece = rows // 2
    return both[:piece], swap_tp(both[piece:].astype(BF16), 2)


def gather_tp(piece):
    near = jnp.concatenate([piece, swap_tp(piece, 2)], 0)
    return jnp.concatenate([near, swap_tp(near, 1)], 0)


def tree_out(own, myself, devices):
    held = own
    bit = 1
    while bit < devices // 2:
        pairs = [(i, i + bit) for i in range(bit)]
        pairs += [(devices - 1 - a, devices - 1 - b) for a, b in pairs]
        got = lax.ppermute(held, "seq", pairs)
        lower = (myself >= bit) & (myself < 2 * bit)
        rest = devices - 1 - myself
        upper = (rest >= bit) & (rest < 2 * bit)
        held = jnp.where(lower | upper, got, held)
        bit *= 2
    other = lax.ppermute(held, "seq", [(i, i ^ bit) for i in range(devices)])
    low = myself < devices // 2
    return jnp.where(low, held, other), jnp.where(low, other, held)


def tree_in(for_first, for_last, myself, devices, join):
    low = myself < devices // 2
    bit = devices // 2
    mine = jnp.where(low, for_first, for_last)
    given = jnp.where(low, for_last, for_first)
    mine = join(mine, lax.ppermute(given, "seq", [(i, i ^ bit) for i in range(devices)]))
    while bit > 1:
        bit //= 2
        pairs = [(i + bit, i) for i in range(bit)]
        pairs += [(devices - 1 - a, devices - 1 - b) for a, b in pairs]
        mine = join(mine, lax.ppermute(mine, "seq", pairs))
    return mine


def to_owners(slots):
    return lax.all_to_all(slots, "seq", split_axis=0, concat_axis=0, tiled=True)


def per_device(
    layer_input,
    out_grad,
    norm1_gain,
    norm1_shift,
    w_qkv,
    w_out,
    norm2_gain,
    norm2_shift,
    w_up,
    w_down,
    key_keep,
    rand_blocks,
):
    batches, per, width = layer_input.shape
    local = w_qkv.shape[2]
    devices = lax.axis_size("seq")
    myself = lax.axis_index("seq")
    tp_count = lax.axis_size("tp")
    tp_place = lax.axis_index("tp")
    assert local == 3 * HD and tp_count == 4 and devices % 2 == 0
    share = per // tp_count
    bd = per // BLOCK
    total = batches * bd
    blocks_all = bd * devices
    groups = 2 if batches % 2 == 0 else 1
    seqs = batches // groups
    piece = seqs * share
    refs = total * RANDS
    slots_per = max(1, -(-refs // devices))
    slots = devices * slots_per
    i32 = jnp.int32
    row = lambda v: v.reshape(1, -1)
    gain1, shift1, gain2, shift2 = map(row, (norm1_gain, norm1_shift, norm2_gain, norm2_shift))
    meta = jnp.stack(
        [tp_place, (myself == 0).astype(i32), (myself == devices - 1).astype(i32)]
    ).astype(i32)

    blank = jnp.zeros((width, HD), BF16)
    wq, wk, wv = (w_qkv[:, c] for c in range(3))
    scale = 1.0 / math.sqrt(HD)
    w640 = jnp.concatenate(
        [wq * jnp.asarray(scale, BF16), blank, wk[:, : 2 * HD], wv[:, : 2 * HD], wk[:, 2 * HD :], wv[:, 2 * HD :]], 1
    )
    wo256 = jnp.concatenate([w_out[:, : 2 * HD], blank, w_out[:, 2 * HD :]], 1)

    x_rows = layer_input.reshape(batches * per, width)
    first, q, kv = project(x_rows, gain1, shift1, w640)
    q_blocks = q.reshape(total, BLOCK, 4 * HD)
    kv_blocks = kv.reshape(total, BLOCK, 6 * HD)
    q_seqs = q.reshape(batches, per, 4 * HD)
    kv_seqs = kv.reshape(batches, per, 6 * HD)

    table = (
        rand_blocks.reshape(batches, devices, bd, RANDS).transpose(1, 0, 2, 3).reshape(devices, refs)
    )
    owners = table // bd
    source = (jnp.arange(refs, dtype=i32) // (bd * RANDS))[None] * bd + table - owners * bd
    order = jnp.arange(refs, dtype=i32)
    earlier = order[None, :] < order[:, None]
    rank = jnp.sum(((owners[:, :, None] == owners[:, None, :]) & earlier[None]).astype(i32), -1)
    places = jnp.arange(slots_per, dtype=i32)
    asked = (owners == myself)[:, None, :] & (rank[:, None, :] == places[None, :, None])
    source_of = jnp.sum(jnp.where(asked, source[:, None, :], 0), -1).reshape(slots)
    valid = jnp.sum(asked.astype(i32), -1).reshape(slots)
    my_owner = lax.dynamic_index_in_dim(owners, myself, 0, False)
    my_rank = lax.dynamic_index_in_dim(rank, myself, 0, False)
    slot_of = my_owner * slots_per + my_rank
    query_of = jnp.sum(
        jnp.where(
            slot_of[None, :] == jnp.arange(slots, dtype=i32)[:, None], (order // RANDS)[None, :], 0
        ),
        -1,
    )

    rand_kv = to_owners(gather(kv_blocks, source_of))
    ends = jnp.where(
        myself < devices // 2,
        jnp.concatenate([q_seqs[:, :BLOCK], kv_seqs[:, :BLOCK]], 2),
        jnp.concatenate([q_seqs[:, per - BLOCK :], kv_seqs[:, per - BLOCK :]], 2),
    )
    lead0, lead1 = tree_out(ends, myself, devices)
    up = [(i, i + 1) for i in range(devices - 1)]
    down = [(b, a) for a, b in up]
    low = lax.ppermute(kv_seqs[:, per - BLOCK :], "seq", up)
    high = lax.ppermute(kv_seqs[:, :BLOCK], "seq", down)

    keep = key_keep.reshape(batches, blocks_all, BLOCK)
    padded = jnp.pad(keep, ((0, 0), (1, 1), (0, 0)))
    window = lax.dynamic_slice_in_dim(padded, myself * bd, bd + 2, 1)
    mine = lax.dynamic_index_in_dim(table, myself, 0, False).reshape(batches, bd * RANDS)
    hot = (mine[:, :, None] == jnp.arange(blocks_all, dtype=i32)).astype(BF16)
    rand_keep = jnp.einsum("mjn,mnb->mjb", hot, keep.astype(BF16)).astype(i32)
    listed_keep = jnp.concatenate(
        [window[:, i : i + bd] for i in range(3)]
        + [
            jnp.broadcast_to(keep[:, :1], (batches, bd, BLOCK)),
            jnp.broadcast_to(keep[:, blocks_all - 1 :], (batches, bd, BLOCK)),
            rand_keep.reshape(batches, bd, RANDS * BLOCK),
        ],
        2,
    )
    bias = jnp.where(listed_keep > 0, 0.0, NEG).astype(F32).reshape(total, 1, 8 * BLOCK)
    own_keep = window[:, 1 : bd + 1]
    own_bias = jnp.where(own_keep > 0, 0.0, NEG).astype(F32)
    seq_bias = own_bias.reshape(batches, 1, per)
    column_bias = jnp.broadcast_to(own_bias.reshape(total, BLOCK, 1), (total, BLOCK, 2 * HD))

    part = sds((batches, BLOCK, 4 * HD), F32)
    part0, part1 = call(lead_fwd_kernel, (part, part), name="lead_fwd")(
        lead0, lead1, kv_seqs, seq_bias
    )
    lead_part = tree_in(part0, part1, myself, devices, merge)
    lead_out, lead_lse = call(
        lead_finish_kernel, (sds(part.shape, BF16), sds((batches, BLOCK, 2 * HD), F32)), name="lead_finish"
    )(lead_part)

    def own_share(value, g):
        return lax.dynamic_slice(
            value, (g * seqs, tp_place * share, 0), (seqs, share, width)
        ).reshape(piece, width)

    def in_pos_order(value, g):
        return jnp.concatenate(
            [
                lax.dynamic_slice(
                    value, (g * seqs, (tp_place ^ SWAP[k]) * share, 0), (seqs, share, width)
                ).reshape(piece, width)
                for k in range(4)
            ],
            0,
        )

    x_share = [own_share(layer_input, g) for g in range(groups)]
    og_share = [own_share(out_grad, g) for g in range(groups)]
    og_pos = [in_pos_order(out_grad, g) for g in range(groups)]
    grad_up = [dot_nn(og_pos[g], w_down) for g in range(groups)]

    mixed, lse = [], []
    for g in range(groups):
        seq_at = slice(g * seqs, (g + 1) * seqs)
        at = slice(g * seqs * bd, (g + 1) * seqs * bd)
        out, stat = call(
            partial(sparse_fwd_kernel, g * seqs * bd, seqs, per, share),
            (sds((4 * piece, 4 * HD), BF16), sds((seqs * bd, BLOCK, 2 * HD), F32)),
            (
                pltpu.VMEM((seqs, per + 2 * BLOCK, 6 * HD), BF16),
                pltpu.VMEM((8 * BLOCK, 6 * HD), BF16),
            ),
            name="sparse_fwd",
        )(
            q_blocks[at], kv_seqs[seq_at], low[seq_at], high[seq_at], lead0[seq_at], lead1[seq_at],
            rand_kv, bias[at], lead_out[seq_at], smem=(slot_of, meta),
        )
        mixed.append(out)
        lse.append(stat)
    lse = jnp.concatenate(lse, 0)

    q_slots, _ = lax.optimization_barrier((gather(q_blocks, query_of), rand_kv))
    rand_q = to_owners(q_slots)

    hidden, act, ups, pres, back = [], [], [], [], []
    for g in range(groups):
        kept, got = scatter_tp(dot_nt(mixed[g], wo256).astype(BF16))
        h, a = call(
            mid_fwd_kernel, (sds((piece, width), F32), sds((piece, width), BF16)), name="mid_fwd"
        )(kept, got, x_share[g], gain2, shift2)
        hidden.append(h)
        act.append(gather_tp(a))
    for g in range(groups):
        u, p, b = ffn(act[g], grad_up[g], w_up)
        ups.append(u)
        pres.append(p)
        back.append(b)

    total_grad, sums2, mixed_grad, attn_grad = [], [], [], []
    for g in range(groups):
        kept, got = scatter_tp(back[g])
        t, a, s = call(
            mid_bwd_kernel,
            (sds((piece, width), F32), sds((piece, width), BF16), sds((2, width), F32)),
            name="mid_bwd",
        )(kept, got, hidden[g], og_share[g], gain2)
        total_grad.append(t)
        sums2.append(s)
        attn_grad.append(gather_tp(a))
        mixed_grad.append(dot_nn(attn_grad[g], wo256).astype(BF16))

    outputs = []
    for g in range(groups):
        kept, got = scatter_tp(dot_nt(ups[g], w_down).astype(BF16))
        outputs.append((hidden[g] + kept + got.astype(F32)).reshape(seqs, share, width))
    layer_output = jnp.concatenate(outputs, 0)
    every = lambda parts: jnp.concatenate(parts, 0)
    gw_down = dot_tn(every(og_pos), every(ups))
    gw_up = dot_tn(every(act), every(pres))
    gw_out = dot_tn(every(attn_grad), every(mixed))
    gw_out = jnp.concatenate([gw_out[:, : 2 * HD], gw_out[:, 3 * HD :]], 1)

    grads, sent, lead_grad = call(
        partial(heads_grad_kernel, groups, seqs, per, share),
        (
            sds((total, BLOCK, 4 * HD), BF16),
            sds((slots, BLOCK, 4 * HD), BF16),
            sds((batches, BLOCK, 4 * HD), BF16),
        ),
        (pltpu.VMEM((8, 2 * HD), F32),),
        name="heads_grad",
    )(*mixed_grad, *mixed, lse, lead_lse, smem=(query_of, meta))
    rand_do = to_owners(sent)
    lead_do0, lead_do1 = tree_out(lead_grad, myself, devices)
    end = sds((batches, BLOCK, 6 * HD), BF16)
    dq, dkv, ret_low, ret_high, dlead0, dlead1 = call(
        partial(sparse_bwd_kernel, batches, per),
        (
            sds((total, BLOCK, 4 * HD), F32),
            sds((batches, per, 6 * HD), F32),
            end,
            end,
            sds(end.shape, F32),
            sds(end.shape, F32),
        ),
        (
            pltpu.VMEM((batches, per + 2 * BLOCK, 6 * HD), BF16),
            pltpu.VMEM((8 * BLOCK, 6 * HD), BF16),
            pltpu.VMEM((batches, per + 2 * BLOCK, 6 * HD), F32),
            pltpu.VMEM((batches, 2 * BLOCK, 6 * HD), F32),
        ),
        name="sparse_bwd",
    )(
        q_blocks, kv_seqs, low, high, lead0, lead1, rand_kv, bias, grads, smem=(slot_of,)
    )
    from_low = lax.ppermute(ret_high, "seq", up)
    from_high = lax.ppermute(ret_low, "seq", down)
    dkv_lead, dq0, dq1 = call(
        lead_bwd_kernel, (sds((batches, per, 6 * HD), F32), part, part), name="lead_bwd"
    )(lead0, lead1, lead_do0, lead_do1, kv_seqs, seq_bias)
    add = lambda a, b: (a.astype(F32) + b.astype(F32)).astype(BF16)
    ends_grad = tree_in(
        jnp.concatenate([dq0, dlead0], 2).astype(BF16),
        jnp.concatenate([dq1, dlead1], 2).astype(BF16),
        myself,
        devices,
        add,
    )
    gw_qkv, first_back, sums1 = call(
        partial(tail_kernel, groups, seqs, per, share),
        (sds((width, 10 * HD), BF16), sds((groups, 4 * piece, width), BF16), sds((2, width), F32)),
        (pltpu.VMEM((total, BLOCK, 6 * HD), F32), pltpu.VMEM((total * BLOCK, 10 * HD), BF16)),
        name="tail",
    )(
        rand_q, rand_do, kv_blocks, column_bias, dq, dkv.reshape(total, BLOCK, 6 * HD),
        dkv_lead.reshape(total, BLOCK, 6 * HD), from_low, from_high, ends_grad, first, x_rows, w640,
        smem=(source_of, valid, meta),
    )

    input_parts = []
    for g in range(groups):
        kept, got = scatter_tp(first_back[g])
        input_parts.append(
            call(end_kernel, sds((piece, width), F32), name="end")(
                kept, got, x_share[g], total_grad[g], gain1
            ).reshape(seqs, share, width)
        )
    input_grad = jnp.concatenate(input_parts, 0)

    ff = lax.psum_scatter(
        jnp.concatenate([gw_down, gw_up, gw_out], 1).astype(BF16), "seq", scatter_dimension=0, tiled=True
    ).astype(F32)
    hidden_here = w_up.shape[1]
    g_down, g_up, g_out = ff[:, :hidden_here], ff[:, hidden_here : 2 * hidden_here], ff[:, 2 * hidden_here :]
    rows = width // devices
    gq = to_owners(gw_qkv).reshape(devices, rows, 10 * HD).astype(F32).sum(0)
    g_qkv = jnp.stack(
        [
            gq[:, : 3 * HD] * scale,
            jnp.concatenate([gq[:, 4 * HD : 6 * HD], gq[:, 8 * HD : 9 * HD]], 1),
            jnp.concatenate([gq[:, 6 * HD : 8 * HD], gq[:, 9 * HD :]], 1),
        ],
        1,
    )
    norms = jnp.concatenate([sums1, sum(sums2)], 0).reshape(4, devices, 1, rows)
    norms = jnp.broadcast_to(norms.transpose(1, 2, 0, 3), (devices, tp_count, 4, rows))
    norms = lax.all_to_all(
        norms.reshape(devices * tp_count, 4, rows), ("seq", "tp"), split_axis=0, concat_axis=0, tiled=True
    ).sum(0)
    return (
        layer_output, input_grad, g_qkv, g_out, g_up, g_down, norms[0], norms[1], norms[2], norms[3],
    )


def solution(mesh):
    return jax.shard_map(
        per_device,
        mesh=mesh,
        in_specs=(
            P(None, "seq", None),
            P(None, "seq", None),
            P(),
            P(),
            P(None, None, "tp"),
            P(None, "tp"),
            P(),
            P(),
            P(None, "tp"),
            P(None, "tp"),
            P(),
            P(),
        ),
        out_specs=(
            P(None, ("seq", "tp"), None),
            P(None, ("seq", "tp"), None),
            P("seq", None, "tp"),
            P("seq", "tp"),
            P("seq", "tp"),
            P("seq", "tp"),
            P("seq"),
            P("seq"),
            P("seq"),
            P("seq"),
        ),
        check_vma=False,
    )
```

```python
from functools import partial
import math

import jax
import jax.numpy as jnp
from jax import lax
from jax.experimental import pallas as pl
from jax.experimental.pallas import tpu as pltpu
from jax.sharding import PartitionSpec as P

HD = 64
BLOCK = 64
RANDS = 3
EPS = 1e-06
SWAP = (0, 2, 1, 3)
NEG = -1e30
F32 = jnp.float32
BF16 = jnp.bfloat16
VMEM = pl.BlockSpec(memory_space=pltpu.VMEM)
SMEM = pl.BlockSpec(memory_space=pltpu.SMEM)
MIB = 1024 * 1024


def sds(shape, kind):
    return jax.ShapeDtypeStruct(shape, kind)


PARAMS = pltpu.CompilerParams(vmem_limit_bytes=56 * MIB)
SMALL = pltpu.CompilerParams(vmem_limit_bytes=12 * MIB)


def part_of(array, at, count):
    return array, at, count


SHORT = pl.CostEstimate(flops=0, transcendentals=0, bytes_accessed=1024)


def call(body, outs, scratch=(), name=None, limit=PARAMS):
    def run(*args, smem=()):
        specs = [SMEM] * len(smem)
        arrays = []
        for arg in args:
            if isinstance(arg, tuple):
                array, at, count = arg
                shape = (array.shape[0] // count,) + array.shape[1:]
                index = (at,) + (0,) * (array.ndim - 1)
                specs.append(pl.BlockSpec(shape, lambda i, index=index: index))
                arrays.append(array)
            else:
                specs.append(VMEM)
                arrays.append(arg)
        return pl.pallas_call(
            body,
            out_shape=outs,
            grid=(1,),
            in_specs=specs,
            out_specs=jax.tree.map(lambda _: VMEM, outs),
            scratch_shapes=list(scratch),
            compiler_params=limit,
            cost_estimate=SHORT,
            name=name,
        )(*smem, *arrays)

    return run


def share_call(body, outs, blocks, name, limit=SMALL):
    def run(meta, seqs, share, *args):
        def spec(value, group, pos):
            return pl.BlockSpec(
                (seqs, share, value.shape[2]), lambda i, meta_ref: (group, meta_ref[0] ^ SWAP[pos], 0)
            )

        return pl.pallas_call(
            body,
            out_shape=outs,
            grid_spec=pltpu.PrefetchScalarGridSpec(
                num_scalar_prefetch=1,
                grid=(1,),
                in_specs=[spec(*b) for b in blocks] + [VMEM] * len(args),
                out_specs=jax.tree.map(lambda _: VMEM, outs),
            ),
            compiler_params=limit,
            cost_estimate=SHORT,
            name=name,
        )(meta, *(b[0] for b in blocks), *args)

    return run


def dot_nt(a, b):
    return lax.dot_general(a, b, (((1,), (1,)), ((), ())), preferred_element_type=F32)


def dot_tn(a, b):
    return lax.dot_general(a, b, (((0,), (0,)), ((), ())), preferred_element_type=F32)


def dot_nn(a, b):
    return lax.dot_general(a, b, (((1,), (0,)), ((), ())), preferred_element_type=F32)


def two_heads(tile):
    lane = lax.broadcasted_iota(jnp.int32, tile.shape, 1)
    zero = jnp.zeros_like(tile)
    return jnp.concatenate([jnp.where(lane < HD, tile, zero), jnp.where(lane >= HD, tile, zero)], 0)


def pick_heads(pair, rows):
    lane = lax.broadcasted_iota(jnp.int32, (rows, 2 * HD), 1)
    return jnp.where(lane < HD, pair[:rows], pair[rows:])


def half(tile, upper):
    lane = lax.broadcasted_iota(jnp.int32, tile.shape, 1)
    return jnp.where((lane >= HD) if upper else (lane < HD), tile, jnp.zeros_like(tile))


def lanes_of(columns, rows):
    lane = lax.broadcasted_iota(jnp.int32, (rows, 2 * HD), 1)
    out = jnp.zeros((rows, 2 * HD), F32)
    for at, column in enumerate(columns):
        out = jnp.where(lane == at, column, out)
    return out


def hi_lo(value):
    hi = value.astype(BF16).astype(F32)
    return hi, value - hi


def norm_rows(hidden):
    center = hidden - jnp.mean(hidden, -1, keepdims=True)
    inverse = lax.rsqrt(jnp.mean(center * center, -1, keepdims=True) + EPS)
    return center * inverse, inverse


def norm_rows_back(grad, normed, inverse, gain):
    scaled = grad * gain
    return inverse * (
        scaled
        - jnp.mean(scaled, -1, keepdims=True)
        - normed * jnp.mean(scaled * normed, -1, keepdims=True)
    )


def after(value, *others):
    return lax.optimization_barrier((value,) + others)[0]


def project_kernel(x_ref, gain_ref, shift_ref, raw_ref, first_ref, q_ref, kv_ref, w_ref):
    @pl.when(pl.program_id(0) == 0)
    def _():
        w_ref[:, : 3 * HD] = raw_ref[0] * jnp.asarray(1.0 / math.sqrt(HD), BF16)
        w_ref[:, 3 * HD : 4 * HD] = jnp.zeros((w_ref.shape[0], HD), BF16)
        w_ref[:, 4 * HD : 6 * HD] = raw_ref[1, :, : 2 * HD]
        w_ref[:, 6 * HD : 8 * HD] = raw_ref[2, :, : 2 * HD]
        w_ref[:, 8 * HD :] = jnp.concatenate([raw_ref[1, :, 2 * HD :], raw_ref[2, :, 2 * HD :]], 1)

    normed, _ = norm_rows(x_ref[...].astype(F32))
    first = (normed * gain_ref[...][None] + shift_ref[...][None]).astype(BF16)
    first_ref[...] = first
    out = dot_nn(first, w_ref[...]).astype(BF16)
    q_ref[...] = out[:, : 4 * HD]
    kv_ref[...] = out[:, 4 * HD :]


def project(x, gain, shift, raw):
    rows, width = x.shape
    tile = min(rows, 256)
    row = lambda w: pl.BlockSpec((tile, w), lambda i: (i, 0))
    vector = pl.BlockSpec((width,), lambda i: (0,))
    whole = pl.BlockSpec((width, 10 * HD), lambda i: (0, 0))
    low = lambda *shape: sds(shape, BF16)
    return pl.pallas_call(
        project_kernel,
        grid=(rows // tile,),
        out_shape=(low(rows, width), low(rows, 4 * HD), low(rows, 6 * HD), low(width, 10 * HD)),
        in_specs=[row(width), vector, vector, pl.BlockSpec(raw.shape, lambda i: (0, 0, 0))],
        out_specs=(row(width), row(4 * HD), row(6 * HD), whole),
        compiler_params=PARAMS,
        cost_estimate=SHORT,
        name="project",
    )(x, gain, shift, raw)


def wide_out(w_ref):
    blank = jnp.zeros((w_ref.shape[0], HD), BF16)
    return jnp.concatenate([w_ref[:, : 2 * HD], blank, w_ref[:, 2 * HD :]], 1)


def dispatch_kernel(bd, index_ref, meta_ref, q_ref, kv_ref, sent_ref, ends_ref, low_ref, high_ref):
    def step(slot, _):
        sent_ref[slot] = kv_ref[index_ref[slot]]
        return 0

    lax.fori_loop(0, sent_ref.shape[0], step, 0, unroll=4)
    at = jnp.where(meta_ref[1] == 1, 0, bd - 1)
    root = (meta_ref[1] + meta_ref[2]) == 1
    for m in range(low_ref.shape[0]):
        low_ref[m] = kv_ref[m * bd]
        high_ref[m] = kv_ref[m * bd + bd - 1]
        zero = lambda v: jnp.where(root, v, jnp.zeros_like(v))
        ends_ref[m, :, : 4 * HD] = zero(q_ref[m * bd + at])
        ends_ref[m, :, 4 * HD :] = zero(kv_ref[m * bd + at])


def bias_kernel(bd, blocks_all, table_ref, meta_ref, keep_ref, bias_ref, seq_ref, column_ref):
    low = lambda keep: jnp.where(keep > 0, 0.0, NEG)
    for m in range(seq_ref.shape[0]):
        for b in range(bd):
            i = m * bd + b
            here = meta_ref[4] * bd + b

            def row(block, inside=True):
                return low(jnp.where(inside, keep_ref[pl.ds(m * blocks_all + block, 1)], 0))

            own = row(here)
            listed = [
                row(jnp.maximum(here - 1, 0), here > 0),
                own,
                row(jnp.minimum(here + 1, blocks_all - 1), here < blocks_all - 1),
                row(0),
                row(blocks_all - 1),
            ] + [row(table_ref[i * RANDS + j]) for j in range(RANDS)]
            bias_ref[i] = jnp.concatenate(listed, 1)
            seq_ref[m, :, b * BLOCK : (b + 1) * BLOCK] = own
            column_ref[i] = jnp.transpose(jnp.broadcast_to(own, (2 * HD, BLOCK)))


def gather_kernel(index_ref, blocks_ref, out_ref):
    def step(slot, _):
        out_ref[slot] = blocks_ref[index_ref[slot]]
        return 0

    lax.fori_loop(0, out_ref.shape[0], step, 0, unroll=4)


def lead_fwd_kernel(meta_ref, kv_ref, bias_ref, lead0_ref, lead1_ref, mine_ref, given_ref):
    low = meta_ref[3]
    rows = 2 * BLOCK
    for m in range(kv_ref.shape[0]):
        both = lambda lo, hi: jnp.concatenate([lead0_ref[m, :, lo:hi], lead1_ref[m, :, lo:hi]], 0)
        bias = bias_ref[m]
        pair = dot_nt(two_heads(both(0, 2 * HD)), kv_ref[m, :, : 2 * HD]) + bias
        last = dot_nt(both(2 * HD, 4 * HD), kv_ref[m, :, 4 * HD :]) + bias
        top_a = jnp.max(pair, -1, keepdims=True)
        top_b = jnp.max(last, -1, keepdims=True)
        exp_a = jnp.exp(pair - top_a)
        exp_b = jnp.exp(last - top_b)
        sum_a = jnp.sum(exp_a, -1, keepdims=True)
        sum_b = jnp.sum(exp_b, -1, keepdims=True)
        out0 = pick_heads(dot_nn(exp_a.astype(BF16), kv_ref[m, :, 2 * HD : 4 * HD]), rows)
        out1 = half(dot_nn(exp_b.astype(BF16), kv_ref[m, :, 4 * HD :]), True)
        out1 = out1 + lanes_of(
            [top_a[:rows], top_a[rows:], top_b, sum_a[:rows], sum_a[rows:], sum_b], rows
        )
        for part_ref, first in ((mine_ref, low == 1), (given_ref, low == 0)):
            part_ref[m, :, : 2 * HD] = jnp.where(first, out0[:BLOCK], out0[BLOCK:])
            part_ref[m, :, 2 * HD :] = jnp.where(first, out1[:BLOCK], out1[BLOCK:])


def merge_parts(parts):
    lane = lax.broadcasted_iota(jnp.int32, (BLOCK, 2 * HD), 1)
    stats = [p[:, 2 * HD :] for p in parts]
    top = stats[0]
    for st in stats[1:]:
        top = jnp.maximum(top, st)
    tops = [top[:, h : h + 1] for h in range(3)]
    sums = [0.0, 0.0, 0.0]
    out0, out1 = 0.0, 0.0
    for p, st in zip(parts, stats):
        scale = [jnp.exp(st[:, h : h + 1] - tops[h]) for h in range(3)]
        sums = [sums[h] + st[:, 3 + h : 4 + h] * scale[h] for h in range(3)]
        out0 = out0 + p[:, : 2 * HD] * jnp.where(lane < HD, scale[0], scale[1])
        out1 = out1 + st * scale[2]
    return out0, jnp.where(lane >= HD, out1, 0.0), tops, sums


def merge_kernel(a_ref, b_ref, out_ref):
    for m in range(a_ref.shape[0]):
        out0, out1, tops, sums = merge_parts([a_ref[m], b_ref[m]])
        out_ref[m, :, : 2 * HD] = out0
        out_ref[m, :, 2 * HD :] = out1 + lanes_of(tops + sums, BLOCK)


def merge(a, b):
    return call(merge_kernel, sds(a.shape, F32), name="merge", limit=SMALL)(a, b)


def lead_finish_kernel(*refs):
    part_refs, (out_ref, lse_ref) = refs[:-2], refs[-2:]
    lane = lax.broadcasted_iota(jnp.int32, (BLOCK, 2 * HD), 1)
    for m in range(out_ref.shape[0]):
        out0, out1, tops, sums = merge_parts([p[m] for p in part_refs])
        out_ref[m, :, : 2 * HD] = (out0 / jnp.where(lane < HD, sums[0], sums[1])).astype(BF16)
        out_ref[m, :, 2 * HD :] = (out1 / sums[2]).astype(BF16)
        lse_ref[m] = lanes_of([tops[h] + jnp.log(sums[h]) for h in range(3)], BLOCK)


def fill_ext(ext_ref, kv_ref, low_ref, high_ref, seqs, per):
    for m in range(seqs):
        ext_ref[m, :BLOCK] = low_ref[m]
        ext_ref[m, BLOCK : BLOCK + per] = kv_ref[m]
        ext_ref[m, BLOCK + per :] = high_ref[m]


def fill_listed(listed_ref, ext_ref, lead0_ref, lead1_ref, rand_ref, slot_ref, m, b, block):
    listed_ref[: 3 * BLOCK] = ext_ref[m, pl.ds(pl.multiple_of(b * BLOCK, BLOCK), 3 * BLOCK)]
    listed_ref[3 * BLOCK : 4 * BLOCK] = lead0_ref[m, :, 4 * HD :]
    listed_ref[4 * BLOCK : 5 * BLOCK] = lead1_ref[m, :, 4 * HD :]
    for j in range(RANDS):
        listed_ref[(5 + j) * BLOCK : (6 + j) * BLOCK] = rand_ref[slot_ref[block * RANDS + j]]


def pos_of(meta_ref, at):
    j = at ^ meta_ref[0]
    return ((j & 1) << 1) | (j >> 1)


def sparse_fwd_kernel(
    first, seqs, per, share, slot_ref, meta_ref, q_ref, kv_ref, low_ref, high_ref, lead0_ref,
    lead1_ref, rand_ref, bias_ref, lead_out_ref, wo_ref, out_ref, lse_ref, part0_ref, part1_ref,
    part2_ref, part3_ref, ext_ref, listed_ref,
):
    blocks = per // BLOCK
    chunk = min(share, BLOCK)
    fill_ext(ext_ref, kv_ref, low_ref, high_ref, seqs, per)

    def attend(i, here):
        m, b = i // blocks, i % blocks
        fill_listed(here, ext_ref, lead0_ref, lead1_ref, rand_ref, slot_ref, m, b, first + i)
        bias = bias_ref[i]
        pair = dot_nt(two_heads(q_ref[i, :, : 2 * HD]), here[:, : 2 * HD]) + bias
        last = dot_nt(q_ref[i, :, 2 * HD :], here[:, 4 * HD :]) + bias
        top_a = jnp.max(pair, -1, keepdims=True)
        top_b = jnp.max(last, -1, keepdims=True)
        exp_a = jnp.exp(pair - top_a)
        exp_b = jnp.exp(last - top_b)
        sum_a = jnp.sum(exp_a, -1, keepdims=True)
        sum_b = jnp.sum(exp_b, -1, keepdims=True)
        prob_a = (exp_a * (1.0 / sum_a)).astype(BF16)
        prob_b = (exp_b * (1.0 / sum_b)).astype(BF16)
        out0 = pick_heads(dot_nn(prob_a, here[:, 2 * HD : 4 * HD]), BLOCK).astype(BF16)
        out1 = half(dot_nn(prob_b, here[:, 4 * HD :]), True).astype(BF16)
        lse_a = top_a + jnp.log(sum_a)
        lse_b = top_b + jnp.log(sum_b)
        lse_ref[pl.ds(pl.multiple_of(i * BLOCK, BLOCK), BLOCK)] = lanes_of(
            [lse_a[:BLOCK], lse_a[BLOCK:], lse_b], BLOCK
        )
        is_lead = ((b == 0) & (meta_ref[1] == 1)) | ((b == blocks - 1) & (meta_ref[2] == 1))
        out0 = jnp.where(is_lead, lead_out_ref[m, :, : 2 * HD], out0)
        out1 = jnp.where(is_lead, lead_out_ref[m, :, 2 * HD :], out1)
        for c in range(BLOCK // chunk):
            token = b * BLOCK + c * chunk
            at = token // share
            row = pos_of(meta_ref, at) * (seqs * share) + m * share + (token - at * share)
            rows = pl.ds(pl.multiple_of(row, chunk), chunk)
            out_ref[rows, : 2 * HD] = out0[c * chunk : (c + 1) * chunk]
            out_ref[rows, 2 * HD :] = out1[c * chunk : (c + 1) * chunk]

    def step(j, _):
        attend(2 * j, listed_ref.at[0])
        attend(2 * j + 1, listed_ref.at[1])
        return 0

    lax.fori_loop(0, seqs * blocks // 2, step, 0)
    piece = seqs * share
    wo = wide_out(wo_ref)
    for k, part_ref in enumerate((part0_ref, part1_ref, part2_ref, part3_ref)):
        part_ref[...] = dot_nt(out_ref[k * piece : (k + 1) * piece], wo).astype(BF16)


def total_of(refs):
    return refs[0][...].astype(F32) + refs[1][...].astype(F32) + refs[2][...].astype(F32)


def mid_fwd_kernel(meta_ref, x_ref, own_ref, core_ref, y_ref, gain_ref, shift_ref, hidden_ref, act_ref):
    x = x_ref[...].reshape(hidden_ref.shape).astype(F32)
    hidden = total_of((own_ref, core_ref, y_ref)) + x
    normed, _ = norm_rows(hidden)
    hidden_ref[...] = hidden
    act_ref[...] = (normed * gain_ref[...][None] + shift_ref[...][None]).astype(BF16)


def ffn_kernel(meta_ref, *refs):
    gu_refs, act_refs, w_ref, outs = refs[:4], refs[4:8], refs[8], refs[9:]
    rows = act_refs[0].shape[0]
    for k in (3, 2, 1, 0):
        up_ref, pre_ref, back_ref = outs[3 * k : 3 * k + 3]
        pre = dot_nn(act_refs[k][...], w_ref[...])
        phi = 0.5 + 0.5 * lax.erf(pre * (1.0 / math.sqrt(2.0)))
        density = jnp.exp(-0.5 * pre * pre) * (1.0 / math.sqrt(2.0 * math.pi))
        up_ref[...] = (pre * phi).astype(BF16)
        gu = gu_refs[k][...].reshape(rows, gu_refs[k].shape[2])
        grad_pre = (gu * (phi + pre * density)).astype(BF16)
        pre_ref[...] = grad_pre
        back_ref[...] = dot_nt(grad_pre, w_ref[...]).astype(BF16)


def mid_bwd_kernel(
    meta_ref, og_ref, own_ref, core_ref, y_ref, hidden_ref, gain_ref, total_ref, low_ref, sums_ref
):
    grad = total_of((own_ref, core_ref, y_ref))
    normed, inverse = norm_rows(hidden_ref[...])
    og = og_ref[...].reshape(hidden_ref.shape).astype(F32)
    total = og + norm_rows_back(grad, normed, inverse, gain_ref[...][None])
    total_ref[...] = total
    low_ref[...] = total.astype(BF16)
    sums_ref[0:1] = jnp.sum(grad * normed, 0, keepdims=True)
    sums_ref[1:2] = jnp.sum(grad, 0, keepdims=True)


def end_kernel(groups, meta_ref, *refs):
    x_refs, refs = refs[:groups], refs[groups:]
    gain_ref, out_ref = refs[-2:]
    seqs = x_refs[0].shape[0]
    for g in range(groups):
        grad = total_of(refs[4 * g : 4 * g + 3])
        normed, inverse = norm_rows(x_refs[g][...].reshape(grad.shape).astype(F32))
        total = refs[4 * g + 3][...] + norm_rows_back(grad, normed, inverse, gain_ref[...][None])
        out_ref[g * seqs : (g + 1) * seqs] = total.reshape(x_refs[g].shape)


def output_kernel(groups, *refs):
    out_ref = refs[-1]
    seqs, share, width = out_ref.shape
    seqs //= groups
    for g in range(groups):
        total = total_of(refs[4 * g : 4 * g + 3]) + refs[4 * g + 3][...]
        out_ref[g * seqs : (g + 1) * seqs] = total.reshape(seqs, share, width)


def heads_grad_kernel(groups, seqs, per, share, index_ref, meta_ref, wo_ref, lead_lse_ref, *refs):
    pieces, mixed_refs = refs[: 4 * groups], refs[4 * groups : 5 * groups]
    lse_refs = refs[5 * groups : 6 * groups]
    grads_ref, sent_ref, lead_ref = refs[6 * groups :]
    wo = wide_out(wo_ref)
    blocks = per // BLOCK
    rows_of = seqs * share
    for g in range(groups):
        for k in range(4):
            grad = dot_nn(pieces[4 * g + k][...], wo)
            low = grad.astype(BF16)
            prod = low.astype(F32) * mixed_refs[g][k * rows_of : (k + 1) * rows_of].astype(F32)
            deltas = [
                jnp.sum(half(prod[:, : 2 * HD], False), -1, keepdims=True),
                jnp.sum(half(prod[:, : 2 * HD], True), -1, keepdims=True),
                jnp.sum(half(prod[:, 2 * HD :], True), -1, keepdims=True),
            ]
            d_hi, d_lo = zip(*(hi_lo(d) for d in deltas))
            spare = [jnp.zeros_like(d_hi[0])] * 6
            stats = lanes_of(spare + list(d_hi + d_lo), rows_of)
            for m in range(seqs):
                at = slice(m * share, (m + 1) * share)
                inside = m * per + (meta_ref[0] ^ SWAP[k]) * share
                rows = pl.ds(pl.multiple_of(g * seqs * per + inside, share), share)
                lse = lse_refs[g][pl.ds(pl.multiple_of(inside, share), share)]
                l_hi, l_lo = zip(*(hi_lo(lse[:, h : h + 1]) for h in range(3)))
                grads_ref[rows, : 2 * HD] = low[at, : 2 * HD]
                grads_ref[rows, 2 * HD :] = (
                    half(grad[at, 2 * HD :], True) + stats[at] + lanes_of(l_hi + l_lo, share)
                ).astype(BF16)
    lane = lax.broadcasted_iota(jnp.int32, (BLOCK, 2 * HD), 1)
    lead_ref[...] = jnp.zeros_like(lead_ref)
    for end, b in ((1, 0), (2, blocks - 1)):

        @pl.when(meta_ref[end] == 1)
        def _(b=b):
            for m in range(groups * seqs):
                rows = slice(m * per + b * BLOCK, m * per + (b + 1) * BLOCK)
                l_hi, l_lo = zip(*(hi_lo(lead_lse_ref[m, :, h : h + 1]) for h in range(3)))
                tile1 = grads_ref[rows, 2 * HD :]
                lead_ref[m, :, : 2 * HD] = grads_ref[rows, : 2 * HD]
                lead_ref[m, :, 2 * HD :] = jnp.where(
                    lane < 6, lanes_of(l_hi + l_lo, BLOCK), tile1.astype(F32)
                ).astype(BF16)
                grads_ref[rows, : 2 * HD] = jnp.zeros((BLOCK, 2 * HD), BF16)
                grads_ref[rows, 2 * HD :] = jnp.where(lane < 6, tile1.astype(F32), 0.0).astype(BF16)

    def send(slot, _):
        at = pl.multiple_of(index_ref[slot] * BLOCK, BLOCK)
        sent_ref[slot] = grads_ref[pl.ds(at, BLOCK)]
        return 0

    lax.fori_loop(0, sent_ref.shape[0], send, 0, unroll=4)


def row_stats(tile):
    st = tile.astype(F32)
    lse = [st[:, h : h + 1] + st[:, 3 + h : 4 + h] for h in range(3)]
    delta = [st[:, 6 + h : 7 + h] + st[:, 9 + h : 10 + h] for h in range(3)]
    return lse, delta


def sparse_bwd_kernel(
    batches, per, slot_ref, q_ref, kv_ref, low_ref, high_ref, lead0_ref, lead1_ref, rand_ref,
    bias_ref, grads_ref, dq_ref, dkv_ref, ret_low_ref, ret_high_ref, dlead0_ref, dlead1_ref,
    ext_ref, listed_ref, dext_ref, dlead_ref,
):
    blocks = per // BLOCK
    near = 6 * BLOCK
    fill_ext(ext_ref, kv_ref, low_ref, high_ref, batches, per)
    dext_ref[...] = jnp.zeros_like(dext_ref)
    dlead_ref[...] = jnp.zeros_like(dlead_ref)

    def attend(i, here):
        m, b = i // blocks, i % blocks
        fill_listed(here, ext_ref, lead0_ref, lead1_ref, rand_ref, slot_ref, m, b, i)
        bias = bias_ref[i]
        tile1 = grads_ref[i, :, 2 * HD :]
        lse, delta = row_stats(tile1)
        q_a, q_b = two_heads(q_ref[i, :, : 2 * HD]), q_ref[i, :, 2 * HD :]
        do_a, do_b = two_heads(grads_ref[i, :, : 2 * HD]), half(tile1, True)
        prob_a = jnp.exp(dot_nt(q_a, here[:, : 2 * HD]) + bias - jnp.concatenate(lse[:2], 0))
        prob_b = jnp.exp(dot_nt(q_b, here[:, 4 * HD :]) + bias - lse[2])
        ds_a = prob_a * (dot_nt(do_a, here[:, 2 * HD : 4 * HD]) - jnp.concatenate(delta[:2], 0))
        ds_b = prob_b * (dot_nt(do_b, here[:, 4 * HD :]) - delta[2])
        ds_a, ds_b = ds_a.astype(BF16), ds_b.astype(BF16)
        dq_ref[i, :, : 2 * HD] = pick_heads(dot_nn(ds_a, here[:, : 2 * HD]), BLOCK)
        dq_ref[i, :, 2 * HD :] = half(dot_nn(ds_b, here[:, 4 * HD :]), False)
        prob_a, prob_b = prob_a[:, :near].astype(BF16), prob_b[:, :near].astype(BF16)
        dkv = jnp.concatenate(
            [
                dot_tn(ds_a[:, :near], q_a),
                dot_tn(prob_a, do_a),
                dot_tn(ds_b[:, :near], q_b) + dot_tn(prob_b, do_b),
            ],
            1,
        )
        return m, b, dkv

    def step(j, _):
        done = [attend(2 * j + n, listed_ref.at[n]) for n in range(2)]
        for m, b, dkv in done:
            dext_ref[m, pl.ds(pl.multiple_of(b * BLOCK, BLOCK), 3 * BLOCK)] += dkv[: 3 * BLOCK]
            dlead_ref[m] += dkv[3 * BLOCK : 5 * BLOCK]
        return 0

    lax.fori_loop(0, batches * blocks // 2, step, 0)
    for m in range(batches):
        ret_low_ref[m] = dext_ref[m, :BLOCK].astype(BF16)
        dkv_ref[m] = dext_ref[m, BLOCK : BLOCK + per]
        ret_high_ref[m] = dext_ref[m, BLOCK + per :].astype(BF16)
        dlead0_ref[m] = dlead_ref[m, :BLOCK]
        dlead1_ref[m] = dlead_ref[m, BLOCK:]


def lead_bwd_kernel(
    meta_ref, lead0_ref, lead1_ref, kv_ref, bias_ref, sparse_ref, dlead0_ref, dlead1_ref, do0_ref, do1_ref,
    dkv_ref, mine_ref, given_ref,
):
    low = meta_ref[3]
    rows = 2 * BLOCK
    for m in range(kv_ref.shape[0]):
        both = lambda a, b, lo, hi: jnp.concatenate([a[m, :, lo:hi], b[m, :, lo:hi]], 0)
        tile1 = both(do0_ref, do1_ref, 2 * HD, 4 * HD)
        lse, delta = row_stats(tile1)
        q_a = two_heads(both(lead0_ref, lead1_ref, 0, 2 * HD))
        q_b = both(lead0_ref, lead1_ref, 2 * HD, 4 * HD)
        do_a, do_b = two_heads(both(do0_ref, do1_ref, 0, 2 * HD)), half(tile1, True)
        k_a, v_a, kv_b = kv_ref[m, :, : 2 * HD], kv_ref[m, :, 2 * HD : 4 * HD], kv_ref[m, :, 4 * HD :]
        bias = bias_ref[m]
        prob_a = jnp.exp(dot_nt(q_a, k_a) + bias - jnp.concatenate(lse[:2], 0))
        prob_b = jnp.exp(dot_nt(q_b, kv_b) + bias - lse[2])
        ds_a = (prob_a * (dot_nt(do_a, v_a) - jnp.concatenate(delta[:2], 0))).astype(BF16)
        ds_b = (prob_b * (dot_nt(do_b, kv_b) - delta[2])).astype(BF16)
        dq_a = pick_heads(dot_nn(ds_a, k_a), rows)
        dq_b = half(dot_nn(ds_b, kv_b), False)
        for part_ref, first in ((mine_ref, low == 1), (given_ref, low == 0)):
            part_ref[m, :, : 2 * HD] = jnp.where(first, dq_a[:BLOCK], dq_a[BLOCK:]).astype(BF16)
            part_ref[m, :, 2 * HD : 4 * HD] = jnp.where(first, dq_b[:BLOCK], dq_b[BLOCK:]).astype(BF16)
            part_ref[m, :, 4 * HD :] = jnp.where(first, dlead0_ref[m], dlead1_ref[m]).astype(BF16)
        dkv_ref[m, :, : 2 * HD] = sparse_ref[m, :, : 2 * HD] + dot_tn(ds_a, q_a)
        dkv_ref[m, :, 2 * HD : 4 * HD] = sparse_ref[m, :, 2 * HD : 4 * HD] + dot_tn(
            prob_a.astype(BF16), do_a
        )
        dkv_ref[m, :, 4 * HD :] = (
            sparse_ref[m, :, 4 * HD :] + dot_tn(ds_b, q_b) + dot_tn(prob_b.astype(BF16), do_b)
        )


def split_rows(devices, meta_ref, grad_ref, keep_ref, send_ref):
    rows = keep_ref.shape[1]
    even = (meta_ref[4] & 1) == 0
    for z in range(devices // 2):
        one = grad_ref[2 * z * rows : (2 * z + 1) * rows].astype(BF16)
        two = grad_ref[(2 * z + 1) * rows : (2 * z + 2) * rows].astype(BF16)
        keep_ref[z] = jnp.where(even, one, two)
        send_ref[z] = jnp.where(even, two, one)


def ffn_grad_kernel(groups, seqs, per, share, devices, meta_ref, og_ref, *refs):
    count = 4 * groups
    ups, acts, pres = (refs[n * count : (n + 1) * count] for n in range(3))
    keep_ref, send_ref, left_ref, right_ref, grad_ref = refs[3 * count :]
    piece = seqs * share
    hidden = ups[0].shape[1]
    for g in range(groups):
        for k in range(4):
            for m in range(seqs):
                row = (g * seqs + m) * per + (meta_ref[0] ^ SWAP[k]) * share
                rows = pl.ds(pl.multiple_of(row, share), share)
                right_ref[rows] = ups[4 * g + k][m * share : (m + 1) * share]
    grad_ref[:, :hidden] = dot_tn(og_ref[...], right_ref[...])
    for n in range(count):
        left_ref[n * piece : (n + 1) * piece] = acts[n][...]
        right_ref[n * piece : (n + 1) * piece] = pres[n][...]
    grad_ref[:, hidden:] = dot_tn(left_ref[...], right_ref[...])
    split_rows(devices, meta_ref, grad_ref, keep_ref, send_ref)


def out_grad_kernel(groups, devices, meta_ref, *refs):
    pieces, mixed_refs = refs[: 4 * groups], refs[4 * groups : 5 * groups]
    keep_ref, send_ref, left_ref, grad_ref = refs[5 * groups :]
    piece = pieces[0].shape[0]
    total = 0.0
    for g in range(groups):
        for k in range(4):
            left_ref[k * piece : (k + 1) * piece] = pieces[4 * g + k][...]
        total = total + dot_tn(left_ref[...], mixed_refs[g][...])
    grad_ref[...] = total
    split_rows(devices, meta_ref, grad_ref, keep_ref, send_ref)


def fold_kernel(meta_ref, keep_ref, got_ref, own_ref, *send_refs):
    z = meta_ref[4] >> 1
    for n, ref in enumerate((own_ref,) + send_refs):
        total = keep_ref[z ^ n].astype(F32) + got_ref[z ^ n].astype(F32)
        ref[...] = total.astype(ref.dtype)


def tail_kernel(
    seqs, per, devices, index_ref, valid_ref, meta_ref, q_got_ref, do_got_ref, kv_ref, column_ref,
    dq_ref, dkv_ref, ret_low_ref, ret_high_ref, first_ref, *refs,
):
    ends_refs = refs[:-6]
    gqkv_ref, keep_ref, send_ref, acc_ref, grad_ref, extra_ref = refs[-6:]
    blocks = per // BLOCK
    batches = dkv_ref.shape[0] // blocks
    total = batches * blocks
    head, tail = meta_ref[1], meta_ref[2]
    acc_ref[...] = dkv_ref[...]
    for m in range(batches):
        acc_ref[m * blocks] += ret_low_ref[m].astype(F32)
        acc_ref[m * blocks + blocks - 1] += ret_high_ref[m].astype(F32)
        ends = ends_refs[0][m].astype(F32)
        for ref in ends_refs[1:]:
            ends = ends + ref[m].astype(F32)
        extra_ref[m] = ends

    def block_grads(c):
        at = index_ref[c]
        live = valid_ref[c] == 1
        kv = kv_ref[at]
        tile1 = do_got_ref[c, :, 2 * HD :]
        stats = jnp.transpose(tile1.astype(F32))
        lse = [stats[h : h + 1] + stats[3 + h : 4 + h] for h in range(3)]
        delta = [stats[6 + h : 7 + h] + stats[9 + h : 10 + h] for h in range(3)]
        q_a, q_b = two_heads(q_got_ref[c, :, : 2 * HD]), q_got_ref[c, :, 2 * HD :]
        do_a, do_b = two_heads(do_got_ref[c, :, : 2 * HD]), half(tile1, True)
        bias = column_ref[at]
        drop = lambda v: jnp.where(live, v, 0.0)
        prob_a = drop(
            jnp.exp(dot_nt(kv[:, : 2 * HD], q_a) + bias - jnp.concatenate(lse[:2], 1))
        )
        prob_b = drop(jnp.exp(dot_nt(kv[:, 4 * HD :], q_b) + bias[:, :BLOCK] - lse[2]))
        ds_a = prob_a * (dot_nt(kv[:, 2 * HD : 4 * HD], do_a) - jnp.concatenate(delta[:2], 1))
        ds_b = prob_b * (dot_nt(kv[:, 4 * HD :], do_b) - delta[2])
        return at, (
            dot_nn(ds_a.astype(BF16), q_a),
            dot_nn(prob_a.astype(BF16), do_a),
            dot_nn(ds_b.astype(BF16), q_b) + dot_nn(prob_b.astype(BF16), do_b),
        )

    slots = q_got_ref.shape[0]
    wide = 4 if slots % 4 == 0 else 1

    def slot(j, _):
        done = [block_grads(wide * j + n) for n in range(wide)]
        for at, tiles in done:
            for n, tile in enumerate(tiles):
                acc_ref[at, :, n * 2 * HD : (n + 1) * 2 * HD] += tile
        return 0

    lax.fori_loop(0, slots // wide, slot, 0)
    for end, b in ((head, 0), (tail, blocks - 1)):

        @pl.when(end == 1)
        def _(b=b):
            for m in range(batches):
                acc_ref[m * blocks + b] += extra_ref[m, :, 4 * HD :]

    gqkv_ref[:, : 4 * HD] = dq_ref[...].reshape(total * BLOCK, 4 * HD).astype(BF16)
    gqkv_ref[:, 4 * HD :] = acc_ref[...].reshape(total * BLOCK, 6 * HD).astype(BF16)
    for end, b in ((head, 0), (tail, blocks - 1)):

        @pl.when(end == 1)
        def _(b=b):
            for m in range(batches):
                at = m * blocks + b
                gqkv_ref[at * BLOCK : (at + 1) * BLOCK, : 4 * HD] = (
                    dq_ref[at] + extra_ref[m, :, : 4 * HD]
                ).astype(BF16)

    grad_ref[...] = dot_tn(first_ref[...], gqkv_ref[...])
    split_rows(devices, meta_ref, grad_ref, keep_ref, send_ref)


def back_kernel(groups, seqs, per, share, meta_ref, gqkv_ref, x_ref, w_ref, *refs):
    back_refs, sums_ref = refs[:-1], refs[-1]
    tile = 2 * share
    scale_sum, shift_sum = 0.0, 0.0
    for g in range(groups):
        for m in range(seqs):
            for n in range(per // tile):
                row = (g * seqs + m) * per + n * tile
                back = dot_nt(gqkv_ref[row : row + tile], w_ref[...])
                normed, _ = norm_rows(x_ref[row : row + tile].astype(F32))
                scale_sum = scale_sum + jnp.sum(back * normed, 0, keepdims=True)
                shift_sum = shift_sum + jnp.sum(back, 0, keepdims=True)
                low = back.astype(BF16)
                for half_at in range(2):
                    k = pos_of(meta_ref, 2 * n + half_at)
                    value = low[half_at * share : (half_at + 1) * share]

                    for pos in range(4):

                        @pl.when(k == pos)
                        def _(pos=pos, value=value):
                            back_refs[4 * g + pos][m * share : (m + 1) * share] = value

    sums_ref[0:1] = scale_sum
    sums_ref[1:2] = shift_sum


def swap_tp(value, bit):
    return lax.ppermute(value, "tp", [(i, i ^ bit) for i in range(lax.axis_size("tp"))])


def scatter_tp(parts):
    far = swap_tp(parts[3], 1)
    near = swap_tp(parts[2], 1)
    both = (parts[1].astype(F32) + far.astype(F32)).astype(BF16)
    return parts[0], near, swap_tp(both, 2)


def gather_tp(piece):
    cross = swap_tp(piece, 2)
    return piece, cross, swap_tp(piece, 1), swap_tp(cross, 1)


def mirrored(pairs, last):
    return pairs + [(last - a, last - b) for a, b in pairs]


SECOND = [(1, 3), (4, 5), (2, 6), (0, 7)]


def in_first_group(myself, devices):
    if devices == 8:
        return (myself == 0) | (myself == 1) | (myself == 2) | (myself == 4)
    return myself < devices // 2


def spread(own, myself, devices, *before_last):
    last = devices - 1
    held = own
    if devices == 8:
        for k in (1, 2, 4):
            held = held + lax.ppermute(own, "seq", mirrored([(0, k)], last))
        held = after(held, *before_last)
        other = lax.ppermute(held, "seq", mirrored(SECOND, last))
    else:
        bit = 1
        while bit < devices // 2:
            held = held + lax.ppermute(held, "seq", mirrored([(i, i + bit) for i in range(bit)], last))
            bit *= 2
        other = lax.ppermute(held, "seq", [(i, i ^ bit) for i in range(devices)])
    first = in_first_group(myself, devices)
    return jnp.where(first, held, other), jnp.where(first, other, held)


def collect(mine, given, devices, join):
    last = devices - 1
    if devices == 8:
        mine = join(mine, lax.ppermute(given, "seq", mirrored([(b, a) for a, b in SECOND], last)))
        return [mine] + [lax.ppermute(mine, "seq", mirrored([(k, 0)], last)) for k in (1, 2, 4)]
    bit = devices // 2
    mine = join(mine, lax.ppermute(given, "seq", [(i, i ^ bit) for i in range(devices)]))
    while bit > 1:
        bit //= 2
        mine = join(mine, lax.ppermute(mine, "seq", mirrored([(i + bit, i) for i in range(bit)], last)))
    return [mine]


def to_owners(slots):
    return lax.all_to_all(slots, "seq", split_axis=0, concat_axis=0, tiled=True)


def sum_seq(keep, send, meta, devices, *before_second):
    got = after(lax.ppermute(send, "seq", [(i, i ^ 1) for i in range(devices)]), *before_second)
    count, rows, lanes = keep.shape
    if count == 4:
        low = sds((rows, lanes), BF16)
        own, *out = call(
            fold_kernel, (sds((rows, lanes), F32), low, low, low), name="fold")(keep, got, smem=(meta,))
        for n, piece in enumerate(out):
            own = own + lax.ppermute(
                piece, "seq", [(i, i ^ (2 * (n + 1))) for i in range(devices)]
            ).astype(F32)
        return own
    total = (keep.astype(F32) + got.astype(F32)).astype(BF16)
    sides = [[i for i in range(devices) if i % 2 == side] for side in range(2)]
    got = lax.all_to_all(
        total, "seq", split_axis=0, concat_axis=0, tiled=True, axis_index_groups=sides
    )
    return got.astype(F32).sum(0)


def per_device(
    layer_input,
    out_grad,
    norm1_gain,
    norm1_shift,
    w_qkv,
    w_out,
    norm2_gain,
    norm2_shift,
    w_up,
    w_down,
    key_keep,
    rand_blocks,
):
    batches, per, width = layer_input.shape
    local = w_qkv.shape[2]
    devices = lax.axis_size("seq")
    myself = lax.axis_index("seq")
    tp_count = lax.axis_size("tp")
    tp_place = lax.axis_index("tp")
    assert local == 3 * HD and tp_count == 4 and devices % 2 == 0 and batches % 2 == 0
    share = per // tp_count
    bd = per // BLOCK
    total = batches * bd
    blocks_all = bd * devices
    groups = 2
    seqs = batches // groups
    piece = seqs * share
    refs = total * RANDS
    slots_per = max(1, -(-refs // devices))
    slots = devices * slots_per
    hidden_here = w_up.shape[1]
    rows = width // devices
    i32 = jnp.int32
    flag = lambda v: v.astype(i32)
    meta = jnp.stack(
        [
            tp_place, flag(myself == 0), flag(myself == devices - 1), flag(in_first_group(myself, devices)), myself,
        ]
    ).astype(i32)

    scale = 1.0 / math.sqrt(HD)
    x_rows = layer_input.reshape(batches * per, width)
    first, q, kv, w640 = project(x_rows, norm1_gain, norm1_shift, w_qkv.transpose(1, 0, 2))
    q_blocks = q.reshape(total, BLOCK, 4 * HD)
    kv_blocks = kv.reshape(total, BLOCK, 6 * HD)
    kv_seqs = kv.reshape(batches, per, 6 * HD)

    table = (
        rand_blocks.reshape(batches, devices, bd, RANDS).transpose(1, 0, 2, 3).reshape(devices, refs)
    )
    owners = table // bd
    source = (jnp.arange(refs, dtype=i32) // (bd * RANDS))[None] * bd + table - owners * bd
    order = jnp.arange(refs, dtype=i32)
    earlier = order[None, :] < order[:, None]
    rank = jnp.sum(((owners[:, :, None] == owners[:, None, :]) & earlier[None]).astype(i32), -1)
    places = jnp.arange(slots_per, dtype=i32)
    asked = (owners == myself)[:, None, :] & (rank[:, None, :] == places[None, :, None])
    source_of = jnp.sum(jnp.where(asked, source[:, None, :], 0), -1).reshape(slots)
    valid = jnp.sum(asked.astype(i32), -1).reshape(slots)
    my_owner = lax.dynamic_index_in_dim(owners, myself, 0, False)
    my_rank = lax.dynamic_index_in_dim(rank, myself, 0, False)
    slot_of = my_owner * slots_per + my_rank
    mine = lax.dynamic_index_in_dim(table, myself, 0, False)
    query_of = jnp.sum(
        jnp.where(
            slot_of[None, :] == jnp.arange(slots, dtype=i32)[:, None], (order // RANDS)[None, :], 0
        ),
        -1,
    )

    end_kv = sds((batches, BLOCK, 6 * HD), BF16)
    end_all = sds((batches, BLOCK, 10 * HD), BF16)
    sent, ends, kv_low, kv_high = call(
        partial(dispatch_kernel, bd),
        (sds((slots, BLOCK, 6 * HD), BF16), end_all, end_kv, end_kv),
        name="dispatch",
    )(q_blocks, kv_blocks, smem=(source_of, meta))
    rand_kv = to_owners(sent)
    up = [(i, i + 1) for i in range(devices - 1)]
    down = [(b, a) for a, b in up]
    low = lax.ppermute(kv_high, "seq", up)
    high = lax.ppermute(kv_low, "seq", down)

    bias, seq_bias, column_bias = call(
        partial(bias_kernel, bd, blocks_all),
        (
            sds((total, 1, 8 * BLOCK), F32),
            sds((batches, 1, per), F32),
            sds((total, BLOCK, 2 * HD), F32),
        ),
        name="bias",
    )(key_keep.reshape(batches * blocks_all, BLOCK), smem=(mine, meta))

    grad_up = dot_nn(out_grad.reshape(batches * per, width), w_down)
    grad_up = grad_up.reshape(batches, per, hidden_here)

    lead0, lead1 = spread(ends, myself, devices, bias, grad_up)

    part = sds((batches, BLOCK, 4 * HD), F32)
    part_mine, part_given = call(lead_fwd_kernel, (part, part), name="lead_fwd")(
        kv_seqs, after(seq_bias, low, high), lead0, lead1, smem=(meta,)
    )
    lead_out, lead_lse = call(
        lead_finish_kernel,
        (sds(part.shape, BF16), sds((batches, BLOCK, 2 * HD), F32)),
        name="lead_finish",
        limit=SMALL,
    )(*collect(part_mine, part_given, devices, merge))

    low_piece = sds((piece, width), BF16)
    mixed, lse, attn_parts = [], [], []
    for g in range(groups):
        half_of = lambda array, g=g: part_of(array, g, groups)
        out, stat, *parts = call(
            partial(sparse_fwd_kernel, g * seqs * bd, seqs, per, share),
            (sds((4 * piece, 4 * HD), BF16), sds((seqs * per, 2 * HD), F32)) + (low_piece,) * 4,
            (
                pltpu.VMEM((seqs, per + 2 * BLOCK, 6 * HD), BF16),
                pltpu.VMEM((2, 8 * BLOCK, 6 * HD), BF16),
            ),
            name="sparse_fwd",
        )(
            half_of(q_blocks), half_of(kv_seqs), half_of(low), half_of(high), half_of(lead0), half_of(lead1),
            rand_kv, half_of(bias), half_of(lead_out), w_out, smem=(slot_of, meta),
        )
        mixed.append(out)
        lse.append(stat)
        attn_parts.append(parts)

    flat = lambda lists: [v for group in lists for v in group]
    high_piece = sds((piece, width), F32)
    hidden, act, total_grad, sums2, attn_grad = [], [], [], [], []
    ups, pres, back_parts = [], [], []
    for g in range(groups):
        h, a = share_call(mid_fwd_kernel, (high_piece, low_piece), [(layer_input, g, 0)], "mid_fwd")(
            meta, seqs, share, *scatter_tp(attn_parts[g]), after(norm2_gain, mixed[-1], *hidden), norm2_shift
        )
        hidden.append(h)
        act.append(gather_tp(a))
    q_late = after(q_blocks, *hidden, act[0][1])
    q_slots = call(gather_kernel, sds((slots, BLOCK, 4 * HD), BF16), name="gather")(q_late, smem=(query_of,))
    rand_q = to_owners(q_slots)
    low_hidden = sds((piece, hidden_here), BF16)
    for g in range(groups):
        out = share_call(
            ffn_kernel, (low_hidden, low_hidden, low_piece) * 4, [(grad_up, g, k) for k in range(4)], "ffn", PARAMS
        )(meta, seqs, share, *act[g], w_up)
        ups.append(out[0::3])
        pres.append(out[1::3])
        back_parts.append(out[2::3])
    lanes = 2 * hidden_here
    halves = sds((devices // 2, rows, lanes), BF16)
    ff_keep, ff_send = call(
        partial(ffn_grad_kernel, groups, seqs, per, share, devices),
        (halves, halves),
        (
            pltpu.VMEM((batches * per, width), BF16),
            pltpu.VMEM((batches * per, hidden_here), BF16),
            pltpu.VMEM((width, lanes), F32),
        ),
        name="ffn_grad",
    )(
        out_grad.reshape(batches * per, width), *flat(ups), *flat(act), *flat(pres), smem=(meta,)
    )
    for g in range(groups):
        t, a, s = share_call(
            mid_bwd_kernel, (high_piece, low_piece, sds((2, width), F32)), [(out_grad, g, 0)], "mid_bwd"
        )(meta, seqs, share, *scatter_tp(back_parts[g]), hidden[g], norm2_gain)
        total_grad.append(t)
        sums2.append(s)
        attn_grad.append(gather_tp(a))

    grads, sent, lead_grad = call(
        partial(heads_grad_kernel, groups, seqs, per, share),
        (
            sds((batches * per, 4 * HD), BF16),
            sds((slots, BLOCK, 4 * HD), BF16),
            sds((batches, BLOCK, 4 * HD), BF16),
        ),
        name="heads_grad",
    )(after(w_out, ff_send), lead_lse, *attn_grad[0], *attn_grad[1], *mixed, *lse, smem=(query_of, meta))
    lead_do = spread(lead_grad, myself, devices)
    rand_do = to_owners(after(sent, lead_do[0], rand_q))
    dend = sds(end_kv.shape, F32)
    dq, dkv, ret_low, ret_high, dlead0, dlead1 = call(
        partial(sparse_bwd_kernel, batches, per),
        (sds((total, BLOCK, 4 * HD), F32), sds((batches, per, 6 * HD), F32), end_kv, end_kv, dend, dend),
        (
            pltpu.VMEM((batches, per + 2 * BLOCK, 6 * HD), BF16),
            pltpu.VMEM((2, 8 * BLOCK, 6 * HD), BF16),
            pltpu.VMEM((batches, per + 2 * BLOCK, 6 * HD), F32),
            pltpu.VMEM((batches, 2 * BLOCK, 6 * HD), F32),
        ),
        name="sparse_bwd",
    )(
        q_blocks, kv_seqs, low, high, lead0, lead1, rand_kv, bias,
        after(grads, *lead_do).reshape(total, BLOCK, 4 * HD), smem=(slot_of,),
    )
    from_low = lax.ppermute(ret_high, "seq", up)
    from_high = lax.ppermute(ret_low, "seq", down)
    dkv, ends_mine, ends_given = call(
        lead_bwd_kernel, (sds((batches, per, 6 * HD), F32), end_all, end_all), name="lead_bwd"
    )(lead0, lead1, kv_seqs, seq_bias, dkv, dlead0, dlead1, *lead_do, smem=(meta,))
    add = lambda a, b: (a.astype(F32) + b.astype(F32)).astype(BF16)
    ends_got = collect(ends_mine, ends_given, devices, add)

    outputs = []
    for g in range(groups):
        parts = [dot_nt(ups[g][k], w_down).astype(BF16) for k in range(4)]
        outputs += [*scatter_tp(parts), hidden[g]]
    layer_output = call(
        partial(output_kernel, groups), sds((batches, share, width), F32), name="output")(*outputs)
    halves = sds((devices // 2, rows, 4 * HD), BF16)
    out_keep, out_send = call(
        partial(out_grad_kernel, groups, devices),
        (halves, halves),
        (pltpu.VMEM((4 * piece, width), BF16), pltpu.VMEM((width, 4 * HD), F32)),
        name="out_grad",
    )(*flat(attn_grad), *mixed, smem=(after(meta, ends_mine),))

    halves = sds((devices // 2, rows, 10 * HD), BF16)
    gqkv, qkv_keep, qkv_send = call(
        partial(tail_kernel, seqs, per, devices),
        (sds((total * BLOCK, 10 * HD), BF16), halves, halves),
        (
            pltpu.VMEM((total, BLOCK, 6 * HD), F32),
            pltpu.VMEM((width, 10 * HD), F32),
            pltpu.VMEM((batches, BLOCK, 10 * HD), F32),
        ),
        name="tail",
    )(
        rand_q, rand_do, kv_blocks, column_bias, dq, dkv.reshape(total, BLOCK, 6 * HD), from_low,
        from_high, first, *ends_got, smem=(source_of, valid, meta),
    )
    gq = sum_seq(qkv_keep, qkv_send, meta, devices)
    ff = sum_seq(ff_keep, ff_send, meta, devices, rand_do)
    g_down, g_up = ff[:, :hidden_here], ff[:, hidden_here:]
    g_out = sum_seq(out_keep, out_send, meta, devices, rand_do)
    g_out = jnp.concatenate([g_out[:, : 2 * HD], g_out[:, 3 * HD :]], 1)
    *first_back, sums1 = call(
        partial(back_kernel, groups, seqs, per, share),
        (low_piece,) * (4 * groups) + (sds((2, width), F32),),
        name="back")(gqkv, x_rows, w640, smem=(meta,))
    terms = []
    for g in range(groups):
        terms += [*scatter_tp(first_back[4 * g : 4 * g + 4]), total_grad[g]]
    sums1 = after(sums1, terms[1])
    input_grad = share_call(
        partial(end_kernel, groups),
        sds((batches, share, width), F32),
        [(layer_input, g, 0) for g in range(groups)],
        "end",
    )(meta, seqs, share, *terms, norm1_gain)

    g_qkv = jnp.stack(
        [
            gq[:, : 3 * HD] * scale,
            jnp.concatenate([gq[:, 4 * HD : 6 * HD], gq[:, 8 * HD : 9 * HD]], 1),
            jnp.concatenate([gq[:, 6 * HD : 8 * HD], gq[:, 9 * HD :]], 1),
        ],
        1,
    )
    norms = jnp.concatenate([sums1, sum(sums2)], 0).reshape(4, devices, 1, rows)
    norms = jnp.broadcast_to(norms.transpose(1, 2, 0, 3), (devices, tp_count, 4, rows))
    norms = lax.all_to_all(
        norms.reshape(devices * tp_count, 4, rows), ("seq", "tp"), split_axis=0, concat_axis=0, tiled=True
    ).sum(0)
    return (
        layer_output, input_grad, g_qkv, g_out, g_up, g_down, norms[0], norms[1], norms[2], norms[3],
    )


def solution(mesh):
    return jax.shard_map(
        per_device,
        mesh=mesh,
        in_specs=(
            P(None, "seq", None),
            P(None, "seq", None),
            P(),
            P(),
            P(None, None, "tp"),
            P(None, "tp"),
            P(),
            P(),
            P(None, "tp"),
            P(None, "tp"),
            P(),
            P(),
        ),
        out_specs=(
            P(None, ("seq", "tp"), None),
            P(None, ("seq", "tp"), None),
            P("seq", None, "tp"),
            P("seq", "tp"),
            P("seq", "tp"),
            P("seq", "tp"),
            P("seq"),
            P("seq"),
            P("seq"),
            P("seq"),
        ),
        check_vma=False,
    )
```

```python
from functools import partial
import math

import jax
import jax.numpy as jnp
from jax import lax
from jax.experimental import pallas as pl
from jax.experimental.pallas import tpu as pltpu
from jax.sharding import PartitionSpec as P

HD = 64
BLOCK = 64
RANDS = 3
EPS = 1e-06
SWAP = (0, 2, 1, 3)
NEG = -1e30
F32 = jnp.float32
BF16 = jnp.bfloat16
VMEM = pl.BlockSpec(memory_space=pltpu.VMEM)
SMEM = pl.BlockSpec(memory_space=pltpu.SMEM)
MIB = 1024 * 1024


def sds(shape, kind):
    return jax.ShapeDtypeStruct(shape, kind)


PARAMS = pltpu.CompilerParams(vmem_limit_bytes=56 * MIB)
SMALL = pltpu.CompilerParams(vmem_limit_bytes=12 * MIB)


def after(value, *others):
    return lax.optimization_barrier((value,) + others)[0]


class Chain:
    last = ()

    def link(self, value):
        return after(value, *self.last) if self.last else value

    def done(self, outs):
        self.last = (jax.tree.leaves(outs)[0],)
        return outs


CHAIN = Chain()


def part_of(array, at, count):
    return array, at, count


TIMES = {
    "project": 6, "dispatch": 3, "bias": 2, "lead_fwd": 4, "sparse_fwd": 7, "merge": 1, "lead_finish": 1, "out_project": 1,
    "mid_fwd": 1, "gather": 2, "ffn": 6, "ffn_grad": 7, "mid_bwd": 1, "heads_grad": 5, "lead_grad": 1, "sparse_bwd": 13,
    "fold_near": 3, "down": 6, "lead_bwd": 5, "slots": 14, "tail": 5, "fold_far": 2, "back": 7, "output": 1,
    "fold": 2, "end": 2,
}
HINT = 1.75e6


def cost(name):
    return pl.CostEstimate(flops=0, transcendentals=0, bytes_accessed=int(TIMES[name] * HINT))


def call(body, outs, scratch=(), name=None, limit=PARAMS):
    def run(*args, smem=()):
        specs = [SMEM] * len(smem)
        arrays = []
        if smem:
            smem = (CHAIN.link(smem[0]),) + tuple(smem[1:])
        else:
            args = (CHAIN.link(args[0]),) + args[1:]
        for arg in args:
            if isinstance(arg, tuple):
                array, at, count = arg
                shape = (array.shape[0] // count,) + array.shape[1:]
                index = (at,) + (0,) * (array.ndim - 1)
                specs.append(pl.BlockSpec(shape, lambda i, index=index: index))
                arrays.append(array)
            else:
                specs.append(VMEM)
                arrays.append(arg)
        return CHAIN.done(
            pl.pallas_call(
                body,
                out_shape=outs,
                grid=(1,),
                in_specs=specs,
                out_specs=jax.tree.map(lambda _: VMEM, outs),
                scratch_shapes=list(scratch),
                compiler_params=limit,
                cost_estimate=cost(name),
                name=name,
            )(*smem, *arrays)
        )

    return run


def share_call(body, outs, blocks, name, limit=SMALL):
    def run(meta, seqs, share, *args):
        def spec(value, group, pos):
            return pl.BlockSpec(
                (seqs, share, value.shape[2]), lambda i, meta_ref: (group, meta_ref[0] ^ SWAP[pos], 0)
            )

        return CHAIN.done(
            pl.pallas_call(
                body,
                out_shape=outs,
                grid_spec=pltpu.PrefetchScalarGridSpec(
                    num_scalar_prefetch=1,
                    grid=(1,),
                    in_specs=[spec(*b) for b in blocks] + [VMEM] * len(args),
                    out_specs=jax.tree.map(lambda _: VMEM, outs),
                ),
                compiler_params=limit,
                cost_estimate=cost(name),
                name=name,
            )(CHAIN.link(meta), *(b[0] for b in blocks), *args)
        )

    return run


def dot_nt(a, b):
    return lax.dot_general(a, b, (((1,), (1,)), ((), ())), preferred_element_type=F32)


def dot_tn(a, b):
    return lax.dot_general(a, b, (((0,), (0,)), ((), ())), preferred_element_type=F32)


def dot_nn(a, b):
    return lax.dot_general(a, b, (((1,), (0,)), ((), ())), preferred_element_type=F32)


def two_heads(tile):
    lane = lax.broadcasted_iota(jnp.int32, tile.shape, 1)
    zero = jnp.zeros_like(tile)
    return jnp.concatenate([jnp.where(lane < HD, tile, zero), jnp.where(lane >= HD, tile, zero)], 0)


def pick_heads(pair, rows):
    lane = lax.broadcasted_iota(jnp.int32, (rows, 2 * HD), 1)
    return jnp.where(lane < HD, pair[:rows], pair[rows:])


def half(tile, upper):
    lane = lax.broadcasted_iota(jnp.int32, tile.shape, 1)
    return jnp.where((lane >= HD) if upper else (lane < HD), tile, jnp.zeros_like(tile))


def lanes_of(columns, rows):
    lane = lax.broadcasted_iota(jnp.int32, (rows, 2 * HD), 1)
    out = jnp.zeros((rows, 2 * HD), F32)
    for at, column in enumerate(columns):
        out = jnp.where(lane == at, column, out)
    return out


def hi_lo(value):
    hi = value.astype(BF16).astype(F32)
    return hi, value - hi


def norm_rows(hidden):
    center = hidden - jnp.mean(hidden, -1, keepdims=True)
    inverse = lax.rsqrt(jnp.mean(center * center, -1, keepdims=True) + EPS)
    return center * inverse, inverse


def norm_rows_back(grad, normed, inverse, gain):
    scaled = grad * gain
    return inverse * (
        scaled
        - jnp.mean(scaled, -1, keepdims=True)
        - normed * jnp.mean(scaled * normed, -1, keepdims=True)
    )


def project_kernel(x_ref, gain_ref, shift_ref, raw_ref, first_ref, q_ref, kv_ref, w_ref):
    @pl.when(pl.program_id(0) == 0)
    def _():
        w_ref[:, : 3 * HD] = raw_ref[0] * jnp.asarray(1.0 / math.sqrt(HD), BF16)
        w_ref[:, 3 * HD : 4 * HD] = jnp.zeros((w_ref.shape[0], HD), BF16)
        w_ref[:, 4 * HD : 6 * HD] = raw_ref[1, :, : 2 * HD]
        w_ref[:, 6 * HD : 8 * HD] = raw_ref[2, :, : 2 * HD]
        w_ref[:, 8 * HD :] = jnp.concatenate([raw_ref[1, :, 2 * HD :], raw_ref[2, :, 2 * HD :]], 1)

    normed, _ = norm_rows(x_ref[...].astype(F32))
    first = (normed * gain_ref[...][None] + shift_ref[...][None]).astype(BF16)
    first_ref[...] = first
    out = dot_nn(first, w_ref[...]).astype(BF16)
    q_ref[...] = out[:, : 4 * HD]
    kv_ref[...] = out[:, 4 * HD :]


def project(x, gain, shift, raw):
    rows, width = x.shape
    tile = min(rows, 256)
    row = lambda w: pl.BlockSpec((tile, w), lambda i: (i, 0))
    vector = pl.BlockSpec((width,), lambda i: (0,))
    whole = lambda w: pl.BlockSpec((width, w), lambda i: (0, 0))
    low = lambda *shape: sds(shape, BF16)
    return pl.pallas_call(
        project_kernel,
        grid=(rows // tile,),
        out_shape=(low(rows, width), low(rows, 4 * HD), low(rows, 6 * HD), low(width, 10 * HD)),
        in_specs=[
            row(width), vector, vector, pl.BlockSpec(raw.shape, lambda i: (0, 0, 0)),
        ],
        out_specs=(row(width), row(4 * HD), row(6 * HD), whole(10 * HD)),
        compiler_params=PARAMS,
        cost_estimate=cost("project"),
        name="project",
    )(x, gain, shift, raw)


def dispatch_kernel(bd, index_ref, kv_ref, sent_ref, low_ref, high_ref):
    def step(slot, _):
        sent_ref[slot] = kv_ref[index_ref[slot]]
        return 0

    lax.fori_loop(0, sent_ref.shape[0], step, 0, unroll=4)
    for m in range(low_ref.shape[0]):
        low_ref[m] = kv_ref[m * bd]
        high_ref[m] = kv_ref[m * bd + bd - 1]


def bias_kernel(bd, blocks_all, table_ref, meta_ref, keep_ref, raw_ref, bias_ref, seq_ref, column_ref, wo_ref):
    wo_ref[:, : 2 * HD] = raw_ref[:, : 2 * HD]
    blank = jnp.zeros((wo_ref.shape[0], HD), BF16)
    wo_ref[:, 2 * HD :] = jnp.concatenate([blank, raw_ref[:, 2 * HD :]], 1)
    low = lambda keep: jnp.where(keep > 0, 0.0, NEG)
    for m in range(seq_ref.shape[0]):
        for b in range(bd):
            i = m * bd + b
            here = meta_ref[4] * bd + b

            def row(block, inside=True):
                return low(jnp.where(inside, keep_ref[pl.ds(m * blocks_all + block, 1)], 0))

            own = row(here)
            listed = [
                row(jnp.maximum(here - 1, 0), here > 0),
                own,
                row(jnp.minimum(here + 1, blocks_all - 1), here < blocks_all - 1),
                row(0),
                row(blocks_all - 1),
            ] + [row(table_ref[i * RANDS + j]) for j in range(RANDS)]
            bias_ref[i] = jnp.concatenate(listed, 1)
            seq_ref[m, :, b * BLOCK : (b + 1) * BLOCK] = own
            column_ref[i] = jnp.transpose(jnp.broadcast_to(own, (2 * HD, BLOCK)))


def gather_kernel(index_ref, blocks_ref, out_ref):
    def step(slot, _):
        out_ref[slot] = blocks_ref[index_ref[slot]]
        return 0

    lax.fori_loop(0, out_ref.shape[0], step, 0, unroll=4)


def lead_fwd_kernel(
    meta_ref, kv_ref, bias_ref, x0_ref, x1_ref, gain_ref, shift_ref, w_ref, first0_ref, first1_ref,
    lead0_ref, lead1_ref, mine_ref, given_ref,
):
    for x_ref, first_ref, lead_ref in ((x0_ref, first0_ref, lead0_ref), (x1_ref, first1_ref, lead1_ref)):
        normed, _ = norm_rows(x_ref[...].reshape(-1, x_ref.shape[2]).astype(F32))
        first = (normed * gain_ref[...][None] + shift_ref[...][None]).astype(BF16)
        first_ref[...] = first
        lead_ref[...] = dot_nn(first, w_ref[...]).astype(BF16).reshape(lead_ref.shape)
    low = meta_ref[3]
    rows = 2 * BLOCK
    for m in range(kv_ref.shape[0]):
        both = lambda lo, hi: jnp.concatenate([lead0_ref[m, :, lo:hi], lead1_ref[m, :, lo:hi]], 0)
        bias = bias_ref[m]
        pair = dot_nt(two_heads(both(0, 2 * HD)), kv_ref[m, :, : 2 * HD]) + bias
        last = dot_nt(both(2 * HD, 4 * HD), kv_ref[m, :, 4 * HD :]) + bias
        top_a = jnp.max(pair, -1, keepdims=True)
        top_b = jnp.max(last, -1, keepdims=True)
        exp_a = jnp.exp(pair - top_a)
        exp_b = jnp.exp(last - top_b)
        sum_a = jnp.sum(exp_a, -1, keepdims=True)
        sum_b = jnp.sum(exp_b, -1, keepdims=True)
        out0 = pick_heads(dot_nn(exp_a.astype(BF16), kv_ref[m, :, 2 * HD : 4 * HD]), rows)
        out1 = half(dot_nn(exp_b.astype(BF16), kv_ref[m, :, 4 * HD :]), True)
        out1 = out1 + lanes_of(
            [top_a[:rows], top_a[rows:], top_b, sum_a[:rows], sum_a[rows:], sum_b], rows
        )
        for part_ref, first in ((mine_ref, low == 1), (given_ref, low == 0)):
            part_ref[m, :, : 2 * HD] = jnp.where(first, out0[:BLOCK], out0[BLOCK:])
            part_ref[m, :, 2 * HD :] = jnp.where(first, out1[:BLOCK], out1[BLOCK:])


def merge_parts(parts):
    lane = lax.broadcasted_iota(jnp.int32, (BLOCK, 2 * HD), 1)
    stats = [p[:, 2 * HD :] for p in parts]
    top = stats[0]
    for st in stats[1:]:
        top = jnp.maximum(top, st)
    tops = [top[:, h : h + 1] for h in range(3)]
    sums = [0.0, 0.0, 0.0]
    out0, out1 = 0.0, 0.0
    for p, st in zip(parts, stats):
        scale = [jnp.exp(st[:, h : h + 1] - tops[h]) for h in range(3)]
        sums = [sums[h] + st[:, 3 + h : 4 + h] * scale[h] for h in range(3)]
        out0 = out0 + p[:, : 2 * HD] * jnp.where(lane < HD, scale[0], scale[1])
        out1 = out1 + st * scale[2]
    return out0, jnp.where(lane >= HD, out1, 0.0), tops, sums


def merge_kernel(a_ref, b_ref, out_ref):
    for m in range(a_ref.shape[0]):
        out0, out1, tops, sums = merge_parts([a_ref[m], b_ref[m]])
        out_ref[m, :, : 2 * HD] = out0
        out_ref[m, :, 2 * HD :] = out1 + lanes_of(tops + sums, BLOCK)


def merge(a, b):
    return call(merge_kernel, sds(a.shape, F32), name="merge", limit=SMALL)(a, b)


def lead_finish_kernel(*refs):
    part_refs, (out_ref, lse_ref) = refs[:-2], refs[-2:]
    lane = lax.broadcasted_iota(jnp.int32, (BLOCK, 2 * HD), 1)
    for m in range(out_ref.shape[0]):
        out0, out1, tops, sums = merge_parts([p[m] for p in part_refs])
        out_ref[m, :, : 2 * HD] = (out0 / jnp.where(lane < HD, sums[0], sums[1])).astype(BF16)
        out_ref[m, :, 2 * HD :] = (out1 / sums[2]).astype(BF16)
        lse_ref[m] = lanes_of([tops[h] + jnp.log(sums[h]) for h in range(3)], BLOCK)


def fill_ext(ext_ref, kv_ref, low_ref, high_ref, seqs, per):
    for m in range(seqs):
        ext_ref[m, :BLOCK] = low_ref[m]
        ext_ref[m, BLOCK : BLOCK + per] = kv_ref[m]
        ext_ref[m, BLOCK + per :] = high_ref[m]


def fill_listed(listed_ref, ext_ref, lead0_ref, lead1_ref, rand_ref, slot_ref, m, b, block):
    listed_ref[: 3 * BLOCK] = ext_ref[m, pl.ds(pl.multiple_of(b * BLOCK, BLOCK), 3 * BLOCK)]
    listed_ref[3 * BLOCK : 4 * BLOCK] = lead0_ref[m, :, 4 * HD :]
    listed_ref[4 * BLOCK : 5 * BLOCK] = lead1_ref[m, :, 4 * HD :]
    for j in range(RANDS):
        listed_ref[(5 + j) * BLOCK : (6 + j) * BLOCK] = rand_ref[slot_ref[block * RANDS + j]]


def pos_of(meta_ref, at):
    j = at ^ meta_ref[0]
    return ((j & 1) << 1) | (j >> 1)


def sparse_fwd_kernel(
    first, seqs, per, share, slot_ref, meta_ref, q_ref, kv_ref, low_ref, high_ref, lead0_ref,
    lead1_ref, rand_ref, bias_ref, out_ref, lse_ref, ext_ref, listed_ref,
):
    blocks = per // BLOCK
    chunk = min(share, BLOCK)
    fill_ext(ext_ref, kv_ref, low_ref, high_ref, seqs, per)

    def attend(i, here):
        m, b = i // blocks, i % blocks
        fill_listed(here, ext_ref, lead0_ref, lead1_ref, rand_ref, slot_ref, m, b, first + i)
        bias = bias_ref[i]
        pair = dot_nt(two_heads(q_ref[i, :, : 2 * HD]), here[:, : 2 * HD]) + bias
        last = dot_nt(q_ref[i, :, 2 * HD :], here[:, 4 * HD :]) + bias
        top_a = jnp.max(pair, -1, keepdims=True)
        top_b = jnp.max(last, -1, keepdims=True)
        exp_a = jnp.exp(pair - top_a)
        exp_b = jnp.exp(last - top_b)
        sum_a = jnp.sum(exp_a, -1, keepdims=True)
        sum_b = jnp.sum(exp_b, -1, keepdims=True)
        prob_a = (exp_a * (1.0 / sum_a)).astype(BF16)
        prob_b = (exp_b * (1.0 / sum_b)).astype(BF16)
        out0 = pick_heads(dot_nn(prob_a, here[:, 2 * HD : 4 * HD]), BLOCK).astype(BF16)
        out1 = half(dot_nn(prob_b, here[:, 4 * HD :]), True).astype(BF16)
        lse_a = top_a + jnp.log(sum_a)
        lse_b = top_b + jnp.log(sum_b)
        lse_ref[pl.ds(pl.multiple_of(i * BLOCK, BLOCK), BLOCK)] = lanes_of(
            [lse_a[:BLOCK], lse_a[BLOCK:], lse_b], BLOCK
        )
        for c in range(BLOCK // chunk):
            token = b * BLOCK + c * chunk
            at = token // share
            row = pos_of(meta_ref, at) * (seqs * share) + m * share + (token - at * share)
            rows = pl.ds(pl.multiple_of(row, chunk), chunk)
            out_ref[rows, : 2 * HD] = out0[c * chunk : (c + 1) * chunk]
            out_ref[rows, 2 * HD :] = out1[c * chunk : (c + 1) * chunk]

    def step(j, _):
        attend(2 * j, listed_ref.at[0])
        attend(2 * j + 1, listed_ref.at[1])
        return 0

    lax.fori_loop(0, seqs * blocks // 2, step, 0)


def out_project_kernel(groups, seqs, per, share, meta_ref, wo_ref, lead_out_ref, *refs):
    attn_refs, mixed_refs, part_refs = refs[:groups], refs[groups : 2 * groups], refs[2 * groups :]
    blocks = per // BLOCK
    chunk = min(share, BLOCK)
    piece = seqs * share
    for g in range(groups):
        mixed_refs[g][...] = attn_refs[g][...]
    for end, b in ((1, 0), (2, blocks - 1)):

        @pl.when(meta_ref[end] == 1)
        def _(b=b):
            for g in range(groups):
                for m in range(seqs):
                    for c in range(BLOCK // chunk):
                        token = b * BLOCK + c * chunk
                        at = token // share
                        row = pos_of(meta_ref, at) * piece + m * share + (token - at * share)
                        rows = pl.ds(pl.multiple_of(row, chunk), chunk)
                        mixed_refs[g][rows] = lead_out_ref[g * seqs + m, c * chunk : (c + 1) * chunk]

    wo = wo_ref[...]
    for g in range(groups):
        for k in range(4):
            rows = slice(k * piece, (k + 1) * piece)
            part_refs[4 * g + k][...] = dot_nt(mixed_refs[g][rows], wo).astype(BF16)


def down_kernel(*refs):
    count = len(refs) // 2
    for n in range(count):
        refs[count + 1 + n][...] = dot_nt(refs[n][...], refs[count][...]).astype(BF16)


def total_of(refs):
    return refs[0][...].astype(F32) + refs[1][...].astype(F32) + refs[2][...].astype(F32)


def mid_fwd_kernel(meta_ref, x_ref, own_ref, core_ref, y_ref, gain_ref, shift_ref, hidden_ref, act_ref):
    x = x_ref[...].reshape(hidden_ref.shape).astype(F32)
    hidden = total_of((own_ref, core_ref, y_ref)) + x
    normed, _ = norm_rows(hidden)
    hidden_ref[...] = hidden
    act_ref[...] = (normed * gain_ref[...][None] + shift_ref[...][None]).astype(BF16)


def ffn_kernel(meta_ref, *refs):
    gu_refs, act_refs, w_ref, outs = refs[:4], refs[4:8], refs[8], refs[9:]
    rows = act_refs[0].shape[0]
    for k in (3, 2, 1, 0):
        up_ref, pre_ref, back_ref = outs[3 * k : 3 * k + 3]
        pre = dot_nn(act_refs[k][...], w_ref[...])
        phi = 0.5 + 0.5 * lax.erf(pre * (1.0 / math.sqrt(2.0)))
        density = jnp.exp(-0.5 * pre * pre) * (1.0 / math.sqrt(2.0 * math.pi))
        up_ref[...] = (pre * phi).astype(BF16)
        gu = gu_refs[k][...].reshape(rows, gu_refs[k].shape[2])
        grad_pre = (gu * (phi + pre * density)).astype(BF16)
        pre_ref[...] = grad_pre
        back_ref[...] = dot_nt(grad_pre, w_ref[...]).astype(BF16)


def mid_bwd_kernel(
    meta_ref, og_ref, own_ref, core_ref, y_ref, hidden_ref, gain_ref, total_ref, low_ref, sums_ref
):
    grad = total_of((own_ref, core_ref, y_ref))
    normed, inverse = norm_rows(hidden_ref[...])
    og = og_ref[...].reshape(hidden_ref.shape).astype(F32)
    total = og + norm_rows_back(grad, normed, inverse, gain_ref[...][None])
    total_ref[...] = total
    low_ref[...] = total.astype(BF16)
    sums_ref[0:1] = jnp.sum(grad * normed, 0, keepdims=True)
    sums_ref[1:2] = jnp.sum(grad, 0, keepdims=True)


def end_kernel(groups, meta_ref, *refs):
    x_refs, refs = refs[:groups], refs[groups:]
    gain_ref, out_ref = refs[-2:]
    seqs = x_refs[0].shape[0]
    for g in range(groups):
        grad = total_of(refs[4 * g : 4 * g + 3])
        normed, inverse = norm_rows(x_refs[g][...].reshape(grad.shape).astype(F32))
        total = refs[4 * g + 3][...] + norm_rows_back(grad, normed, inverse, gain_ref[...][None])
        out_ref[g * seqs : (g + 1) * seqs] = total.reshape(x_refs[g].shape)


def output_kernel(groups, *refs):
    out_ref = refs[-1]
    seqs, share, width = out_ref.shape
    seqs //= groups
    for g in range(groups):
        total = total_of(refs[4 * g : 4 * g + 3]) + refs[4 * g + 3][...]
        out_ref[g * seqs : (g + 1) * seqs] = total.reshape(seqs, share, width)


def lead_grad_kernel(groups, seqs, per, share, meta_ref, wo_ref, lead_lse_ref, lead_out_ref, *refs):
    pieces, lead_ref, rows_ref = refs[:-2], refs[-2], refs[-1]
    blocks = per // BLOCK
    chunk = min(share, BLOCK)
    root = (meta_ref[1] + meta_ref[2]) == 1
    lead_ref[...] = jnp.zeros_like(lead_ref)
    token = jnp.where(meta_ref[1] == 1, 0, (blocks - 1) * BLOCK)
    for g in range(groups):
        for m in range(seqs):
            for c in range(BLOCK // chunk):
                at = (token + c * chunk) // share
                inside = pl.multiple_of(m * share + (token + c * chunk - at * share), chunk)
                for k in range(4):

                    @pl.when(root & (pos_of(meta_ref, at) == k))
                    def _(k=k, g=g, m=m, c=c, inside=inside):
                        to = (g * seqs + m) * BLOCK + c * chunk
                        rows_ref[to : to + chunk] = pieces[4 * g + k][pl.ds(inside, chunk)]

    @pl.when(root)
    def _():
        total = groups * seqs * BLOCK
        grad = dot_nn(rows_ref[...], wo_ref[...])
        low = grad.astype(BF16)
        prod = low.astype(F32) * lead_out_ref[...].reshape(total, 4 * HD).astype(F32)
        deltas = [
            jnp.sum(half(prod[:, : 2 * HD], False), -1, keepdims=True),
            jnp.sum(half(prod[:, : 2 * HD], True), -1, keepdims=True),
            jnp.sum(half(prod[:, 2 * HD :], True), -1, keepdims=True),
        ]
        d_hi, d_lo = zip(*(hi_lo(d) for d in deltas))
        lse = lead_lse_ref[...].reshape(total, 2 * HD)
        l_hi, l_lo = zip(*(hi_lo(lse[:, h : h + 1]) for h in range(3)))
        stats = lanes_of(l_hi + l_lo + d_hi + d_lo, total)
        tile1 = (half(grad[:, 2 * HD :], True) + stats).astype(BF16)
        lead_ref[:, :, : 2 * HD] = low[:, : 2 * HD].reshape(groups * seqs, BLOCK, 2 * HD)
        lead_ref[:, :, 2 * HD :] = tile1.reshape(groups * seqs, BLOCK, 2 * HD)


def heads_grad_kernel(groups, seqs, per, share, index_ref, meta_ref, wo_ref, *refs):
    pieces, mixed_refs = refs[: 4 * groups], refs[4 * groups : 5 * groups]
    lse_refs = refs[5 * groups : 6 * groups]
    grads_ref, sent_ref = refs[6 * groups :]
    wo = wo_ref[...]
    blocks = per // BLOCK
    rows_of = seqs * share
    for g in range(groups):
        for k in range(4):
            grad = dot_nn(pieces[4 * g + k][...], wo)
            low = grad.astype(BF16)
            prod = low.astype(F32) * mixed_refs[g][k * rows_of : (k + 1) * rows_of].astype(F32)
            deltas = [
                jnp.sum(half(prod[:, : 2 * HD], False), -1, keepdims=True),
                jnp.sum(half(prod[:, : 2 * HD], True), -1, keepdims=True),
                jnp.sum(half(prod[:, 2 * HD :], True), -1, keepdims=True),
            ]
            d_hi, d_lo = zip(*(hi_lo(d) for d in deltas))
            spare = [jnp.zeros_like(d_hi[0])] * 6
            stats = lanes_of(spare + list(d_hi + d_lo), rows_of)
            for m in range(seqs):
                at = slice(m * share, (m + 1) * share)
                inside = m * per + (meta_ref[0] ^ SWAP[k]) * share
                rows = pl.ds(pl.multiple_of(g * seqs * per + inside, share), share)
                lse = lse_refs[g][pl.ds(pl.multiple_of(inside, share), share)]
                l_hi, l_lo = zip(*(hi_lo(lse[:, h : h + 1]) for h in range(3)))
                grads_ref[rows, : 2 * HD] = low[at, : 2 * HD]
                grads_ref[rows, 2 * HD :] = (
                    half(grad[at, 2 * HD :], True) + stats[at] + lanes_of(l_hi + l_lo, share)
                ).astype(BF16)
    lane = lax.broadcasted_iota(jnp.int32, (BLOCK, 2 * HD), 1)
    for end, b in ((1, 0), (2, blocks - 1)):

        @pl.when(meta_ref[end] == 1)
        def _(b=b):
            for m in range(groups * seqs):
                rows = slice(m * per + b * BLOCK, m * per + (b + 1) * BLOCK)
                tile1 = grads_ref[rows, 2 * HD :].astype(F32)
                grads_ref[rows, : 2 * HD] = jnp.zeros((BLOCK, 2 * HD), BF16)
                grads_ref[rows, 2 * HD :] = jnp.where(lane < 6, tile1, 0.0).astype(BF16)

    def send(slot, _):
        at = pl.multiple_of(index_ref[slot] * BLOCK, BLOCK)
        sent_ref[slot] = grads_ref[pl.ds(at, BLOCK)]
        return 0

    lax.fori_loop(0, sent_ref.shape[0], send, 0, unroll=4)


def row_stats(tile):
    st = tile.astype(F32)
    lse = [st[:, h : h + 1] + st[:, 3 + h : 4 + h] for h in range(3)]
    delta = [st[:, 6 + h : 7 + h] + st[:, 9 + h : 10 + h] for h in range(3)]
    return lse, delta


def sparse_bwd_kernel(
    batches, per, slot_ref, q_ref, kv_ref, low_ref, high_ref, lead0_ref, lead1_ref, rand_ref,
    bias_ref, grads_ref, dq_ref, dkv_ref, ret_low_ref, ret_high_ref, dlead0_ref, dlead1_ref,
    ext_ref, listed_ref, dext_ref, dlead_ref,
):
    blocks = per // BLOCK
    near = 6 * BLOCK
    fill_ext(ext_ref, kv_ref, low_ref, high_ref, batches, per)
    dext_ref[...] = jnp.zeros_like(dext_ref)
    dlead_ref[...] = jnp.zeros_like(dlead_ref)

    def attend(i, here):
        m, b = i // blocks, i % blocks
        fill_listed(here, ext_ref, lead0_ref, lead1_ref, rand_ref, slot_ref, m, b, i)
        bias = bias_ref[i]
        tile1 = grads_ref[i, :, 2 * HD :]
        lse, delta = row_stats(tile1)
        q_a, q_b = two_heads(q_ref[i, :, : 2 * HD]), q_ref[i, :, 2 * HD :]
        do_a, do_b = two_heads(grads_ref[i, :, : 2 * HD]), half(tile1, True)
        prob_a = jnp.exp(dot_nt(q_a, here[:, : 2 * HD]) + bias - jnp.concatenate(lse[:2], 0))
        prob_b = jnp.exp(dot_nt(q_b, here[:, 4 * HD :]) + bias - lse[2])
        ds_a = prob_a * (dot_nt(do_a, here[:, 2 * HD : 4 * HD]) - jnp.concatenate(delta[:2], 0))
        ds_b = prob_b * (dot_nt(do_b, here[:, 4 * HD :]) - delta[2])
        ds_a, ds_b = ds_a.astype(BF16), ds_b.astype(BF16)
        dq_ref[i, :, : 2 * HD] = pick_heads(dot_nn(ds_a, here[:, : 2 * HD]), BLOCK)
        dq_ref[i, :, 2 * HD :] = half(dot_nn(ds_b, here[:, 4 * HD :]), False)
        prob_a, prob_b = prob_a[:, :near].astype(BF16), prob_b[:, :near].astype(BF16)
        dkv = jnp.concatenate(
            [
                dot_tn(ds_a[:, :near], q_a),
                dot_tn(prob_a, do_a),
                dot_tn(ds_b[:, :near], q_b) + dot_tn(prob_b, do_b),
            ],
            1,
        )
        return m, b, dkv

    def step(j, _):
        done = [attend(2 * j + n, listed_ref.at[n]) for n in range(2)]
        for m, b, dkv in done:
            dext_ref[m, pl.ds(pl.multiple_of(b * BLOCK, BLOCK), 3 * BLOCK)] += dkv[: 3 * BLOCK]
            dlead_ref[m] += dkv[3 * BLOCK : 5 * BLOCK]
        return 0

    lax.fori_loop(0, batches * blocks // 2, step, 0)
    for m in range(batches):
        ret_low_ref[m] = dext_ref[m, :BLOCK].astype(BF16)
        dkv_ref[m] = dext_ref[m, BLOCK : BLOCK + per]
        ret_high_ref[m] = dext_ref[m, BLOCK + per :].astype(BF16)
        dlead0_ref[m] = dlead_ref[m, :BLOCK]
        dlead1_ref[m] = dlead_ref[m, BLOCK:]


def lead_bwd_kernel(
    meta_ref, lead0_ref, lead1_ref, kv_ref, bias_ref, sparse_ref, dlead0_ref, dlead1_ref, do0_ref, do1_ref,
    dkv_ref, mine_ref, given_ref,
):
    low = meta_ref[3]
    rows = 2 * BLOCK
    for m in range(kv_ref.shape[0]):
        both = lambda a, b, lo, hi: jnp.concatenate([a[m, :, lo:hi], b[m, :, lo:hi]], 0)
        tile1 = both(do0_ref, do1_ref, 2 * HD, 4 * HD)
        lse, delta = row_stats(tile1)
        q_a = two_heads(both(lead0_ref, lead1_ref, 0, 2 * HD))
        q_b = both(lead0_ref, lead1_ref, 2 * HD, 4 * HD)
        do_a, do_b = two_heads(both(do0_ref, do1_ref, 0, 2 * HD)), half(tile1, True)
        k_a, v_a, kv_b = kv_ref[m, :, : 2 * HD], kv_ref[m, :, 2 * HD : 4 * HD], kv_ref[m, :, 4 * HD :]
        bias = bias_ref[m]
        prob_a = jnp.exp(dot_nt(q_a, k_a) + bias - jnp.concatenate(lse[:2], 0))
        prob_b = jnp.exp(dot_nt(q_b, kv_b) + bias - lse[2])
        ds_a = (prob_a * (dot_nt(do_a, v_a) - jnp.concatenate(delta[:2], 0))).astype(BF16)
        ds_b = (prob_b * (dot_nt(do_b, kv_b) - delta[2])).astype(BF16)
        dq_a = pick_heads(dot_nn(ds_a, k_a), rows)
        dq_b = half(dot_nn(ds_b, kv_b), False)
        for part_ref, first in ((mine_ref, low == 1), (given_ref, low == 0)):
            part_ref[m, :, : 2 * HD] = jnp.where(first, dq_a[:BLOCK], dq_a[BLOCK:]).astype(BF16)
            part_ref[m, :, 2 * HD : 4 * HD] = jnp.where(first, dq_b[:BLOCK], dq_b[BLOCK:]).astype(BF16)
            part_ref[m, :, 4 * HD :] = jnp.where(first, dlead0_ref[m], dlead1_ref[m]).astype(BF16)
        dkv_ref[m, :, : 2 * HD] = sparse_ref[m, :, : 2 * HD] + dot_tn(ds_a, q_a)
        dkv_ref[m, :, 2 * HD : 4 * HD] = sparse_ref[m, :, 2 * HD : 4 * HD] + dot_tn(
            prob_a.astype(BF16), do_a
        )
        dkv_ref[m, :, 4 * HD :] = (
            sparse_ref[m, :, 4 * HD :] + dot_tn(ds_b, q_b) + dot_tn(prob_b.astype(BF16), do_b)
        )


def split_rows(devices, meta_ref, grad_ref, keep_ref, send_ref):
    rows = keep_ref.shape[1]
    even = (meta_ref[4] & 1) == 0
    for z in range(devices // 2):
        one = grad_ref[2 * z * rows : (2 * z + 1) * rows].astype(BF16)
        two = grad_ref[(2 * z + 1) * rows : (2 * z + 2) * rows].astype(BF16)
        keep_ref[z] = jnp.where(even, one, two)
        send_ref[z] = jnp.where(even, two, one)


def ffn_grad_kernel(groups, seqs, per, share, devices, meta_ref, og_ref, *refs):
    count = 4 * groups
    ups, acts, pres = (refs[n * count : (n + 1) * count] for n in range(3))
    keep_ref, send_ref, left_ref, right_ref, grad_ref = refs[3 * count :]
    piece = seqs * share
    hidden = ups[0].shape[1]
    for g in range(groups):
        for k in range(4):
            for m in range(seqs):
                row = (g * seqs + m) * per + (meta_ref[0] ^ SWAP[k]) * share
                rows = pl.ds(pl.multiple_of(row, share), share)
                right_ref[rows] = ups[4 * g + k][m * share : (m + 1) * share]
    grad_ref[:, :hidden] = dot_tn(og_ref[...], right_ref[...])
    for n in range(count):
        left_ref[n * piece : (n + 1) * piece] = acts[n][...]
        right_ref[n * piece : (n + 1) * piece] = pres[n][...]
    grad_ref[:, hidden:] = dot_tn(left_ref[...], right_ref[...])
    split_rows(devices, meta_ref, grad_ref, keep_ref, send_ref)


def fold_kernel(count, meta_ref, *refs):
    pairs, out_refs = refs[: 2 * count], refs[2 * count :]
    z = meta_ref[4] >> 1
    for n, ref in enumerate(out_refs):
        at = 0
        for keep_ref, got_ref in zip(pairs[::2], pairs[1::2]):
            lanes = keep_ref.shape[2]
            total = keep_ref[z ^ n].astype(F32) + got_ref[z ^ n].astype(F32)
            ref[:, at : at + lanes] = total.astype(ref.dtype)
            at += lanes


def fold_half_kernel(bit, meta_ref, keep_ref, got_ref, own_ref, send_ref):
    place = (meta_ref[4] >> bit) & 1
    for n in range(own_ref.shape[0]):
        for ref, side in ((own_ref, place), (send_ref, 1 - place)):
            at = 2 * n + side
            ref[n] = (keep_ref[at].astype(F32) + got_ref[at].astype(F32)).astype(ref.dtype)


def slots_kernel(
    index_ref, valid_ref, q_got_ref, do_got_ref, kv_ref, column_ref, dkv_ref, acc_ref
):
    acc_ref[...] = dkv_ref[...]

    def block_grads(c):
        at = index_ref[c]
        live = valid_ref[c] == 1
        kv = kv_ref[at]
        tile1 = do_got_ref[c, :, 2 * HD :]
        stats = jnp.transpose(tile1.astype(F32))
        lse = [stats[h : h + 1] + stats[3 + h : 4 + h] for h in range(3)]
        delta = [stats[6 + h : 7 + h] + stats[9 + h : 10 + h] for h in range(3)]
        q_a, q_b = two_heads(q_got_ref[c, :, : 2 * HD]), q_got_ref[c, :, 2 * HD :]
        do_a, do_b = two_heads(do_got_ref[c, :, : 2 * HD]), half(tile1, True)
        bias = column_ref[at]
        drop = lambda v: jnp.where(live, v, 0.0)
        prob_a = drop(
            jnp.exp(dot_nt(kv[:, : 2 * HD], q_a) + bias - jnp.concatenate(lse[:2], 1))
        )
        prob_b = drop(jnp.exp(dot_nt(kv[:, 4 * HD :], q_b) + bias[:, :BLOCK] - lse[2]))
        ds_a = prob_a * (dot_nt(kv[:, 2 * HD : 4 * HD], do_a) - jnp.concatenate(delta[:2], 1))
        ds_b = prob_b * (dot_nt(kv[:, 4 * HD :], do_b) - delta[2])
        return at, (
            dot_nn(ds_a.astype(BF16), q_a),
            dot_nn(prob_a.astype(BF16), do_a),
            dot_nn(ds_b.astype(BF16), q_b) + dot_nn(prob_b.astype(BF16), do_b),
        )

    slots = q_got_ref.shape[0]
    wide = 4 if slots % 4 == 0 else 1

    def slot(j, _):
        done = [block_grads(wide * j + n) for n in range(wide)]
        for at, tiles in done:
            for n, tile in enumerate(tiles):
                acc_ref[at, :, n * 2 * HD : (n + 1) * 2 * HD] += tile
        return 0

    lax.fori_loop(0, slots // wide, slot, 0)


def tail_kernel(
    groups, per, devices, meta_ref, dq_ref, dkv_ref, ret_low_ref, ret_high_ref, first_ref, first0_ref, first1_ref,
    mine_ref, given_ref, *refs,
):
    pieces, mixed_refs = refs[: 4 * groups], refs[4 * groups : 5 * groups]
    w_ref, gain_ref, shift_ref = refs[5 * groups : 5 * groups + 3]
    gqkv_ref, keep_ref, send_ref, sums_ref, grad_ref, left_ref = refs[5 * groups + 3 :]
    blocks = per // BLOCK
    batches = dkv_ref.shape[0] // blocks
    gqkv_ref[:, : 4 * HD] = dq_ref[...].reshape(-1, 4 * HD).astype(BF16)
    gqkv_ref[:, 4 * HD :] = dkv_ref[...].reshape(-1, 6 * HD).astype(BF16)
    for m in range(batches):
        i = m * blocks
        low, high = ret_low_ref[m].astype(F32), ret_high_ref[m].astype(F32)
        if blocks == 1:
            gqkv_ref[i * BLOCK : (i + 1) * BLOCK, 4 * HD :] = (dkv_ref[i] + low + high).astype(BF16)
        else:
            j = i + blocks - 1
            gqkv_ref[i * BLOCK : (i + 1) * BLOCK, 4 * HD :] = (dkv_ref[i] + low).astype(BF16)
            gqkv_ref[j * BLOCK : (j + 1) * BLOCK, 4 * HD :] = (dkv_ref[j] + high).astype(BF16)
    lead = meta_ref[3] == 1
    rows = batches * BLOCK
    mine, given = mine_ref[...].reshape(rows, 10 * HD), given_ref[...].reshape(rows, 10 * HD)
    ends = jnp.concatenate([jnp.where(lead, mine, given), jnp.where(lead, given, mine)], 0)
    firsts = jnp.concatenate([first0_ref[...], first1_ref[...]], 0)
    grad = dot_tn(first_ref[...], gqkv_ref[...]) + dot_tn(firsts, ends)
    grad_ref[:, : 10 * HD] = grad
    columns = jnp.sum(gqkv_ref[...].astype(F32), 0, keepdims=True)
    columns = columns + jnp.sum(ends.astype(F32), 0, keepdims=True)
    c_hi, c_lo = hi_lo(columns)
    c_rows = jnp.concatenate([c_hi, c_lo] * 8, 0).astype(BF16)
    shift_sum = dot_nt(c_rows, w_ref[...])
    shift_sum = shift_sum[0:1] + shift_sum[1:2]
    along = jnp.sum(grad * w_ref[...].astype(F32), -1, keepdims=True)
    along = jnp.transpose(jnp.broadcast_to(along, (grad.shape[0], 2 * HD)))[0:1]
    sums_ref[0:1] = (along - shift_ref[...][None] * shift_sum) / gain_ref[...][None]
    sums_ref[1:2] = shift_sum
    piece = pieces[0].shape[0]
    total = 0.0
    for g in range(groups):
        for k in range(4):
            left_ref[k * piece : (k + 1) * piece] = pieces[4 * g + k][...]
        total = total + dot_tn(left_ref[...], mixed_refs[g][...])
    grad_ref[:, 10 * HD :] = total
    split_rows(devices, meta_ref, grad_ref, keep_ref, send_ref)


def back_kernel(groups, seqs, per, share, meta_ref, gqkv_ref, w_ref, *refs):
    count = 4 * groups
    ends_refs, back_refs, all_ref = refs[: -count - 1], refs[-count - 1 : -1], refs[-1]
    blocks = per // BLOCK
    all_ref[...] = gqkv_ref[...]
    for end, b in ((1, 0), (2, blocks - 1)):

        @pl.when(meta_ref[end] == 1)
        def _(b=b):
            for m in range(groups * seqs):
                rows = slice(m * per + b * BLOCK, m * per + (b + 1) * BLOCK)
                total = all_ref[rows].astype(F32)
                for ref in ends_refs:
                    total = total + ref[m].astype(F32)
                all_ref[rows] = total.astype(BF16)

    for g in range(groups):
        for k in range(4):
            for m in range(seqs):
                row = (g * seqs + m) * per + (meta_ref[0] ^ SWAP[k]) * share
                rows = pl.ds(pl.multiple_of(row, share), share)
                back = dot_nt(all_ref[rows], w_ref[...]).astype(BF16)
                back_refs[4 * g + k][m * share : (m + 1) * share] = back


def swap_tp(value, bit):
    return lax.ppermute(value, "tp", [(i, i ^ bit) for i in range(lax.axis_size("tp"))])


def scatter_tp(parts):
    far = swap_tp(parts[3], 1)
    near = swap_tp(parts[2], 1)
    both = (parts[1].astype(F32) + far.astype(F32)).astype(BF16)
    return parts[0], near, swap_tp(both, 2)


def gather_tp(piece):
    cross = swap_tp(piece, 2)
    return piece, cross, swap_tp(piece, 1), swap_tp(cross, 1)


def mirrored(pairs, last):
    return pairs + [(last - a, last - b) for a, b in pairs]


SECOND = [(1, 3), (4, 5), (2, 6), (0, 7)]


def in_first_group(myself, devices):
    if devices == 8:
        return (myself == 0) | (myself == 1) | (myself == 2) | (myself == 4)
    return myself < devices // 2


def spread(own, myself, devices, *before_last):
    last = devices - 1
    held = own
    if devices == 8:
        for k in (1, 2, 4):
            held = held + lax.ppermute(own, "seq", mirrored([(0, k)], last))
        held = after(held, *before_last)
        other = lax.ppermute(held, "seq", mirrored(SECOND, last))
    else:
        bit = 1
        while bit < devices // 2:
            held = held + lax.ppermute(held, "seq", mirrored([(i, i + bit) for i in range(bit)], last))
            bit *= 2
        other = lax.ppermute(held, "seq", [(i, i ^ bit) for i in range(devices)])
    first = in_first_group(myself, devices)
    return jnp.where(first, held, other), jnp.where(first, other, held), other


def collect_first(given, devices):
    last = devices - 1
    if devices == 8:
        return lax.ppermute(given, "seq", mirrored([(b, a) for a, b in SECOND], last))
    return lax.ppermute(given, "seq", [(i, i ^ (devices // 2)) for i in range(devices)])


def collect_rest(mine, devices, join):
    last = devices - 1
    if devices == 8:
        return [mine] + [lax.ppermute(mine, "seq", mirrored([(k, 0)], last)) for k in (1, 2, 4)]
    bit = devices // 2
    while bit > 1:
        bit //= 2
        mine = join(mine, lax.ppermute(mine, "seq", mirrored([(i + bit, i) for i in range(bit)], last)))
    return [mine]


def to_owners(slots):
    return lax.all_to_all(slots, "seq", split_axis=0, concat_axis=0, tiled=True)


def sum_seq_first(send, devices):
    return lax.ppermute(send, "seq", [(i, i ^ 1) for i in range(devices)])


def sum_seq_rest(pairs, meta, devices):
    count, rows = pairs[0][0].shape[:2]
    lanes = sum(keep.shape[2] for keep, _ in pairs)
    if count == 4:
        low = sds((rows, lanes), BF16)
        own, *out = call(
            partial(fold_kernel, len(pairs)), (sds((rows, lanes), F32), low, low, low), name="fold"
        )(*(v for pair in pairs for v in pair), smem=(meta,))
        return [own] + [
            lax.ppermute(piece, "seq", [(i, i ^ (2 * (n + 1))) for i in range(devices)])
            for n, piece in enumerate(out)
        ]
    total = [(keep.astype(F32) + got.astype(F32)).astype(BF16) for keep, got in pairs]
    return across(jnp.concatenate(total, 2), devices)


def across(total, devices):
    sides = [[i for i in range(devices) if i % 2 == side] for side in range(2)]
    got = lax.all_to_all(
        total, "seq", split_axis=0, concat_axis=0, tiled=True, axis_index_groups=sides
    )
    return [got[n] for n in range(total.shape[0])]


def sum_seq_second(keep, got, meta, devices):
    count, rows, lanes = keep.shape
    if count != 4:
        return keep, got
    low = sds((2, rows, lanes), BF16)
    keep, send = call(partial(fold_half_kernel, 1), (low, low), name="fold_near")(keep, got, smem=(meta,))
    return keep, lax.ppermute(send, "seq", [(i, i ^ 2) for i in range(devices)])


def sum_seq_third(pair, meta, devices):
    keep, got = pair
    count, rows, lanes = keep.shape
    if count != 2:
        return across((keep.astype(F32) + got.astype(F32)).astype(BF16), devices)
    one = lambda kind: sds((1, rows, lanes), kind)
    own, send = call(partial(fold_half_kernel, 2), (one(F32), one(BF16)), name="fold_far")(
        keep, got, smem=(meta,)
    )
    return own[0], lax.ppermute(send, "seq", [(i, i ^ 4) for i in range(devices)])[0]


def sum_of(terms):
    total = terms[0].astype(F32)
    for term in terms[1:]:
        total = total + term.astype(F32)
    return total


def per_device(
    layer_input,
    out_grad,
    norm1_gain,
    norm1_shift,
    w_qkv,
    w_out,
    norm2_gain,
    norm2_shift,
    w_up,
    w_down,
    key_keep,
    rand_blocks,
):
    batches, per, width = layer_input.shape
    local = w_qkv.shape[2]
    devices = lax.axis_size("seq")
    myself = lax.axis_index("seq")
    tp_count = lax.axis_size("tp")
    tp_place = lax.axis_index("tp")
    assert local == 3 * HD and tp_count == 4 and devices % 2 == 0 and batches % 2 == 0
    share = per // tp_count
    bd = per // BLOCK
    total = batches * bd
    blocks_all = bd * devices
    groups = 2
    seqs = batches // groups
    piece = seqs * share
    refs = total * RANDS
    slots_per = max(1, -(-refs // devices))
    slots = devices * slots_per
    hidden_here = w_up.shape[1]
    rows = width // devices
    i32 = jnp.int32
    flag = lambda v: v.astype(i32)
    meta = jnp.stack(
        [
            tp_place, flag(myself == 0), flag(myself == devices - 1), flag(in_first_group(myself, devices)), myself,
        ]
    ).astype(i32)

    CHAIN.last = ()
    scale = 1.0 / math.sqrt(HD)
    x_rows = layer_input.reshape(batches * per, width)
    first, q, kv, w640 = CHAIN.done(project(x_rows, norm1_gain, norm1_shift, w_qkv.transpose(1, 0, 2)))
    is_first, is_last = myself == 0, myself == devices - 1
    ends = jnp.where(is_first, layer_input[:, :BLOCK], layer_input[:, per - BLOCK :])
    ends = jnp.where(is_first | is_last, ends, jnp.zeros_like(ends))
    lead_x0, lead_x1, arrived = spread(ends, myself, devices, kv)
    q_blocks = q.reshape(total, BLOCK, 4 * HD)
    kv_blocks = kv.reshape(total, BLOCK, 6 * HD)
    kv_seqs = kv.reshape(batches, per, 6 * HD)

    table = (
        rand_blocks.reshape(batches, devices, bd, RANDS).transpose(1, 0, 2, 3).reshape(devices, refs)
    )
    owners = table // bd
    source = (jnp.arange(refs, dtype=i32) // (bd * RANDS))[None] * bd + table - owners * bd
    order = jnp.arange(refs, dtype=i32)
    earlier = order[None, :] < order[:, None]
    rank = jnp.sum(((owners[:, :, None] == owners[:, None, :]) & earlier[None]).astype(i32), -1)
    places = jnp.arange(slots_per, dtype=i32)
    asked = (owners == myself)[:, None, :] & (rank[:, None, :] == places[None, :, None])
    source_of = jnp.sum(jnp.where(asked, source[:, None, :], 0), -1).reshape(slots)
    valid = jnp.sum(asked.astype(i32), -1).reshape(slots)
    my_owner = lax.dynamic_index_in_dim(owners, myself, 0, False)
    my_rank = lax.dynamic_index_in_dim(rank, myself, 0, False)
    slot_of = my_owner * slots_per + my_rank
    mine = lax.dynamic_index_in_dim(table, myself, 0, False)
    query_of = jnp.sum(
        jnp.where(
            slot_of[None, :] == jnp.arange(slots, dtype=i32)[:, None], (order // RANDS)[None, :], 0
        ),
        -1,
    )

    end_kv = sds((batches, BLOCK, 6 * HD), BF16)
    end_all = sds((batches, BLOCK, 10 * HD), BF16)
    sent, kv_low, kv_high = call(
        partial(dispatch_kernel, bd),
        (sds((slots, BLOCK, 6 * HD), BF16), end_kv, end_kv),
        name="dispatch",
    )(kv_blocks, smem=(source_of,))
    rand_kv = to_owners(after(sent, arrived))
    up = [(i, i + 1) for i in range(devices - 1)]
    down = [(b, a) for a, b in up]
    low = lax.ppermute(kv_high, "seq", up)
    high = lax.ppermute(kv_low, "seq", down)

    bias, seq_bias, column_bias, wo256 = call(
        partial(bias_kernel, bd, blocks_all),
        (
            sds((total, 1, 8 * BLOCK), F32),
            sds((batches, 1, per), F32),
            sds((total, BLOCK, 2 * HD), F32),
            sds((width, 4 * HD), BF16),
        ),
        name="bias",
    )(key_keep.reshape(batches * blocks_all, BLOCK), w_out, smem=(mine, meta))

    grad_up = dot_nn(out_grad.reshape(batches * per, width), w_down)
    grad_up = grad_up.reshape(batches, per, hidden_here)

    part = sds((batches, BLOCK, 4 * HD), F32)
    low_piece = sds((piece, width), BF16)
    high_piece = sds((piece, width), F32)
    attn, lse = [], []

    def attend(g):
        half_of = lambda array: part_of(array, g, groups)
        out, stat = call(
            partial(sparse_fwd_kernel, g * seqs * bd, seqs, per, share),
            (sds((4 * piece, 4 * HD), BF16), sds((seqs * per, 2 * HD), F32)),
            (
                pltpu.VMEM((seqs, per + 2 * BLOCK, 6 * HD), BF16),
                pltpu.VMEM((2, 8 * BLOCK, 6 * HD), BF16),
            ),
            name="sparse_fwd",
        )(
            half_of(q_blocks), half_of(kv_seqs), half_of(low), half_of(high), half_of(lead0), half_of(lead1),
            rand_kv, half_of(bias), smem=(slot_of, meta),
        )
        attn.append(out)
        lse.append(stat)

    lead_rows = sds((batches * BLOCK, width), BF16)
    lead_first0, lead_first1, lead0, lead1, part_mine, part_given = call(
        lead_fwd_kernel, (lead_rows, lead_rows, end_all, end_all, part, part), name="lead_fwd"
    )(kv_seqs, after(seq_bias, grad_up), lead_x0, lead_x1, norm1_gain, norm1_shift, w640, smem=(meta,))
    part_got = collect_first(part_given, devices)
    q_slots = call(gather_kernel, sds((slots, BLOCK, 4 * HD), BF16), name="gather")(q_blocks, smem=(query_of,))
    rand_q = to_owners(after(q_slots, rand_kv, part_got, low, high))
    attend(0)
    lead_parts = collect_rest(merge(part_mine, part_got), devices, merge)
    attend(1)
    lead_out, lead_lse = call(
        lead_finish_kernel,
        (sds(part.shape, BF16), sds((batches, BLOCK, 2 * HD), F32)),
        name="lead_finish",
        limit=SMALL,
    )(*lead_parts)
    out = call(
        partial(out_project_kernel, groups, seqs, per, share),
        (sds((4 * piece, 4 * HD), BF16),) * groups + (low_piece,) * (4 * groups),
        name="out_project",
        limit=SMALL,
    )(wo256, lead_out, *attn, smem=(meta,))
    mixed = out[:groups]
    attn_parts = [scatter_tp(out[groups + 4 * g : groups + 4 * g + 4]) for g in range(groups)]

    flat = lambda lists: [v for group in lists for v in group]
    hidden, act, total_grad, sums2, attn_grad = [], [], [], [], []
    ups, pres, back_parts, down_parts = [], [], [], []
    for g in range(groups):
        h, a = share_call(mid_fwd_kernel, (high_piece, low_piece), [(layer_input, g, 0)], "mid_fwd")(
            meta, seqs, share, *attn_parts[g], norm2_gain, norm2_shift
        )
        hidden.append(h)
        act.append(gather_tp(a))
    low_hidden = sds((piece, hidden_here), BF16)
    for g in range(groups):
        out = share_call(
            ffn_kernel, (low_hidden, low_hidden, low_piece) * 4, [(grad_up, g, k) for k in range(4)], "ffn", PARAMS
        )(meta, seqs, share, *act[g], w_up)
        ups.append(out[0::3])
        pres.append(out[1::3])
        back_parts.append(scatter_tp(out[2::3]))
    for g in range(groups):
        t, a, s = share_call(
            mid_bwd_kernel, (high_piece, low_piece, sds((2, width), F32)), [(out_grad, g, 0)], "mid_bwd"
        )(meta, seqs, share, *back_parts[g], hidden[g], norm2_gain)
        total_grad.append(t)
        sums2.append(s)
        if g == 0:
            lanes = 2 * hidden_here
            halves = sds((devices // 2, rows, lanes), BF16)
            ff_keep, ff_send = call(
                partial(ffn_grad_kernel, groups, seqs, per, share, devices),
                (halves, halves),
                (
                    pltpu.VMEM((batches * per, width), BF16),
                    pltpu.VMEM((batches * per, hidden_here), BF16),
                    pltpu.VMEM((width, lanes), F32),
                ),
                name="ffn_grad",
            )(
                out_grad.reshape(batches * per, width), *flat(ups), *flat(act), *flat(pres), smem=(meta,)
            )
            ff_got = sum_seq_first(ff_send, devices)
        if g == groups - 1:
            down_parts = call(down_kernel, (low_piece,) * (4 * groups), name="down")(*flat(ups), w_down)
        attn_grad.append(gather_tp(a))

    lead_grad = call(
        partial(lead_grad_kernel, groups, seqs, per, share),
        sds((batches, BLOCK, 4 * HD), BF16),
        (pltpu.VMEM((batches * BLOCK, width), BF16),),
        name="lead_grad",
        limit=SMALL,
    )(wo256, lead_lse, lead_out, *flat(attn_grad), smem=(meta,))
    grads, sent = call(
        partial(heads_grad_kernel, groups, seqs, per, share),
        (sds((batches * per, 4 * HD), BF16), sds((slots, BLOCK, 4 * HD), BF16)),
        name="heads_grad",
    )(wo256, *flat(attn_grad), *mixed, *lse, smem=(query_of, meta))
    *lead_do, arrived = spread(lead_grad, myself, devices, sent)
    rand_do = to_owners(after(sent, arrived, rand_q, ff_got))
    dend = sds(end_kv.shape, F32)
    dq, dkv, ret_low, ret_high, dlead0, dlead1 = call(
        partial(sparse_bwd_kernel, batches, per),
        (sds((total, BLOCK, 4 * HD), F32), sds((batches, per, 6 * HD), F32), end_kv, end_kv, dend, dend),
        (
            pltpu.VMEM((batches, per + 2 * BLOCK, 6 * HD), BF16),
            pltpu.VMEM((2, 8 * BLOCK, 6 * HD), BF16),
            pltpu.VMEM((batches, per + 2 * BLOCK, 6 * HD), F32),
            pltpu.VMEM((batches, 2 * BLOCK, 6 * HD), F32),
        ),
        name="sparse_bwd",
    )(
        q_blocks, kv_seqs, low, high, lead0, lead1, rand_kv, bias,
        after(grads, *lead_do).reshape(total, BLOCK, 4 * HD), smem=(slot_of,),
    )
    from_low = lax.ppermute(ret_high, "seq", up)
    from_high = lax.ppermute(ret_low, "seq", down)
    dkv, ends_mine, ends_given = call(
        lead_bwd_kernel, (sds((batches, per, 6 * HD), F32), end_all, end_all), name="lead_bwd"
    )(lead0, lead1, kv_seqs, seq_bias, dkv, dlead0, dlead1, *lead_do, smem=(meta,))
    add = lambda a, b: (a.astype(F32) + b.astype(F32)).astype(BF16)
    ends_first = collect_first(ends_given, devices)
    outputs = []
    for g in range(groups):
        late = [after(down_parts[4 * g + k], ret_low) for k in range(4)]
        outputs += [*scatter_tp(late), hidden[g]]

    layer_output = call(
        partial(output_kernel, groups), sds((batches, share, width), F32), name="output", limit=SMALL
    )(*outputs)
    ff_more = sum_seq_second(ff_keep, ff_got, meta, devices)

    ends_got = collect_rest(add(after(ends_mine, layer_output, ff_more[0]), ends_first), devices, add)

    dkv = call(slots_kernel, sds((total, BLOCK, 6 * HD), F32), name="slots")(
        rand_q, rand_do, kv_blocks, column_bias,
        dkv.reshape(total, BLOCK, 6 * HD), smem=(source_of, valid),
    )
    halves = sds((devices // 2, rows, 14 * HD), BF16)
    gqkv, qkv_keep, qkv_send, sums1 = call(
        partial(tail_kernel, groups, per, devices),
        (sds((total * BLOCK, 10 * HD), BF16), halves, halves, sds((2, width), F32)),
        (pltpu.VMEM((width, 14 * HD), F32), pltpu.VMEM((4 * piece, width), BF16)),
        name="tail",
    )(
        dq, dkv, from_low, from_high, first, lead_first0, lead_first1, ends_mine, ends_given,
        *flat(attn_grad), *mixed, w640, norm1_gain, norm1_shift, smem=(meta,),
    )
    norms = jnp.concatenate([sums1, sum(sums2)], 0).reshape(4, devices, 1, rows)
    norms = jnp.broadcast_to(norms.transpose(1, 2, 0, 3), (devices, tp_count, 4, rows))
    norms = lax.all_to_all(
        norms.reshape(devices * tp_count, 4, rows), ("seq", "tp"), split_axis=0, concat_axis=0, tiled=True
    )
    qkv_got = sum_seq_first(qkv_send, devices)
    ff = sum_seq_third(ff_more, meta, devices)
    first_back = call(
        partial(back_kernel, groups, seqs, per, share),
        (low_piece,) * (4 * groups),
        (pltpu.VMEM((total * BLOCK, 10 * HD), BF16),),
        name="back",
    )(gqkv, w640, *ends_got, smem=(meta,))
    terms = []
    for g in range(groups):
        terms += [*scatter_tp(first_back[4 * g : 4 * g + 4]), total_grad[g]]
    gq = sum_seq_rest([(qkv_keep, qkv_got)], meta, devices)
    input_grad = share_call(
        partial(end_kernel, groups),
        sds((batches, share, width), F32),
        [(layer_input, g, 0) for g in range(groups)],
        "end",
    )(meta, seqs, share, *terms, norm1_gain)

    norms = norms.sum(0)
    ff = sum_of(ff)
    g_down, g_up = ff[:, :hidden_here], ff[:, hidden_here:]
    gq = sum_of(gq)
    g_out = jnp.concatenate([gq[:, 10 * HD : 12 * HD], gq[:, 13 * HD :]], 1)
    g_qkv = jnp.stack(
        [
            gq[:, : 3 * HD] * scale,
            jnp.concatenate([gq[:, 4 * HD : 6 * HD], gq[:, 8 * HD : 9 * HD]], 1),
            jnp.concatenate([gq[:, 6 * HD : 8 * HD], gq[:, 9 * HD : 10 * HD]], 1),
        ],
        1,
    )
    return (
        layer_output, input_grad, g_qkv, g_out, g_up, g_down, norms[0], norms[1], norms[2], norms[3],
    )


def solution(mesh):
    return jax.shard_map(
        per_device,
        mesh=mesh,
        in_specs=(
            P(None, "seq", None),
            P(None, "seq", None),
            P(),
            P(),
            P(None, None, "tp"),
            P(None, "tp"),
            P(),
            P(),
            P(None, "tp"),
            P(None, "tp"),
            P(),
            P(),
        ),
        out_specs=(
            P(None, ("seq", "tp"), None),
            P(None, ("seq", "tp"), None),
            P("seq", None, "tp"),
            P("seq", "tp"),
            P("seq", "tp"),
            P("seq", "tp"),
            P("seq"),
            P("seq"),
            P("seq"),
            P("seq"),
        ),
        check_vma=False,
    )
```

```python
from functools import partial
import math

import jax
import jax.numpy as jnp
from jax import lax
from jax.experimental import pallas as pl
from jax.experimental.pallas import tpu as pltpu
from jax.sharding import PartitionSpec as P

HD = 64
BLOCK = 64
RANDS = 3
EPS = 1e-06
SWAP = (0, 2, 1, 3)
NEG = -1e30
F32 = jnp.float32
BF16 = jnp.bfloat16
VMEM = pl.BlockSpec(memory_space=pltpu.VMEM)
SMEM = pl.BlockSpec(memory_space=pltpu.SMEM)
MIB = 1024 * 1024


def sds(shape, kind):
    return jax.ShapeDtypeStruct(shape, kind)


PARAMS = pltpu.CompilerParams(vmem_limit_bytes=56 * MIB)
SMALL = pltpu.CompilerParams(vmem_limit_bytes=12 * MIB)


def after(value, *others):
    return lax.optimization_barrier((value,) + others)[0]


class Chain:
    last = ()

    def link(self, value):
        return after(value, *self.last) if self.last else value

    def done(self, outs):
        self.last = (jax.tree.leaves(outs)[0],)
        return outs


CHAIN = Chain()


def part_of(array, at, count):
    return array, at, count


TIMES = {
    "project": 6, "dispatch": 3, "bias": 2, "lead_fwd": 4, "sparse_fwd": 7, "merge": 1, "lead_finish": 1, "out_project": 1,
    "mid_fwd": 1, "gather": 2, "ffn": 6, "ffn_grad": 7, "mid_bwd": 1, "heads_grad": 5, "lead_grad": 1, "sparse_bwd": 13,
    "fold_near": 3, "down": 6, "lead_bwd": 5, "slots": 14, "tail": 5, "fold_far": 2, "back": 7, "output": 1,
    "fold": 2, "end": 2,
}
HINT = 1.75e6


def cost(name):
    return pl.CostEstimate(flops=0, transcendentals=0, bytes_accessed=int(TIMES[name] * HINT))


def call(body, outs, scratch=(), name=None, limit=PARAMS):
    def run(*args, smem=()):
        specs = [SMEM] * len(smem)
        arrays = []
        if smem:
            smem = (CHAIN.link(smem[0]),) + tuple(smem[1:])
        else:
            args = (CHAIN.link(args[0]),) + args[1:]
        for arg in args:
            if isinstance(arg, tuple):
                array, at, count = arg
                shape = (array.shape[0] // count,) + array.shape[1:]
                index = (at,) + (0,) * (array.ndim - 1)
                specs.append(pl.BlockSpec(shape, lambda i, index=index: index))
                arrays.append(array)
            else:
                specs.append(VMEM)
                arrays.append(arg)
        return CHAIN.done(
            pl.pallas_call(
                body,
                out_shape=outs,
                grid=(1,),
                in_specs=specs,
                out_specs=jax.tree.map(lambda _: VMEM, outs),
                scratch_shapes=list(scratch),
                compiler_params=limit,
                cost_estimate=cost(name),
                name=name,
            )(*smem, *arrays)
        )

    return run


def share_call(body, outs, blocks, name, limit=SMALL):
    def run(meta, seqs, share, *args):
        def spec(value, group, pos):
            return pl.BlockSpec(
                (seqs, share, value.shape[2]), lambda i, meta_ref: (group, meta_ref[0] ^ SWAP[pos], 0)
            )

        return CHAIN.done(
            pl.pallas_call(
                body,
                out_shape=outs,
                grid_spec=pltpu.PrefetchScalarGridSpec(
                    num_scalar_prefetch=1,
                    grid=(1,),
                    in_specs=[spec(*b) for b in blocks] + [VMEM] * len(args),
                    out_specs=jax.tree.map(lambda _: VMEM, outs),
                ),
                compiler_params=limit,
                cost_estimate=cost(name),
                name=name,
            )(CHAIN.link(meta), *(b[0] for b in blocks), *args)
        )

    return run


def dot_nt(a, b):
    return lax.dot_general(a, b, (((1,), (1,)), ((), ())), preferred_element_type=F32)


def dot_tn(a, b):
    return lax.dot_general(a, b, (((0,), (0,)), ((), ())), preferred_element_type=F32)


def dot_nn(a, b):
    return lax.dot_general(a, b, (((1,), (0,)), ((), ())), preferred_element_type=F32)


def two_heads(tile):
    lane = lax.broadcasted_iota(jnp.int32, tile.shape, 1)
    zero = jnp.zeros_like(tile)
    return jnp.concatenate([jnp.where(lane < HD, tile, zero), jnp.where(lane >= HD, tile, zero)], 0)


def pick_heads(pair, rows):
    lane = lax.broadcasted_iota(jnp.int32, (rows, 2 * HD), 1)
    return jnp.where(lane < HD, pair[:rows], pair[rows:])


def half(tile, upper):
    lane = lax.broadcasted_iota(jnp.int32, tile.shape, 1)
    return jnp.where((lane >= HD) if upper else (lane < HD), tile, jnp.zeros_like(tile))


def lanes_of(columns, rows):
    lane = lax.broadcasted_iota(jnp.int32, (rows, 2 * HD), 1)
    out = jnp.zeros((rows, 2 * HD), F32)
    for at, column in enumerate(columns):
        out = jnp.where(lane == at, column, out)
    return out


def hi_lo(value):
    hi = value.astype(BF16).astype(F32)
    return hi, value - hi


def norm_rows(hidden):
    center = hidden - jnp.mean(hidden, -1, keepdims=True)
    inverse = lax.rsqrt(jnp.mean(center * center, -1, keepdims=True) + EPS)
    return center * inverse, inverse


def norm_rows_back(grad, normed, inverse, gain):
    scaled = grad * gain
    return inverse * (
        scaled
        - jnp.mean(scaled, -1, keepdims=True)
        - normed * jnp.mean(scaled * normed, -1, keepdims=True)
    )


def project_kernel(x_ref, gain_ref, shift_ref, raw_ref, first_ref, q_ref, kv_ref, w_ref):
    @pl.when(pl.program_id(0) == 0)
    def _():
        w_ref[:, : 3 * HD] = raw_ref[0] * jnp.asarray(1.0 / math.sqrt(HD), BF16)
        w_ref[:, 3 * HD : 4 * HD] = jnp.zeros((w_ref.shape[0], HD), BF16)
        w_ref[:, 4 * HD : 6 * HD] = raw_ref[1, :, : 2 * HD]
        w_ref[:, 6 * HD : 8 * HD] = raw_ref[2, :, : 2 * HD]
        w_ref[:, 8 * HD :] = jnp.concatenate([raw_ref[1, :, 2 * HD :], raw_ref[2, :, 2 * HD :]], 1)

    normed, _ = norm_rows(x_ref[...].astype(F32))
    first = (normed * gain_ref[...][None] + shift_ref[...][None]).astype(BF16)
    first_ref[...] = first
    out = dot_nn(first, w_ref[...]).astype(BF16)
    q_ref[...] = out[:, : 4 * HD]
    kv_ref[...] = out[:, 4 * HD :]


def project(x, gain, shift, raw):
    rows, width = x.shape
    tile = min(rows, 256)
    row = lambda w: pl.BlockSpec((tile, w), lambda i: (i, 0))
    vector = pl.BlockSpec((width,), lambda i: (0,))
    whole = lambda w: pl.BlockSpec((width, w), lambda i: (0, 0))
    low = lambda *shape: sds(shape, BF16)
    return pl.pallas_call(
        project_kernel,
        grid=(rows // tile,),
        out_shape=(low(rows, width), low(rows, 4 * HD), low(rows, 6 * HD), low(width, 10 * HD)),
        in_specs=[
            row(width), vector, vector, pl.BlockSpec(raw.shape, lambda i: (0, 0, 0)),
        ],
        out_specs=(row(width), row(4 * HD), row(6 * HD), whole(10 * HD)),
        compiler_params=PARAMS,
        cost_estimate=cost("project"),
        name="project",
    )(x, gain, shift, raw)


def dispatch_kernel(bd, index_ref, kv_ref, sent_ref, low_ref, high_ref):
    def step(slot, _):
        sent_ref[slot] = kv_ref[index_ref[slot]]
        return 0

    lax.fori_loop(0, sent_ref.shape[0], step, 0, unroll=4)
    for m in range(low_ref.shape[0]):
        low_ref[m] = kv_ref[m * bd]
        high_ref[m] = kv_ref[m * bd + bd - 1]


def bias_kernel(bd, blocks_all, table_ref, meta_ref, keep_ref, raw_ref, bias_ref, seq_ref, column_ref, wo_ref):
    wo_ref[:, : 2 * HD] = raw_ref[:, : 2 * HD]
    blank = jnp.zeros((wo_ref.shape[0], HD), BF16)
    wo_ref[:, 2 * HD :] = jnp.concatenate([blank, raw_ref[:, 2 * HD :]], 1)
    low = lambda keep: jnp.where(keep > 0, 0.0, NEG)
    for m in range(seq_ref.shape[0]):
        for b in range(bd):
            i = m * bd + b
            here = meta_ref[4] * bd + b

            def row(block, inside=True):
                return low(jnp.where(inside, keep_ref[pl.ds(m * blocks_all + block, 1)], 0))

            own = row(here)
            listed = [
                row(jnp.maximum(here - 1, 0), here > 0),
                own,
                row(jnp.minimum(here + 1, blocks_all - 1), here < blocks_all - 1),
                row(0),
                row(blocks_all - 1),
            ] + [row(table_ref[i * RANDS + j]) for j in range(RANDS)]
            bias_ref[i] = jnp.concatenate(listed, 1)
            seq_ref[m, :, b * BLOCK : (b + 1) * BLOCK] = own
            column_ref[i] = jnp.transpose(jnp.broadcast_to(own, (2 * HD, BLOCK)))


def gather_kernel(index_ref, blocks_ref, out_ref):
    def step(slot, _):
        out_ref[slot] = blocks_ref[index_ref[slot]]
        return 0

    lax.fori_loop(0, out_ref.shape[0], step, 0, unroll=4)


def lead_fwd_kernel(
    meta_ref, kv_ref, bias_ref, x0_ref, x1_ref, gain_ref, shift_ref, w_ref, first0_ref, first1_ref,
    lead0_ref, lead1_ref, mine_ref, given_ref,
):
    for x_ref, first_ref, lead_ref in ((x0_ref, first0_ref, lead0_ref), (x1_ref, first1_ref, lead1_ref)):
        normed, _ = norm_rows(x_ref[...].reshape(-1, x_ref.shape[2]).astype(F32))
        first = (normed * gain_ref[...][None] + shift_ref[...][None]).astype(BF16)
        first_ref[...] = first
        lead_ref[...] = dot_nn(first, w_ref[...]).astype(BF16).reshape(lead_ref.shape)
    low = meta_ref[3]
    rows = 2 * BLOCK
    for m in range(kv_ref.shape[0]):
        both = lambda lo, hi: jnp.concatenate([lead0_ref[m, :, lo:hi], lead1_ref[m, :, lo:hi]], 0)
        bias = bias_ref[m]
        pair = dot_nt(two_heads(both(0, 2 * HD)), kv_ref[m, :, : 2 * HD]) + bias
        last = dot_nt(both(2 * HD, 4 * HD), kv_ref[m, :, 4 * HD :]) + bias
        top_a = jnp.max(pair, -1, keepdims=True)
        top_b = jnp.max(last, -1, keepdims=True)
        exp_a = jnp.exp(pair - top_a)
        exp_b = jnp.exp(last - top_b)
        sum_a = jnp.sum(exp_a, -1, keepdims=True)
        sum_b = jnp.sum(exp_b, -1, keepdims=True)
        out0 = pick_heads(dot_nn(exp_a.astype(BF16), kv_ref[m, :, 2 * HD : 4 * HD]), rows)
        out1 = half(dot_nn(exp_b.astype(BF16), kv_ref[m, :, 4 * HD :]), True)
        out1 = out1 + lanes_of(
            [top_a[:rows], top_a[rows:], top_b, sum_a[:rows], sum_a[rows:], sum_b], rows
        )
        for part_ref, first in ((mine_ref, low == 1), (given_ref, low == 0)):
            part_ref[m, :, : 2 * HD] = jnp.where(first, out0[:BLOCK], out0[BLOCK:])
            part_ref[m, :, 2 * HD :] = jnp.where(first, out1[:BLOCK], out1[BLOCK:])


def merge_parts(parts):
    lane = lax.broadcasted_iota(jnp.int32, (BLOCK, 2 * HD), 1)
    stats = [p[:, 2 * HD :] for p in parts]
    top = stats[0]
    for st in stats[1:]:
        top = jnp.maximum(top, st)
    tops = [top[:, h : h + 1] for h in range(3)]
    sums = [0.0, 0.0, 0.0]
    out0, out1 = 0.0, 0.0
    for p, st in zip(parts, stats):
        scale = [jnp.exp(st[:, h : h + 1] - tops[h]) for h in range(3)]
        sums = [sums[h] + st[:, 3 + h : 4 + h] * scale[h] for h in range(3)]
        out0 = out0 + p[:, : 2 * HD] * jnp.where(lane < HD, scale[0], scale[1])
        out1 = out1 + st * scale[2]
    return out0, jnp.where(lane >= HD, out1, 0.0), tops, sums


def merge_kernel(a_ref, b_ref, out_ref):
    for m in range(a_ref.shape[0]):
        out0, out1, tops, sums = merge_parts([a_ref[m], b_ref[m]])
        out_ref[m, :, : 2 * HD] = out0
        out_ref[m, :, 2 * HD :] = out1 + lanes_of(tops + sums, BLOCK)


def merge(a, b):
    return call(merge_kernel, sds(a.shape, F32), name="merge", limit=SMALL)(a, b)


def lead_finish_kernel(*refs):
    part_refs, (out_ref, lse_ref) = refs[:-2], refs[-2:]
    lane = lax.broadcasted_iota(jnp.int32, (BLOCK, 2 * HD), 1)
    for m in range(out_ref.shape[0]):
        out0, out1, tops, sums = merge_parts([p[m] for p in part_refs])
        out_ref[m, :, : 2 * HD] = (out0 / jnp.where(lane < HD, sums[0], sums[1])).astype(BF16)
        out_ref[m, :, 2 * HD :] = (out1 / sums[2]).astype(BF16)
        lse_ref[m] = lanes_of([tops[h] + jnp.log(sums[h]) for h in range(3)], BLOCK)


def fill_ext(ext_ref, kv_ref, low_ref, high_ref, seqs, per):
    for m in range(seqs):
        ext_ref[m, :BLOCK] = low_ref[m]
        ext_ref[m, BLOCK : BLOCK + per] = kv_ref[m]
        ext_ref[m, BLOCK + per :] = high_ref[m]


def fill_listed(listed_ref, ext_ref, lead0_ref, lead1_ref, rand_ref, slot_ref, m, b, block):
    listed_ref[: 3 * BLOCK] = ext_ref[m, pl.ds(pl.multiple_of(b * BLOCK, BLOCK), 3 * BLOCK)]
    listed_ref[3 * BLOCK : 4 * BLOCK] = lead0_ref[m, :, 4 * HD :]
    listed_ref[4 * BLOCK : 5 * BLOCK] = lead1_ref[m, :, 4 * HD :]
    for j in range(RANDS):
        listed_ref[(5 + j) * BLOCK : (6 + j) * BLOCK] = rand_ref[slot_ref[block * RANDS + j]]


def pos_of(meta_ref, at):
    j = at ^ meta_ref[0]
    return ((j & 1) << 1) | (j >> 1)


def sparse_fwd_kernel(
    first, seqs, per, share, slot_ref, meta_ref, q_ref, kv_ref, low_ref, high_ref, lead0_ref,
    lead1_ref, rand_ref, bias_ref, out_ref, lse_ref, ext_ref, listed_ref,
):
    blocks = per // BLOCK
    chunk = min(share, BLOCK)
    fill_ext(ext_ref, kv_ref, low_ref, high_ref, seqs, per)

    def attend(i, here):
        m, b = i // blocks, i % blocks
        fill_listed(here, ext_ref, lead0_ref, lead1_ref, rand_ref, slot_ref, m, b, first + i)
        bias = bias_ref[i]
        pair = dot_nt(two_heads(q_ref[i, :, : 2 * HD]), here[:, : 2 * HD]) + bias
        last = dot_nt(q_ref[i, :, 2 * HD :], here[:, 4 * HD :]) + bias
        top_a = jnp.max(pair, -1, keepdims=True)
        top_b = jnp.max(last, -1, keepdims=True)
        exp_a = jnp.exp(pair - top_a)
        exp_b = jnp.exp(last - top_b)
        sum_a = jnp.sum(exp_a, -1, keepdims=True)
        sum_b = jnp.sum(exp_b, -1, keepdims=True)
        prob_a = (exp_a * (1.0 / sum_a)).astype(BF16)
        prob_b = (exp_b * (1.0 / sum_b)).astype(BF16)
        out0 = pick_heads(dot_nn(prob_a, here[:, 2 * HD : 4 * HD]), BLOCK).astype(BF16)
        out1 = half(dot_nn(prob_b, here[:, 4 * HD :]), True).astype(BF16)
        lse_a = top_a + jnp.log(sum_a)
        lse_b = top_b + jnp.log(sum_b)
        lse_ref[pl.ds(pl.multiple_of(i * BLOCK, BLOCK), BLOCK)] = lanes_of(
            [lse_a[:BLOCK], lse_a[BLOCK:], lse_b], BLOCK
        )
        for c in range(BLOCK // chunk):
            token = b * BLOCK + c * chunk
            at = token // share
            row = pos_of(meta_ref, at) * (seqs * share) + m * share + (token - at * share)
            rows = pl.ds(pl.multiple_of(row, chunk), chunk)
            out_ref[rows, : 2 * HD] = out0[c * chunk : (c + 1) * chunk]
            out_ref[rows, 2 * HD :] = out1[c * chunk : (c + 1) * chunk]

    def step(j, _):
        attend(2 * j, listed_ref.at[0])
        attend(2 * j + 1, listed_ref.at[1])
        return 0

    lax.fori_loop(0, seqs * blocks // 2, step, 0)


def out_project_kernel(groups, seqs, per, share, meta_ref, wo_ref, lead_out_ref, *refs):
    attn_refs, mixed_refs, part_refs = refs[:groups], refs[groups : 2 * groups], refs[2 * groups :]
    blocks = per // BLOCK
    chunk = min(share, BLOCK)
    piece = seqs * share
    for g in range(groups):
        mixed_refs[g][...] = attn_refs[g][...]
    for end, b in ((1, 0), (2, blocks - 1)):

        @pl.when(meta_ref[end] == 1)
        def _(b=b):
            for g in range(groups):
                for m in range(seqs):
                    for c in range(BLOCK // chunk):
                        token = b * BLOCK + c * chunk
                        at = token // share
                        row = pos_of(meta_ref, at) * piece + m * share + (token - at * share)
                        rows = pl.ds(pl.multiple_of(row, chunk), chunk)
                        mixed_refs[g][rows] = lead_out_ref[g * seqs + m, c * chunk : (c + 1) * chunk]

    wo = wo_ref[...]
    for g in range(groups):
        for k in range(4):
            rows = slice(k * piece, (k + 1) * piece)
            part_refs[4 * g + k][...] = dot_nt(mixed_refs[g][rows], wo).astype(BF16)


def down_kernel(groups, *refs):
    up_refs, w_ref, out_refs = refs[: 4 * groups], refs[4 * groups], refs[4 * groups + 1 :]
    rows = up_refs[0].shape[0]
    for g in range(groups):
        for k in range(4):
            out = dot_nt(up_refs[4 * g + k][...], w_ref[...]).astype(BF16)
            out_refs[k][g * rows : (g + 1) * rows] = out


def total_of(refs):
    return refs[0][...].astype(F32) + refs[1][...].astype(F32) + refs[2][...].astype(F32)


def mid_fwd_kernel(meta_ref, x_ref, own_ref, core_ref, y_ref, gain_ref, shift_ref, hidden_ref, act_ref):
    x = x_ref[...].reshape(hidden_ref.shape).astype(F32)
    hidden = total_of((own_ref, core_ref, y_ref)) + x
    normed, _ = norm_rows(hidden)
    hidden_ref[...] = hidden
    act_ref[...] = (normed * gain_ref[...][None] + shift_ref[...][None]).astype(BF16)


def ffn_kernel(meta_ref, *refs):
    gu_refs, act_refs, w_ref, outs = refs[:4], refs[4:8], refs[8], refs[9:]
    rows = act_refs[0].shape[0]
    for k in (3, 2, 1, 0):
        up_ref, pre_ref, back_ref = outs[3 * k : 3 * k + 3]
        pre = dot_nn(act_refs[k][...], w_ref[...])
        phi = 0.5 + 0.5 * lax.erf(pre * (1.0 / math.sqrt(2.0)))
        density = jnp.exp(-0.5 * pre * pre) * (1.0 / math.sqrt(2.0 * math.pi))
        up_ref[...] = (pre * phi).astype(BF16)
        gu = gu_refs[k][...].reshape(rows, gu_refs[k].shape[2])
        grad_pre = (gu * (phi + pre * density)).astype(BF16)
        pre_ref[...] = grad_pre
        back_ref[...] = dot_nt(grad_pre, w_ref[...]).astype(BF16)


def mid_bwd_kernel(
    meta_ref, og_ref, own_ref, core_ref, y_ref, hidden_ref, gain_ref, total_ref, low_ref, sums_ref
):
    grad = total_of((own_ref, core_ref, y_ref))
    normed, inverse = norm_rows(hidden_ref[...])
    og = og_ref[...].reshape(hidden_ref.shape).astype(F32)
    total = og + norm_rows_back(grad, normed, inverse, gain_ref[...][None])
    total_ref[...] = total
    low_ref[...] = total.astype(BF16)
    sums_ref[0:1] = jnp.sum(grad * normed, 0, keepdims=True)
    sums_ref[1:2] = jnp.sum(grad, 0, keepdims=True)


def end_kernel(groups, meta_ref, *refs):
    x_refs, refs = refs[:groups], refs[groups:]
    own_ref, core_ref, y_ref = refs[:3]
    gain_ref, out_ref = refs[-2:]
    seqs = x_refs[0].shape[0]
    rows = own_ref.shape[0] // groups
    for g in range(groups):
        part = slice(g * rows, (g + 1) * rows)
        grad = total_of([ref.at[part] for ref in (own_ref, core_ref, y_ref)])
        normed, inverse = norm_rows(x_refs[g][...].reshape(grad.shape).astype(F32))
        total = refs[3 + g][...] + norm_rows_back(grad, normed, inverse, gain_ref[...][None])
        out_ref[g * seqs : (g + 1) * seqs] = total.reshape(x_refs[g].shape)


def output_kernel(groups, own_ref, core_ref, y_ref, *refs):
    out_ref = refs[-1]
    seqs, share, width = out_ref.shape
    seqs //= groups
    rows = seqs * share
    for g in range(groups):
        part = slice(g * rows, (g + 1) * rows)
        total = total_of([ref.at[part] for ref in (own_ref, core_ref, y_ref)]) + refs[g][...]
        out_ref[g * seqs : (g + 1) * seqs] = total.reshape(seqs, share, width)


def lead_grad_kernel(groups, seqs, per, share, meta_ref, wo_ref, lead_lse_ref, lead_out_ref, *refs):
    pieces, lead_ref, rows_ref = refs[:-2], refs[-2], refs[-1]
    blocks = per // BLOCK
    chunk = min(share, BLOCK)
    root = (meta_ref[1] + meta_ref[2]) == 1
    lead_ref[...] = jnp.zeros_like(lead_ref)
    token = jnp.where(meta_ref[1] == 1, 0, (blocks - 1) * BLOCK)
    for g in range(groups):
        for m in range(seqs):
            for c in range(BLOCK // chunk):
                at = (token + c * chunk) // share
                inside = pl.multiple_of(m * share + (token + c * chunk - at * share), chunk)
                for k in range(4):

                    @pl.when(root & (pos_of(meta_ref, at) == k))
                    def _(k=k, g=g, m=m, c=c, inside=inside):
                        to = (g * seqs + m) * BLOCK + c * chunk
                        rows_ref[to : to + chunk] = pieces[4 * g + k][pl.ds(inside, chunk)]

    @pl.when(root)
    def _():
        total = groups * seqs * BLOCK
        grad = dot_nn(rows_ref[...], wo_ref[...])
        low = grad.astype(BF16)
        prod = low.astype(F32) * lead_out_ref[...].reshape(total, 4 * HD).astype(F32)
        deltas = [
            jnp.sum(half(prod[:, : 2 * HD], False), -1, keepdims=True),
            jnp.sum(half(prod[:, : 2 * HD], True), -1, keepdims=True),
            jnp.sum(half(prod[:, 2 * HD :], True), -1, keepdims=True),
        ]
        d_hi, d_lo = zip(*(hi_lo(d) for d in deltas))
        lse = lead_lse_ref[...].reshape(total, 2 * HD)
        l_hi, l_lo = zip(*(hi_lo(lse[:, h : h + 1]) for h in range(3)))
        stats = lanes_of(l_hi + l_lo + d_hi + d_lo, total)
        tile1 = (half(grad[:, 2 * HD :], True) + stats).astype(BF16)
        lead_ref[:, :, : 2 * HD] = low[:, : 2 * HD].reshape(groups * seqs, BLOCK, 2 * HD)
        lead_ref[:, :, 2 * HD :] = tile1.reshape(groups * seqs, BLOCK, 2 * HD)


def heads_grad_kernel(groups, seqs, per, share, index_ref, meta_ref, wo_ref, *refs):
    pieces, mixed_refs = refs[: 4 * groups], refs[4 * groups : 5 * groups]
    lse_refs = refs[5 * groups : 6 * groups]
    grads_ref, sent_ref = refs[6 * groups :]
    wo = wo_ref[...]
    blocks = per // BLOCK
    rows_of = seqs * share
    for g in range(groups):
        for k in range(4):
            grad = dot_nn(pieces[4 * g + k][...], wo)
            low = grad.astype(BF16)
            prod = low.astype(F32) * mixed_refs[g][k * rows_of : (k + 1) * rows_of].astype(F32)
            deltas = [
                jnp.sum(half(prod[:, : 2 * HD], False), -1, keepdims=True),
                jnp.sum(half(prod[:, : 2 * HD], True), -1, keepdims=True),
                jnp.sum(half(prod[:, 2 * HD :], True), -1, keepdims=True),
            ]
            d_hi, d_lo = zip(*(hi_lo(d) for d in deltas))
            spare = [jnp.zeros_like(d_hi[0])] * 6
            stats = lanes_of(spare + list(d_hi + d_lo), rows_of)
            for m in range(seqs):
                at = slice(m * share, (m + 1) * share)
                inside = m * per + (meta_ref[0] ^ SWAP[k]) * share
                rows = pl.ds(pl.multiple_of(g * seqs * per + inside, share), share)
                lse = lse_refs[g][pl.ds(pl.multiple_of(inside, share), share)]
                l_hi, l_lo = zip(*(hi_lo(lse[:, h : h + 1]) for h in range(3)))
                grads_ref[rows, : 2 * HD] = low[at, : 2 * HD]
                grads_ref[rows, 2 * HD :] = (
                    half(grad[at, 2 * HD :], True) + stats[at] + lanes_of(l_hi + l_lo, share)
                ).astype(BF16)
    lane = lax.broadcasted_iota(jnp.int32, (BLOCK, 2 * HD), 1)
    for end, b in ((1, 0), (2, blocks - 1)):

        @pl.when(meta_ref[end] == 1)
        def _(b=b):
            for m in range(groups * seqs):
                rows = slice(m * per + b * BLOCK, m * per + (b + 1) * BLOCK)
                tile1 = grads_ref[rows, 2 * HD :].astype(F32)
                grads_ref[rows, : 2 * HD] = jnp.zeros((BLOCK, 2 * HD), BF16)
                grads_ref[rows, 2 * HD :] = jnp.where(lane < 6, tile1, 0.0).astype(BF16)

    def send(slot, _):
        at = pl.multiple_of(index_ref[slot] * BLOCK, BLOCK)
        sent_ref[slot] = grads_ref[pl.ds(at, BLOCK)]
        return 0

    lax.fori_loop(0, sent_ref.shape[0], send, 0, unroll=4)


def row_stats(tile):
    st = tile.astype(F32)
    lse = [st[:, h : h + 1] + st[:, 3 + h : 4 + h] for h in range(3)]
    delta = [st[:, 6 + h : 7 + h] + st[:, 9 + h : 10 + h] for h in range(3)]
    return lse, delta


def sparse_bwd_kernel(
    batches, per, slot_ref, q_ref, kv_ref, low_ref, high_ref, lead0_ref, lead1_ref, rand_ref,
    bias_ref, grads_ref, dq_ref, dkv_ref, ret_low_ref, ret_high_ref, dlead0_ref, dlead1_ref,
    ext_ref, listed_ref, dext_ref, dlead_ref,
):
    blocks = per // BLOCK
    near = 6 * BLOCK
    fill_ext(ext_ref, kv_ref, low_ref, high_ref, batches, per)
    dext_ref[...] = jnp.zeros_like(dext_ref)
    dlead_ref[...] = jnp.zeros_like(dlead_ref)

    def attend(i, here):
        m, b = i // blocks, i % blocks
        fill_listed(here, ext_ref, lead0_ref, lead1_ref, rand_ref, slot_ref, m, b, i)
        bias = bias_ref[i]
        tile1 = grads_ref[i, :, 2 * HD :]
        lse, delta = row_stats(tile1)
        q_a, q_b = two_heads(q_ref[i, :, : 2 * HD]), q_ref[i, :, 2 * HD :]
        do_a, do_b = two_heads(grads_ref[i, :, : 2 * HD]), half(tile1, True)
        prob_a = jnp.exp(dot_nt(q_a, here[:, : 2 * HD]) + bias - jnp.concatenate(lse[:2], 0))
        prob_b = jnp.exp(dot_nt(q_b, here[:, 4 * HD :]) + bias - lse[2])
        ds_a = prob_a * (dot_nt(do_a, here[:, 2 * HD : 4 * HD]) - jnp.concatenate(delta[:2], 0))
        ds_b = prob_b * (dot_nt(do_b, here[:, 4 * HD :]) - delta[2])
        ds_a, ds_b = ds_a.astype(BF16), ds_b.astype(BF16)
        dq_ref[i, :, : 2 * HD] = pick_heads(dot_nn(ds_a, here[:, : 2 * HD]), BLOCK)
        dq_ref[i, :, 2 * HD :] = half(dot_nn(ds_b, here[:, 4 * HD :]), False)
        prob_a, prob_b = prob_a[:, :near].astype(BF16), prob_b[:, :near].astype(BF16)
        dkv = jnp.concatenate(
            [
                dot_tn(ds_a[:, :near], q_a),
                dot_tn(prob_a, do_a),
                dot_tn(ds_b[:, :near], q_b) + dot_tn(prob_b, do_b),
            ],
            1,
        )
        return m, b, dkv

    def step(j, _):
        done = [attend(2 * j + n, listed_ref.at[n]) for n in range(2)]
        for m, b, dkv in done:
            dext_ref[m, pl.ds(pl.multiple_of(b * BLOCK, BLOCK), 3 * BLOCK)] += dkv[: 3 * BLOCK]
            dlead_ref[m] += dkv[3 * BLOCK : 5 * BLOCK]
        return 0

    lax.fori_loop(0, batches * blocks // 2, step, 0)
    for m in range(batches):
        ret_low_ref[m] = dext_ref[m, :BLOCK].astype(BF16)
        dkv_ref[m] = dext_ref[m, BLOCK : BLOCK + per]
        ret_high_ref[m] = dext_ref[m, BLOCK + per :].astype(BF16)
        dlead0_ref[m] = dlead_ref[m, :BLOCK]
        dlead1_ref[m] = dlead_ref[m, BLOCK:]


def lead_bwd_kernel(
    meta_ref, lead0_ref, lead1_ref, kv_ref, bias_ref, sparse_ref, dlead0_ref, dlead1_ref, do0_ref, do1_ref,
    dkv_ref, mine_ref, given_ref,
):
    low = meta_ref[3]
    rows = 2 * BLOCK
    for m in range(kv_ref.shape[0]):
        both = lambda a, b, lo, hi: jnp.concatenate([a[m, :, lo:hi], b[m, :, lo:hi]], 0)
        tile1 = both(do0_ref, do1_ref, 2 * HD, 4 * HD)
        lse, delta = row_stats(tile1)
        q_a = two_heads(both(lead0_ref, lead1_ref, 0, 2 * HD))
        q_b = both(lead0_ref, lead1_ref, 2 * HD, 4 * HD)
        do_a, do_b = two_heads(both(do0_ref, do1_ref, 0, 2 * HD)), half(tile1, True)
        k_a, v_a, kv_b = kv_ref[m, :, : 2 * HD], kv_ref[m, :, 2 * HD : 4 * HD], kv_ref[m, :, 4 * HD :]
        bias = bias_ref[m]
        prob_a = jnp.exp(dot_nt(q_a, k_a) + bias - jnp.concatenate(lse[:2], 0))
        prob_b = jnp.exp(dot_nt(q_b, kv_b) + bias - lse[2])
        ds_a = (prob_a * (dot_nt(do_a, v_a) - jnp.concatenate(delta[:2], 0))).astype(BF16)
        ds_b = (prob_b * (dot_nt(do_b, kv_b) - delta[2])).astype(BF16)
        dq_a = pick_heads(dot_nn(ds_a, k_a), rows)
        dq_b = half(dot_nn(ds_b, kv_b), False)
        for part_ref, first in ((mine_ref, low == 1), (given_ref, low == 0)):
            part_ref[m, :, : 2 * HD] = jnp.where(first, dq_a[:BLOCK], dq_a[BLOCK:]).astype(BF16)
            part_ref[m, :, 2 * HD : 4 * HD] = jnp.where(first, dq_b[:BLOCK], dq_b[BLOCK:]).astype(BF16)
            part_ref[m, :, 4 * HD :] = jnp.where(first, dlead0_ref[m], dlead1_ref[m]).astype(BF16)
        dkv_ref[m, :, : 2 * HD] = sparse_ref[m, :, : 2 * HD] + dot_tn(ds_a, q_a)
        dkv_ref[m, :, 2 * HD : 4 * HD] = sparse_ref[m, :, 2 * HD : 4 * HD] + dot_tn(
            prob_a.astype(BF16), do_a
        )
        dkv_ref[m, :, 4 * HD :] = (
            sparse_ref[m, :, 4 * HD :] + dot_tn(ds_b, q_b) + dot_tn(prob_b.astype(BF16), do_b)
        )


def split_rows(meta_ref, grad_ref, keep_ref, send_ref, lanes=slice(None)):
    count, rows, _ = keep_ref.shape
    even = (meta_ref[4] & 1) == 0
    for z in range(count):
        one = grad_ref[2 * z * rows : (2 * z + 1) * rows, lanes].astype(BF16)
        two = grad_ref[(2 * z + 1) * rows : (2 * z + 2) * rows, lanes].astype(BF16)
        keep_ref[z] = jnp.where(even, one, two)
        send_ref[z] = jnp.where(even, two, one)


def ffn_grad_kernel(groups, seqs, per, share, meta_ref, og_ref, *refs):
    count = 4 * groups
    ups, acts, pres = (refs[n * count : (n + 1) * count] for n in range(3))
    keep0_ref, send0_ref, keep1_ref, send1_ref, left_ref, right_ref, grad_ref = refs[3 * count :]
    piece = seqs * share
    hidden = ups[0].shape[1]
    for g in range(groups):
        for k in range(4):
            for m in range(seqs):
                row = (g * seqs + m) * per + (meta_ref[0] ^ SWAP[k]) * share
                rows = pl.ds(pl.multiple_of(row, share), share)
                right_ref[rows] = ups[4 * g + k][m * share : (m + 1) * share]
    grad_ref[:, :hidden] = dot_tn(og_ref[...], right_ref[...])
    for n in range(count):
        left_ref[n * piece : (n + 1) * piece] = acts[n][...]
        right_ref[n * piece : (n + 1) * piece] = pres[n][...]
    grad_ref[:, hidden:] = dot_tn(left_ref[...], right_ref[...])
    split_rows(meta_ref, grad_ref, keep0_ref, send0_ref, slice(0, hidden))
    split_rows(meta_ref, grad_ref, keep1_ref, send1_ref, slice(hidden, 2 * hidden))


def fold_kernel(count, meta_ref, *refs):
    pairs, out_refs = refs[: 2 * count], refs[2 * count :]
    z = meta_ref[4] >> 1
    for n, ref in enumerate(out_refs):
        at = 0
        for keep_ref, got_ref in zip(pairs[::2], pairs[1::2]):
            lanes = keep_ref.shape[2]
            total = keep_ref[z ^ n].astype(F32) + got_ref[z ^ n].astype(F32)
            ref[:, at : at + lanes] = total.astype(ref.dtype)
            at += lanes


def slots_kernel(
    index_ref, valid_ref, q_got_ref, do_got_ref, kv_ref, column_ref, dkv_ref, acc_ref
):
    acc_ref[...] = dkv_ref[...]

    def block_grads(c):
        at = index_ref[c]
        live = valid_ref[c] == 1
        kv = kv_ref[at]
        tile1 = do_got_ref[c, :, 2 * HD :]
        stats = jnp.transpose(tile1.astype(F32))
        lse = [stats[h : h + 1] + stats[3 + h : 4 + h] for h in range(3)]
        delta = [stats[6 + h : 7 + h] + stats[9 + h : 10 + h] for h in range(3)]
        q_a, q_b = two_heads(q_got_ref[c, :, : 2 * HD]), q_got_ref[c, :, 2 * HD :]
        do_a, do_b = two_heads(do_got_ref[c, :, : 2 * HD]), half(tile1, True)
        bias = column_ref[at]
        drop = lambda v: jnp.where(live, v, 0.0)
        prob_a = drop(
            jnp.exp(dot_nt(kv[:, : 2 * HD], q_a) + bias - jnp.concatenate(lse[:2], 1))
        )
        prob_b = drop(jnp.exp(dot_nt(kv[:, 4 * HD :], q_b) + bias[:, :BLOCK] - lse[2]))
        ds_a = prob_a * (dot_nt(kv[:, 2 * HD : 4 * HD], do_a) - jnp.concatenate(delta[:2], 1))
        ds_b = prob_b * (dot_nt(kv[:, 4 * HD :], do_b) - delta[2])
        return at, (
            dot_nn(ds_a.astype(BF16), q_a),
            dot_nn(prob_a.astype(BF16), do_a),
            dot_nn(ds_b.astype(BF16), q_b) + dot_nn(prob_b.astype(BF16), do_b),
        )

    slots = q_got_ref.shape[0]
    wide = 4 if slots % 4 == 0 else 1

    def slot(j, _):
        done = [block_grads(wide * j + n) for n in range(wide)]
        for at, tiles in done:
            for n, tile in enumerate(tiles):
                acc_ref[at, :, n * 2 * HD : (n + 1) * 2 * HD] += tile
        return 0

    lax.fori_loop(0, slots // wide, slot, 0)


def tail_kernel(
    groups, seqs, per, share, devices, meta_ref, dq_ref, dkv_ref, ret_low_ref, ret_high_ref, first_ref, first0_ref,
    first1_ref, mine_ref, given_ref, *refs,
):
    pieces, mixed_refs = refs[: 4 * groups], refs[4 * groups : 5 * groups]
    w_ref, gain_ref, shift_ref = refs[5 * groups : 5 * groups + 3]
    count = 4
    sums_refs = refs[5 * groups + 3 : 6 * groups + 3]
    ends_refs, back_refs = refs[6 * groups + 3 : -count - 5], refs[-count - 5 : -5]
    keep_ref, send_ref, gqkv_ref, grad_ref, left_ref = refs[-5:]
    blocks = per // BLOCK
    batches = dkv_ref.shape[0] // blocks
    gqkv_ref[:, : 4 * HD] = dq_ref[...].reshape(-1, 4 * HD).astype(BF16)
    gqkv_ref[:, 4 * HD :] = dkv_ref[...].reshape(-1, 6 * HD).astype(BF16)
    for m in range(batches):
        i = m * blocks
        low, high = ret_low_ref[m].astype(F32), ret_high_ref[m].astype(F32)
        if blocks == 1:
            gqkv_ref[i * BLOCK : (i + 1) * BLOCK, 4 * HD :] = (dkv_ref[i] + low + high).astype(BF16)
        else:
            j = i + blocks - 1
            gqkv_ref[i * BLOCK : (i + 1) * BLOCK, 4 * HD :] = (dkv_ref[i] + low).astype(BF16)
            gqkv_ref[j * BLOCK : (j + 1) * BLOCK, 4 * HD :] = (dkv_ref[j] + high).astype(BF16)
    lead = meta_ref[3] == 1
    rows = batches * BLOCK
    mine, given = mine_ref[...].reshape(rows, 10 * HD), given_ref[...].reshape(rows, 10 * HD)
    ends = jnp.concatenate([jnp.where(lead, mine, given), jnp.where(lead, given, mine)], 0)
    firsts = jnp.concatenate([first0_ref[...], first1_ref[...]], 0)
    grad = dot_tn(first_ref[...], gqkv_ref[...]) + dot_tn(firsts, ends)
    grad_ref[:, : 10 * HD] = grad
    columns = jnp.sum(gqkv_ref[...].astype(F32), 0, keepdims=True)
    columns = columns + jnp.sum(ends.astype(F32), 0, keepdims=True)
    weights = w_ref[...].astype(F32)
    along = jnp.sum(grad * weights, -1, keepdims=True)
    shift_sum = jnp.sum(columns * weights, -1, keepdims=True)
    rows_in = [gain_ref[...][None], shift_ref[...][None]]
    rows_in += [sum(ref[n : n + 1] for ref in sums_refs) for n in range(2)]
    rows_in.append(jnp.zeros((4, grad.shape[0]), F32))
    gain, shift, gain2_sum, shift2_sum = (
        jnp.transpose(jnp.concatenate(rows_in, 0))[:, n : n + 1] for n in range(4)
    )
    stats = lanes_of([(along - shift * shift_sum) / gain, shift_sum, gain2_sum, shift2_sum], grad.shape[0])
    lane = lax.broadcasted_iota(jnp.int32, stats.shape, 1)
    moved = jnp.concatenate([stats[:, HD:], stats[:, :HD]], 1)
    grad_ref[:, 2 * HD : 4 * HD] = jnp.where(lane < HD, grad[:, 2 * HD : 4 * HD], moved)
    piece = pieces[0].shape[0]
    total = 0.0
    for g in range(groups):
        for k in range(4):
            left_ref[k * piece : (k + 1) * piece] = pieces[4 * g + k][...]
        total = total + dot_tn(left_ref[...], mixed_refs[g][...])
    grad_ref[:, 10 * HD :] = total
    split_rows(meta_ref, grad_ref, keep_ref, send_ref)
    for end, b in ((1, 0), (2, blocks - 1)):

        @pl.when(meta_ref[end] == 1)
        def _(b=b):
            for m in range(groups * seqs):
                rows = slice(m * per + b * BLOCK, m * per + (b + 1) * BLOCK)
                total = gqkv_ref[rows].astype(F32)
                for ref in ends_refs:
                    total = total + ref[m].astype(F32)
                gqkv_ref[rows] = total.astype(BF16)

    for g in range(groups):
        for k in range(4):
            for m in range(seqs):
                row = (g * seqs + m) * per + (meta_ref[0] ^ SWAP[k]) * share
                rows = pl.ds(pl.multiple_of(row, share), share)
                back = dot_nt(gqkv_ref[rows], w_ref[...]).astype(BF16)
                back_refs[k][(g * seqs + m) * share : (g * seqs + m + 1) * share] = back


def swap_tp(value, bit):
    return lax.ppermute(value, "tp", [(i, i ^ bit) for i in range(lax.axis_size("tp"))])


def scatter_tp(parts):
    far = swap_tp(parts[3], 1)
    near = swap_tp(parts[2], 1)
    both = (parts[1].astype(F32) + far.astype(F32)).astype(BF16)
    return parts[0], near, swap_tp(both, 2)


def gather_tp(piece, before_first=(), before_last=()):
    cross = swap_tp(after(piece, *before_first) if before_first else piece, 2)
    return piece, cross, swap_tp(piece, 1), swap_tp(after(cross, *before_last) if before_last else cross, 1)


def mirrored(pairs, last):
    return pairs + [(last - a, last - b) for a, b in pairs]


SECOND = [(1, 3), (4, 5), (2, 6), (0, 7)]


def in_first_group(myself, devices):
    if devices == 8:
        return (myself == 0) | (myself == 1) | (myself == 2) | (myself == 4)
    return myself < devices // 2


def spread(own, myself, devices, *before_last):
    last = devices - 1
    held = own
    if devices == 8:
        for k in (1, 2, 4):
            held = held + lax.ppermute(own, "seq", mirrored([(0, k)], last))
        held = after(held, *before_last)
        other = lax.ppermute(held, "seq", mirrored(SECOND, last))
    else:
        bit = 1
        while bit < devices // 2:
            held = held + lax.ppermute(held, "seq", mirrored([(i, i + bit) for i in range(bit)], last))
            bit *= 2
        other = lax.ppermute(held, "seq", [(i, i ^ bit) for i in range(devices)])
    first = in_first_group(myself, devices)
    return jnp.where(first, held, other), jnp.where(first, other, held), other


def collect_first(given, devices):
    last = devices - 1
    if devices == 8:
        return lax.ppermute(given, "seq", mirrored([(b, a) for a, b in SECOND], last))
    return lax.ppermute(given, "seq", [(i, i ^ (devices // 2)) for i in range(devices)])


def collect_rest(mine, devices, join):
    last = devices - 1
    if devices == 8:
        return [mine] + [lax.ppermute(mine, "seq", mirrored([(k, 0)], last)) for k in (1, 2, 4)]
    bit = devices // 2
    while bit > 1:
        bit //= 2
        mine = join(mine, lax.ppermute(mine, "seq", mirrored([(i + bit, i) for i in range(bit)], last)))
    return [mine]


def to_owners(slots):
    return lax.all_to_all(slots, "seq", split_axis=0, concat_axis=0, tiled=True)


def sum_seq_first(send, devices):
    return lax.ppermute(send, "seq", [(i, i ^ 1) for i in range(devices)])


def sum_seq_rest(pairs, meta, devices):
    count, rows = pairs[0][0].shape[:2]
    lanes = sum(keep.shape[2] for keep, _ in pairs)
    if count == 4:
        low = sds((rows, lanes), BF16)
        own, *out = call(
            partial(fold_kernel, len(pairs)), (sds((rows, lanes), F32), low, low, low), name="fold"
        )(*(v for pair in pairs for v in pair), smem=(meta,))
        return [own] + [
            lax.ppermute(piece, "seq", [(i, i ^ (2 * (n + 1))) for i in range(devices)])
            for n, piece in enumerate(out)
        ]
    total = [(keep.astype(F32) + got.astype(F32)).astype(BF16) for keep, got in pairs]
    return across(jnp.concatenate(total, 2), devices)


def across(total, devices):
    sides = [[i for i in range(devices) if i % 2 == side] for side in range(2)]
    got = lax.all_to_all(
        total, "seq", split_axis=0, concat_axis=0, tiled=True, axis_index_groups=sides
    )
    return [got[n] for n in range(total.shape[0])]


def sum_of(terms):
    total = terms[0].astype(F32)
    for term in terms[1:]:
        total = total + term.astype(F32)
    return total


def per_device(
    layer_input,
    out_grad,
    norm1_gain,
    norm1_shift,
    w_qkv,
    w_out,
    norm2_gain,
    norm2_shift,
    w_up,
    w_down,
    key_keep,
    rand_blocks,
):
    batches, per, width = layer_input.shape
    local = w_qkv.shape[2]
    devices = lax.axis_size("seq")
    myself = lax.axis_index("seq")
    tp_count = lax.axis_size("tp")
    tp_place = lax.axis_index("tp")
    assert local == 3 * HD and tp_count == 4 and devices % 2 == 0 and batches % 2 == 0
    share = per // tp_count
    bd = per // BLOCK
    total = batches * bd
    blocks_all = bd * devices
    groups = 2
    seqs = batches // groups
    piece = seqs * share
    refs = total * RANDS
    slots_per = max(1, -(-refs // devices))
    slots = devices * slots_per
    hidden_here = w_up.shape[1]
    rows = width // devices
    i32 = jnp.int32
    flag = lambda v: v.astype(i32)
    meta = jnp.stack(
        [
            tp_place, flag(myself == 0), flag(myself == devices - 1), flag(in_first_group(myself, devices)), myself,
        ]
    ).astype(i32)

    CHAIN.last = ()
    scale = 1.0 / math.sqrt(HD)
    x_rows = layer_input.reshape(batches * per, width)
    first, q, kv, w640 = CHAIN.done(project(x_rows, norm1_gain, norm1_shift, w_qkv.transpose(1, 0, 2)))
    is_first, is_last = myself == 0, myself == devices - 1
    ends = jnp.where(is_first, layer_input[:, :BLOCK], layer_input[:, per - BLOCK :])
    ends = jnp.where(is_first | is_last, ends, jnp.zeros_like(ends))
    lead_x0, lead_x1, arrived = spread(ends, myself, devices, kv)
    q_blocks = q.reshape(total, BLOCK, 4 * HD)
    kv_blocks = kv.reshape(total, BLOCK, 6 * HD)
    kv_seqs = kv.reshape(batches, per, 6 * HD)

    table = (
        rand_blocks.reshape(batches, devices, bd, RANDS).transpose(1, 0, 2, 3).reshape(devices, refs)
    )
    owners = table // bd
    source = (jnp.arange(refs, dtype=i32) // (bd * RANDS))[None] * bd + table - owners * bd
    order = jnp.arange(refs, dtype=i32)
    earlier = order[None, :] < order[:, None]
    rank = jnp.sum(((owners[:, :, None] == owners[:, None, :]) & earlier[None]).astype(i32), -1)
    places = jnp.arange(slots_per, dtype=i32)
    asked = (owners == myself)[:, None, :] & (rank[:, None, :] == places[None, :, None])
    source_of = jnp.sum(jnp.where(asked, source[:, None, :], 0), -1).reshape(slots)
    valid = jnp.sum(asked.astype(i32), -1).reshape(slots)
    my_owner = lax.dynamic_index_in_dim(owners, myself, 0, False)
    my_rank = lax.dynamic_index_in_dim(rank, myself, 0, False)
    slot_of = my_owner * slots_per + my_rank
    mine = lax.dynamic_index_in_dim(table, myself, 0, False)
    query_of = jnp.sum(
        jnp.where(
            slot_of[None, :] == jnp.arange(slots, dtype=i32)[:, None], (order // RANDS)[None, :], 0
        ),
        -1,
    )

    end_kv = sds((batches, BLOCK, 6 * HD), BF16)
    end_all = sds((batches, BLOCK, 10 * HD), BF16)
    sent, kv_low, kv_high = call(
        partial(dispatch_kernel, bd),
        (sds((slots, BLOCK, 6 * HD), BF16), end_kv, end_kv),
        name="dispatch",
    )(kv_blocks, smem=(source_of,))
    rand_kv = to_owners(after(sent, arrived))
    up = [(i, i + 1) for i in range(devices - 1)]
    down = [(b, a) for a, b in up]
    low = lax.ppermute(kv_high, "seq", up)
    high = lax.ppermute(kv_low, "seq", down)

    bias, seq_bias, column_bias, wo256 = call(
        partial(bias_kernel, bd, blocks_all),
        (
            sds((total, 1, 8 * BLOCK), F32),
            sds((batches, 1, per), F32),
            sds((total, BLOCK, 2 * HD), F32),
            sds((width, 4 * HD), BF16),
        ),
        name="bias",
    )(key_keep.reshape(batches * blocks_all, BLOCK), w_out, smem=(mine, meta))

    grad_up = dot_nn(out_grad.reshape(batches * per, width), w_down)
    grad_up = grad_up.reshape(batches, per, hidden_here)

    part = sds((batches, BLOCK, 4 * HD), F32)
    low_piece = sds((piece, width), BF16)
    low_pieces = sds((groups * piece, width), BF16)
    high_piece = sds((piece, width), F32)
    attn, lse = [], []

    def attend(g):
        half_of = lambda array: part_of(array, g, groups)
        out, stat = call(
            partial(sparse_fwd_kernel, g * seqs * bd, seqs, per, share),
            (sds((4 * piece, 4 * HD), BF16), sds((seqs * per, 2 * HD), F32)),
            (
                pltpu.VMEM((seqs, per + 2 * BLOCK, 6 * HD), BF16),
                pltpu.VMEM((2, 8 * BLOCK, 6 * HD), BF16),
            ),
            name="sparse_fwd",
        )(
            half_of(q_blocks), half_of(kv_seqs), half_of(low), half_of(high), half_of(lead0), half_of(lead1),
            rand_kv, half_of(bias), smem=(slot_of, meta),
        )
        attn.append(out)
        lse.append(stat)

    lead_rows = sds((batches * BLOCK, width), BF16)
    lead_first0, lead_first1, lead0, lead1, part_mine, part_given = call(
        lead_fwd_kernel, (lead_rows, lead_rows, end_all, end_all, part, part), name="lead_fwd"
    )(kv_seqs, after(seq_bias, grad_up), lead_x0, lead_x1, norm1_gain, norm1_shift, w640, smem=(meta,))
    part_got = collect_first(part_given, devices)
    q_slots = call(gather_kernel, sds((slots, BLOCK, 4 * HD), BF16), name="gather")(q_blocks, smem=(query_of,))
    rand_q = to_owners(after(q_slots, rand_kv, part_got, low, high))
    attend(0)
    lead_parts = collect_rest(merge(part_mine, part_got), devices, merge)
    attend(1)
    lead_out, lead_lse = call(
        lead_finish_kernel,
        (sds(part.shape, BF16), sds((batches, BLOCK, 2 * HD), F32)),
        name="lead_finish",
        limit=SMALL,
    )(*lead_parts)
    out = call(
        partial(out_project_kernel, groups, seqs, per, share),
        (sds((4 * piece, 4 * HD), BF16),) * groups + (low_piece,) * (4 * groups),
        name="out_project",
        limit=SMALL,
    )(wo256, lead_out, *attn, smem=(meta,))
    mixed = out[:groups]
    attn_parts = [scatter_tp(out[groups + 4 * g : groups + 4 * g + 4]) for g in range(groups)]

    flat = lambda lists: [v for group in lists for v in group]
    hidden, act, total_grad, sums2, attn_grad = [], [], [], [], []
    ups, pres, back_parts, down_parts = [], [], [], []
    for g in range(groups):
        h, a = share_call(mid_fwd_kernel, (high_piece, low_piece), [(layer_input, g, 0)], "mid_fwd")(
            meta, seqs, share, *attn_parts[g], norm2_gain, norm2_shift
        )
        hidden.append(h)
        act.append(gather_tp(a, attn_parts[-1][2:]))
    low_hidden = sds((piece, hidden_here), BF16)
    for g in range(groups):
        out = share_call(
            ffn_kernel, (low_hidden, low_hidden, low_piece) * 4, [(grad_up, g, k) for k in range(4)], "ffn", PARAMS
        )(meta, seqs, share, *act[g], w_up)
        ups.append(out[0::3])
        pres.append(out[1::3])
        back_parts.append(scatter_tp(out[2::3]))
    for g in range(groups):
        t, a, s = share_call(
            mid_bwd_kernel, (high_piece, low_piece, sds((2, width), F32)), [(out_grad, g, 0)], "mid_bwd"
        )(meta, seqs, share, *back_parts[g], hidden[g], norm2_gain)
        total_grad.append(t)
        sums2.append(s)
        if g == 0:
            down_parts = call(partial(down_kernel, groups), (low_pieces,) * 4, name="down")(*flat(ups), w_down)
            attn_grad.append(gather_tp(a))
        if g == groups - 1:
            halves = sds((devices // 2, rows, hidden_here), BF16)
            ff_keep0, ff_send0, ff_keep1, ff_send1 = call(
                partial(ffn_grad_kernel, groups, seqs, per, share),
                (halves,) * 4,
                (
                    pltpu.VMEM((batches * per, width), BF16),
                    pltpu.VMEM((batches * per, hidden_here), BF16),
                    pltpu.VMEM((width, 2 * hidden_here), F32),
                ),
                name="ffn_grad",
            )(
                out_grad.reshape(batches * per, width), *flat(ups), *flat(act), *flat(pres), smem=(meta,)
            )
            attn_grad.append(gather_tp(a, (), (ff_send0,)))
            ff_got0 = sum_seq_first(after(ff_send0, attn_grad[-1][1]), devices)

    lead_grad = call(
        partial(lead_grad_kernel, groups, seqs, per, share),
        sds((batches, BLOCK, 4 * HD), BF16),
        (pltpu.VMEM((batches * BLOCK, width), BF16),),
        name="lead_grad",
        limit=SMALL,
    )(wo256, lead_lse, lead_out, *flat(attn_grad), smem=(meta,))
    grads, sent = call(
        partial(heads_grad_kernel, groups, seqs, per, share),
        (sds((batches * per, 4 * HD), BF16), sds((slots, BLOCK, 4 * HD), BF16)),
        name="heads_grad",
    )(wo256, *flat(attn_grad), *mixed, *lse, smem=(query_of, meta))
    *lead_do, arrived = spread(lead_grad, myself, devices, sent)
    rand_do = to_owners(after(sent, arrived, rand_q, ff_got0))
    ff_got1 = sum_seq_first(after(ff_send1, arrived), devices)
    dend = sds(end_kv.shape, F32)
    dq, dkv, ret_low, ret_high, dlead0, dlead1 = call(
        partial(sparse_bwd_kernel, batches, per),
        (sds((total, BLOCK, 4 * HD), F32), sds((batches, per, 6 * HD), F32), end_kv, end_kv, dend, dend),
        (
            pltpu.VMEM((batches, per + 2 * BLOCK, 6 * HD), BF16),
            pltpu.VMEM((2, 8 * BLOCK, 6 * HD), BF16),
            pltpu.VMEM((batches, per + 2 * BLOCK, 6 * HD), F32),
            pltpu.VMEM((batches, 2 * BLOCK, 6 * HD), F32),
        ),
        name="sparse_bwd",
    )(
        q_blocks, kv_seqs, low, high, lead0, lead1, rand_kv, bias,
        after(grads, *lead_do).reshape(total, BLOCK, 4 * HD), smem=(slot_of,),
    )
    from_low = lax.ppermute(ret_high, "seq", up)
    from_high = lax.ppermute(ret_low, "seq", down)
    dkv, ends_mine, ends_given = call(
        lead_bwd_kernel, (sds((batches, per, 6 * HD), F32), end_all, end_all), name="lead_bwd"
    )(lead0, lead1, kv_seqs, seq_bias, dkv, dlead0, dlead1, *lead_do, smem=(meta,))
    add = lambda a, b: (a.astype(F32) + b.astype(F32)).astype(BF16)
    ends_first = collect_first(ends_given, devices)
    ends_got = collect_rest(add(after(ends_mine, from_low, from_high), ends_first), devices, add)

    dkv = call(slots_kernel, sds((total, BLOCK, 6 * HD), F32), name="slots")(
        rand_q, rand_do, kv_blocks, column_bias,
        dkv.reshape(total, BLOCK, 6 * HD), smem=(source_of, valid),
    )
    ff_half = jnp.concatenate(
        [
            (keep.astype(F32) + got.astype(F32)).astype(BF16)
            for keep, got in ((ff_keep0, ff_got0), (after(ff_keep1, dkv), after(ff_got1, dkv)))
        ],
        2,
    )
    ff = across(after(ff_half, *ends_got), devices)
    halves = sds((devices // 2, rows, 14 * HD), BF16)
    *first_back, qkv_keep, qkv_send = call(
        partial(tail_kernel, groups, seqs, per, share, devices),
        (low_pieces,) * 4 + (halves, halves),
        (
            pltpu.VMEM((total * BLOCK, 10 * HD), BF16),
            pltpu.VMEM((width, 14 * HD), F32),
            pltpu.VMEM((4 * piece, width), BF16),
        ),
        name="tail",
    )(
        dq, dkv, from_low, from_high, first, lead_first0, lead_first1, ends_mine, ends_given,
        *flat(attn_grad), *mixed, w640, norm1_gain, norm1_shift, *sums2, *ends_got, smem=(meta,),
    )
    qkv_got = sum_seq_first(qkv_send, devices)
    terms = scatter_tp(first_back)
    out_terms = scatter_tp([after(part, first_back[0]) for part in down_parts])
    ff = sum_of(ff)
    gq = sum_seq_rest([(qkv_keep, after(qkv_got, ff))], meta, devices)
    input_grad = share_call(
        partial(end_kernel, groups),
        sds((batches, share, width), F32),
        [(layer_input, g, 0) for g in range(groups)],
        "end",
    )(meta, seqs, share, *terms, *total_grad, norm1_gain)
    layer_output = call(
        partial(output_kernel, groups), sds((batches, share, width), F32), name="output", limit=SMALL
    )(*out_terms, *hidden)

    g_down, g_up = ff[:, :hidden_here], ff[:, hidden_here:]
    gq = sum_of(gq)
    norms = gq[:, 3 * HD : 4 * HD]
    norms = norms + swap_tp(norms, 1)
    norms = norms + swap_tp(norms, 2)
    g_out = jnp.concatenate([gq[:, 10 * HD : 12 * HD], gq[:, 13 * HD :]], 1)
    g_qkv = jnp.stack(
        [
            gq[:, : 3 * HD] * scale,
            jnp.concatenate([gq[:, 4 * HD : 6 * HD], gq[:, 8 * HD : 9 * HD]], 1),
            jnp.concatenate([gq[:, 6 * HD : 8 * HD], gq[:, 9 * HD : 10 * HD]], 1),
        ],
        1,
    )
    return (
        layer_output, input_grad, g_qkv, g_out, g_up, g_down, norms[:, 0], norms[:, 1], norms[:, 2], norms[:, 3],
    )


def solution(mesh):
    return jax.shard_map(
        per_device,
        mesh=mesh,
        in_specs=(
            P(None, "seq", None),
            P(None, "seq", None),
            P(),
            P(),
            P(None, None, "tp"),
            P(None, "tp"),
            P(),
            P(),
            P(None, "tp"),
            P(None, "tp"),
            P(),
            P(),
        ),
        out_specs=(
            P(None, ("seq", "tp"), None),
            P(None, ("seq", "tp"), None),
            P("seq", None, "tp"),
            P("seq", "tp"),
            P("seq", "tp"),
            P("seq", "tp"),
            P("seq"),
            P("seq"),
            P("seq"),
            P("seq"),
        ),
        check_vma=False,
    )
```

```python
from functools import partial
import math

import jax
import jax.numpy as jnp
from jax import lax
from jax.experimental import pallas as pl
from jax.experimental.pallas import tpu as pltpu
from jax.sharding import PartitionSpec as P

HD = 64
BLOCK = 64
RANDS = 3
EPS = 1e-06
SWAP = (0, 2, 1, 3)
NEG = -1e30
Q_LANES = (128, 192, 0)
O_LANES = (0, 64, 192)
K_PART = slice(128, 384)
V_PART = slice(0, 256)
F32 = jnp.float32
BF16 = jnp.bfloat16
VMEM = pl.BlockSpec(memory_space=pltpu.VMEM)
SMEM = pl.BlockSpec(memory_space=pltpu.SMEM)
MIB = 1024 * 1024


def sds(shape, kind):
    return jax.ShapeDtypeStruct(shape, kind)


PARAMS = pltpu.CompilerParams(vmem_limit_bytes=56 * MIB)
SMALL = pltpu.CompilerParams(vmem_limit_bytes=12 * MIB)
MIDDLE = pltpu.CompilerParams(vmem_limit_bytes=24 * MIB)


def after(value, *others):
    return lax.optimization_barrier((value,) + others)[0]


class Chain:
    last = ()

    def link(self, value):
        return after(value, *self.last) if self.last else value

    def done(self, outs):
        self.last = (jax.tree.leaves(outs)[0],)
        return outs


CHAIN = Chain()


def part_of(array, at, count):
    return array, at, count


TIMES = {
    "project": 6, "dispatch": 3, "bias": 2, "lead_fwd": 4, "sparse_fwd": 7, "merge": 1, "lead_finish": 1, "out_project": 1,
    "mid_fwd": 1, "gather": 2, "ffn": 6, "ffn_grad": 7, "mid_bwd": 1, "heads_grad": 5, "lead_grad": 1, "sparse_bwd": 13,
    "fold_near": 3, "down": 6, "lead_bwd": 5, "slots": 14, "tail": 5, "fold_far": 2, "back": 7, "output": 1,
    "fold": 2, "end": 2,
}
HINT = 1.75e6


def cost(name):
    return pl.CostEstimate(flops=0, transcendentals=0, bytes_accessed=int(TIMES[name] * HINT))


def call(body, outs, scratch=(), name=None, limit=PARAMS):
    def run(*args, smem=()):
        specs = [SMEM] * len(smem)
        arrays = []
        if smem:
            smem = (CHAIN.link(smem[0]),) + tuple(smem[1:])
        else:
            args = (CHAIN.link(args[0]),) + args[1:]
        for arg in args:
            if isinstance(arg, tuple):
                array, at, count = arg
                shape = (array.shape[0] // count,) + array.shape[1:]
                index = (at,) + (0,) * (array.ndim - 1)
                specs.append(pl.BlockSpec(shape, lambda i, index=index: index))
                arrays.append(array)
            else:
                specs.append(VMEM)
                arrays.append(arg)
        return CHAIN.done(
            pl.pallas_call(
                body,
                out_shape=outs,
                grid=(1,),
                in_specs=specs,
                out_specs=jax.tree.map(lambda _: VMEM, outs),
                scratch_shapes=list(scratch),
                compiler_params=limit,
                cost_estimate=cost(name),
                name=name,
            )(*smem, *arrays)
        )

    return run


def share_call(body, outs, blocks, name, limit=SMALL):
    def run(meta, seqs, share, *args):
        def spec(value, group, pos):
            return pl.BlockSpec(
                (seqs, share, value.shape[2]), lambda i, meta_ref: (group, meta_ref[0] ^ SWAP[pos], 0)
            )

        return CHAIN.done(
            pl.pallas_call(
                body,
                out_shape=outs,
                grid_spec=pltpu.PrefetchScalarGridSpec(
                    num_scalar_prefetch=1,
                    grid=(1,),
                    in_specs=[spec(*b) for b in blocks] + [VMEM] * len(args),
                    out_specs=jax.tree.map(lambda _: VMEM, outs),
                ),
                compiler_params=limit,
                cost_estimate=cost(name),
                name=name,
            )(CHAIN.link(meta), *(b[0] for b in blocks), *args)
        )

    return run


def dot_nt(a, b):
    return lax.dot_general(a, b, (((1,), (1,)), ((), ())), preferred_element_type=F32)


def dot_tn(a, b):
    return lax.dot_general(a, b, (((0,), (0,)), ((), ())), preferred_element_type=F32)


def dot_nn(a, b):
    return lax.dot_general(a, b, (((1,), (0,)), ((), ())), preferred_element_type=F32)


def stack(rows, lanes):
    lane = lax.broadcasted_iota(jnp.int32, rows.shape, 1)
    zero = jnp.zeros_like(rows)
    return jnp.concatenate([jnp.where((lane >= at) & (lane < at + HD), rows, zero) for at in lanes], 0)


def unstack(stacked, lanes):
    rows = stacked.shape[0] // 3
    lane = lax.broadcasted_iota(jnp.int32, (rows, stacked.shape[1]), 1)
    out = jnp.zeros((rows, stacked.shape[1]), stacked.dtype)
    for h, at in enumerate(lanes):
        out = jnp.where((lane >= at) & (lane < at + HD), stacked[h * rows : (h + 1) * rows], out)
    return out


def thirds(column):
    rows = column.shape[0] // 3
    return [column[h * rows : (h + 1) * rows] for h in range(3)]


def half(tile, upper):
    lane = lax.broadcasted_iota(jnp.int32, tile.shape, 1)
    return jnp.where((lane >= HD) if upper else (lane < HD), tile, jnp.zeros_like(tile))


def lanes_of(columns, rows):
    lane = lax.broadcasted_iota(jnp.int32, (rows, 2 * HD), 1)
    out = jnp.zeros((rows, 2 * HD), F32)
    for at, column in enumerate(columns):
        out = jnp.where(lane == at, column, out)
    return out


def hi_lo(value):
    hi = value.astype(BF16).astype(F32)
    return hi, value - hi


def norm_rows(hidden):
    center = hidden - jnp.mean(hidden, -1, keepdims=True)
    inverse = lax.rsqrt(jnp.mean(center * center, -1, keepdims=True) + EPS)
    return center * inverse, inverse


def norm_rows_back(grad, normed, inverse, gain):
    scaled = grad * gain
    return inverse * (
        scaled
        - jnp.mean(scaled, -1, keepdims=True)
        - normed * jnp.mean(scaled * normed, -1, keepdims=True)
    )


def project_kernel(x_ref, gain_ref, shift_ref, raw_ref, first_ref, q_ref, kv_ref, w_ref):
    @pl.when(pl.program_id(0) == 0)
    def _():
        scale = jnp.asarray(1.0 / math.sqrt(HD), BF16)
        blank = jnp.zeros((w_ref.shape[0], HD), BF16)
        w_ref[:, : 2 * HD] = jnp.concatenate([raw_ref[0, :, 2 * HD :] * scale, blank], 1)
        w_ref[:, 2 * HD : 4 * HD] = raw_ref[0, :, : 2 * HD] * scale
        w_ref[:, 4 * HD : 6 * HD] = raw_ref[2, :, : 2 * HD]
        w_ref[:, 6 * HD : 8 * HD] = jnp.concatenate([raw_ref[1, :, 2 * HD :], raw_ref[2, :, 2 * HD :]], 1)
        w_ref[:, 8 * HD :] = raw_ref[1, :, : 2 * HD]

    normed, _ = norm_rows(x_ref[...].astype(F32))
    first = (normed * gain_ref[...][None] + shift_ref[...][None]).astype(BF16)
    first_ref[...] = first
    out = dot_nn(first, w_ref[...]).astype(BF16)
    q_ref[...] = out[:, : 4 * HD]
    kv_ref[...] = out[:, 4 * HD :]


def project(x, gain, shift, raw):
    rows, width = x.shape
    tile = min(rows, 256)
    row = lambda w: pl.BlockSpec((tile, w), lambda i: (i, 0))
    vector = pl.BlockSpec((width,), lambda i: (0,))
    whole = lambda w: pl.BlockSpec((width, w), lambda i: (0, 0))
    low = lambda *shape: sds(shape, BF16)
    return pl.pallas_call(
        project_kernel,
        grid=(rows // tile,),
        out_shape=(low(rows, width), low(rows, 4 * HD), low(rows, 6 * HD), low(width, 10 * HD)),
        in_specs=[
            row(width), vector, vector, pl.BlockSpec(raw.shape, lambda i: (0, 0, 0)),
        ],
        out_specs=(row(width), row(4 * HD), row(6 * HD), whole(10 * HD)),
        compiler_params=PARAMS,
        cost_estimate=cost("project"),
        name="project",
    )(x, gain, shift, raw)


def dispatch_kernel(bd, index_ref, kv_ref, sent_ref, low_ref, high_ref):
    def step(slot, _):
        sent_ref[slot] = kv_ref[index_ref[slot]]
        return 0

    lax.fori_loop(0, sent_ref.shape[0], step, 0, unroll=4)
    for m in range(low_ref.shape[0]):
        low_ref[m] = kv_ref[m * bd]
        high_ref[m] = kv_ref[m * bd + bd - 1]


def bias_kernel(bd, blocks_all, table_ref, meta_ref, keep_ref, raw_ref, bias_ref, seq_ref, column_ref, wo_ref):
    wo_ref[:, : 2 * HD] = raw_ref[:, : 2 * HD]
    blank = jnp.zeros((wo_ref.shape[0], HD), BF16)
    wo_ref[:, 2 * HD :] = jnp.concatenate([blank, raw_ref[:, 2 * HD :]], 1)
    low = lambda keep: jnp.where(keep > 0, 0.0, NEG)
    for m in range(seq_ref.shape[0]):
        for b in range(bd):
            i = m * bd + b
            here = meta_ref[4] * bd + b

            def row(block, inside=True):
                return low(jnp.where(inside, keep_ref[pl.ds(m * blocks_all + block, 1)], 0))

            own = row(here)
            listed = [
                row(jnp.maximum(here - 1, 0), here > 0),
                own,
                row(jnp.minimum(here + 1, blocks_all - 1), here < blocks_all - 1),
                row(0),
                row(blocks_all - 1),
            ] + [row(table_ref[i * RANDS + j]) for j in range(RANDS)]
            bias_ref[i] = jnp.concatenate(listed, 1)
            seq_ref[m, :, b * BLOCK : (b + 1) * BLOCK] = own
            column_ref[i] = jnp.transpose(jnp.broadcast_to(own, (4 * HD, BLOCK)))


def gather_kernel(index_ref, blocks_ref, out_ref):
    def step(slot, _):
        out_ref[slot] = blocks_ref[index_ref[slot]]
        return 0

    lax.fori_loop(0, out_ref.shape[0], step, 0, unroll=4)


def lead_fwd_kernel(
    meta_ref, kv_ref, bias_ref, x0_ref, x1_ref, gain_ref, shift_ref, w_ref, first0_ref, first1_ref,
    lead0_ref, lead1_ref, mine_ref, given_ref,
):
    for x_ref, first_ref, lead_ref in ((x0_ref, first0_ref, lead0_ref), (x1_ref, first1_ref, lead1_ref)):
        normed, _ = norm_rows(x_ref[...].reshape(-1, x_ref.shape[2]).astype(F32))
        first = (normed * gain_ref[...][None] + shift_ref[...][None]).astype(BF16)
        first_ref[...] = first
        lead_ref[...] = dot_nn(first, w_ref[...]).astype(BF16).reshape(lead_ref.shape)
    low = meta_ref[3]
    for m in range(kv_ref.shape[0]):
        queries = jnp.concatenate([lead0_ref[m, :, : 4 * HD], lead1_ref[m, :, : 4 * HD]], 0)
        scores = dot_nt(stack(queries, Q_LANES), kv_ref[m, :, K_PART]) + bias_ref[m]
        top = jnp.max(scores, -1, keepdims=True)
        expo = jnp.exp(scores - top)
        total = jnp.sum(expo, -1, keepdims=True)
        out = unstack(dot_nn(expo.astype(BF16), kv_ref[m, :, V_PART]), O_LANES)
        stats = lanes_of(thirds(top) + thirds(total), 2 * BLOCK)
        for part_ref, first in ((mine_ref, low == 1), (given_ref, low == 0)):
            for lanes, value in ((slice(0, 2 * HD), out[:, : 2 * HD]), (slice(2 * HD, 4 * HD), out[:, 2 * HD :] + stats)):
                part_ref[m, :, lanes] = jnp.where(first, value[:BLOCK], value[BLOCK:])


def merge_parts(parts):
    lane = lax.broadcasted_iota(jnp.int32, (BLOCK, 2 * HD), 1)
    stats = [p[:, 2 * HD :] for p in parts]
    top = stats[0]
    for st in stats[1:]:
        top = jnp.maximum(top, st)
    tops = [top[:, h : h + 1] for h in range(3)]
    sums = [0.0, 0.0, 0.0]
    out0, out1 = 0.0, 0.0
    for p, st in zip(parts, stats):
        scale = [jnp.exp(st[:, h : h + 1] - tops[h]) for h in range(3)]
        sums = [sums[h] + st[:, 3 + h : 4 + h] * scale[h] for h in range(3)]
        out0 = out0 + p[:, : 2 * HD] * jnp.where(lane < HD, scale[0], scale[1])
        out1 = out1 + st * scale[2]
    return out0, jnp.where(lane >= HD, out1, 0.0), tops, sums


def merge_kernel(a_ref, b_ref, out_ref):
    for m in range(a_ref.shape[0]):
        out0, out1, tops, sums = merge_parts([a_ref[m], b_ref[m]])
        out_ref[m, :, : 2 * HD] = out0
        out_ref[m, :, 2 * HD :] = out1 + lanes_of(tops + sums, BLOCK)


def merge(a, b):
    return call(merge_kernel, sds(a.shape, F32), name="merge", limit=SMALL)(a, b)


def lead_finish_kernel(*refs):
    part_refs, (out_ref, lse_ref) = refs[:-2], refs[-2:]
    lane = lax.broadcasted_iota(jnp.int32, (BLOCK, 2 * HD), 1)
    for m in range(out_ref.shape[0]):
        out0, out1, tops, sums = merge_parts([p[m] for p in part_refs])
        out_ref[m, :, : 2 * HD] = (out0 / jnp.where(lane < HD, sums[0], sums[1])).astype(BF16)
        out_ref[m, :, 2 * HD :] = (out1 / sums[2]).astype(BF16)
        lse_ref[m] = lanes_of([tops[h] + jnp.log(sums[h]) for h in range(3)], BLOCK)


def fill_ext(ext_ref, kv_ref, low_ref, high_ref, seqs, per):
    for m in range(seqs):
        ext_ref[m, :BLOCK] = low_ref[m]
        ext_ref[m, BLOCK : BLOCK + per] = kv_ref[m]
        ext_ref[m, BLOCK + per :] = high_ref[m]


def fill_listed(listed_ref, ext_ref, lead0_ref, lead1_ref, rand_ref, slot_ref, m, b, block):
    listed_ref[: 3 * BLOCK] = ext_ref[m, pl.ds(pl.multiple_of(b * BLOCK, BLOCK), 3 * BLOCK)]
    listed_ref[3 * BLOCK : 4 * BLOCK] = lead0_ref[m, :, 4 * HD :]
    listed_ref[4 * BLOCK : 5 * BLOCK] = lead1_ref[m, :, 4 * HD :]
    for j in range(RANDS):
        listed_ref[(5 + j) * BLOCK : (6 + j) * BLOCK] = rand_ref[slot_ref[block * RANDS + j]]


def pos_of(meta_ref, at):
    j = at ^ meta_ref[0]
    return ((j & 1) << 1) | (j >> 1)


def sparse_fwd_kernel(
    first, seqs, per, share, slot_ref, meta_ref, q_ref, kv_ref, low_ref, high_ref, lead0_ref,
    lead1_ref, rand_ref, bias_ref, out_ref, lse_ref, ext_ref, listed_ref,
):
    blocks = per // BLOCK
    chunk = min(share, BLOCK)
    fill_ext(ext_ref, kv_ref, low_ref, high_ref, seqs, per)

    def attend(i, here):
        m, b = i // blocks, i % blocks
        fill_listed(here, ext_ref, lead0_ref, lead1_ref, rand_ref, slot_ref, m, b, first + i)
        scores = dot_nt(stack(q_ref[i], Q_LANES), here[:, K_PART]) + bias_ref[i]
        top = jnp.max(scores, -1, keepdims=True)
        expo = jnp.exp(scores - top)
        total = jnp.sum(expo, -1, keepdims=True)
        prob = (expo * (1.0 / total)).astype(BF16)
        out = unstack(dot_nn(prob, here[:, V_PART]), O_LANES).astype(BF16)
        lse_ref[pl.ds(pl.multiple_of(i * BLOCK, BLOCK), BLOCK)] = lanes_of(
            thirds(top + jnp.log(total)), BLOCK
        )
        for c in range(BLOCK // chunk):
            token = b * BLOCK + c * chunk
            at = token // share
            row = pos_of(meta_ref, at) * (seqs * share) + m * share + (token - at * share)
            rows = pl.ds(pl.multiple_of(row, chunk), chunk)
            out_ref[rows] = out[c * chunk : (c + 1) * chunk]

    def step(j, _):
        attend(2 * j, listed_ref.at[0])
        attend(2 * j + 1, listed_ref.at[1])
        return 0

    lax.fori_loop(0, seqs * blocks // 2, step, 0)


def out_project_kernel(groups, seqs, per, share, meta_ref, wo_ref, lead_out_ref, *refs):
    attn_refs, mixed_refs, part_refs = refs[:groups], refs[groups : 2 * groups], refs[2 * groups :]
    blocks = per // BLOCK
    chunk = min(share, BLOCK)
    piece = seqs * share
    for g in range(groups):
        mixed_refs[g][...] = attn_refs[g][...]
    for end, b in ((1, 0), (2, blocks - 1)):

        @pl.when(meta_ref[end] == 1)
        def _(b=b):
            for g in range(groups):
                for m in range(seqs):
                    for c in range(BLOCK // chunk):
                        token = b * BLOCK + c * chunk
                        at = token // share
                        row = pos_of(meta_ref, at) * piece + m * share + (token - at * share)
                        rows = pl.ds(pl.multiple_of(row, chunk), chunk)
                        mixed_refs[g][rows] = lead_out_ref[g * seqs + m, c * chunk : (c + 1) * chunk]

    wo = wo_ref[...]
    for g in range(groups):
        for k in range(4):
            rows = slice(k * piece, (k + 1) * piece)
            part_refs[4 * g + k][...] = dot_nt(mixed_refs[g][rows], wo).astype(BF16)


def down_kernel(groups, *refs):
    up_refs, w_ref, out_refs = refs[: 4 * groups], refs[4 * groups], refs[4 * groups + 1 :]
    rows = up_refs[0].shape[0]
    for g in range(groups):
        for k in range(4):
            out = dot_nt(up_refs[4 * g + k][...], w_ref[...]).astype(BF16)
            out_refs[k][g * rows : (g + 1) * rows] = out


def total_of(refs):
    return refs[0][...].astype(F32) + refs[1][...].astype(F32) + refs[2][...].astype(F32)


def mid_fwd_kernel(meta_ref, x_ref, own_ref, core_ref, y_ref, gain_ref, shift_ref, hidden_ref, act_ref):
    x = x_ref[...].reshape(hidden_ref.shape).astype(F32)
    hidden = total_of((own_ref, core_ref, y_ref)) + x
    normed, _ = norm_rows(hidden)
    hidden_ref[...] = hidden
    act_ref[...] = (normed * gain_ref[...][None] + shift_ref[...][None]).astype(BF16)


def ffn_kernel(meta_ref, *refs):
    gu_refs, act_refs, w_ref, outs = refs[:4], refs[4:8], refs[8], refs[9:]
    rows = act_refs[0].shape[0]
    for k in (3, 2, 1, 0):
        up_ref, pre_ref, back_ref = outs[3 * k : 3 * k + 3]
        pre = dot_nn(act_refs[k][...], w_ref[...])
        phi = 0.5 + 0.5 * lax.erf(pre * (1.0 / math.sqrt(2.0)))
        density = jnp.exp(-0.5 * pre * pre) * (1.0 / math.sqrt(2.0 * math.pi))
        up_ref[...] = (pre * phi).astype(BF16)
        gu = gu_refs[k][...].reshape(rows, gu_refs[k].shape[2])
        grad_pre = (gu * (phi + pre * density)).astype(BF16)
        pre_ref[...] = grad_pre
        back_ref[...] = dot_nt(grad_pre, w_ref[...]).astype(BF16)


def mid_bwd_kernel(
    meta_ref, og_ref, own_ref, core_ref, y_ref, hidden_ref, gain_ref, total_ref, low_ref, sums_ref
):
    grad = total_of((own_ref, core_ref, y_ref))
    normed, inverse = norm_rows(hidden_ref[...])
    og = og_ref[...].reshape(hidden_ref.shape).astype(F32)
    total = og + norm_rows_back(grad, normed, inverse, gain_ref[...][None])
    total_ref[...] = total
    low_ref[...] = total.astype(BF16)
    sums_ref[0:1] = jnp.sum(grad * normed, 0, keepdims=True)
    sums_ref[1:2] = jnp.sum(grad, 0, keepdims=True)


def end_kernel(groups, meta_ref, *refs):
    x_refs, refs = refs[:groups], refs[groups:]
    own_ref, core_ref, y_ref = refs[:3]
    gain_ref, out_ref = refs[-2:]
    seqs = x_refs[0].shape[0]
    rows = own_ref.shape[0] // groups
    for g in range(groups):
        part = slice(g * rows, (g + 1) * rows)
        grad = total_of([ref.at[part] for ref in (own_ref, core_ref, y_ref)])
        normed, inverse = norm_rows(x_refs[g][...].reshape(grad.shape).astype(F32))
        total = refs[3 + g][...] + norm_rows_back(grad, normed, inverse, gain_ref[...][None])
        out_ref[g * seqs : (g + 1) * seqs] = total.reshape(x_refs[g].shape)


def output_kernel(groups, own_ref, core_ref, y_ref, *refs):
    out_ref = refs[-1]
    seqs, share, width = out_ref.shape
    seqs //= groups
    rows = seqs * share
    for g in range(groups):
        part = slice(g * rows, (g + 1) * rows)
        total = total_of([ref.at[part] for ref in (own_ref, core_ref, y_ref)]) + refs[g][...]
        out_ref[g * seqs : (g + 1) * seqs] = total.reshape(seqs, share, width)


def lead_grad_kernel(groups, seqs, per, share, meta_ref, wo_ref, lead_lse_ref, lead_out_ref, *refs):
    pieces, lead_ref, rows_ref = refs[:-2], refs[-2], refs[-1]
    blocks = per // BLOCK
    chunk = min(share, BLOCK)
    root = (meta_ref[1] + meta_ref[2]) == 1
    lead_ref[...] = jnp.zeros_like(lead_ref)
    token = jnp.where(meta_ref[1] == 1, 0, (blocks - 1) * BLOCK)
    for g in range(groups):
        for m in range(seqs):
            for c in range(BLOCK // chunk):
                at = (token + c * chunk) // share
                inside = pl.multiple_of(m * share + (token + c * chunk - at * share), chunk)
                for k in range(4):

                    @pl.when(root & (pos_of(meta_ref, at) == k))
                    def _(k=k, g=g, m=m, c=c, inside=inside):
                        to = (g * seqs + m) * BLOCK + c * chunk
                        rows_ref[to : to + chunk] = pieces[4 * g + k][pl.ds(inside, chunk)]

    @pl.when(root)
    def _():
        total = groups * seqs * BLOCK
        grad = dot_nn(rows_ref[...], wo_ref[...])
        low = grad.astype(BF16)
        prod = low.astype(F32) * lead_out_ref[...].reshape(total, 4 * HD).astype(F32)
        deltas = [
            jnp.sum(half(prod[:, : 2 * HD], False), -1, keepdims=True),
            jnp.sum(half(prod[:, : 2 * HD], True), -1, keepdims=True),
            jnp.sum(half(prod[:, 2 * HD :], True), -1, keepdims=True),
        ]
        d_hi, d_lo = zip(*(hi_lo(d) for d in deltas))
        lse = lead_lse_ref[...].reshape(total, 2 * HD)
        l_hi, l_lo = zip(*(hi_lo(lse[:, h : h + 1]) for h in range(3)))
        stats = lanes_of(l_hi + l_lo + d_hi + d_lo, total)
        tile1 = (half(grad[:, 2 * HD :], True) + stats).astype(BF16)
        lead_ref[:, :, : 2 * HD] = low[:, : 2 * HD].reshape(groups * seqs, BLOCK, 2 * HD)
        lead_ref[:, :, 2 * HD :] = tile1.reshape(groups * seqs, BLOCK, 2 * HD)


def heads_grad_kernel(groups, seqs, per, share, index_ref, meta_ref, wo_ref, *refs):
    pieces, mixed_refs = refs[: 4 * groups], refs[4 * groups : 5 * groups]
    lse_refs = refs[5 * groups : 6 * groups]
    grads_ref, sent_ref = refs[6 * groups :]
    wo = wo_ref[...]
    blocks = per // BLOCK
    rows_of = seqs * share
    for g in range(groups):
        for k in range(4):
            grad = dot_nn(pieces[4 * g + k][...], wo)
            low = grad.astype(BF16)
            prod = low.astype(F32) * mixed_refs[g][k * rows_of : (k + 1) * rows_of].astype(F32)
            deltas = [
                jnp.sum(half(prod[:, : 2 * HD], False), -1, keepdims=True),
                jnp.sum(half(prod[:, : 2 * HD], True), -1, keepdims=True),
                jnp.sum(half(prod[:, 2 * HD :], True), -1, keepdims=True),
            ]
            d_hi, d_lo = zip(*(hi_lo(d) for d in deltas))
            spare = [jnp.zeros_like(d_hi[0])] * 6
            stats = lanes_of(spare + list(d_hi + d_lo), rows_of)
            for m in range(seqs):
                at = slice(m * share, (m + 1) * share)
                inside = m * per + (meta_ref[0] ^ SWAP[k]) * share
                rows = pl.ds(pl.multiple_of(g * seqs * per + inside, share), share)
                lse = lse_refs[g][pl.ds(pl.multiple_of(inside, share), share)]
                l_hi, l_lo = zip(*(hi_lo(lse[:, h : h + 1]) for h in range(3)))
                grads_ref[rows, : 2 * HD] = low[at, : 2 * HD]
                grads_ref[rows, 2 * HD :] = (
                    half(grad[at, 2 * HD :], True) + stats[at] + lanes_of(l_hi + l_lo, share)
                ).astype(BF16)
    lane = lax.broadcasted_iota(jnp.int32, (BLOCK, 2 * HD), 1)
    for end, b in ((1, 0), (2, blocks - 1)):

        @pl.when(meta_ref[end] == 1)
        def _(b=b):
            for m in range(groups * seqs):
                rows = slice(m * per + b * BLOCK, m * per + (b + 1) * BLOCK)
                tile1 = grads_ref[rows, 2 * HD :].astype(F32)
                grads_ref[rows, : 2 * HD] = jnp.zeros((BLOCK, 2 * HD), BF16)
                grads_ref[rows, 2 * HD :] = jnp.where(lane < 6, tile1, 0.0).astype(BF16)

    def send(slot, _):
        at = pl.multiple_of(index_ref[slot] * BLOCK, BLOCK)
        sent_ref[slot] = grads_ref[pl.ds(at, BLOCK)]
        return 0

    lax.fori_loop(0, sent_ref.shape[0], send, 0, unroll=4)


def row_stats(tile):
    st = tile.astype(F32)
    lse = [st[:, h : h + 1] + st[:, 3 + h : 4 + h] for h in range(3)]
    delta = [st[:, 6 + h : 7 + h] + st[:, 9 + h : 10 + h] for h in range(3)]
    return lse, delta


def kv_grad(v_part, k_part):
    return jnp.concatenate([v_part[:, : 2 * HD], v_part[:, 2 * HD :] + k_part[:, : 2 * HD], k_part[:, 2 * HD :]], 1)


def sparse_bwd_kernel(
    batches, per, slot_ref, q_ref, kv_ref, low_ref, high_ref, lead0_ref, lead1_ref, rand_ref,
    bias_ref, grads_ref, dq_ref, dkv_ref, ret_low_ref, ret_high_ref, dlead0_ref, dlead1_ref,
    ext_ref, listed_ref, dext_ref, dlead_ref,
):
    blocks = per // BLOCK
    near = 6 * BLOCK
    fill_ext(ext_ref, kv_ref, low_ref, high_ref, batches, per)
    dext_ref[...] = jnp.zeros_like(dext_ref)
    dlead_ref[...] = jnp.zeros_like(dlead_ref)

    def attend(i, here):
        m, b = i // blocks, i % blocks
        fill_listed(here, ext_ref, lead0_ref, lead1_ref, rand_ref, slot_ref, m, b, i)
        grads = grads_ref[i]
        lse, delta = row_stats(grads[:, 2 * HD :])
        queries, grads = stack(q_ref[i], Q_LANES), stack(grads, O_LANES)
        prob = jnp.exp(dot_nt(queries, here[:, K_PART]) + bias_ref[i] - jnp.concatenate(lse, 0))
        ds = prob * (dot_nt(grads, here[:, V_PART]) - jnp.concatenate(delta, 0))
        ds = ds.astype(BF16)
        dq_ref[i] = unstack(dot_nn(ds, here[:, K_PART]), Q_LANES)
        dkv = kv_grad(dot_tn(prob[:, :near].astype(BF16), grads), dot_tn(ds[:, :near], queries))
        return m, b, dkv

    def step(j, _):
        done = [attend(2 * j + n, listed_ref.at[n]) for n in range(2)]
        for m, b, dkv in done:
            dext_ref[m, pl.ds(pl.multiple_of(b * BLOCK, BLOCK), 3 * BLOCK)] += dkv[: 3 * BLOCK]
            dlead_ref[m] += dkv[3 * BLOCK : 5 * BLOCK]
        return 0

    lax.fori_loop(0, batches * blocks // 2, step, 0)
    for m in range(batches):
        ret_low_ref[m] = dext_ref[m, :BLOCK].astype(BF16)
        dkv_ref[m] = dext_ref[m, BLOCK : BLOCK + per]
        ret_high_ref[m] = dext_ref[m, BLOCK + per :].astype(BF16)
        dlead0_ref[m] = dlead_ref[m, :BLOCK]
        dlead1_ref[m] = dlead_ref[m, BLOCK:]


def lead_bwd_kernel(
    meta_ref, lead0_ref, lead1_ref, kv_ref, bias_ref, sparse_ref, dlead0_ref, dlead1_ref, do0_ref, do1_ref,
    dkv_ref, mine_ref, given_ref,
):
    low = meta_ref[3]
    for m in range(kv_ref.shape[0]):
        grads = jnp.concatenate([do0_ref[m], do1_ref[m]], 0)
        lse, delta = row_stats(grads[:, 2 * HD :])
        queries = jnp.concatenate([lead0_ref[m, :, : 4 * HD], lead1_ref[m, :, : 4 * HD]], 0)
        queries, grads = stack(queries, Q_LANES), stack(grads, O_LANES)
        keys, values = kv_ref[m, :, K_PART], kv_ref[m, :, V_PART]
        prob = jnp.exp(dot_nt(queries, keys) + bias_ref[m] - jnp.concatenate(lse, 0))
        ds = (prob * (dot_nt(grads, values) - jnp.concatenate(delta, 0))).astype(BF16)
        dq = unstack(dot_nn(ds, keys), Q_LANES)
        for part_ref, first in ((mine_ref, low == 1), (given_ref, low == 0)):
            part_ref[m, :, : 4 * HD] = jnp.where(first, dq[:BLOCK], dq[BLOCK:]).astype(BF16)
            part_ref[m, :, 4 * HD :] = jnp.where(first, dlead0_ref[m], dlead1_ref[m]).astype(BF16)
        dkv_ref[m] = sparse_ref[m] + kv_grad(dot_tn(prob.astype(BF16), grads), dot_tn(ds, queries))


def split_rows(meta_ref, grad_ref, keep_ref, send_ref, lanes=slice(None)):
    count, rows, _ = keep_ref.shape
    even = (meta_ref[4] & 1) == 0
    for z in range(count):
        one = grad_ref[2 * z * rows : (2 * z + 1) * rows, lanes].astype(BF16)
        two = grad_ref[(2 * z + 1) * rows : (2 * z + 2) * rows, lanes].astype(BF16)
        keep_ref[z] = jnp.where(even, one, two)
        send_ref[z] = jnp.where(even, two, one)


def ffn_grad_kernel(groups, seqs, per, share, meta_ref, og_ref, *refs):
    count = 4 * groups
    ups, acts, pres = (refs[n * count : (n + 1) * count] for n in range(3))
    keep0_ref, send0_ref, keep1_ref, send1_ref, left_ref, right_ref, grad_ref = refs[3 * count :]
    piece = seqs * share
    hidden = ups[0].shape[1]
    for g in range(groups):
        for k in range(4):
            for m in range(seqs):
                row = (g * seqs + m) * per + (meta_ref[0] ^ SWAP[k]) * share
                rows = pl.ds(pl.multiple_of(row, share), share)
                right_ref[rows] = ups[4 * g + k][m * share : (m + 1) * share]
    grad_ref[:, :hidden] = dot_tn(og_ref[...], right_ref[...])
    for n in range(count):
        left_ref[n * piece : (n + 1) * piece] = acts[n][...]
        right_ref[n * piece : (n + 1) * piece] = pres[n][...]
    grad_ref[:, hidden:] = dot_tn(left_ref[...], right_ref[...])
    split_rows(meta_ref, grad_ref, keep0_ref, send0_ref, slice(0, hidden))
    split_rows(meta_ref, grad_ref, keep1_ref, send1_ref, slice(hidden, 2 * hidden))


def fold_kernel(count, meta_ref, *refs):
    pairs, out_refs = refs[: 2 * count], refs[2 * count :]
    z = meta_ref[4] >> 1
    for n, ref in enumerate(out_refs):
        at = 0
        for keep_ref, got_ref in zip(pairs[::2], pairs[1::2]):
            lanes = keep_ref.shape[2]
            total = keep_ref[z ^ n].astype(F32) + got_ref[z ^ n].astype(F32)
            ref[:, at : at + lanes] = total.astype(ref.dtype)
            at += lanes


def slots_kernel(
    index_ref, valid_ref, q_got_ref, do_got_ref, kv_ref, column_ref, dkv_ref, acc_ref
):
    acc_ref[...] = dkv_ref[...]

    def block_grads(c):
        at = index_ref[c]
        live = valid_ref[c] == 1
        kv = kv_ref[at]
        grads = do_got_ref[c]
        stats = jnp.transpose(grads[:, 2 * HD :].astype(F32))
        lse = [stats[h : h + 1] + stats[3 + h : 4 + h] for h in range(3)]
        delta = [stats[6 + h : 7 + h] + stats[9 + h : 10 + h] for h in range(3)]
        queries, grads = stack(q_got_ref[c], Q_LANES), stack(grads, O_LANES)
        bias = column_ref[at][:, : 3 * BLOCK]
        prob = jnp.exp(dot_nt(kv[:, K_PART], queries) + bias - jnp.concatenate(lse, 1))
        prob = jnp.where(live, prob, 0.0)
        ds = prob * (dot_nt(kv[:, V_PART], grads) - jnp.concatenate(delta, 1))
        return at, kv_grad(dot_nn(prob.astype(BF16), grads), dot_nn(ds.astype(BF16), queries))

    slots = q_got_ref.shape[0]
    wide = 4 if slots % 4 == 0 else 1

    def slot(j, _):
        done = [block_grads(wide * j + n) for n in range(wide)]
        for at, grad in done:
            acc_ref[at] += grad
        return 0

    lax.fori_loop(0, slots // wide, slot, 0)


def tail_kernel(
    groups, seqs, per, share, devices, meta_ref, dq_ref, dkv_ref, ret_low_ref, ret_high_ref, first_ref, first0_ref,
    first1_ref, mine_ref, given_ref, *refs,
):
    pieces, mixed_refs = refs[: 4 * groups], refs[4 * groups : 5 * groups]
    w_ref, gain_ref, shift_ref = refs[5 * groups : 5 * groups + 3]
    count = 4
    sums_refs = refs[5 * groups + 3 : 6 * groups + 3]
    ends_refs, back_refs = refs[6 * groups + 3 : -count - 5], refs[-count - 5 : -5]
    keep_ref, send_ref, gqkv_ref, grad_ref, left_ref = refs[-5:]
    blocks = per // BLOCK
    batches = dkv_ref.shape[0] // blocks
    gqkv_ref[:, : 4 * HD] = dq_ref[...].reshape(-1, 4 * HD).astype(BF16)
    gqkv_ref[:, 4 * HD :] = dkv_ref[...].reshape(-1, 6 * HD).astype(BF16)
    for m in range(batches):
        i = m * blocks
        low, high = ret_low_ref[m].astype(F32), ret_high_ref[m].astype(F32)
        if blocks == 1:
            gqkv_ref[i * BLOCK : (i + 1) * BLOCK, 4 * HD :] = (dkv_ref[i] + low + high).astype(BF16)
        else:
            j = i + blocks - 1
            gqkv_ref[i * BLOCK : (i + 1) * BLOCK, 4 * HD :] = (dkv_ref[i] + low).astype(BF16)
            gqkv_ref[j * BLOCK : (j + 1) * BLOCK, 4 * HD :] = (dkv_ref[j] + high).astype(BF16)
    lead = meta_ref[3] == 1
    rows = batches * BLOCK
    mine, given = mine_ref[...].reshape(rows, 10 * HD), given_ref[...].reshape(rows, 10 * HD)
    ends = jnp.concatenate([jnp.where(lead, mine, given), jnp.where(lead, given, mine)], 0)
    firsts = jnp.concatenate([first0_ref[...], first1_ref[...]], 0)
    grad = dot_tn(first_ref[...], gqkv_ref[...]) + dot_tn(firsts, ends)
    grad_ref[:, : 10 * HD] = grad
    columns = jnp.sum(gqkv_ref[...].astype(F32), 0, keepdims=True)
    columns = columns + jnp.sum(ends.astype(F32), 0, keepdims=True)
    weights = w_ref[...].astype(F32)
    along = jnp.sum(grad * weights, -1, keepdims=True)
    shift_sum = jnp.sum(columns * weights, -1, keepdims=True)
    rows_in = [gain_ref[...][None], shift_ref[...][None]]
    rows_in += [sum(ref[n : n + 1] for ref in sums_refs) for n in range(2)]
    rows_in.append(jnp.zeros((4, grad.shape[0]), F32))
    gain, shift, gain2_sum, shift2_sum = (
        jnp.transpose(jnp.concatenate(rows_in, 0))[:, n : n + 1] for n in range(4)
    )
    stats = lanes_of([(along - shift * shift_sum) / gain, shift_sum, gain2_sum, shift2_sum], grad.shape[0])
    lane = lax.broadcasted_iota(jnp.int32, stats.shape, 1)
    moved = jnp.concatenate([stats[:, HD:], stats[:, :HD]], 1)
    grad_ref[:, : 2 * HD] = jnp.where(lane < HD, grad[:, : 2 * HD], moved)
    piece = pieces[0].shape[0]
    total = 0.0
    for g in range(groups):
        for k in range(4):
            left_ref[k * piece : (k + 1) * piece] = pieces[4 * g + k][...]
        total = total + dot_tn(left_ref[...], mixed_refs[g][...])
    grad_ref[:, 10 * HD :] = total
    split_rows(meta_ref, grad_ref, keep_ref, send_ref)
    for end, b in ((1, 0), (2, blocks - 1)):

        @pl.when(meta_ref[end] == 1)
        def _(b=b):
            for m in range(groups * seqs):
                rows = slice(m * per + b * BLOCK, m * per + (b + 1) * BLOCK)
                total = gqkv_ref[rows].astype(F32)
                for ref in ends_refs:
                    total = total + ref[m].astype(F32)
                gqkv_ref[rows] = total.astype(BF16)

    for g in range(groups):
        for k in range(4):
            for m in range(seqs):
                row = (g * seqs + m) * per + (meta_ref[0] ^ SWAP[k]) * share
                rows = pl.ds(pl.multiple_of(row, share), share)
                back = dot_nt(gqkv_ref[rows], w_ref[...]).astype(BF16)
                back_refs[k][(g * seqs + m) * share : (g * seqs + m + 1) * share] = back


def swap_tp(value, bit):
    return lax.ppermute(value, "tp", [(i, i ^ bit) for i in range(lax.axis_size("tp"))])


def scatter_tp(parts):
    far = swap_tp(parts[3], 1)
    near = swap_tp(parts[2], 1)
    both = (parts[1].astype(F32) + far.astype(F32)).astype(BF16)
    return parts[0], near, swap_tp(both, 2)


def gather_tp(piece, before_first=(), before_last=()):
    cross = swap_tp(after(piece, *before_first) if before_first else piece, 2)
    return piece, cross, swap_tp(piece, 1), swap_tp(after(cross, *before_last) if before_last else cross, 1)


def mirrored(pairs, last):
    return pairs + [(last - a, last - b) for a, b in pairs]


SECOND = [(1, 3), (4, 5), (2, 6), (0, 7)]


def in_first_group(myself, devices):
    if devices == 8:
        return (myself == 0) | (myself == 1) | (myself == 2) | (myself == 4)
    return myself < devices // 2


def spread(own, myself, devices, *before_last):
    last = devices - 1
    held = own
    if devices == 8:
        for k in (1, 2, 4):
            held = held + lax.ppermute(own, "seq", mirrored([(0, k)], last))
        held = after(held, *before_last)
        other = lax.ppermute(held, "seq", mirrored(SECOND, last))
    else:
        bit = 1
        while bit < devices // 2:
            held = held + lax.ppermute(held, "seq", mirrored([(i, i + bit) for i in range(bit)], last))
            bit *= 2
        other = lax.ppermute(held, "seq", [(i, i ^ bit) for i in range(devices)])
    first = in_first_group(myself, devices)
    return jnp.where(first, held, other), jnp.where(first, other, held), other


def collect_first(given, devices):
    last = devices - 1
    if devices == 8:
        return lax.ppermute(given, "seq", mirrored([(b, a) for a, b in SECOND], last))
    return lax.ppermute(given, "seq", [(i, i ^ (devices // 2)) for i in range(devices)])


def collect_rest(mine, devices, join):
    last = devices - 1
    if devices == 8:
        return [mine] + [lax.ppermute(mine, "seq", mirrored([(k, 0)], last)) for k in (1, 2, 4)]
    bit = devices // 2
    while bit > 1:
        bit //= 2
        mine = join(mine, lax.ppermute(mine, "seq", mirrored([(i + bit, i) for i in range(bit)], last)))
    return [mine]


def to_owners(slots):
    return lax.all_to_all(slots, "seq", split_axis=0, concat_axis=0, tiled=True)


def sum_seq_first(send, devices):
    return lax.ppermute(send, "seq", [(i, i ^ 1) for i in range(devices)])


def sum_seq_rest(pairs, meta, devices):
    count, rows = pairs[0][0].shape[:2]
    lanes = sum(keep.shape[2] for keep, _ in pairs)
    if count == 4:
        low = sds((rows, lanes), BF16)
        own, *out = call(
            partial(fold_kernel, len(pairs)), (sds((rows, lanes), F32), low, low, low), name="fold"
        )(*(v for pair in pairs for v in pair), smem=(meta,))
        return [own] + [
            lax.ppermute(piece, "seq", [(i, i ^ (2 * (n + 1))) for i in range(devices)])
            for n, piece in enumerate(out)
        ]
    total = [(keep.astype(F32) + got.astype(F32)).astype(BF16) for keep, got in pairs]
    return across(jnp.concatenate(total, 2), devices)


def across(total, devices):
    sides = [[i for i in range(devices) if i % 2 == side] for side in range(2)]
    got = lax.all_to_all(
        total, "seq", split_axis=0, concat_axis=0, tiled=True, axis_index_groups=sides
    )
    return [got[n] for n in range(total.shape[0])]


def sum_of(terms):
    total = terms[0].astype(F32)
    for term in terms[1:]:
        total = total + term.astype(F32)
    return total


def per_device(
    layer_input,
    out_grad,
    norm1_gain,
    norm1_shift,
    w_qkv,
    w_out,
    norm2_gain,
    norm2_shift,
    w_up,
    w_down,
    key_keep,
    rand_blocks,
):
    batches, per, width = layer_input.shape
    local = w_qkv.shape[2]
    devices = lax.axis_size("seq")
    myself = lax.axis_index("seq")
    tp_count = lax.axis_size("tp")
    tp_place = lax.axis_index("tp")
    assert local == 3 * HD and tp_count == 4 and devices % 2 == 0 and batches % 2 == 0
    share = per // tp_count
    bd = per // BLOCK
    total = batches * bd
    blocks_all = bd * devices
    groups = 2
    seqs = batches // groups
    piece = seqs * share
    refs = total * RANDS
    slots_per = max(1, -(-refs // devices))
    slots = devices * slots_per
    hidden_here = w_up.shape[1]
    rows = width // devices
    i32 = jnp.int32
    flag = lambda v: v.astype(i32)
    meta = jnp.stack(
        [
            tp_place, flag(myself == 0), flag(myself == devices - 1), flag(in_first_group(myself, devices)), myself,
        ]
    ).astype(i32)

    CHAIN.last = ()
    scale = 1.0 / math.sqrt(HD)
    x_rows = layer_input.reshape(batches * per, width)
    first, q, kv, w640 = CHAIN.done(project(x_rows, norm1_gain, norm1_shift, w_qkv.transpose(1, 0, 2)))
    is_first, is_last = myself == 0, myself == devices - 1
    ends = jnp.where(is_first, layer_input[:, :BLOCK], layer_input[:, per - BLOCK :])
    ends = jnp.where(is_first | is_last, ends, jnp.zeros_like(ends))
    lead_x0, lead_x1, arrived = spread(ends, myself, devices, kv)
    q_blocks = q.reshape(total, BLOCK, 4 * HD)
    kv_blocks = kv.reshape(total, BLOCK, 6 * HD)
    kv_seqs = kv.reshape(batches, per, 6 * HD)

    table = (
        rand_blocks.reshape(batches, devices, bd, RANDS).transpose(1, 0, 2, 3).reshape(devices, refs)
    )
    owners = table // bd
    source = (jnp.arange(refs, dtype=i32) // (bd * RANDS))[None] * bd + table - owners * bd
    order = jnp.arange(refs, dtype=i32)
    earlier = order[None, :] < order[:, None]
    rank = jnp.sum(((owners[:, :, None] == owners[:, None, :]) & earlier[None]).astype(i32), -1)
    places = jnp.arange(slots_per, dtype=i32)
    asked = (owners == myself)[:, None, :] & (rank[:, None, :] == places[None, :, None])
    source_of = jnp.sum(jnp.where(asked, source[:, None, :], 0), -1).reshape(slots)
    valid = jnp.sum(asked.astype(i32), -1).reshape(slots)
    my_owner = lax.dynamic_index_in_dim(owners, myself, 0, False)
    my_rank = lax.dynamic_index_in_dim(rank, myself, 0, False)
    slot_of = my_owner * slots_per + my_rank
    mine = lax.dynamic_index_in_dim(table, myself, 0, False)
    query_of = jnp.sum(
        jnp.where(
            slot_of[None, :] == jnp.arange(slots, dtype=i32)[:, None], (order // RANDS)[None, :], 0
        ),
        -1,
    )

    end_kv = sds((batches, BLOCK, 6 * HD), BF16)
    end_all = sds((batches, BLOCK, 10 * HD), BF16)
    sent, kv_low, kv_high = call(
        partial(dispatch_kernel, bd),
        (sds((slots, BLOCK, 6 * HD), BF16), end_kv, end_kv),
        name="dispatch",
    )(kv_blocks, smem=(source_of,))
    rand_kv = to_owners(after(sent, arrived))
    up = [(i, i + 1) for i in range(devices - 1)]
    down = [(b, a) for a, b in up]
    low = lax.ppermute(kv_high, "seq", up)
    high = lax.ppermute(kv_low, "seq", down)

    bias, seq_bias, column_bias, wo256 = call(
        partial(bias_kernel, bd, blocks_all),
        (
            sds((total, 1, 8 * BLOCK), F32),
            sds((batches, 1, per), F32),
            sds((total, BLOCK, 4 * HD), F32),
            sds((width, 4 * HD), BF16),
        ),
        name="bias",
    )(key_keep.reshape(batches * blocks_all, BLOCK), w_out, smem=(mine, meta))

    grad_up = dot_nn(out_grad.reshape(batches * per, width), w_down)
    grad_up = grad_up.reshape(batches, per, hidden_here)

    part = sds((batches, BLOCK, 4 * HD), F32)
    low_piece = sds((piece, width), BF16)
    low_pieces = sds((groups * piece, width), BF16)
    high_piece = sds((piece, width), F32)
    attn, lse = [], []

    def attend(g):
        half_of = lambda array: part_of(array, g, groups)
        out, stat = call(
            partial(sparse_fwd_kernel, g * seqs * bd, seqs, per, share),
            (sds((4 * piece, 4 * HD), BF16), sds((seqs * per, 2 * HD), F32)),
            (
                pltpu.VMEM((seqs, per + 2 * BLOCK, 6 * HD), BF16),
                pltpu.VMEM((2, 8 * BLOCK, 6 * HD), BF16),
            ),
            name="sparse_fwd",
        )(
            half_of(q_blocks), half_of(kv_seqs), half_of(low), half_of(high), half_of(lead0), half_of(lead1),
            rand_kv, half_of(bias), smem=(slot_of, meta),
        )
        attn.append(out)
        lse.append(stat)

    lead_rows = sds((batches * BLOCK, width), BF16)
    lead_first0, lead_first1, lead0, lead1, part_mine, part_given = call(
        lead_fwd_kernel, (lead_rows, lead_rows, end_all, end_all, part, part), name="lead_fwd"
    )(kv_seqs, after(seq_bias, grad_up), lead_x0, lead_x1, norm1_gain, norm1_shift, w640, smem=(meta,))
    part_got = collect_first(part_given, devices)
    q_slots = call(gather_kernel, sds((slots, BLOCK, 4 * HD), BF16), name="gather")(q_blocks, smem=(query_of,))
    rand_q = to_owners(after(q_slots, rand_kv, part_got, low, high))
    attend(0)
    lead_parts = collect_rest(merge(part_mine, part_got), devices, merge)
    attend(1)
    lead_out, lead_lse = call(
        lead_finish_kernel,
        (sds(part.shape, BF16), sds((batches, BLOCK, 2 * HD), F32)),
        name="lead_finish",
        limit=SMALL,
    )(*lead_parts)
    out = call(
        partial(out_project_kernel, groups, seqs, per, share),
        (sds((4 * piece, 4 * HD), BF16),) * groups + (low_piece,) * (4 * groups),
        name="out_project",
        limit=SMALL,
    )(wo256, lead_out, *attn, smem=(meta,))
    mixed = out[:groups]
    attn_parts = [scatter_tp(out[groups + 4 * g : groups + 4 * g + 4]) for g in range(groups)]

    flat = lambda lists: [v for group in lists for v in group]
    hidden, act, total_grad, sums2, attn_grad = [], [], [], [], []
    ups, pres, back_parts, down_parts = [], [], [], []
    for g in range(groups):
        h, a = share_call(mid_fwd_kernel, (high_piece, low_piece), [(layer_input, g, 0)], "mid_fwd")(
            meta, seqs, share, *attn_parts[g], norm2_gain, norm2_shift
        )
        hidden.append(h)
        act.append(gather_tp(a, attn_parts[-1][2:]))
    low_hidden = sds((piece, hidden_here), BF16)
    for g in range(groups):
        out = share_call(
            ffn_kernel, (low_hidden, low_hidden, low_piece) * 4, [(grad_up, g, k) for k in range(4)], "ffn", MIDDLE
        )(meta, seqs, share, *act[g], w_up)
        ups.append(out[0::3])
        pres.append(out[1::3])
        back_parts.append(scatter_tp(out[2::3]))
    for g in range(groups):
        t, a, s = share_call(
            mid_bwd_kernel, (high_piece, low_piece, sds((2, width), F32)), [(out_grad, g, 0)], "mid_bwd"
        )(meta, seqs, share, *back_parts[g], hidden[g], norm2_gain)
        total_grad.append(t)
        sums2.append(s)
        if g == 0:
            down_parts = call(partial(down_kernel, groups), (low_pieces,) * 4, name="down", limit=MIDDLE)(*flat(ups), w_down)
            attn_grad.append(gather_tp(a))
        if g == groups - 1:
            halves = sds((devices // 2, rows, hidden_here), BF16)
            ff_keep0, ff_send0, ff_keep1, ff_send1 = call(
                partial(ffn_grad_kernel, groups, seqs, per, share),
                (halves,) * 4,
                (
                    pltpu.VMEM((batches * per, width), BF16),
                    pltpu.VMEM((batches * per, hidden_here), BF16),
                    pltpu.VMEM((width, 2 * hidden_here), F32),
                ),
                name="ffn_grad",
                limit=MIDDLE,
            )(
                out_grad.reshape(batches * per, width), *flat(ups), *flat(act), *flat(pres), smem=(meta,)
            )
            attn_grad.append(gather_tp(a, (), (ff_send0,)))
            ff_got0 = sum_seq_first(after(ff_send0, attn_grad[-1][1]), devices)

    lead_grad = call(
        partial(lead_grad_kernel, groups, seqs, per, share),
        sds((batches, BLOCK, 4 * HD), BF16),
        (pltpu.VMEM((batches * BLOCK, width), BF16),),
        name="lead_grad",
        limit=SMALL,
    )(wo256, lead_lse, lead_out, *flat(attn_grad), smem=(meta,))
    grads, sent = call(
        partial(heads_grad_kernel, groups, seqs, per, share),
        (sds((batches * per, 4 * HD), BF16), sds((slots, BLOCK, 4 * HD), BF16)),
        name="heads_grad",
        limit=MIDDLE,
    )(wo256, *flat(attn_grad), *mixed, *lse, smem=(query_of, meta))
    *lead_do, arrived = spread(lead_grad, myself, devices, sent)
    rand_do = to_owners(after(sent, arrived, rand_q, ff_got0))
    ff_got1 = sum_seq_first(after(ff_send1, arrived), devices)
    dend = sds(end_kv.shape, F32)
    dq, dkv, ret_low, ret_high, dlead0, dlead1 = call(
        partial(sparse_bwd_kernel, batches, per),
        (sds((total, BLOCK, 4 * HD), F32), sds((batches, per, 6 * HD), F32), end_kv, end_kv, dend, dend),
        (
            pltpu.VMEM((batches, per + 2 * BLOCK, 6 * HD), BF16),
            pltpu.VMEM((2, 8 * BLOCK, 6 * HD), BF16),
            pltpu.VMEM((batches, per + 2 * BLOCK, 6 * HD), F32),
            pltpu.VMEM((batches, 2 * BLOCK, 6 * HD), F32),
        ),
        name="sparse_bwd",
    )(
        q_blocks, kv_seqs, low, high, lead0, lead1, rand_kv, bias,
        after(grads, *lead_do).reshape(total, BLOCK, 4 * HD), smem=(slot_of,),
    )
    from_low = lax.ppermute(ret_high, "seq", up)
    from_high = lax.ppermute(ret_low, "seq", down)
    dkv, ends_mine, ends_given = call(
        lead_bwd_kernel, (sds((batches, per, 6 * HD), F32), end_all, end_all), name="lead_bwd"
    )(lead0, lead1, kv_seqs, seq_bias, dkv, dlead0, dlead1, *lead_do, smem=(meta,))
    add = lambda a, b: (a.astype(F32) + b.astype(F32)).astype(BF16)
    ends_first = collect_first(ends_given, devices)
    ends_got = collect_rest(add(after(ends_mine, from_low, from_high), ends_first), devices, add)

    dkv = call(slots_kernel, sds((total, BLOCK, 6 * HD), F32), name="slots")(
        rand_q, rand_do, kv_blocks, column_bias,
        dkv.reshape(total, BLOCK, 6 * HD), smem=(source_of, valid),
    )
    ff_half = jnp.concatenate(
        [
            (keep.astype(F32) + got.astype(F32)).astype(BF16)
            for keep, got in ((ff_keep0, ff_got0), (after(ff_keep1, dkv), after(ff_got1, dkv)))
        ],
        2,
    )
    ff = across(after(ff_half, *ends_got), devices)
    halves = sds((devices // 2, rows, 14 * HD), BF16)
    *first_back, qkv_keep, qkv_send = call(
        partial(tail_kernel, groups, seqs, per, share, devices),
        (low_pieces,) * 4 + (halves, halves),
        (
            pltpu.VMEM((total * BLOCK, 10 * HD), BF16),
            pltpu.VMEM((width, 14 * HD), F32),
            pltpu.VMEM((4 * piece, width), BF16),
        ),
        name="tail",
    )(
        dq, dkv, from_low, from_high, first, lead_first0, lead_first1, ends_mine, ends_given,
        *flat(attn_grad), *mixed, w640, norm1_gain, norm1_shift, *sums2, *ends_got, smem=(meta,),
    )
    qkv_got = sum_seq_first(qkv_send, devices)
    terms = scatter_tp(first_back)
    out_terms = scatter_tp([after(part, first_back[0]) for part in down_parts])
    ff = sum_of(ff)
    gq = sum_seq_rest([(qkv_keep, after(qkv_got, ff))], meta, devices)
    input_grad = share_call(
        partial(end_kernel, groups),
        sds((batches, share, width), F32),
        [(layer_input, g, 0) for g in range(groups)],
        "end",
    )(meta, seqs, share, *terms, *total_grad, norm1_gain)
    layer_output = call(
        partial(output_kernel, groups), sds((batches, share, width), F32), name="output", limit=SMALL
    )(*out_terms, *hidden)

    g_down, g_up = ff[:, :hidden_here], ff[:, hidden_here:]
    gq = sum_of(gq)
    norms = gq[:, HD : 2 * HD]
    norms = norms + swap_tp(norms, 1)
    norms = norms + swap_tp(norms, 2)
    g_out = jnp.concatenate([gq[:, 10 * HD : 12 * HD], gq[:, 13 * HD :]], 1)
    g_qkv = jnp.stack(
        [
            jnp.concatenate([gq[:, 2 * HD : 4 * HD], gq[:, :HD]], 1) * scale,
            jnp.concatenate([gq[:, 8 * HD : 10 * HD], gq[:, 6 * HD : 7 * HD]], 1),
            jnp.concatenate([gq[:, 4 * HD : 6 * HD], gq[:, 7 * HD : 8 * HD]], 1),
        ],
        1,
    )
    return (
        layer_output, input_grad, g_qkv, g_out, g_up, g_down, norms[:, 0], norms[:, 1], norms[:, 2], norms[:, 3],
    )


def solution(mesh):
    return jax.shard_map(
        per_device,
        mesh=mesh,
        in_specs=(
            P(None, "seq", None),
            P(None, "seq", None),
            P(),
            P(),
            P(None, None, "tp"),
            P(None, "tp"),
            P(),
            P(),
            P(None, "tp"),
            P(None, "tp"),
            P(),
            P(),
        ),
        out_specs=(
            P(None, ("seq", "tp"), None),
            P(None, ("seq", "tp"), None),
            P("seq", None, "tp"),
            P("seq", "tp"),
            P("seq", "tp"),
            P("seq", "tp"),
            P("seq"),
            P("seq"),
            P("seq"),
            P("seq"),
        ),
        check_vma=False,
    )
```

```python
from functools import partial
import math

import jax
import jax.numpy as jnp
from jax import lax
from jax.experimental import pallas as pl
from jax.experimental.pallas import tpu as pltpu
from jax.sharding import PartitionSpec as P

HD = 64
BLOCK = 64
RANDS = 3
EPS = 1e-06
SWAP = (0, 2, 1, 3)
NEG = -1e30
Q_LANES = (128, 192, 0)
O_LANES = (0, 64, 192)
K_PART = slice(128, 384)
V_PART = slice(0, 256)
F32 = jnp.float32
BF16 = jnp.bfloat16
VMEM = pl.BlockSpec(memory_space=pltpu.VMEM)
SMEM = pl.BlockSpec(memory_space=pltpu.SMEM)
MIB = 1024 * 1024


def sds(shape, kind):
    return jax.ShapeDtypeStruct(shape, kind)


PARAMS = pltpu.CompilerParams(vmem_limit_bytes=56 * MIB)
SMALL = pltpu.CompilerParams(vmem_limit_bytes=12 * MIB)
MIDDLE = pltpu.CompilerParams(vmem_limit_bytes=24 * MIB)


def after(value, *others):
    return lax.optimization_barrier((value,) + others)[0]


class Chain:
    last = ()

    def link(self, value):
        return after(value, *self.last) if self.last else value

    def done(self, outs):
        self.last = (jax.tree.leaves(outs)[0],)
        return outs


CHAIN = Chain()


def part_of(array, at, count):
    return array, at, count


TIMES = {
    "project": 6, "dispatch": 3, "bias": 2, "lead_fwd": 4, "sparse_fwd": 7, "merge": 1, "lead_finish": 1, "out_project": 1,
    "mid_fwd": 1, "gather": 2, "ffn": 6, "ffn_grad": 7, "mid_bwd": 1, "heads_grad": 5, "lead_grad": 1, "sparse_bwd": 13,
    "fold_near": 3, "down": 6, "lead_bwd": 5, "slots": 14, "tail": 5, "fold_far": 2, "back": 7, "output": 1,
    "fold": 2, "end": 2,
}
HINT = 1.75e6


def cost(name):
    return pl.CostEstimate(flops=0, transcendentals=0, bytes_accessed=int(TIMES[name] * HINT))


def call(body, outs, scratch=(), name=None, limit=PARAMS):
    def run(*args, smem=()):
        specs = [SMEM] * len(smem)
        arrays = []
        if smem:
            smem = (CHAIN.link(smem[0]),) + tuple(smem[1:])
        else:
            args = (CHAIN.link(args[0]),) + args[1:]
        for arg in args:
            if isinstance(arg, tuple):
                array, at, count = arg
                shape = (array.shape[0] // count,) + array.shape[1:]
                index = (at,) + (0,) * (array.ndim - 1)
                specs.append(pl.BlockSpec(shape, lambda i, index=index: index))
                arrays.append(array)
            else:
                specs.append(VMEM)
                arrays.append(arg)
        return CHAIN.done(
            pl.pallas_call(
                body,
                out_shape=outs,
                grid=(1,),
                in_specs=specs,
                out_specs=jax.tree.map(lambda _: VMEM, outs),
                scratch_shapes=list(scratch),
                compiler_params=limit,
                cost_estimate=cost(name),
                name=name,
            )(*smem, *arrays)
        )

    return run


def share_call(body, outs, blocks, name, limit=SMALL):
    def run(meta, seqs, share, *args):
        def spec(value, group, pos):
            return pl.BlockSpec(
                (seqs, share, value.shape[2]), lambda i, meta_ref: (group, meta_ref[0] ^ SWAP[pos], 0)
            )

        return CHAIN.done(
            pl.pallas_call(
                body,
                out_shape=outs,
                grid_spec=pltpu.PrefetchScalarGridSpec(
                    num_scalar_prefetch=1,
                    grid=(1,),
                    in_specs=[spec(*b) for b in blocks] + [VMEM] * len(args),
                    out_specs=jax.tree.map(lambda _: VMEM, outs),
                ),
                compiler_params=limit,
                cost_estimate=cost(name),
                name=name,
            )(CHAIN.link(meta), *(b[0] for b in blocks), *args)
        )

    return run


def dot_nt(a, b):
    return lax.dot_general(a, b, (((1,), (1,)), ((), ())), preferred_element_type=F32)


def dot_tn(a, b):
    return lax.dot_general(a, b, (((0,), (0,)), ((), ())), preferred_element_type=F32)


def dot_nn(a, b):
    return lax.dot_general(a, b, (((1,), (0,)), ((), ())), preferred_element_type=F32)


def stack(rows, lanes):
    lane = lax.broadcasted_iota(jnp.int32, rows.shape, 1)
    zero = jnp.zeros_like(rows)
    return jnp.concatenate([jnp.where((lane >= at) & (lane < at + HD), rows, zero) for at in lanes], 0)


def unstack(stacked, lanes):
    rows = stacked.shape[0] // 3
    lane = lax.broadcasted_iota(jnp.int32, (rows, stacked.shape[1]), 1)
    out = jnp.zeros((rows, stacked.shape[1]), stacked.dtype)
    for h, at in enumerate(lanes):
        out = jnp.where((lane >= at) & (lane < at + HD), stacked[h * rows : (h + 1) * rows], out)
    return out


def thirds(column):
    rows = column.shape[0] // 3
    return [column[h * rows : (h + 1) * rows] for h in range(3)]


def half(tile, upper):
    lane = lax.broadcasted_iota(jnp.int32, tile.shape, 1)
    return jnp.where((lane >= HD) if upper else (lane < HD), tile, jnp.zeros_like(tile))


def lanes_of(columns, rows):
    lane = lax.broadcasted_iota(jnp.int32, (rows, 2 * HD), 1)
    out = jnp.zeros((rows, 2 * HD), F32)
    for at, column in enumerate(columns):
        out = jnp.where(lane == at, column, out)
    return out


def hi_lo(value):
    hi = value.astype(BF16).astype(F32)
    return hi, value - hi


def norm_rows(hidden):
    center = hidden - jnp.mean(hidden, -1, keepdims=True)
    inverse = lax.rsqrt(jnp.mean(center * center, -1, keepdims=True) + EPS)
    return center * inverse, inverse


def norm_rows_back(grad, normed, inverse, gain):
    scaled = grad * gain
    return inverse * (
        scaled
        - jnp.mean(scaled, -1, keepdims=True)
        - normed * jnp.mean(scaled * normed, -1, keepdims=True)
    )


def project_kernel(x_ref, gain_ref, shift_ref, raw_ref, first_ref, q_ref, kv_ref, w_ref):
    @pl.when(pl.program_id(0) == 0)
    def _():
        scale = jnp.asarray(1.0 / math.sqrt(HD), BF16)
        blank = jnp.zeros((w_ref.shape[0], HD), BF16)
        w_ref[:, : 2 * HD] = jnp.concatenate([raw_ref[0, :, 2 * HD :] * scale, blank], 1)
        w_ref[:, 2 * HD : 4 * HD] = raw_ref[0, :, : 2 * HD] * scale
        w_ref[:, 4 * HD : 6 * HD] = raw_ref[2, :, : 2 * HD]
        w_ref[:, 6 * HD : 8 * HD] = jnp.concatenate([raw_ref[1, :, 2 * HD :], raw_ref[2, :, 2 * HD :]], 1)
        w_ref[:, 8 * HD :] = raw_ref[1, :, : 2 * HD]

    normed, _ = norm_rows(x_ref[...].astype(F32))
    first = (normed * gain_ref[...][None] + shift_ref[...][None]).astype(BF16)
    first_ref[...] = first
    out = dot_nn(first, w_ref[...]).astype(BF16)
    q_ref[...] = out[:, : 4 * HD]
    kv_ref[...] = out[:, 4 * HD :]


def project(x, gain, shift, raw):
    rows, width = x.shape
    tile = min(rows, 256)
    row = lambda w: pl.BlockSpec((tile, w), lambda i: (i, 0))
    vector = pl.BlockSpec((width,), lambda i: (0,))
    whole = lambda w: pl.BlockSpec((width, w), lambda i: (0, 0))
    low = lambda *shape: sds(shape, BF16)
    return pl.pallas_call(
        project_kernel,
        grid=(rows // tile,),
        out_shape=(low(rows, width), low(rows, 4 * HD), low(rows, 6 * HD), low(width, 10 * HD)),
        in_specs=[
            row(width), vector, vector, pl.BlockSpec(raw.shape, lambda i: (0, 0, 0)),
        ],
        out_specs=(row(width), row(4 * HD), row(6 * HD), whole(10 * HD)),
        compiler_params=PARAMS,
        cost_estimate=cost("project"),
        name="project",
    )(x, gain, shift, raw)


def dispatch_kernel(bd, index_ref, kv_ref, sent_ref, low_ref, high_ref):
    def step(slot, _):
        sent_ref[slot] = kv_ref[index_ref[slot]]
        return 0

    lax.fori_loop(0, sent_ref.shape[0], step, 0, unroll=4)
    for m in range(low_ref.shape[0]):
        low_ref[m] = kv_ref[m * bd]
        high_ref[m] = kv_ref[m * bd + bd - 1]


def bias_kernel(bd, blocks_all, table_ref, meta_ref, keep_ref, raw_ref, bias_ref, seq_ref, column_ref, wo_ref):
    wo_ref[:, : 2 * HD] = raw_ref[:, : 2 * HD]
    blank = jnp.zeros((wo_ref.shape[0], HD), BF16)
    wo_ref[:, 2 * HD :] = jnp.concatenate([blank, raw_ref[:, 2 * HD :]], 1)
    low = lambda keep: jnp.where(keep > 0, 0.0, NEG)
    for m in range(seq_ref.shape[0]):
        for b in range(bd):
            i = m * bd + b
            here = meta_ref[4] * bd + b

            def row(block, inside=True):
                return low(jnp.where(inside, keep_ref[pl.ds(m * blocks_all + block, 1)], 0))

            own = row(here)
            listed = [
                row(jnp.maximum(here - 1, 0), here > 0),
                own,
                row(jnp.minimum(here + 1, blocks_all - 1), here < blocks_all - 1),
                row(0),
                row(blocks_all - 1),
            ] + [row(table_ref[i * RANDS + j]) for j in range(RANDS)]
            bias_ref[i] = jnp.concatenate(listed, 1)
            seq_ref[m, :, b * BLOCK : (b + 1) * BLOCK] = own
            column_ref[i] = jnp.transpose(jnp.broadcast_to(own, (4 * HD, BLOCK)))


def gather_kernel(index_ref, blocks_ref, out_ref):
    def step(slot, _):
        out_ref[slot] = blocks_ref[index_ref[slot]]
        return 0

    lax.fori_loop(0, out_ref.shape[0], step, 0, unroll=4)


def lead_fwd_kernel(
    meta_ref, kv_ref, bias_ref, x0_ref, x1_ref, gain_ref, shift_ref, w_ref, first0_ref, first1_ref,
    lead0_ref, lead1_ref, mine_ref, given_ref,
):
    for x_ref, first_ref, lead_ref in ((x0_ref, first0_ref, lead0_ref), (x1_ref, first1_ref, lead1_ref)):
        normed, _ = norm_rows(x_ref[...].reshape(-1, x_ref.shape[2]).astype(F32))
        first = (normed * gain_ref[...][None] + shift_ref[...][None]).astype(BF16)
        first_ref[...] = first
        lead_ref[...] = dot_nn(first, w_ref[...]).astype(BF16).reshape(lead_ref.shape)
    low = meta_ref[3]
    for m in range(kv_ref.shape[0]):
        queries = jnp.concatenate([lead0_ref[m, :, : 4 * HD], lead1_ref[m, :, : 4 * HD]], 0)
        scores = dot_nt(stack(queries, Q_LANES), kv_ref[m, :, K_PART]) + bias_ref[m]
        top = jnp.max(scores, -1, keepdims=True)
        expo = jnp.exp(scores - top)
        total = jnp.sum(expo, -1, keepdims=True)
        out = unstack(dot_nn(expo.astype(BF16), kv_ref[m, :, V_PART]), O_LANES)
        stats = lanes_of(thirds(top) + thirds(total), 2 * BLOCK)
        for part_ref, first in ((mine_ref, low == 1), (given_ref, low == 0)):
            for lanes, value in ((slice(0, 2 * HD), out[:, : 2 * HD]), (slice(2 * HD, 4 * HD), out[:, 2 * HD :] + stats)):
                part_ref[m, :, lanes] = jnp.where(first, value[:BLOCK], value[BLOCK:])


def merge_parts(parts):
    lane = lax.broadcasted_iota(jnp.int32, (BLOCK, 2 * HD), 1)
    stats = [p[:, 2 * HD :] for p in parts]
    top = stats[0]
    for st in stats[1:]:
        top = jnp.maximum(top, st)
    tops = [top[:, h : h + 1] for h in range(3)]
    sums = [0.0, 0.0, 0.0]
    out0, out1 = 0.0, 0.0
    for p, st in zip(parts, stats):
        scale = [jnp.exp(st[:, h : h + 1] - tops[h]) for h in range(3)]
        sums = [sums[h] + st[:, 3 + h : 4 + h] * scale[h] for h in range(3)]
        out0 = out0 + p[:, : 2 * HD] * jnp.where(lane < HD, scale[0], scale[1])
        out1 = out1 + st * scale[2]
    return out0, jnp.where(lane >= HD, out1, 0.0), tops, sums


def merge_kernel(a_ref, b_ref, out_ref):
    for m in range(a_ref.shape[0]):
        out0, out1, tops, sums = merge_parts([a_ref[m], b_ref[m]])
        out_ref[m, :, : 2 * HD] = out0
        out_ref[m, :, 2 * HD :] = out1 + lanes_of(tops + sums, BLOCK)


def merge(a, b):
    return call(merge_kernel, sds(a.shape, F32), name="merge", limit=SMALL)(a, b)


def lead_finish_kernel(*refs):
    part_refs, (out_ref, lse_ref) = refs[:-2], refs[-2:]
    lane = lax.broadcasted_iota(jnp.int32, (BLOCK, 2 * HD), 1)
    for m in range(out_ref.shape[0]):
        out0, out1, tops, sums = merge_parts([p[m] for p in part_refs])
        out_ref[m, :, : 2 * HD] = (out0 / jnp.where(lane < HD, sums[0], sums[1])).astype(BF16)
        out_ref[m, :, 2 * HD :] = (out1 / sums[2]).astype(BF16)
        lse_ref[m] = lanes_of([tops[h] + jnp.log(sums[h]) for h in range(3)], BLOCK)


def fill_ext(ext_ref, kv_ref, low_ref, high_ref, seqs, per):
    for m in range(seqs):
        ext_ref[m, :BLOCK] = low_ref[m]
        ext_ref[m, BLOCK : BLOCK + per] = kv_ref[m]
        ext_ref[m, BLOCK + per :] = high_ref[m]


def fill_listed(listed_ref, ext_ref, lead0_ref, lead1_ref, rand_ref, slot_ref, m, b, block):
    listed_ref[: 3 * BLOCK] = ext_ref[m, pl.ds(pl.multiple_of(b * BLOCK, BLOCK), 3 * BLOCK)]
    listed_ref[3 * BLOCK : 4 * BLOCK] = lead0_ref[m, :, 4 * HD :]
    listed_ref[4 * BLOCK : 5 * BLOCK] = lead1_ref[m, :, 4 * HD :]
    for j in range(RANDS):
        listed_ref[(5 + j) * BLOCK : (6 + j) * BLOCK] = rand_ref[slot_ref[block * RANDS + j]]


def pos_of(meta_ref, at):
    j = at ^ meta_ref[0]
    return ((j & 1) << 1) | (j >> 1)


def sparse_fwd_kernel(
    first, seqs, per, share, slot_ref, meta_ref, q_ref, kv_ref, low_ref, high_ref, lead0_ref,
    lead1_ref, rand_ref, bias_ref, out_ref, lse_ref, ext_ref, listed_ref,
):
    blocks = per // BLOCK
    chunk = min(share, BLOCK)
    fill_ext(ext_ref, kv_ref, low_ref, high_ref, seqs, per)

    def attend(i, here):
        m, b = i // blocks, i % blocks
        fill_listed(here, ext_ref, lead0_ref, lead1_ref, rand_ref, slot_ref, m, b, first + i)
        scores = dot_nt(stack(q_ref[i], Q_LANES), here[:, K_PART]) + bias_ref[i]
        top = jnp.max(scores, -1, keepdims=True)
        expo = jnp.exp(scores - top)
        total = jnp.sum(expo, -1, keepdims=True)
        prob = (expo * (1.0 / total)).astype(BF16)
        out = unstack(dot_nn(prob, here[:, V_PART]), O_LANES).astype(BF16)
        lse_ref[pl.ds(pl.multiple_of(i * BLOCK, BLOCK), BLOCK)] = lanes_of(
            thirds(top + jnp.log(total)), BLOCK
        )
        for c in range(BLOCK // chunk):
            token = b * BLOCK + c * chunk
            at = token // share
            row = pos_of(meta_ref, at) * (seqs * share) + m * share + (token - at * share)
            rows = pl.ds(pl.multiple_of(row, chunk), chunk)
            out_ref[rows] = out[c * chunk : (c + 1) * chunk]

    def step(j, _):
        attend(2 * j, listed_ref.at[0])
        attend(2 * j + 1, listed_ref.at[1])
        return 0

    lax.fori_loop(0, seqs * blocks // 2, step, 0)


def out_project_kernel(groups, seqs, per, share, meta_ref, wo_ref, lead_out_ref, *refs):
    attn_refs, mixed_refs, part_refs = refs[:groups], refs[groups : 2 * groups], refs[2 * groups :]
    blocks = per // BLOCK
    chunk = min(share, BLOCK)
    piece = seqs * share
    for g in range(groups):
        mixed_refs[g][...] = attn_refs[g][...]
    for end, b in ((1, 0), (2, blocks - 1)):

        @pl.when(meta_ref[end] == 1)
        def _(b=b):
            for g in range(groups):
                for m in range(seqs):
                    for c in range(BLOCK // chunk):
                        token = b * BLOCK + c * chunk
                        at = token // share
                        row = pos_of(meta_ref, at) * piece + m * share + (token - at * share)
                        rows = pl.ds(pl.multiple_of(row, chunk), chunk)
                        mixed_refs[g][rows] = lead_out_ref[g * seqs + m, c * chunk : (c + 1) * chunk]

    wo = wo_ref[...]
    for g in range(groups):
        for k in range(4):
            rows = slice(k * piece, (k + 1) * piece)
            part_refs[4 * g + k][...] = dot_nt(mixed_refs[g][rows], wo).astype(BF16)


def down_kernel(groups, *refs):
    up_refs, w_ref, out_refs = refs[: 4 * groups], refs[4 * groups], refs[4 * groups + 1 :]
    rows = up_refs[0].shape[0]
    for g in range(groups):
        for k in range(4):
            out = dot_nt(up_refs[4 * g + k][...], w_ref[...]).astype(BF16)
            out_refs[k][g * rows : (g + 1) * rows] = out


def total_of(refs):
    return refs[0][...].astype(F32) + refs[1][...].astype(F32) + refs[2][...].astype(F32)


def mid_fwd_kernel(meta_ref, x_ref, own_ref, core_ref, y_ref, gain_ref, shift_ref, hidden_ref, act_ref):
    x = x_ref[...].reshape(hidden_ref.shape).astype(F32)
    hidden = total_of((own_ref, core_ref, y_ref)) + x
    normed, _ = norm_rows(hidden)
    hidden_ref[...] = hidden
    act_ref[...] = (normed * gain_ref[...][None] + shift_ref[...][None]).astype(BF16)


def ffn_kernel(meta_ref, *refs):
    gu_refs, act_refs, w_ref, outs = refs[:4], refs[4:8], refs[8], refs[9:]
    rows = act_refs[0].shape[0]
    for k in (3, 2, 1, 0):
        up_ref, pre_ref, back_ref = outs[3 * k : 3 * k + 3]
        pre = dot_nn(act_refs[k][...], w_ref[...])
        phi = 0.5 + 0.5 * lax.erf(pre * (1.0 / math.sqrt(2.0)))
        density = jnp.exp(-0.5 * pre * pre) * (1.0 / math.sqrt(2.0 * math.pi))
        up_ref[...] = (pre * phi).astype(BF16)
        gu = gu_refs[k][...].reshape(rows, gu_refs[k].shape[2])
        grad_pre = (gu * (phi + pre * density)).astype(BF16)
        pre_ref[...] = grad_pre
        back_ref[...] = dot_nt(grad_pre, w_ref[...]).astype(BF16)


def mid_bwd_kernel(
    meta_ref, og_ref, own_ref, core_ref, y_ref, hidden_ref, gain_ref, total_ref, low_ref, sums_ref
):
    grad = total_of((own_ref, core_ref, y_ref))
    normed, inverse = norm_rows(hidden_ref[...])
    og = og_ref[...].reshape(hidden_ref.shape).astype(F32)
    total = og + norm_rows_back(grad, normed, inverse, gain_ref[...][None])
    total_ref[...] = total
    low_ref[...] = total.astype(BF16)
    sums_ref[0:1] = jnp.sum(grad * normed, 0, keepdims=True)
    sums_ref[1:2] = jnp.sum(grad, 0, keepdims=True)


def end_kernel(groups, meta_ref, *refs):
    x_refs, refs = refs[:groups], refs[groups:]
    own_ref, core_ref, y_ref = refs[:3]
    gain_ref, out_ref = refs[-2:]
    seqs = x_refs[0].shape[0]
    rows = own_ref.shape[0] // groups
    for g in range(groups):
        part = slice(g * rows, (g + 1) * rows)
        grad = total_of([ref.at[part] for ref in (own_ref, core_ref, y_ref)])
        normed, inverse = norm_rows(x_refs[g][...].reshape(grad.shape).astype(F32))
        total = refs[3 + g][...] + norm_rows_back(grad, normed, inverse, gain_ref[...][None])
        out_ref[g * seqs : (g + 1) * seqs] = total.reshape(x_refs[g].shape)


def output_kernel(groups, own_ref, core_ref, y_ref, *refs):
    out_ref = refs[-1]
    seqs, share, width = out_ref.shape
    seqs //= groups
    rows = seqs * share
    for g in range(groups):
        part = slice(g * rows, (g + 1) * rows)
        total = total_of([ref.at[part] for ref in (own_ref, core_ref, y_ref)]) + refs[g][...]
        out_ref[g * seqs : (g + 1) * seqs] = total.reshape(seqs, share, width)


def lead_grad_kernel(groups, seqs, per, share, meta_ref, wo_ref, lead_lse_ref, lead_out_ref, *refs):
    pieces, lead_ref, rows_ref = refs[:-2], refs[-2], refs[-1]
    blocks = per // BLOCK
    chunk = min(share, BLOCK)
    root = (meta_ref[1] + meta_ref[2]) == 1
    lead_ref[...] = jnp.zeros_like(lead_ref)
    token = jnp.where(meta_ref[1] == 1, 0, (blocks - 1) * BLOCK)
    for g in range(groups):
        for m in range(seqs):
            for c in range(BLOCK // chunk):
                at = (token + c * chunk) // share
                inside = pl.multiple_of(m * share + (token + c * chunk - at * share), chunk)
                for k in range(4):

                    @pl.when(root & (pos_of(meta_ref, at) == k))
                    def _(k=k, g=g, m=m, c=c, inside=inside):
                        to = (g * seqs + m) * BLOCK + c * chunk
                        rows_ref[to : to + chunk] = pieces[4 * g + k][pl.ds(inside, chunk)]

    @pl.when(root)
    def _():
        total = groups * seqs * BLOCK
        grad = dot_nn(rows_ref[...], wo_ref[...])
        low = grad.astype(BF16)
        prod = low.astype(F32) * lead_out_ref[...].reshape(total, 4 * HD).astype(F32)
        deltas = [
            jnp.sum(half(prod[:, : 2 * HD], False), -1, keepdims=True),
            jnp.sum(half(prod[:, : 2 * HD], True), -1, keepdims=True),
            jnp.sum(half(prod[:, 2 * HD :], True), -1, keepdims=True),
        ]
        d_hi, d_lo = zip(*(hi_lo(d) for d in deltas))
        lse = lead_lse_ref[...].reshape(total, 2 * HD)
        l_hi, l_lo = zip(*(hi_lo(lse[:, h : h + 1]) for h in range(3)))
        stats = lanes_of(l_hi + l_lo + d_hi + d_lo, total)
        tile1 = (half(grad[:, 2 * HD :], True) + stats).astype(BF16)
        lead_ref[:, :, : 2 * HD] = low[:, : 2 * HD].reshape(groups * seqs, BLOCK, 2 * HD)
        lead_ref[:, :, 2 * HD :] = tile1.reshape(groups * seqs, BLOCK, 2 * HD)


def heads_grad_kernel(groups, seqs, per, share, index_ref, meta_ref, wo_ref, *refs):
    pieces, mixed_refs = refs[: 4 * groups], refs[4 * groups : 5 * groups]
    lse_refs = refs[5 * groups : 6 * groups]
    grads_ref, sent_ref = refs[6 * groups :]
    wo = wo_ref[...]
    blocks = per // BLOCK
    rows_of = seqs * share
    for g in range(groups):
        for k in range(4):
            grad = dot_nn(pieces[4 * g + k][...], wo)
            low = grad.astype(BF16)
            prod = low.astype(F32) * mixed_refs[g][k * rows_of : (k + 1) * rows_of].astype(F32)
            deltas = [
                jnp.sum(half(prod[:, : 2 * HD], False), -1, keepdims=True),
                jnp.sum(half(prod[:, : 2 * HD], True), -1, keepdims=True),
                jnp.sum(half(prod[:, 2 * HD :], True), -1, keepdims=True),
            ]
            d_hi, d_lo = zip(*(hi_lo(d) for d in deltas))
            spare = [jnp.zeros_like(d_hi[0])] * 6
            stats = lanes_of(spare + list(d_hi + d_lo), rows_of)
            for m in range(seqs):
                at = slice(m * share, (m + 1) * share)
                inside = m * per + (meta_ref[0] ^ SWAP[k]) * share
                rows = pl.ds(pl.multiple_of(g * seqs * per + inside, share), share)
                lse = lse_refs[g][pl.ds(pl.multiple_of(inside, share), share)]
                l_hi, l_lo = zip(*(hi_lo(lse[:, h : h + 1]) for h in range(3)))
                grads_ref[rows, : 2 * HD] = low[at, : 2 * HD]
                grads_ref[rows, 2 * HD :] = (
                    half(grad[at, 2 * HD :], True) + stats[at] + lanes_of(l_hi + l_lo, share)
                ).astype(BF16)
    lane = lax.broadcasted_iota(jnp.int32, (BLOCK, 2 * HD), 1)
    for end, b in ((1, 0), (2, blocks - 1)):

        @pl.when(meta_ref[end] == 1)
        def _(b=b):
            for m in range(groups * seqs):
                rows = slice(m * per + b * BLOCK, m * per + (b + 1) * BLOCK)
                tile1 = grads_ref[rows, 2 * HD :].astype(F32)
                grads_ref[rows, : 2 * HD] = jnp.zeros((BLOCK, 2 * HD), BF16)
                grads_ref[rows, 2 * HD :] = jnp.where(lane < 6, tile1, 0.0).astype(BF16)

    def send(slot, _):
        at = pl.multiple_of(index_ref[slot] * BLOCK, BLOCK)
        sent_ref[slot] = grads_ref[pl.ds(at, BLOCK)]
        return 0

    lax.fori_loop(0, sent_ref.shape[0], send, 0, unroll=4)


def row_stats(tile):
    st = tile.astype(F32)
    lse = [st[:, h : h + 1] + st[:, 3 + h : 4 + h] for h in range(3)]
    delta = [st[:, 6 + h : 7 + h] + st[:, 9 + h : 10 + h] for h in range(3)]
    return lse, delta


def kv_grad(v_part, k_part):
    return jnp.concatenate([v_part[:, : 2 * HD], v_part[:, 2 * HD :] + k_part[:, : 2 * HD], k_part[:, 2 * HD :]], 1)


def sparse_bwd_kernel(
    batches, per, slot_ref, q_ref, kv_ref, low_ref, high_ref, lead0_ref, lead1_ref, rand_ref,
    bias_ref, grads_ref, dq_ref, dkv_ref, ret_low_ref, ret_high_ref, dlead0_ref, dlead1_ref,
    ext_ref, listed_ref, dext_ref, dlead_ref,
):
    blocks = per // BLOCK
    near = 6 * BLOCK
    fill_ext(ext_ref, kv_ref, low_ref, high_ref, batches, per)
    dext_ref[...] = jnp.zeros_like(dext_ref)
    dlead_ref[...] = jnp.zeros_like(dlead_ref)

    def attend(i, here):
        m, b = i // blocks, i % blocks
        fill_listed(here, ext_ref, lead0_ref, lead1_ref, rand_ref, slot_ref, m, b, i)
        grads = grads_ref[i]
        lse, delta = row_stats(grads[:, 2 * HD :])
        queries, grads = stack(q_ref[i], Q_LANES), stack(grads, O_LANES)
        prob = jnp.exp(dot_nt(queries, here[:, K_PART]) + bias_ref[i] - jnp.concatenate(lse, 0))
        ds = prob * (dot_nt(grads, here[:, V_PART]) - jnp.concatenate(delta, 0))
        ds = ds.astype(BF16)
        dq_ref[i] = unstack(dot_nn(ds, here[:, K_PART]), Q_LANES)
        dkv = kv_grad(dot_tn(prob[:, :near].astype(BF16), grads), dot_tn(ds[:, :near], queries))
        return m, b, dkv

    def step(j, _):
        done = [attend(2 * j + n, listed_ref.at[n]) for n in range(2)]
        for m, b, dkv in done:
            dext_ref[m, pl.ds(pl.multiple_of(b * BLOCK, BLOCK), 3 * BLOCK)] += dkv[: 3 * BLOCK]
            dlead_ref[m] += dkv[3 * BLOCK : 5 * BLOCK]
        return 0

    lax.fori_loop(0, batches * blocks // 2, step, 0)
    for m in range(batches):
        ret_low_ref[m] = dext_ref[m, :BLOCK].astype(BF16)
        dkv_ref[m] = dext_ref[m, BLOCK : BLOCK + per]
        ret_high_ref[m] = dext_ref[m, BLOCK + per :].astype(BF16)
        dlead0_ref[m] = dlead_ref[m, :BLOCK]
        dlead1_ref[m] = dlead_ref[m, BLOCK:]


def lead_bwd_kernel(
    meta_ref, lead0_ref, lead1_ref, kv_ref, bias_ref, sparse_ref, dlead0_ref, dlead1_ref, do0_ref, do1_ref,
    dkv_ref, mine_ref, given_ref,
):
    low = meta_ref[3]
    for m in range(kv_ref.shape[0]):
        grads = jnp.concatenate([do0_ref[m], do1_ref[m]], 0)
        lse, delta = row_stats(grads[:, 2 * HD :])
        queries = jnp.concatenate([lead0_ref[m, :, : 4 * HD], lead1_ref[m, :, : 4 * HD]], 0)
        queries, grads = stack(queries, Q_LANES), stack(grads, O_LANES)
        keys, values = kv_ref[m, :, K_PART], kv_ref[m, :, V_PART]
        prob = jnp.exp(dot_nt(queries, keys) + bias_ref[m] - jnp.concatenate(lse, 0))
        ds = (prob * (dot_nt(grads, values) - jnp.concatenate(delta, 0))).astype(BF16)
        dq = unstack(dot_nn(ds, keys), Q_LANES)
        for part_ref, first in ((mine_ref, low == 1), (given_ref, low == 0)):
            part_ref[m, :, : 4 * HD] = jnp.where(first, dq[:BLOCK], dq[BLOCK:]).astype(BF16)
            part_ref[m, :, 4 * HD :] = jnp.where(first, dlead0_ref[m], dlead1_ref[m]).astype(BF16)
        dkv_ref[m] = sparse_ref[m] + kv_grad(dot_tn(prob.astype(BF16), grads), dot_tn(ds, queries))


def split_rows(meta_ref, grad_ref, keep_ref, send_ref, lanes=slice(None)):
    count, rows, _ = keep_ref.shape
    even = (meta_ref[4] & 1) == 0
    for z in range(count):
        one = grad_ref[2 * z * rows : (2 * z + 1) * rows, lanes].astype(BF16)
        two = grad_ref[(2 * z + 1) * rows : (2 * z + 2) * rows, lanes].astype(BF16)
        keep_ref[z] = jnp.where(even, one, two)
        send_ref[z] = jnp.where(even, two, one)


def ffn_grad_kernel(groups, seqs, per, share, meta_ref, og_ref, *refs):
    count = 4 * groups
    ups, acts, pres = (refs[n * count : (n + 1) * count] for n in range(3))
    keep0_ref, send0_ref, keep1_ref, send1_ref, left_ref, right_ref, grad_ref = refs[3 * count :]
    piece = seqs * share
    hidden = ups[0].shape[1]
    for g in range(groups):
        for k in range(4):
            for m in range(seqs):
                row = (g * seqs + m) * per + (meta_ref[0] ^ SWAP[k]) * share
                rows = pl.ds(pl.multiple_of(row, share), share)
                right_ref[rows] = ups[4 * g + k][m * share : (m + 1) * share]
    grad_ref[:, :hidden] = dot_tn(og_ref[...], right_ref[...])
    for n in range(count):
        left_ref[n * piece : (n + 1) * piece] = acts[n][...]
        right_ref[n * piece : (n + 1) * piece] = pres[n][...]
    grad_ref[:, hidden:] = dot_tn(left_ref[...], right_ref[...])
    split_rows(meta_ref, grad_ref, keep0_ref, send0_ref, slice(0, hidden))
    split_rows(meta_ref, grad_ref, keep1_ref, send1_ref, slice(hidden, 2 * hidden))


def fold_kernel(count, meta_ref, *refs):
    pairs, out_refs = refs[: 2 * count], refs[2 * count :]
    z = meta_ref[4] >> 1
    for n, ref in enumerate(out_refs):
        at = 0
        for keep_ref, got_ref in zip(pairs[::2], pairs[1::2]):
            lanes = keep_ref.shape[2]
            total = keep_ref[z ^ n].astype(F32) + got_ref[z ^ n].astype(F32)
            ref[:, at : at + lanes] = total.astype(ref.dtype)
            at += lanes


def slots_kernel(
    index_ref, valid_ref, q_got_ref, do_got_ref, kv_ref, column_ref, dkv_ref, acc_ref
):
    acc_ref[...] = dkv_ref[...]

    def block_grads(c):
        at = index_ref[c]
        live = valid_ref[c] == 1
        kv = kv_ref[at]
        grads = do_got_ref[c]
        stats = jnp.transpose(grads[:, 2 * HD :].astype(F32))
        lse = [stats[h : h + 1] + stats[3 + h : 4 + h] for h in range(3)]
        delta = [stats[6 + h : 7 + h] + stats[9 + h : 10 + h] for h in range(3)]
        queries, grads = stack(q_got_ref[c], Q_LANES), stack(grads, O_LANES)
        bias = column_ref[at][:, : 3 * BLOCK]
        prob = jnp.exp(dot_nt(kv[:, K_PART], queries) + bias - jnp.concatenate(lse, 1))
        prob = jnp.where(live, prob, 0.0)
        ds = prob * (dot_nt(kv[:, V_PART], grads) - jnp.concatenate(delta, 1))
        return at, kv_grad(dot_nn(prob.astype(BF16), grads), dot_nn(ds.astype(BF16), queries))

    slots = q_got_ref.shape[0]
    wide = 4 if slots % 4 == 0 else 1

    def slot(j, _):
        done = [block_grads(wide * j + n) for n in range(wide)]
        for at, grad in done:
            acc_ref[at] += grad
        return 0

    lax.fori_loop(0, slots // wide, slot, 0)


def tail_kernel(
    groups, seqs, per, share, devices, meta_ref, dq_ref, dkv_ref, ret_low_ref, ret_high_ref, first_ref, first0_ref,
    first1_ref, mine_ref, given_ref, *refs,
):
    pieces, mixed_refs = refs[: 4 * groups], refs[4 * groups : 5 * groups]
    w_ref, gain_ref, shift_ref = refs[5 * groups : 5 * groups + 3]
    count = 4
    sums_refs = refs[5 * groups + 3 : 6 * groups + 3]
    ends_refs, back_refs = refs[6 * groups + 3 : -count - 5], refs[-count - 5 : -5]
    keep_ref, send_ref, gqkv_ref, grad_ref, left_ref = refs[-5:]
    blocks = per // BLOCK
    batches = dkv_ref.shape[0] // blocks
    gqkv_ref[:, : 4 * HD] = dq_ref[...].reshape(-1, 4 * HD).astype(BF16)
    gqkv_ref[:, 4 * HD :] = dkv_ref[...].reshape(-1, 6 * HD).astype(BF16)
    for m in range(batches):
        i = m * blocks
        low, high = ret_low_ref[m].astype(F32), ret_high_ref[m].astype(F32)
        if blocks == 1:
            gqkv_ref[i * BLOCK : (i + 1) * BLOCK, 4 * HD :] = (dkv_ref[i] + low + high).astype(BF16)
        else:
            j = i + blocks - 1
            gqkv_ref[i * BLOCK : (i + 1) * BLOCK, 4 * HD :] = (dkv_ref[i] + low).astype(BF16)
            gqkv_ref[j * BLOCK : (j + 1) * BLOCK, 4 * HD :] = (dkv_ref[j] + high).astype(BF16)
    lead = meta_ref[3] == 1
    rows = batches * BLOCK
    mine, given = mine_ref[...].reshape(rows, 10 * HD), given_ref[...].reshape(rows, 10 * HD)
    ends = jnp.concatenate([jnp.where(lead, mine, given), jnp.where(lead, given, mine)], 0)
    firsts = jnp.concatenate([first0_ref[...], first1_ref[...]], 0)
    grad = dot_tn(first_ref[...], gqkv_ref[...]) + dot_tn(firsts, ends)
    grad_ref[:, : 10 * HD] = grad
    columns = jnp.sum(gqkv_ref[...].astype(F32), 0, keepdims=True)
    columns = columns + jnp.sum(ends.astype(F32), 0, keepdims=True)
    weights = w_ref[...].astype(F32)
    along = jnp.sum(grad * weights, -1, keepdims=True)
    shift_sum = jnp.sum(columns * weights, -1, keepdims=True)
    rows_in = [gain_ref[...][None], shift_ref[...][None]]
    rows_in += [sum(ref[n : n + 1] for ref in sums_refs) for n in range(2)]
    rows_in.append(jnp.zeros((4, grad.shape[0]), F32))
    gain, shift, gain2_sum, shift2_sum = (
        jnp.transpose(jnp.concatenate(rows_in, 0))[:, n : n + 1] for n in range(4)
    )
    stats = lanes_of([(along - shift * shift_sum) / gain, shift_sum, gain2_sum, shift2_sum], grad.shape[0])
    lane = lax.broadcasted_iota(jnp.int32, stats.shape, 1)
    moved = jnp.concatenate([stats[:, HD:], stats[:, :HD]], 1)
    grad_ref[:, : 2 * HD] = jnp.where(lane < HD, grad[:, : 2 * HD], moved)
    piece = pieces[0].shape[0]
    total = 0.0
    for g in range(groups):
        for k in range(4):
            left_ref[k * piece : (k + 1) * piece] = pieces[4 * g + k][...]
        total = total + dot_tn(left_ref[...], mixed_refs[g][...])
    grad_ref[:, 10 * HD :] = total
    split_rows(meta_ref, grad_ref, keep_ref, send_ref)
    for end, b in ((1, 0), (2, blocks - 1)):

        @pl.when(meta_ref[end] == 1)
        def _(b=b):
            for m in range(groups * seqs):
                rows = slice(m * per + b * BLOCK, m * per + (b + 1) * BLOCK)
                total = gqkv_ref[rows].astype(F32)
                for ref in ends_refs:
                    total = total + ref[m].astype(F32)
                gqkv_ref[rows] = total.astype(BF16)

    for g in range(groups):
        for k in range(4):
            for m in range(seqs):
                row = (g * seqs + m) * per + (meta_ref[0] ^ SWAP[k]) * share
                rows = pl.ds(pl.multiple_of(row, share), share)
                back = dot_nt(gqkv_ref[rows], w_ref[...]).astype(BF16)
                back_refs[k][(g * seqs + m) * share : (g * seqs + m + 1) * share] = back


def swap_tp(value, bit):
    return lax.ppermute(value, "tp", [(i, i ^ bit) for i in range(lax.axis_size("tp"))])


def scatter_tp(parts):
    far = swap_tp(parts[3], 1)
    near = swap_tp(parts[2], 1)
    both = (parts[1].astype(F32) + far.astype(F32)).astype(BF16)
    return parts[0], near, swap_tp(both, 2)


def gather_tp(piece, before_first=(), before_last=()):
    cross = swap_tp(after(piece, *before_first) if before_first else piece, 2)
    return piece, cross, swap_tp(piece, 1), swap_tp(after(cross, *before_last) if before_last else cross, 1)


def mirrored(pairs, last):
    return pairs + [(last - a, last - b) for a, b in pairs]


SECOND = [(1, 3), (4, 5), (2, 6), (0, 7)]


def in_first_group(myself, devices):
    if devices == 8:
        return (myself == 0) | (myself == 1) | (myself == 2) | (myself == 4)
    return myself < devices // 2


def spread(own, myself, devices, *before_last):
    last = devices - 1
    held = own
    if devices == 8:
        for k in (1, 2, 4):
            held = held + lax.ppermute(own, "seq", mirrored([(0, k)], last))
        held = after(held, *before_last)
        other = lax.ppermute(held, "seq", mirrored(SECOND, last))
    else:
        bit = 1
        while bit < devices // 2:
            held = held + lax.ppermute(held, "seq", mirrored([(i, i + bit) for i in range(bit)], last))
            bit *= 2
        other = lax.ppermute(held, "seq", [(i, i ^ bit) for i in range(devices)])
    first = in_first_group(myself, devices)
    return jnp.where(first, held, other), jnp.where(first, other, held), other


def collect_first(given, devices):
    last = devices - 1
    if devices == 8:
        return lax.ppermute(given, "seq", mirrored([(b, a) for a, b in SECOND], last))
    return lax.ppermute(given, "seq", [(i, i ^ (devices // 2)) for i in range(devices)])


def collect_rest(mine, devices, join):
    last = devices - 1
    if devices == 8:
        return [mine] + [lax.ppermute(mine, "seq", mirrored([(k, 0)], last)) for k in (1, 2, 4)]
    bit = devices // 2
    while bit > 1:
        bit //= 2
        mine = join(mine, lax.ppermute(mine, "seq", mirrored([(i + bit, i) for i in range(bit)], last)))
    return [mine]


def to_owners(slots):
    return lax.all_to_all(slots, "seq", split_axis=0, concat_axis=0, tiled=True)


def sum_seq_first(send, devices):
    return lax.ppermute(send, "seq", [(i, i ^ 1) for i in range(devices)])


def sum_seq_rest(pairs, meta, devices):
    count, rows = pairs[0][0].shape[:2]
    lanes = sum(keep.shape[2] for keep, _ in pairs)
    if count == 4:
        low = sds((rows, lanes), BF16)
        own, *out = call(
            partial(fold_kernel, len(pairs)), (sds((rows, lanes), F32), low, low, low), name="fold"
        )(*(v for pair in pairs for v in pair), smem=(meta,))
        return [own] + [
            lax.ppermute(piece, "seq", [(i, i ^ (2 * (n + 1))) for i in range(devices)])
            for n, piece in enumerate(out)
        ]
    total = [(keep.astype(F32) + got.astype(F32)).astype(BF16) for keep, got in pairs]
    return across(jnp.concatenate(total, 2), devices)


def across(total, devices):
    sides = [[i for i in range(devices) if i % 2 == side] for side in range(2)]
    got = lax.all_to_all(
        total, "seq", split_axis=0, concat_axis=0, tiled=True, axis_index_groups=sides
    )
    return [got[n] for n in range(total.shape[0])]


def sum_of(terms):
    total = terms[0].astype(F32)
    for term in terms[1:]:
        total = total + term.astype(F32)
    return total


def per_device(
    layer_input,
    out_grad,
    norm1_gain,
    norm1_shift,
    w_qkv,
    w_out,
    norm2_gain,
    norm2_shift,
    w_up,
    w_down,
    key_keep,
    rand_blocks,
):
    batches, per, width = layer_input.shape
    local = w_qkv.shape[2]
    devices = lax.axis_size("seq")
    myself = lax.axis_index("seq")
    tp_count = lax.axis_size("tp")
    tp_place = lax.axis_index("tp")
    assert local == 3 * HD and tp_count == 4 and devices % 2 == 0 and batches % 2 == 0
    share = per // tp_count
    bd = per // BLOCK
    total = batches * bd
    blocks_all = bd * devices
    groups = 2
    seqs = batches // groups
    piece = seqs * share
    refs = total * RANDS
    slots_per = max(1, -(-refs // devices))
    slots = devices * slots_per
    hidden_here = w_up.shape[1]
    rows = width // devices
    i32 = jnp.int32
    flag = lambda v: v.astype(i32)
    meta = jnp.stack(
        [
            tp_place, flag(myself == 0), flag(myself == devices - 1), flag(in_first_group(myself, devices)), myself,
        ]
    ).astype(i32)

    CHAIN.last = ()
    scale = 1.0 / math.sqrt(HD)
    x_rows = layer_input.reshape(batches * per, width)
    first, q, kv, w640 = CHAIN.done(project(x_rows, norm1_gain, norm1_shift, w_qkv.transpose(1, 0, 2)))
    is_first, is_last = myself == 0, myself == devices - 1
    ends = jnp.where(is_first, layer_input[:, :BLOCK], layer_input[:, per - BLOCK :])
    ends = jnp.where(is_first | is_last, ends, jnp.zeros_like(ends))
    lead_x0, lead_x1, arrived = spread(ends, myself, devices, kv)
    q_blocks = q.reshape(total, BLOCK, 4 * HD)
    kv_blocks = kv.reshape(total, BLOCK, 6 * HD)
    kv_seqs = kv.reshape(batches, per, 6 * HD)

    table = (
        rand_blocks.reshape(batches, devices, bd, RANDS).transpose(1, 0, 2, 3).reshape(devices, refs)
    )
    owners = table // bd
    source = (jnp.arange(refs, dtype=i32) // (bd * RANDS))[None] * bd + table - owners * bd
    order = jnp.arange(refs, dtype=i32)
    earlier = order[None, :] < order[:, None]
    rank = jnp.sum(((owners[:, :, None] == owners[:, None, :]) & earlier[None]).astype(i32), -1)
    places = jnp.arange(slots_per, dtype=i32)
    asked = (owners == myself)[:, None, :] & (rank[:, None, :] == places[None, :, None])
    source_of = jnp.sum(jnp.where(asked, source[:, None, :], 0), -1).reshape(slots)
    valid = jnp.sum(asked.astype(i32), -1).reshape(slots)
    my_owner = lax.dynamic_index_in_dim(owners, myself, 0, False)
    my_rank = lax.dynamic_index_in_dim(rank, myself, 0, False)
    slot_of = my_owner * slots_per + my_rank
    mine = lax.dynamic_index_in_dim(table, myself, 0, False)
    query_of = jnp.sum(
        jnp.where(
            slot_of[None, :] == jnp.arange(slots, dtype=i32)[:, None], (order // RANDS)[None, :], 0
        ),
        -1,
    )

    end_kv = sds((batches, BLOCK, 6 * HD), BF16)
    end_all = sds((batches, BLOCK, 10 * HD), BF16)
    sent, kv_low, kv_high = call(
        partial(dispatch_kernel, bd),
        (sds((slots, BLOCK, 6 * HD), BF16), end_kv, end_kv),
        name="dispatch",
    )(kv_blocks, smem=(source_of,))
    rand_kv = to_owners(after(sent, arrived))
    up = [(i, i + 1) for i in range(devices - 1)]
    down = [(b, a) for a, b in up]
    low = lax.ppermute(kv_high, "seq", up)
    high = lax.ppermute(kv_low, "seq", down)

    bias, seq_bias, column_bias, wo256 = call(
        partial(bias_kernel, bd, blocks_all),
        (
            sds((total, 1, 8 * BLOCK), F32),
            sds((batches, 1, per), F32),
            sds((total, BLOCK, 4 * HD), F32),
            sds((width, 4 * HD), BF16),
        ),
        name="bias",
    )(key_keep.reshape(batches * blocks_all, BLOCK), w_out, smem=(mine, meta))

    grad_up = dot_nn(out_grad.reshape(batches * per, width), w_down)
    grad_up = grad_up.reshape(batches, per, hidden_here)

    part = sds((batches, BLOCK, 4 * HD), F32)
    low_piece = sds((piece, width), BF16)
    low_pieces = sds((groups * piece, width), BF16)
    high_piece = sds((piece, width), F32)
    attn, lse = [], []

    def attend(g):
        half_of = lambda array: part_of(array, g, groups)
        out, stat = call(
            partial(sparse_fwd_kernel, g * seqs * bd, seqs, per, share),
            (sds((4 * piece, 4 * HD), BF16), sds((seqs * per, 2 * HD), F32)),
            (
                pltpu.VMEM((seqs, per + 2 * BLOCK, 6 * HD), BF16),
                pltpu.VMEM((2, 8 * BLOCK, 6 * HD), BF16),
            ),
            name="sparse_fwd",
        )(
            half_of(q_blocks), half_of(kv_seqs), half_of(low), half_of(high), half_of(lead0), half_of(lead1),
            rand_kv, half_of(bias), smem=(slot_of, meta),
        )
        attn.append(out)
        lse.append(stat)

    lead_rows = sds((batches * BLOCK, width), BF16)
    lead_first0, lead_first1, lead0, lead1, part_mine, part_given = call(
        lead_fwd_kernel, (lead_rows, lead_rows, end_all, end_all, part, part), name="lead_fwd"
    )(kv_seqs, after(seq_bias, grad_up), lead_x0, lead_x1, norm1_gain, norm1_shift, w640, smem=(meta,))
    part_got = collect_first(part_given, devices)
    q_slots = call(gather_kernel, sds((slots, BLOCK, 4 * HD), BF16), name="gather")(q_blocks, smem=(query_of,))
    rand_q = to_owners(after(q_slots, rand_kv, part_got, low, high))
    attend(0)
    lead_parts = collect_rest(merge(part_mine, part_got), devices, merge)
    attend(1)
    lead_out, lead_lse = call(
        lead_finish_kernel,
        (sds(part.shape, BF16), sds((batches, BLOCK, 2 * HD), F32)),
        name="lead_finish",
        limit=SMALL,
    )(*lead_parts)
    out = call(
        partial(out_project_kernel, groups, seqs, per, share),
        (sds((4 * piece, 4 * HD), BF16),) * groups + (low_piece,) * (4 * groups),
        name="out_project",
    )(wo256, lead_out, *attn, smem=(meta,))
    mixed = out[:groups]
    attn_parts = [scatter_tp(out[groups + 4 * g : groups + 4 * g + 4]) for g in range(groups)]

    flat = lambda lists: [v for group in lists for v in group]
    hidden, act, total_grad, sums2, attn_grad = [], [], [], [], []
    ups, pres, back_parts, down_parts = [], [], [], []
    for g in range(groups):
        h, a = share_call(mid_fwd_kernel, (high_piece, low_piece), [(layer_input, g, 0)], "mid_fwd")(
            meta, seqs, share, *attn_parts[g], norm2_gain, norm2_shift
        )
        hidden.append(h)
        act.append(gather_tp(a, attn_parts[-1][2:]))
    low_hidden = sds((piece, hidden_here), BF16)
    for g in range(groups):
        out = share_call(
            ffn_kernel, (low_hidden, low_hidden, low_piece) * 4, [(grad_up, g, k) for k in range(4)], "ffn", MIDDLE
        )(meta, seqs, share, *act[g], w_up)
        ups.append(out[0::3])
        pres.append(out[1::3])
        back_parts.append(scatter_tp(out[2::3]))
    for g in range(groups):
        t, a, s = share_call(
            mid_bwd_kernel, (high_piece, low_piece, sds((2, width), F32)), [(out_grad, g, 0)], "mid_bwd"
        )(meta, seqs, share, *back_parts[g], hidden[g], norm2_gain)
        total_grad.append(t)
        sums2.append(s)
        if g == 0:
            down_parts = call(partial(down_kernel, groups), (low_pieces,) * 4, name="down", limit=MIDDLE)(*flat(ups), w_down)
            attn_grad.append(gather_tp(a))
        if g == groups - 1:
            halves = sds((devices // 2, rows, hidden_here), BF16)
            ff_keep0, ff_send0, ff_keep1, ff_send1 = call(
                partial(ffn_grad_kernel, groups, seqs, per, share),
                (halves,) * 4,
                (
                    pltpu.VMEM((batches * per, width), BF16),
                    pltpu.VMEM((batches * per, hidden_here), BF16),
                    pltpu.VMEM((width, 2 * hidden_here), F32),
                ),
                name="ffn_grad",
                limit=MIDDLE,
            )(
                out_grad.reshape(batches * per, width), *flat(ups), *flat(act), *flat(pres), smem=(meta,)
            )
            attn_grad.append(gather_tp(a, (), (ff_send0,)))
            ff_got0 = sum_seq_first(after(ff_send0, attn_grad[-1][1]), devices)

    lead_grad = call(
        partial(lead_grad_kernel, groups, seqs, per, share),
        sds((batches, BLOCK, 4 * HD), BF16),
        (pltpu.VMEM((batches * BLOCK, width), BF16),),
        name="lead_grad",
        limit=SMALL,
    )(wo256, lead_lse, lead_out, *flat(attn_grad), smem=(meta,))
    grads, sent = call(
        partial(heads_grad_kernel, groups, seqs, per, share),
        (sds((batches * per, 4 * HD), BF16), sds((slots, BLOCK, 4 * HD), BF16)),
        name="heads_grad",
        limit=MIDDLE,
    )(wo256, *flat(attn_grad), *mixed, *lse, smem=(query_of, meta))
    *lead_do, arrived = spread(lead_grad, myself, devices, sent)
    rand_do = to_owners(after(sent, arrived, rand_q, ff_got0))
    ff_got1 = sum_seq_first(after(ff_send1, arrived), devices)
    dend = sds(end_kv.shape, F32)
    dq, dkv, ret_low, ret_high, dlead0, dlead1 = call(
        partial(sparse_bwd_kernel, batches, per),
        (sds((total, BLOCK, 4 * HD), F32), sds((batches, per, 6 * HD), F32), end_kv, end_kv, dend, dend),
        (
            pltpu.VMEM((batches, per + 2 * BLOCK, 6 * HD), BF16),
            pltpu.VMEM((2, 8 * BLOCK, 6 * HD), BF16),
            pltpu.VMEM((batches, per + 2 * BLOCK, 6 * HD), F32),
            pltpu.VMEM((batches, 2 * BLOCK, 6 * HD), F32),
        ),
        name="sparse_bwd",
    )(
        q_blocks, kv_seqs, low, high, lead0, lead1, rand_kv, bias,
        after(grads, *lead_do).reshape(total, BLOCK, 4 * HD), smem=(slot_of,),
    )
    from_low = lax.ppermute(ret_high, "seq", up)
    from_high = lax.ppermute(ret_low, "seq", down)
    dkv, ends_mine, ends_given = call(
        lead_bwd_kernel, (sds((batches, per, 6 * HD), F32), end_all, end_all), name="lead_bwd"
    )(lead0, lead1, kv_seqs, seq_bias, dkv, dlead0, dlead1, *lead_do, smem=(meta,))
    add = lambda a, b: (a.astype(F32) + b.astype(F32)).astype(BF16)
    ends_first = collect_first(ends_given, devices)
    ends_got = collect_rest(add(after(ends_mine, from_low, from_high), ends_first), devices, add)

    dkv = call(slots_kernel, sds((total, BLOCK, 6 * HD), F32), name="slots")(
        rand_q, rand_do, kv_blocks, column_bias,
        dkv.reshape(total, BLOCK, 6 * HD), smem=(source_of, valid),
    )
    ff_half = jnp.concatenate(
        [
            (keep.astype(F32) + got.astype(F32)).astype(BF16)
            for keep, got in ((ff_keep0, ff_got0), (after(ff_keep1, dkv), after(ff_got1, dkv)))
        ],
        2,
    )
    ff = across(after(ff_half, *ends_got), devices)
    halves = sds((devices // 2, rows, 14 * HD), BF16)
    *first_back, qkv_keep, qkv_send = call(
        partial(tail_kernel, groups, seqs, per, share, devices),
        (low_pieces,) * 4 + (halves, halves),
        (
            pltpu.VMEM((total * BLOCK, 10 * HD), BF16),
            pltpu.VMEM((width, 14 * HD), F32),
            pltpu.VMEM((4 * piece, width), BF16),
        ),
        name="tail",
    )(
        dq, dkv, from_low, from_high, first, lead_first0, lead_first1, ends_mine, ends_given,
        *flat(attn_grad), *mixed, w640, norm1_gain, norm1_shift, *sums2, *ends_got, smem=(meta,),
    )
    qkv_got = sum_seq_first(qkv_send, devices)
    terms = scatter_tp(first_back)
    out_terms = scatter_tp([after(part, first_back[0]) for part in down_parts])
    ff = sum_of(ff)
    gq = sum_seq_rest([(qkv_keep, after(qkv_got, ff))], meta, devices)
    input_grad = share_call(
        partial(end_kernel, groups),
        sds((batches, share, width), F32),
        [(layer_input, g, 0) for g in range(groups)],
        "end",
    )(meta, seqs, share, *terms, *total_grad, norm1_gain)
    layer_output = call(
        partial(output_kernel, groups), sds((batches, share, width), F32), name="output", limit=SMALL
    )(*out_terms, *hidden)

    g_down, g_up = ff[:, :hidden_here], ff[:, hidden_here:]
    gq = sum_of(gq)
    norms = gq[:, HD : 2 * HD]
    norms = norms + swap_tp(norms, 1)
    norms = norms + swap_tp(norms, 2)
    g_out = jnp.concatenate([gq[:, 10 * HD : 12 * HD], gq[:, 13 * HD :]], 1)
    g_qkv = jnp.stack(
        [
            jnp.concatenate([gq[:, 2 * HD : 4 * HD], gq[:, :HD]], 1) * scale,
            jnp.concatenate([gq[:, 8 * HD : 10 * HD], gq[:, 6 * HD : 7 * HD]], 1),
            jnp.concatenate([gq[:, 4 * HD : 6 * HD], gq[:, 7 * HD : 8 * HD]], 1),
        ],
        1,
    )
    return (
        layer_output, input_grad, g_qkv, g_out, g_up, g_down, norms[:, 0], norms[:, 1], norms[:, 2], norms[:, 3],
    )


def solution(mesh):
    return jax.shard_map(
        per_device,
        mesh=mesh,
        in_specs=(
            P(None, "seq", None),
            P(None, "seq", None),
            P(),
            P(),
            P(None, None, "tp"),
            P(None, "tp"),
            P(),
            P(),
            P(None, "tp"),
            P(None, "tp"),
            P(),
            P(),
        ),
        out_specs=(
            P(None, ("seq", "tp"), None),
            P(None, ("seq", "tp"), None),
            P("seq", None, "tp"),
            P("seq", "tp"),
            P("seq", "tp"),
            P("seq", "tp"),
            P("seq"),
            P("seq"),
            P("seq"),
            P("seq"),
        ),
        check_vma=False,
    )
```

```python
from functools import partial
import math

import jax
import jax.numpy as jnp
from jax import lax
from jax.experimental import pallas as pl
from jax.experimental.pallas import tpu as pltpu
from jax.sharding import PartitionSpec as P

HD = 64
BLOCK = 64
RANDS = 3
EPS = 1e-06
SWAP = (0, 2, 1, 3)
NEG = -1e30
Q_LANES = (128, 192, 0)
O_LANES = (0, 64, 192)
K_PART = slice(128, 384)
V_PART = slice(0, 256)
F32 = jnp.float32
BF16 = jnp.bfloat16
VMEM = pl.BlockSpec(memory_space=pltpu.VMEM)
SMEM = pl.BlockSpec(memory_space=pltpu.SMEM)
MIB = 1024 * 1024


def sds(shape, kind):
    return jax.ShapeDtypeStruct(shape, kind)


PARAMS = pltpu.CompilerParams(vmem_limit_bytes=56 * MIB)
SMALL = pltpu.CompilerParams(vmem_limit_bytes=12 * MIB)
MIDDLE = pltpu.CompilerParams(vmem_limit_bytes=24 * MIB)


def after(value, *others):
    return lax.optimization_barrier((value,) + others)[0]


class Chain:
    last = ()

    def link(self, value):
        return after(value, *self.last) if self.last else value

    def done(self, outs):
        self.last = (jax.tree.leaves(outs)[0],)
        return outs


CHAIN = Chain()


def part_of(array, at, count):
    return array, at, count


TIMES = {
    "project": 6, "dispatch": 3, "bias": 2, "lead_fwd": 4, "sparse_fwd": 7, "merge": 1, "lead_finish": 1, "out_project": 1,
    "mid_fwd": 1, "gather": 2, "ffn": 6, "ffn_grad": 7, "mid_bwd": 1, "heads_grad": 5, "lead_grad": 1, "sparse_bwd": 13,
    "fold_near": 3, "down": 6, "lead_bwd": 5, "slots": 14, "tail": 5, "fold_far": 2, "back": 7, "output": 1,
    "fold": 2, "end": 2,
}
HINT = 1.75e6


def cost(name):
    return pl.CostEstimate(flops=0, transcendentals=0, bytes_accessed=int(TIMES[name] * HINT))


def call(body, outs, scratch=(), name=None, limit=PARAMS):
    def run(*args, smem=()):
        specs = [SMEM] * len(smem)
        arrays = []
        if smem:
            smem = (CHAIN.link(smem[0]),) + tuple(smem[1:])
        else:
            args = (CHAIN.link(args[0]),) + args[1:]
        for arg in args:
            if isinstance(arg, tuple):
                array, at, count = arg
                shape = (array.shape[0] // count,) + array.shape[1:]
                index = (at,) + (0,) * (array.ndim - 1)
                specs.append(pl.BlockSpec(shape, lambda i, index=index: index))
                arrays.append(array)
            else:
                specs.append(VMEM)
                arrays.append(arg)
        return CHAIN.done(
            pl.pallas_call(
                body,
                out_shape=outs,
                grid=(1,),
                in_specs=specs,
                out_specs=jax.tree.map(lambda _: VMEM, outs),
                scratch_shapes=list(scratch),
                compiler_params=limit,
                cost_estimate=cost(name),
                name=name,
            )(*smem, *arrays)
        )

    return run


def share_call(body, outs, blocks, name, limit=SMALL):
    def run(meta, seqs, share, *args):
        def spec(value, group, pos):
            return pl.BlockSpec(
                (seqs, share, value.shape[2]), lambda i, meta_ref: (group, meta_ref[0] ^ SWAP[pos], 0)
            )

        return CHAIN.done(
            pl.pallas_call(
                body,
                out_shape=outs,
                grid_spec=pltpu.PrefetchScalarGridSpec(
                    num_scalar_prefetch=1,
                    grid=(1,),
                    in_specs=[spec(*b) for b in blocks] + [VMEM] * len(args),
                    out_specs=jax.tree.map(lambda _: VMEM, outs),
                ),
                compiler_params=limit,
                cost_estimate=cost(name),
                name=name,
            )(CHAIN.link(meta), *(b[0] for b in blocks), *args)
        )

    return run


def dot_nt(a, b):
    return lax.dot_general(a, b, (((1,), (1,)), ((), ())), preferred_element_type=F32)


def dot_tn(a, b):
    return lax.dot_general(a, b, (((0,), (0,)), ((), ())), preferred_element_type=F32)


def dot_nn(a, b):
    return lax.dot_general(a, b, (((1,), (0,)), ((), ())), preferred_element_type=F32)


def stack(rows, lanes):
    lane = lax.broadcasted_iota(jnp.int32, rows.shape, 1)
    zero = jnp.zeros_like(rows)
    return jnp.concatenate([jnp.where((lane >= at) & (lane < at + HD), rows, zero) for at in lanes], 0)


def unstack(stacked, lanes):
    rows = stacked.shape[0] // 3
    lane = lax.broadcasted_iota(jnp.int32, (rows, stacked.shape[1]), 1)
    out = jnp.zeros((rows, stacked.shape[1]), stacked.dtype)
    for h, at in enumerate(lanes):
        out = jnp.where((lane >= at) & (lane < at + HD), stacked[h * rows : (h + 1) * rows], out)
    return out


def thirds(column):
    rows = column.shape[0] // 3
    return [column[h * rows : (h + 1) * rows] for h in range(3)]


def half(tile, upper):
    lane = lax.broadcasted_iota(jnp.int32, tile.shape, 1)
    return jnp.where((lane >= HD) if upper else (lane < HD), tile, jnp.zeros_like(tile))


def lanes_of(columns, rows):
    lane = lax.broadcasted_iota(jnp.int32, (rows, 2 * HD), 1)
    out = jnp.zeros((rows, 2 * HD), F32)
    for at, column in enumerate(columns):
        out = jnp.where(lane == at, column, out)
    return out


def hi_lo(value):
    hi = value.astype(BF16).astype(F32)
    return hi, value - hi


def norm_rows(hidden):
    center = hidden - jnp.mean(hidden, -1, keepdims=True)
    inverse = lax.rsqrt(jnp.mean(center * center, -1, keepdims=True) + EPS)
    return center * inverse, inverse


def norm_rows_back(grad, normed, inverse, gain):
    scaled = grad * gain
    return inverse * (
        scaled
        - jnp.mean(scaled, -1, keepdims=True)
        - normed * jnp.mean(scaled * normed, -1, keepdims=True)
    )


def project_kernel(x_ref, gain_ref, shift_ref, raw_ref, first_ref, q_ref, kv_ref, w_ref):
    @pl.when(pl.program_id(0) == 0)
    def _():
        scale = jnp.asarray(1.0 / math.sqrt(HD), BF16)
        blank = jnp.zeros((w_ref.shape[0], HD), BF16)
        w_ref[:, : 2 * HD] = jnp.concatenate([raw_ref[0, :, 2 * HD :] * scale, blank], 1)
        w_ref[:, 2 * HD : 4 * HD] = raw_ref[0, :, : 2 * HD] * scale
        w_ref[:, 4 * HD : 6 * HD] = raw_ref[2, :, : 2 * HD]
        w_ref[:, 6 * HD : 8 * HD] = jnp.concatenate([raw_ref[1, :, 2 * HD :], raw_ref[2, :, 2 * HD :]], 1)
        w_ref[:, 8 * HD :] = raw_ref[1, :, : 2 * HD]

    normed, _ = norm_rows(x_ref[...].astype(F32))
    first = (normed * gain_ref[...][None] + shift_ref[...][None]).astype(BF16)
    first_ref[...] = first
    out = dot_nn(first, w_ref[...]).astype(BF16)
    q_ref[...] = out[:, : 4 * HD]
    kv_ref[...] = out[:, 4 * HD :]


def project(x, gain, shift, raw):
    rows, width = x.shape
    tile = min(rows, 256)
    row = lambda w: pl.BlockSpec((tile, w), lambda i: (i, 0))
    vector = pl.BlockSpec((width,), lambda i: (0,))
    whole = lambda w: pl.BlockSpec((width, w), lambda i: (0, 0))
    low = lambda *shape: sds(shape, BF16)
    return pl.pallas_call(
        project_kernel,
        grid=(rows // tile,),
        out_shape=(low(rows, width), low(rows, 4 * HD), low(rows, 6 * HD), low(width, 10 * HD)),
        in_specs=[
            row(width), vector, vector, pl.BlockSpec(raw.shape, lambda i: (0, 0, 0)),
        ],
        out_specs=(row(width), row(4 * HD), row(6 * HD), whole(10 * HD)),
        compiler_params=PARAMS,
        cost_estimate=cost("project"),
        name="project",
    )(x, gain, shift, raw)


def dispatch_kernel(bd, index_ref, kv_ref, sent_ref, low_ref, high_ref):
    def step(slot, _):
        sent_ref[slot] = kv_ref[index_ref[slot]]
        return 0

    lax.fori_loop(0, sent_ref.shape[0], step, 0, unroll=4)
    for m in range(low_ref.shape[0]):
        low_ref[m] = kv_ref[m * bd]
        high_ref[m] = kv_ref[m * bd + bd - 1]


def bias_kernel(bd, blocks_all, table_ref, meta_ref, keep_ref, raw_ref, bias_ref, seq_ref, column_ref, wo_ref):
    wo_ref[:, : 2 * HD] = raw_ref[:, : 2 * HD]
    blank = jnp.zeros((wo_ref.shape[0], HD), BF16)
    wo_ref[:, 2 * HD :] = jnp.concatenate([blank, raw_ref[:, 2 * HD :]], 1)
    low = lambda keep: jnp.where(keep > 0, 0.0, NEG)
    for m in range(seq_ref.shape[0]):
        for b in range(bd):
            i = m * bd + b
            here = meta_ref[4] * bd + b

            def row(block, inside=True):
                return low(jnp.where(inside, keep_ref[pl.ds(m * blocks_all + block, 1)], 0))

            own = row(here)
            listed = [
                row(jnp.maximum(here - 1, 0), here > 0),
                own,
                row(jnp.minimum(here + 1, blocks_all - 1), here < blocks_all - 1),
                row(0),
                row(blocks_all - 1),
            ] + [row(table_ref[i * RANDS + j]) for j in range(RANDS)]
            bias_ref[i] = jnp.concatenate(listed, 1)
            seq_ref[m, :, b * BLOCK : (b + 1) * BLOCK] = own
            column_ref[i] = jnp.transpose(jnp.broadcast_to(own, (4 * HD, BLOCK)))


def gather_kernel(index_ref, blocks_ref, out_ref):
    def step(slot, _):
        out_ref[slot] = blocks_ref[index_ref[slot]]
        return 0

    lax.fori_loop(0, out_ref.shape[0], step, 0, unroll=4)


def lead_fwd_kernel(
    meta_ref, kv_ref, bias_ref, x0_ref, x1_ref, gain_ref, shift_ref, w_ref, first0_ref, first1_ref,
    lead0_ref, lead1_ref, mine_ref, given_ref,
):
    for x_ref, first_ref, lead_ref in ((x0_ref, first0_ref, lead0_ref), (x1_ref, first1_ref, lead1_ref)):
        normed, _ = norm_rows(x_ref[...].reshape(-1, x_ref.shape[2]).astype(F32))
        first = (normed * gain_ref[...][None] + shift_ref[...][None]).astype(BF16)
        first_ref[...] = first
        lead_ref[...] = dot_nn(first, w_ref[...]).astype(BF16).reshape(lead_ref.shape)
    low = meta_ref[3]
    for m in range(kv_ref.shape[0]):
        queries = jnp.concatenate([lead0_ref[m, :, : 4 * HD], lead1_ref[m, :, : 4 * HD]], 0)
        scores = dot_nt(stack(queries, Q_LANES), kv_ref[m, :, K_PART]) + bias_ref[m]
        top = jnp.max(scores, -1, keepdims=True)
        expo = jnp.exp(scores - top)
        total = jnp.sum(expo, -1, keepdims=True)
        out = unstack(dot_nn(expo.astype(BF16), kv_ref[m, :, V_PART]), O_LANES)
        stats = lanes_of(thirds(top) + thirds(total), 2 * BLOCK)
        for part_ref, first in ((mine_ref, low == 1), (given_ref, low == 0)):
            for lanes, value in ((slice(0, 2 * HD), out[:, : 2 * HD]), (slice(2 * HD, 4 * HD), out[:, 2 * HD :] + stats)):
                part_ref[m, :, lanes] = jnp.where(first, value[:BLOCK], value[BLOCK:])


def merge_parts(parts):
    lane = lax.broadcasted_iota(jnp.int32, (BLOCK, 2 * HD), 1)
    stats = [p[:, 2 * HD :] for p in parts]
    top = stats[0]
    for st in stats[1:]:
        top = jnp.maximum(top, st)
    tops = [top[:, h : h + 1] for h in range(3)]
    sums = [0.0, 0.0, 0.0]
    out0, out1 = 0.0, 0.0
    for p, st in zip(parts, stats):
        scale = [jnp.exp(st[:, h : h + 1] - tops[h]) for h in range(3)]
        sums = [sums[h] + st[:, 3 + h : 4 + h] * scale[h] for h in range(3)]
        out0 = out0 + p[:, : 2 * HD] * jnp.where(lane < HD, scale[0], scale[1])
        out1 = out1 + st * scale[2]
    return out0, jnp.where(lane >= HD, out1, 0.0), tops, sums


def merge_kernel(a_ref, b_ref, out_ref):
    for m in range(a_ref.shape[0]):
        out0, out1, tops, sums = merge_parts([a_ref[m], b_ref[m]])
        out_ref[m, :, : 2 * HD] = out0
        out_ref[m, :, 2 * HD :] = out1 + lanes_of(tops + sums, BLOCK)


def merge(a, b):
    return call(merge_kernel, sds(a.shape, F32), name="merge", limit=SMALL)(a, b)


def lead_finish_kernel(*refs):
    part_refs, (out_ref, lse_ref) = refs[:-2], refs[-2:]
    lane = lax.broadcasted_iota(jnp.int32, (BLOCK, 2 * HD), 1)
    for m in range(out_ref.shape[0]):
        out0, out1, tops, sums = merge_parts([p[m] for p in part_refs])
        out_ref[m, :, : 2 * HD] = (out0 / jnp.where(lane < HD, sums[0], sums[1])).astype(BF16)
        out_ref[m, :, 2 * HD :] = (out1 / sums[2]).astype(BF16)
        lse_ref[m] = lanes_of([tops[h] + jnp.log(sums[h]) for h in range(3)], BLOCK)


def fill_ext(ext_ref, kv_ref, low_ref, high_ref, seqs, per):
    for m in range(seqs):
        ext_ref[m, :BLOCK] = low_ref[m]
        ext_ref[m, BLOCK : BLOCK + per] = kv_ref[m]
        ext_ref[m, BLOCK + per :] = high_ref[m]


def fill_listed(listed_ref, ext_ref, lead0_ref, lead1_ref, rand_ref, slot_ref, m, b, block):
    listed_ref[: 3 * BLOCK] = ext_ref[m, pl.ds(pl.multiple_of(b * BLOCK, BLOCK), 3 * BLOCK)]
    listed_ref[3 * BLOCK : 4 * BLOCK] = lead0_ref[m, :, 4 * HD :]
    listed_ref[4 * BLOCK : 5 * BLOCK] = lead1_ref[m, :, 4 * HD :]
    for j in range(RANDS):
        listed_ref[(5 + j) * BLOCK : (6 + j) * BLOCK] = rand_ref[slot_ref[block * RANDS + j]]


def pos_of(meta_ref, at):
    j = at ^ meta_ref[0]
    return ((j & 1) << 1) | (j >> 1)


def sparse_fwd_kernel(
    first, seqs, per, share, slot_ref, meta_ref, q_ref, kv_ref, low_ref, high_ref, lead0_ref,
    lead1_ref, rand_ref, bias_ref, out_ref, lse_ref, ext_ref, listed_ref,
):
    blocks = per // BLOCK
    chunk = min(share, BLOCK)
    fill_ext(ext_ref, kv_ref, low_ref, high_ref, seqs, per)

    def attend(i, here):
        m, b = i // blocks, i % blocks
        fill_listed(here, ext_ref, lead0_ref, lead1_ref, rand_ref, slot_ref, m, b, first + i)
        scores = dot_nt(stack(q_ref[i], Q_LANES), here[:, K_PART]) + bias_ref[i]
        top = jnp.max(scores, -1, keepdims=True)
        expo = jnp.exp(scores - top)
        total = jnp.sum(expo, -1, keepdims=True)
        prob = (expo * (1.0 / total)).astype(BF16)
        out = unstack(dot_nn(prob, here[:, V_PART]), O_LANES).astype(BF16)
        lse_ref[pl.ds(pl.multiple_of(i * BLOCK, BLOCK), BLOCK)] = lanes_of(
            thirds(top + jnp.log(total)), BLOCK
        )
        for c in range(BLOCK // chunk):
            token = b * BLOCK + c * chunk
            at = token // share
            row = pos_of(meta_ref, at) * (seqs * share) + m * share + (token - at * share)
            rows = pl.ds(pl.multiple_of(row, chunk), chunk)
            out_ref[rows] = out[c * chunk : (c + 1) * chunk]

    def step(j, _):
        attend(2 * j, listed_ref.at[0])
        attend(2 * j + 1, listed_ref.at[1])
        return 0

    lax.fori_loop(0, seqs * blocks // 2, step, 0)


def out_project_kernel(groups, seqs, per, share, meta_ref, wo_ref, lead_out_ref, *refs):
    attn_refs, mixed_refs, part_refs = refs[:groups], refs[groups : 2 * groups], refs[2 * groups :]
    blocks = per // BLOCK
    chunk = min(share, BLOCK)
    piece = seqs * share
    for g in range(groups):
        mixed_refs[g][...] = attn_refs[g][...]
    for end, b in ((1, 0), (2, blocks - 1)):

        @pl.when(meta_ref[end] == 1)
        def _(b=b):
            for g in range(groups):
                for m in range(seqs):
                    for c in range(BLOCK // chunk):
                        token = b * BLOCK + c * chunk
                        at = token // share
                        row = pos_of(meta_ref, at) * piece + m * share + (token - at * share)
                        rows = pl.ds(pl.multiple_of(row, chunk), chunk)
                        mixed_refs[g][rows] = lead_out_ref[g * seqs + m, c * chunk : (c + 1) * chunk]

    wo = wo_ref[...]
    for g in range(groups):
        for k in range(4):
            rows = slice(k * piece, (k + 1) * piece)
            part_refs[4 * g + k][...] = dot_nt(mixed_refs[g][rows], wo).astype(BF16)


def down_kernel(groups, *refs):
    up_refs, w_ref, out_refs = refs[: 4 * groups], refs[4 * groups], refs[4 * groups + 1 :]
    rows = up_refs[0].shape[0]
    for g in range(groups):
        for k in range(4):
            out = dot_nt(up_refs[4 * g + k][...], w_ref[...]).astype(BF16)
            out_refs[k][g * rows : (g + 1) * rows] = out


def total_of(refs):
    return refs[0][...].astype(F32) + refs[1][...].astype(F32) + refs[2][...].astype(F32)


def mid_fwd_kernel(meta_ref, x_ref, own_ref, core_ref, y_ref, gain_ref, shift_ref, hidden_ref, act_ref):
    x = x_ref[...].reshape(hidden_ref.shape).astype(F32)
    hidden = total_of((own_ref, core_ref, y_ref)) + x
    normed, _ = norm_rows(hidden)
    hidden_ref[...] = hidden
    act_ref[...] = (normed * gain_ref[...][None] + shift_ref[...][None]).astype(BF16)


def ffn_kernel(meta_ref, *refs):
    gu_refs, act_refs, w_ref, outs = refs[:4], refs[4:8], refs[8], refs[9:]
    rows = act_refs[0].shape[0]
    for k in (3, 2, 1, 0):
        up_ref, pre_ref, back_ref = outs[3 * k : 3 * k + 3]
        pre = dot_nn(act_refs[k][...], w_ref[...])
        phi = 0.5 + 0.5 * lax.erf(pre * (1.0 / math.sqrt(2.0)))
        density = jnp.exp(-0.5 * pre * pre) * (1.0 / math.sqrt(2.0 * math.pi))
        up_ref[...] = (pre * phi).astype(BF16)
        gu = gu_refs[k][...].reshape(rows, gu_refs[k].shape[2])
        grad_pre = (gu * (phi + pre * density)).astype(BF16)
        pre_ref[...] = grad_pre
        back_ref[...] = dot_nt(grad_pre, w_ref[...]).astype(BF16)


def mid_bwd_kernel(
    meta_ref, og_ref, own_ref, core_ref, y_ref, hidden_ref, gain_ref, total_ref, low_ref, sums_ref
):
    grad = total_of((own_ref, core_ref, y_ref))
    normed, inverse = norm_rows(hidden_ref[...])
    og = og_ref[...].reshape(hidden_ref.shape).astype(F32)
    total = og + norm_rows_back(grad, normed, inverse, gain_ref[...][None])
    total_ref[...] = total
    low_ref[...] = total.astype(BF16)
    sums_ref[0:1] = jnp.sum(grad * normed, 0, keepdims=True)
    sums_ref[1:2] = jnp.sum(grad, 0, keepdims=True)


def end_kernel(groups, meta_ref, *refs):
    x_refs, refs = refs[:groups], refs[groups:]
    own_ref, core_ref, y_ref = refs[:3]
    gain_ref, out_ref = refs[-2:]
    seqs = x_refs[0].shape[0]
    rows = own_ref.shape[0] // groups
    for g in range(groups):
        part = slice(g * rows, (g + 1) * rows)
        grad = total_of([ref.at[part] for ref in (own_ref, core_ref, y_ref)])
        normed, inverse = norm_rows(x_refs[g][...].reshape(grad.shape).astype(F32))
        total = refs[3 + g][...] + norm_rows_back(grad, normed, inverse, gain_ref[...][None])
        out_ref[g * seqs : (g + 1) * seqs] = total.reshape(x_refs[g].shape)


def output_kernel(groups, own_ref, core_ref, y_ref, *refs):
    out_ref = refs[-1]
    seqs, share, width = out_ref.shape
    seqs //= groups
    rows = seqs * share
    for g in range(groups):
        part = slice(g * rows, (g + 1) * rows)
        total = total_of([ref.at[part] for ref in (own_ref, core_ref, y_ref)]) + refs[g][...]
        out_ref[g * seqs : (g + 1) * seqs] = total.reshape(seqs, share, width)


def lead_grad_kernel(groups, seqs, per, share, meta_ref, wo_ref, lead_lse_ref, lead_out_ref, *refs):
    pieces, lead_ref, rows_ref = refs[:-2], refs[-2], refs[-1]
    blocks = per // BLOCK
    chunk = min(share, BLOCK)
    root = (meta_ref[1] + meta_ref[2]) == 1
    lead_ref[...] = jnp.zeros_like(lead_ref)
    token = jnp.where(meta_ref[1] == 1, 0, (blocks - 1) * BLOCK)
    for g in range(groups):
        for m in range(seqs):
            for c in range(BLOCK // chunk):
                at = (token + c * chunk) // share
                inside = pl.multiple_of(m * share + (token + c * chunk - at * share), chunk)
                for k in range(4):

                    @pl.when(root & (pos_of(meta_ref, at) == k))
                    def _(k=k, g=g, m=m, c=c, inside=inside):
                        to = (g * seqs + m) * BLOCK + c * chunk
                        rows_ref[to : to + chunk] = pieces[4 * g + k][pl.ds(inside, chunk)]

    @pl.when(root)
    def _():
        total = groups * seqs * BLOCK
        grad = dot_nn(rows_ref[...], wo_ref[...])
        low = grad.astype(BF16)
        prod = low.astype(F32) * lead_out_ref[...].reshape(total, 4 * HD).astype(F32)
        deltas = [
            jnp.sum(half(prod[:, : 2 * HD], False), -1, keepdims=True),
            jnp.sum(half(prod[:, : 2 * HD], True), -1, keepdims=True),
            jnp.sum(half(prod[:, 2 * HD :], True), -1, keepdims=True),
        ]
        d_hi, d_lo = zip(*(hi_lo(d) for d in deltas))
        lse = lead_lse_ref[...].reshape(total, 2 * HD)
        l_hi, l_lo = zip(*(hi_lo(lse[:, h : h + 1]) for h in range(3)))
        stats = lanes_of(l_hi + l_lo + d_hi + d_lo, total)
        tile1 = (half(grad[:, 2 * HD :], True) + stats).astype(BF16)
        lead_ref[:, :, : 2 * HD] = low[:, : 2 * HD].reshape(groups * seqs, BLOCK, 2 * HD)
        lead_ref[:, :, 2 * HD :] = tile1.reshape(groups * seqs, BLOCK, 2 * HD)


def heads_grad_kernel(groups, seqs, per, share, index_ref, meta_ref, wo_ref, *refs):
    pieces, mixed_refs = refs[: 4 * groups], refs[4 * groups : 5 * groups]
    lse_refs = refs[5 * groups : 6 * groups]
    grads_ref, sent_ref = refs[6 * groups :]
    wo = wo_ref[...]
    blocks = per // BLOCK
    rows_of = seqs * share
    for g in range(groups):
        for k in range(4):
            grad = dot_nn(pieces[4 * g + k][...], wo)
            low = grad.astype(BF16)
            prod = low.astype(F32) * mixed_refs[g][k * rows_of : (k + 1) * rows_of].astype(F32)
            deltas = [
                jnp.sum(half(prod[:, : 2 * HD], False), -1, keepdims=True),
                jnp.sum(half(prod[:, : 2 * HD], True), -1, keepdims=True),
                jnp.sum(half(prod[:, 2 * HD :], True), -1, keepdims=True),
            ]
            d_hi, d_lo = zip(*(hi_lo(d) for d in deltas))
            spare = [jnp.zeros_like(d_hi[0])] * 6
            stats = lanes_of(spare + list(d_hi + d_lo), rows_of)
            for m in range(seqs):
                at = slice(m * share, (m + 1) * share)
                inside = m * per + (meta_ref[0] ^ SWAP[k]) * share
                rows = pl.ds(pl.multiple_of(g * seqs * per + inside, share), share)
                lse = lse_refs[g][pl.ds(pl.multiple_of(inside, share), share)]
                l_hi, l_lo = zip(*(hi_lo(lse[:, h : h + 1]) for h in range(3)))
                grads_ref[rows, : 2 * HD] = low[at, : 2 * HD]
                grads_ref[rows, 2 * HD :] = (
                    half(grad[at, 2 * HD :], True) + stats[at] + lanes_of(l_hi + l_lo, share)
                ).astype(BF16)
    lane = lax.broadcasted_iota(jnp.int32, (BLOCK, 2 * HD), 1)
    for end, b in ((1, 0), (2, blocks - 1)):

        @pl.when(meta_ref[end] == 1)
        def _(b=b):
            for m in range(groups * seqs):
                rows = slice(m * per + b * BLOCK, m * per + (b + 1) * BLOCK)
                tile1 = grads_ref[rows, 2 * HD :].astype(F32)
                grads_ref[rows, : 2 * HD] = jnp.zeros((BLOCK, 2 * HD), BF16)
                grads_ref[rows, 2 * HD :] = jnp.where(lane < 6, tile1, 0.0).astype(BF16)

    def send(slot, _):
        at = pl.multiple_of(index_ref[slot] * BLOCK, BLOCK)
        sent_ref[slot] = grads_ref[pl.ds(at, BLOCK)]
        return 0

    lax.fori_loop(0, sent_ref.shape[0], send, 0, unroll=4)


def row_stats(tile):
    st = tile.astype(F32)
    lse = [st[:, h : h + 1] + st[:, 3 + h : 4 + h] for h in range(3)]
    delta = [st[:, 6 + h : 7 + h] + st[:, 9 + h : 10 + h] for h in range(3)]
    return lse, delta


def kv_grad(v_part, k_part):
    return jnp.concatenate([v_part[:, : 2 * HD], v_part[:, 2 * HD :] + k_part[:, : 2 * HD], k_part[:, 2 * HD :]], 1)


def sparse_bwd_kernel(
    batches, per, slot_ref, q_ref, kv_ref, low_ref, high_ref, lead0_ref, lead1_ref, rand_ref,
    bias_ref, grads_ref, dq_ref, dkv_ref, ret_low_ref, ret_high_ref, dlead0_ref, dlead1_ref,
    ext_ref, listed_ref, dext_ref, dlead_ref,
):
    blocks = per // BLOCK
    near = 6 * BLOCK
    fill_ext(ext_ref, kv_ref, low_ref, high_ref, batches, per)
    dext_ref[...] = jnp.zeros_like(dext_ref)
    dlead_ref[...] = jnp.zeros_like(dlead_ref)

    def attend(i, here):
        m, b = i // blocks, i % blocks
        fill_listed(here, ext_ref, lead0_ref, lead1_ref, rand_ref, slot_ref, m, b, i)
        grads = grads_ref[i]
        lse, delta = row_stats(grads[:, 2 * HD :])
        queries, grads = stack(q_ref[i], Q_LANES), stack(grads, O_LANES)
        prob = jnp.exp(dot_nt(queries, here[:, K_PART]) + bias_ref[i] - jnp.concatenate(lse, 0))
        ds = prob * (dot_nt(grads, here[:, V_PART]) - jnp.concatenate(delta, 0))
        ds = ds.astype(BF16)
        dq_ref[i] = unstack(dot_nn(ds, here[:, K_PART]), Q_LANES)
        dkv = kv_grad(dot_tn(prob[:, :near].astype(BF16), grads), dot_tn(ds[:, :near], queries))
        return m, b, dkv

    def step(j, _):
        done = [attend(2 * j + n, listed_ref.at[n]) for n in range(2)]
        for m, b, dkv in done:
            dext_ref[m, pl.ds(pl.multiple_of(b * BLOCK, BLOCK), 3 * BLOCK)] += dkv[: 3 * BLOCK]
            dlead_ref[m] += dkv[3 * BLOCK : 5 * BLOCK]
        return 0

    lax.fori_loop(0, batches * blocks // 2, step, 0)
    for m in range(batches):
        ret_low_ref[m] = dext_ref[m, :BLOCK].astype(BF16)
        dkv_ref[m] = dext_ref[m, BLOCK : BLOCK + per]
        ret_high_ref[m] = dext_ref[m, BLOCK + per :].astype(BF16)
        dlead0_ref[m] = dlead_ref[m, :BLOCK]
        dlead1_ref[m] = dlead_ref[m, BLOCK:]


def lead_bwd_kernel(
    meta_ref, lead0_ref, lead1_ref, kv_ref, bias_ref, sparse_ref, dlead0_ref, dlead1_ref, do0_ref, do1_ref,
    dkv_ref, mine_ref, given_ref,
):
    low = meta_ref[3]
    for m in range(kv_ref.shape[0]):
        grads = jnp.concatenate([do0_ref[m], do1_ref[m]], 0)
        lse, delta = row_stats(grads[:, 2 * HD :])
        queries = jnp.concatenate([lead0_ref[m, :, : 4 * HD], lead1_ref[m, :, : 4 * HD]], 0)
        queries, grads = stack(queries, Q_LANES), stack(grads, O_LANES)
        keys, values = kv_ref[m, :, K_PART], kv_ref[m, :, V_PART]
        prob = jnp.exp(dot_nt(queries, keys) + bias_ref[m] - jnp.concatenate(lse, 0))
        ds = (prob * (dot_nt(grads, values) - jnp.concatenate(delta, 0))).astype(BF16)
        dq = unstack(dot_nn(ds, keys), Q_LANES)
        for part_ref, first in ((mine_ref, low == 1), (given_ref, low == 0)):
            part_ref[m, :, : 4 * HD] = jnp.where(first, dq[:BLOCK], dq[BLOCK:]).astype(BF16)
            part_ref[m, :, 4 * HD :] = jnp.where(first, dlead0_ref[m], dlead1_ref[m]).astype(BF16)
        dkv_ref[m] = sparse_ref[m] + kv_grad(dot_tn(prob.astype(BF16), grads), dot_tn(ds, queries))


def split_rows(meta_ref, grad_ref, keep_ref, send_ref, lanes=slice(None)):
    count, rows, _ = keep_ref.shape
    even = (meta_ref[4] & 1) == 0
    for z in range(count):
        one = grad_ref[2 * z * rows : (2 * z + 1) * rows, lanes].astype(BF16)
        two = grad_ref[(2 * z + 1) * rows : (2 * z + 2) * rows, lanes].astype(BF16)
        keep_ref[z] = jnp.where(even, one, two)
        send_ref[z] = jnp.where(even, two, one)


def ffn_grad_kernel(groups, seqs, per, share, meta_ref, og_ref, *refs):
    count = 4 * groups
    ups, acts, pres = (refs[n * count : (n + 1) * count] for n in range(3))
    keep0_ref, send0_ref, keep1_ref, send1_ref, left_ref, right_ref, grad_ref = refs[3 * count :]
    piece = seqs * share
    hidden = ups[0].shape[1]
    for g in range(groups):
        for k in range(4):
            for m in range(seqs):
                row = (g * seqs + m) * per + (meta_ref[0] ^ SWAP[k]) * share
                rows = pl.ds(pl.multiple_of(row, share), share)
                right_ref[rows] = ups[4 * g + k][m * share : (m + 1) * share]
    grad_ref[:, :hidden] = dot_tn(og_ref[...], right_ref[...])
    for n in range(count):
        left_ref[n * piece : (n + 1) * piece] = acts[n][...]
        right_ref[n * piece : (n + 1) * piece] = pres[n][...]
    grad_ref[:, hidden:] = dot_tn(left_ref[...], right_ref[...])
    split_rows(meta_ref, grad_ref, keep0_ref, send0_ref, slice(0, hidden))
    split_rows(meta_ref, grad_ref, keep1_ref, send1_ref, slice(hidden, 2 * hidden))


def fold_kernel(count, meta_ref, *refs):
    pairs, out_refs = refs[: 2 * count], refs[2 * count :]
    z = meta_ref[4] >> 1
    for n, ref in enumerate(out_refs):
        at = 0
        for keep_ref, got_ref in zip(pairs[::2], pairs[1::2]):
            lanes = keep_ref.shape[2]
            total = keep_ref[z ^ n].astype(F32) + got_ref[z ^ n].astype(F32)
            ref[:, at : at + lanes] = total.astype(ref.dtype)
            at += lanes


def slots_kernel(
    index_ref, valid_ref, q_got_ref, do_got_ref, kv_ref, column_ref, dkv_ref, acc_ref
):
    acc_ref[...] = dkv_ref[...]

    def block_grads(c):
        at = index_ref[c]
        live = valid_ref[c] == 1
        kv = kv_ref[at]
        grads = do_got_ref[c]
        stats = jnp.transpose(grads[:, 2 * HD :].astype(F32))
        lse = [stats[h : h + 1] + stats[3 + h : 4 + h] for h in range(3)]
        delta = [stats[6 + h : 7 + h] + stats[9 + h : 10 + h] for h in range(3)]
        queries, grads = stack(q_got_ref[c], Q_LANES), stack(grads, O_LANES)
        bias = column_ref[at][:, : 3 * BLOCK]
        prob = jnp.exp(dot_nt(kv[:, K_PART], queries) + bias - jnp.concatenate(lse, 1))
        prob = jnp.where(live, prob, 0.0)
        ds = prob * (dot_nt(kv[:, V_PART], grads) - jnp.concatenate(delta, 1))
        return at, kv_grad(dot_nn(prob.astype(BF16), grads), dot_nn(ds.astype(BF16), queries))

    slots = q_got_ref.shape[0]
    wide = 8 if slots % 8 == 0 else 1

    def slot(j, _):
        done = [block_grads(wide * j + n) for n in range(wide)]
        for at, grad in done:
            acc_ref[at] += grad
        return 0

    lax.fori_loop(0, slots // wide, slot, 0)


def tail_kernel(
    groups, seqs, per, share, devices, meta_ref, dq_ref, dkv_ref, ret_low_ref, ret_high_ref, first_ref, first0_ref,
    first1_ref, mine_ref, given_ref, *refs,
):
    pieces, mixed_refs = refs[: 4 * groups], refs[4 * groups : 5 * groups]
    w_ref, gain_ref, shift_ref = refs[5 * groups : 5 * groups + 3]
    count = 4
    sums_refs = refs[5 * groups + 3 : 6 * groups + 3]
    ends_refs, back_refs = refs[6 * groups + 3 : -count - 5], refs[-count - 5 : -5]
    keep_ref, send_ref, gqkv_ref, grad_ref, left_ref = refs[-5:]
    blocks = per // BLOCK
    batches = dkv_ref.shape[0] // blocks
    gqkv_ref[:, : 4 * HD] = dq_ref[...].reshape(-1, 4 * HD).astype(BF16)
    gqkv_ref[:, 4 * HD :] = dkv_ref[...].reshape(-1, 6 * HD).astype(BF16)
    for m in range(batches):
        i = m * blocks
        low, high = ret_low_ref[m].astype(F32), ret_high_ref[m].astype(F32)
        if blocks == 1:
            gqkv_ref[i * BLOCK : (i + 1) * BLOCK, 4 * HD :] = (dkv_ref[i] + low + high).astype(BF16)
        else:
            j = i + blocks - 1
            gqkv_ref[i * BLOCK : (i + 1) * BLOCK, 4 * HD :] = (dkv_ref[i] + low).astype(BF16)
            gqkv_ref[j * BLOCK : (j + 1) * BLOCK, 4 * HD :] = (dkv_ref[j] + high).astype(BF16)
    lead = meta_ref[3] == 1
    rows = batches * BLOCK
    mine, given = mine_ref[...].reshape(rows, 10 * HD), given_ref[...].reshape(rows, 10 * HD)
    ends = jnp.concatenate([jnp.where(lead, mine, given), jnp.where(lead, given, mine)], 0)
    firsts = jnp.concatenate([first0_ref[...], first1_ref[...]], 0)
    grad = dot_tn(first_ref[...], gqkv_ref[...]) + dot_tn(firsts, ends)
    grad_ref[:, : 10 * HD] = grad
    columns = jnp.sum(gqkv_ref[...].astype(F32), 0, keepdims=True)
    columns = columns + jnp.sum(ends.astype(F32), 0, keepdims=True)
    weights = w_ref[...].astype(F32)
    along = jnp.sum(grad * weights, -1, keepdims=True)
    shift_sum = jnp.sum(columns * weights, -1, keepdims=True)
    rows_in = [gain_ref[...][None], shift_ref[...][None]]
    rows_in += [sum(ref[n : n + 1] for ref in sums_refs) for n in range(2)]
    rows_in.append(jnp.zeros((4, grad.shape[0]), F32))
    gain, shift, gain2_sum, shift2_sum = (
        jnp.transpose(jnp.concatenate(rows_in, 0))[:, n : n + 1] for n in range(4)
    )
    stats = lanes_of([(along - shift * shift_sum) / gain, shift_sum, gain2_sum, shift2_sum], grad.shape[0])
    lane = lax.broadcasted_iota(jnp.int32, stats.shape, 1)
    moved = jnp.concatenate([stats[:, HD:], stats[:, :HD]], 1)
    grad_ref[:, : 2 * HD] = jnp.where(lane < HD, grad[:, : 2 * HD], moved)
    piece = pieces[0].shape[0]
    total = 0.0
    for g in range(groups):
        for k in range(4):
            left_ref[k * piece : (k + 1) * piece] = pieces[4 * g + k][...]
        total = total + dot_tn(left_ref[...], mixed_refs[g][...])
    grad_ref[:, 10 * HD :] = total
    split_rows(meta_ref, grad_ref, keep_ref, send_ref)
    for end, b in ((1, 0), (2, blocks - 1)):

        @pl.when(meta_ref[end] == 1)
        def _(b=b):
            for m in range(groups * seqs):
                rows = slice(m * per + b * BLOCK, m * per + (b + 1) * BLOCK)
                total = gqkv_ref[rows].astype(F32)
                for ref in ends_refs:
                    total = total + ref[m].astype(F32)
                gqkv_ref[rows] = total.astype(BF16)

    for g in range(groups):
        for k in range(4):
            for m in range(seqs):
                row = (g * seqs + m) * per + (meta_ref[0] ^ SWAP[k]) * share
                rows = pl.ds(pl.multiple_of(row, share), share)
                back = dot_nt(gqkv_ref[rows], w_ref[...]).astype(BF16)
                back_refs[k][(g * seqs + m) * share : (g * seqs + m + 1) * share] = back


def swap_tp(value, bit):
    return lax.ppermute(value, "tp", [(i, i ^ bit) for i in range(lax.axis_size("tp"))])


def scatter_tp(parts):
    far = swap_tp(parts[3], 1)
    near = swap_tp(parts[2], 1)
    both = (parts[1].astype(F32) + far.astype(F32)).astype(BF16)
    return parts[0], near, swap_tp(both, 2)


def gather_tp(piece, before_first=(), before_last=()):
    cross = swap_tp(after(piece, *before_first) if before_first else piece, 2)
    return piece, cross, swap_tp(piece, 1), swap_tp(after(cross, *before_last) if before_last else cross, 1)


def mirrored(pairs, last):
    return pairs + [(last - a, last - b) for a, b in pairs]


SECOND = [(1, 3), (4, 5), (2, 6), (0, 7)]


def in_first_group(myself, devices):
    if devices == 8:
        return (myself == 0) | (myself == 1) | (myself == 2) | (myself == 4)
    return myself < devices // 2


def spread(own, myself, devices, *before_last):
    last = devices - 1
    held = own
    if devices == 8:
        for k in (1, 2, 4):
            held = held + lax.ppermute(own, "seq", mirrored([(0, k)], last))
        held = after(held, *before_last)
        other = lax.ppermute(held, "seq", mirrored(SECOND, last))
    else:
        bit = 1
        while bit < devices // 2:
            held = held + lax.ppermute(held, "seq", mirrored([(i, i + bit) for i in range(bit)], last))
            bit *= 2
        other = lax.ppermute(held, "seq", [(i, i ^ bit) for i in range(devices)])
    first = in_first_group(myself, devices)
    return jnp.where(first, held, other), jnp.where(first, other, held), other


def collect_first(given, devices):
    last = devices - 1
    if devices == 8:
        return lax.ppermute(given, "seq", mirrored([(b, a) for a, b in SECOND], last))
    return lax.ppermute(given, "seq", [(i, i ^ (devices // 2)) for i in range(devices)])


def collect_rest(mine, devices, join):
    last = devices - 1
    if devices == 8:
        return [mine] + [lax.ppermute(mine, "seq", mirrored([(k, 0)], last)) for k in (1, 2, 4)]
    bit = devices // 2
    while bit > 1:
        bit //= 2
        mine = join(mine, lax.ppermute(mine, "seq", mirrored([(i + bit, i) for i in range(bit)], last)))
    return [mine]


def to_owners(slots):
    return lax.all_to_all(slots, "seq", split_axis=0, concat_axis=0, tiled=True)


def sum_seq_first(send, devices):
    return lax.ppermute(send, "seq", [(i, i ^ 1) for i in range(devices)])


def sum_seq_rest(pairs, meta, devices):
    count, rows = pairs[0][0].shape[:2]
    lanes = sum(keep.shape[2] for keep, _ in pairs)
    if count == 4:
        low = sds((rows, lanes), BF16)
        own, *out = call(
            partial(fold_kernel, len(pairs)), (sds((rows, lanes), F32), low, low, low), name="fold"
        )(*(v for pair in pairs for v in pair), smem=(meta,))
        return [own] + [
            lax.ppermute(piece, "seq", [(i, i ^ (2 * (n + 1))) for i in range(devices)])
            for n, piece in enumerate(out)
        ]
    total = [(keep.astype(F32) + got.astype(F32)).astype(BF16) for keep, got in pairs]
    return across(jnp.concatenate(total, 2), devices)


def across(total, devices):
    sides = [[i for i in range(devices) if i % 2 == side] for side in range(2)]
    got = lax.all_to_all(
        total, "seq", split_axis=0, concat_axis=0, tiled=True, axis_index_groups=sides
    )
    return [got[n] for n in range(total.shape[0])]


def sum_of(terms):
    total = terms[0].astype(F32)
    for term in terms[1:]:
        total = total + term.astype(F32)
    return total


def per_device(
    layer_input,
    out_grad,
    norm1_gain,
    norm1_shift,
    w_qkv,
    w_out,
    norm2_gain,
    norm2_shift,
    w_up,
    w_down,
    key_keep,
    rand_blocks,
):
    batches, per, width = layer_input.shape
    local = w_qkv.shape[2]
    devices = lax.axis_size("seq")
    myself = lax.axis_index("seq")
    tp_count = lax.axis_size("tp")
    tp_place = lax.axis_index("tp")
    assert local == 3 * HD and tp_count == 4 and devices % 2 == 0 and batches % 2 == 0
    share = per // tp_count
    bd = per // BLOCK
    total = batches * bd
    blocks_all = bd * devices
    groups = 2
    seqs = batches // groups
    piece = seqs * share
    refs = total * RANDS
    slots_per = max(1, -(-refs // devices))
    slots = devices * slots_per
    hidden_here = w_up.shape[1]
    rows = width // devices
    i32 = jnp.int32
    flag = lambda v: v.astype(i32)
    meta = jnp.stack(
        [
            tp_place, flag(myself == 0), flag(myself == devices - 1), flag(in_first_group(myself, devices)), myself,
        ]
    ).astype(i32)

    CHAIN.last = ()
    scale = 1.0 / math.sqrt(HD)
    x_rows = layer_input.reshape(batches * per, width)
    first, q, kv, w640 = CHAIN.done(project(x_rows, norm1_gain, norm1_shift, w_qkv.transpose(1, 0, 2)))
    is_first, is_last = myself == 0, myself == devices - 1
    ends = jnp.where(is_first, layer_input[:, :BLOCK], layer_input[:, per - BLOCK :])
    ends = jnp.where(is_first | is_last, ends, jnp.zeros_like(ends))
    lead_x0, lead_x1, arrived = spread(ends, myself, devices, kv)
    q_blocks = q.reshape(total, BLOCK, 4 * HD)
    kv_blocks = kv.reshape(total, BLOCK, 6 * HD)
    kv_seqs = kv.reshape(batches, per, 6 * HD)

    table = (
        rand_blocks.reshape(batches, devices, bd, RANDS).transpose(1, 0, 2, 3).reshape(devices, refs)
    )
    owners = table // bd
    source = (jnp.arange(refs, dtype=i32) // (bd * RANDS))[None] * bd + table - owners * bd
    order = jnp.arange(refs, dtype=i32)
    earlier = order[None, :] < order[:, None]
    rank = jnp.sum(((owners[:, :, None] == owners[:, None, :]) & earlier[None]).astype(i32), -1)
    places = jnp.arange(slots_per, dtype=i32)
    asked = (owners == myself)[:, None, :] & (rank[:, None, :] == places[None, :, None])
    source_of = jnp.sum(jnp.where(asked, source[:, None, :], 0), -1).reshape(slots)
    valid = jnp.sum(asked.astype(i32), -1).reshape(slots)
    my_owner = lax.dynamic_index_in_dim(owners, myself, 0, False)
    my_rank = lax.dynamic_index_in_dim(rank, myself, 0, False)
    slot_of = my_owner * slots_per + my_rank
    mine = lax.dynamic_index_in_dim(table, myself, 0, False)
    query_of = jnp.sum(
        jnp.where(
            slot_of[None, :] == jnp.arange(slots, dtype=i32)[:, None], (order // RANDS)[None, :], 0
        ),
        -1,
    )

    end_kv = sds((batches, BLOCK, 6 * HD), BF16)
    end_all = sds((batches, BLOCK, 10 * HD), BF16)
    sent, kv_low, kv_high = call(
        partial(dispatch_kernel, bd),
        (sds((slots, BLOCK, 6 * HD), BF16), end_kv, end_kv),
        name="dispatch",
    )(kv_blocks, smem=(source_of,))
    rand_kv = to_owners(after(sent, arrived))
    up = [(i, i + 1) for i in range(devices - 1)]
    down = [(b, a) for a, b in up]
    low = lax.ppermute(kv_high, "seq", up)
    high = lax.ppermute(kv_low, "seq", down)

    bias, seq_bias, column_bias, wo256 = call(
        partial(bias_kernel, bd, blocks_all),
        (
            sds((total, 1, 8 * BLOCK), F32),
            sds((batches, 1, per), F32),
            sds((total, BLOCK, 4 * HD), F32),
            sds((width, 4 * HD), BF16),
        ),
        name="bias",
    )(key_keep.reshape(batches * blocks_all, BLOCK), w_out, smem=(mine, meta))

    grad_up = dot_nn(out_grad.reshape(batches * per, width), w_down)
    grad_up = grad_up.reshape(batches, per, hidden_here)

    part = sds((batches, BLOCK, 4 * HD), F32)
    low_piece = sds((piece, width), BF16)
    low_pieces = sds((groups * piece, width), BF16)
    high_piece = sds((piece, width), F32)
    attn, lse = [], []

    def attend(g):
        half_of = lambda array: part_of(array, g, groups)
        out, stat = call(
            partial(sparse_fwd_kernel, g * seqs * bd, seqs, per, share),
            (sds((4 * piece, 4 * HD), BF16), sds((seqs * per, 2 * HD), F32)),
            (
                pltpu.VMEM((seqs, per + 2 * BLOCK, 6 * HD), BF16),
                pltpu.VMEM((2, 8 * BLOCK, 6 * HD), BF16),
            ),
            name="sparse_fwd",
        )(
            half_of(q_blocks), half_of(kv_seqs), half_of(low), half_of(high), half_of(lead0), half_of(lead1),
            rand_kv, half_of(bias), smem=(slot_of, meta),
        )
        attn.append(out)
        lse.append(stat)

    lead_rows = sds((batches * BLOCK, width), BF16)
    lead_first0, lead_first1, lead0, lead1, part_mine, part_given = call(
        lead_fwd_kernel, (lead_rows, lead_rows, end_all, end_all, part, part), name="lead_fwd"
    )(kv_seqs, after(seq_bias, grad_up), lead_x0, lead_x1, norm1_gain, norm1_shift, w640, smem=(meta,))
    part_got = collect_first(part_given, devices)
    q_slots = call(gather_kernel, sds((slots, BLOCK, 4 * HD), BF16), name="gather")(q_blocks, smem=(query_of,))
    rand_q = to_owners(after(q_slots, rand_kv, part_got, low, high))
    attend(0)
    lead_parts = collect_rest(merge(part_mine, part_got), devices, merge)
    attend(1)
    lead_out, lead_lse = call(
        lead_finish_kernel,
        (sds(part.shape, BF16), sds((batches, BLOCK, 2 * HD), F32)),
        name="lead_finish",
        limit=SMALL,
    )(*lead_parts)
    out = call(
        partial(out_project_kernel, groups, seqs, per, share),
        (sds((4 * piece, 4 * HD), BF16),) * groups + (low_piece,) * (4 * groups),
        name="out_project",
    )(wo256, lead_out, *attn, smem=(meta,))
    mixed = out[:groups]
    attn_parts = [scatter_tp(out[groups + 4 * g : groups + 4 * g + 4]) for g in range(groups)]

    flat = lambda lists: [v for group in lists for v in group]
    hidden, act, total_grad, sums2, attn_grad = [], [], [], [], []
    ups, pres, back_parts, down_parts = [], [], [], []
    for g in range(groups):
        h, a = share_call(mid_fwd_kernel, (high_piece, low_piece), [(layer_input, g, 0)], "mid_fwd")(
            meta, seqs, share, *attn_parts[g], norm2_gain, norm2_shift
        )
        hidden.append(h)
        act.append(gather_tp(a, attn_parts[-1][2:]))
    low_hidden = sds((piece, hidden_here), BF16)
    for g in range(groups):
        out = share_call(
            ffn_kernel, (low_hidden, low_hidden, low_piece) * 4, [(grad_up, g, k) for k in range(4)], "ffn", MIDDLE
        )(meta, seqs, share, *act[g], w_up)
        ups.append(out[0::3])
        pres.append(out[1::3])
        back_parts.append(scatter_tp(out[2::3]))
    for g in range(groups):
        t, a, s = share_call(
            mid_bwd_kernel, (high_piece, low_piece, sds((2, width), F32)), [(out_grad, g, 0)], "mid_bwd"
        )(meta, seqs, share, *back_parts[g], hidden[g], norm2_gain)
        total_grad.append(t)
        sums2.append(s)
        if g == 0:
            down_parts = call(partial(down_kernel, groups), (low_pieces,) * 4, name="down", limit=MIDDLE)(*flat(ups), w_down)
            attn_grad.append(gather_tp(a))
        if g == groups - 1:
            halves = sds((devices // 2, rows, hidden_here), BF16)
            ff_keep0, ff_send0, ff_keep1, ff_send1 = call(
                partial(ffn_grad_kernel, groups, seqs, per, share),
                (halves,) * 4,
                (
                    pltpu.VMEM((batches * per, width), BF16),
                    pltpu.VMEM((batches * per, hidden_here), BF16),
                    pltpu.VMEM((width, 2 * hidden_here), F32),
                ),
                name="ffn_grad",
                limit=MIDDLE,
            )(
                out_grad.reshape(batches * per, width), *flat(ups), *flat(act), *flat(pres), smem=(meta,)
            )
            attn_grad.append(gather_tp(a, (), (ff_send0,)))
            ff_got0 = sum_seq_first(after(ff_send0, attn_grad[-1][1]), devices)

    lead_grad = call(
        partial(lead_grad_kernel, groups, seqs, per, share),
        sds((batches, BLOCK, 4 * HD), BF16),
        (pltpu.VMEM((batches * BLOCK, width), BF16),),
        name="lead_grad",
        limit=SMALL,
    )(wo256, lead_lse, lead_out, *flat(attn_grad), smem=(meta,))
    grads, sent = call(
        partial(heads_grad_kernel, groups, seqs, per, share),
        (sds((batches * per, 4 * HD), BF16), sds((slots, BLOCK, 4 * HD), BF16)),
        name="heads_grad",
        limit=MIDDLE,
    )(wo256, *flat(attn_grad), *mixed, *lse, smem=(query_of, meta))
    *lead_do, arrived = spread(lead_grad, myself, devices, sent)
    rand_do = to_owners(after(sent, arrived, rand_q, ff_got0))
    ff_got1 = sum_seq_first(after(ff_send1, arrived), devices)
    dend = sds(end_kv.shape, F32)
    dq, dkv, ret_low, ret_high, dlead0, dlead1 = call(
        partial(sparse_bwd_kernel, batches, per),
        (sds((total, BLOCK, 4 * HD), F32), sds((batches, per, 6 * HD), F32), end_kv, end_kv, dend, dend),
        (
            pltpu.VMEM((batches, per + 2 * BLOCK, 6 * HD), BF16),
            pltpu.VMEM((2, 8 * BLOCK, 6 * HD), BF16),
            pltpu.VMEM((batches, per + 2 * BLOCK, 6 * HD), F32),
            pltpu.VMEM((batches, 2 * BLOCK, 6 * HD), F32),
        ),
        name="sparse_bwd",
    )(
        q_blocks, kv_seqs, low, high, lead0, lead1, rand_kv, bias,
        after(grads, *lead_do).reshape(total, BLOCK, 4 * HD), smem=(slot_of,),
    )
    from_low = lax.ppermute(ret_high, "seq", up)
    from_high = lax.ppermute(ret_low, "seq", down)
    dkv, ends_mine, ends_given = call(
        lead_bwd_kernel, (sds((batches, per, 6 * HD), F32), end_all, end_all), name="lead_bwd"
    )(lead0, lead1, kv_seqs, seq_bias, dkv, dlead0, dlead1, *lead_do, smem=(meta,))
    add = lambda a, b: (a.astype(F32) + b.astype(F32)).astype(BF16)
    ends_first = collect_first(ends_given, devices)
    ends_got = collect_rest(add(after(ends_mine, from_low, from_high), ends_first), devices, add)

    dkv = call(slots_kernel, sds((total, BLOCK, 6 * HD), F32), name="slots")(
        rand_q, rand_do, kv_blocks, column_bias,
        dkv.reshape(total, BLOCK, 6 * HD), smem=(source_of, valid),
    )
    ff_half = jnp.concatenate(
        [
            (keep.astype(F32) + got.astype(F32)).astype(BF16)
            for keep, got in ((ff_keep0, ff_got0), (after(ff_keep1, dkv), after(ff_got1, dkv)))
        ],
        2,
    )
    ff = across(after(ff_half, *ends_got), devices)
    halves = sds((devices // 2, rows, 14 * HD), BF16)
    *first_back, qkv_keep, qkv_send = call(
        partial(tail_kernel, groups, seqs, per, share, devices),
        (low_pieces,) * 4 + (halves, halves),
        (
            pltpu.VMEM((total * BLOCK, 10 * HD), BF16),
            pltpu.VMEM((width, 14 * HD), F32),
            pltpu.VMEM((4 * piece, width), BF16),
        ),
        name="tail",
    )(
        dq, dkv, from_low, from_high, first, lead_first0, lead_first1, ends_mine, ends_given,
        *flat(attn_grad), *mixed, w640, norm1_gain, norm1_shift, *sums2, *ends_got, smem=(meta,),
    )
    qkv_got = sum_seq_first(qkv_send, devices)
    terms = scatter_tp(first_back)
    out_terms = scatter_tp([after(part, first_back[0]) for part in down_parts])
    ff = sum_of(ff)
    gq = sum_seq_rest([(qkv_keep, after(qkv_got, ff))], meta, devices)
    input_grad = share_call(
        partial(end_kernel, groups),
        sds((batches, share, width), F32),
        [(layer_input, g, 0) for g in range(groups)],
        "end",
    )(meta, seqs, share, *terms, *total_grad, norm1_gain)
    layer_output = call(
        partial(output_kernel, groups), sds((batches, share, width), F32), name="output", limit=SMALL
    )(*out_terms, *hidden)

    g_down, g_up = ff[:, :hidden_here], ff[:, hidden_here:]
    gq = sum_of(gq)
    norms = gq[:, HD : 2 * HD]
    norms = norms + swap_tp(norms, 1)
    norms = norms + swap_tp(norms, 2)
    g_out = jnp.concatenate([gq[:, 10 * HD : 12 * HD], gq[:, 13 * HD :]], 1)
    g_qkv = jnp.stack(
        [
            jnp.concatenate([gq[:, 2 * HD : 4 * HD], gq[:, :HD]], 1) * scale,
            jnp.concatenate([gq[:, 8 * HD : 10 * HD], gq[:, 6 * HD : 7 * HD]], 1),
            jnp.concatenate([gq[:, 4 * HD : 6 * HD], gq[:, 7 * HD : 8 * HD]], 1),
        ],
        1,
    )
    return (
        layer_output, input_grad, g_qkv, g_out, g_up, g_down, norms[:, 0], norms[:, 1], norms[:, 2], norms[:, 3],
    )


def solution(mesh):
    return jax.shard_map(
        per_device,
        mesh=mesh,
        in_specs=(
            P(None, "seq", None),
            P(None, "seq", None),
            P(),
            P(),
            P(None, None, "tp"),
            P(None, "tp"),
            P(),
            P(),
            P(None, "tp"),
            P(None, "tp"),
            P(),
            P(),
        ),
        out_specs=(
            P(None, ("seq", "tp"), None),
            P(None, ("seq", "tp"), None),
            P("seq", None, "tp"),
            P("seq", "tp"),
            P("seq", "tp"),
            P("seq", "tp"),
            P("seq"),
            P("seq"),
            P("seq"),
            P("seq"),
        ),
        check_vma=False,
    )
```
